32 devices in a mesh: mapx: 8 (over z, x), mapy: 2 (over y), layer: 2 (over core).
Axes of the slice: x: 2, y: 2, z: 4, core: 2. Of those that a mesh axis runs over, the one named last changes fastest.
Arguments:
- old_state: float32 [8, 2, 2, 6, 8192], P('mapx', 'mapy', 'layer'), as said below
- send_blocks: int32 [8, 2, 2, 10, 16], P('mapx', 'mapy', 'layer'), may hold values from 0 to 63
- node_slots: int32 [8, 2, 2, 4, 512], P('mapx', 'mapy', 'layer'), may hold values from 0 to 20479, as said below
- node_weights: float32 [8, 2, 2, 4, 512], P('mapx', 'mapy', 'layer'), as said below
- front_mask: int32 [8, 2, 2, 512], P('mapx', 'mapy', 'layer'), may hold values 0 or 1
- halo_lists: int32 [8, 2, 2, 6, 256], P('mapx', 'mapy', 'layer'), may hold values from 0 to 511
- elem_nodes: int32 [8, 2, 2, 4, 2560], P('mapx', 'mapy', 'layer'), may hold values from 0 to 2047
- shape_grads: float32 [8, 2, 2, 12, 2560], P('mapx', 'mapy', 'layer'), as said below
- elem_volume: float32 [8, 2, 2, 2560], P('mapx', 'mapy', 'layer'), may hold values from 0.5 to 2
Outputs:
- new_state: float32 [8, 2, 2, 6, 512], P('mapx', 'mapy', 'layer')
- residual: float32 [8, 2, 2, 4, 512], P('mapx', 'mapy', 'layer')
The draws below stay inside these ranges and needn't reach their ends.
Inputs may be any that keep to these rules, and one draw needn't show every extreme that they name: `send_blocks`: each entry names one of the sender's old blocks; a block may go to several peers or twice to one. `node_slots`: indexes the received nodes, ordered by source (mapx offset plus 2, times 2, plus layer index), then slot, then node in the block; only sources inside the device grid are named. `node_weights`: Positive; the four weights of a node sum to one. `halo_lists`: owned nodes kept as ghosts by the neighbour in direction k. `elem_nodes`: local numbering: the owned nodes first, then 256 ghosts for each of the six directions in order. `shape_grads`: the four gradients of an element sum to zero. `old_state`: rows 0 to 3 velocity and pressure, row 4 temperature in [-1, 0], row 5 damage in [0, 0.9].
All inputs are finite; a program needn't handle non-finite values. No bound on the sum of `front_mask` on one device may be relied on, other than what follows from the above.
Results may differ from the reference program's by a relative error of at most 0.00002.
Values sent between devices are 32-bit elements; how exact they have to be, the bound alone decides.
No kernel may reach another device: no remote copies, remote signals or barrier semaphores. Data moves between devices by JAX's collectives and lax.ppermute only.
A program may use at most 64 MiB of HBM per device.

```python
import math
import jax
import jax.numpy as jnp
from jax import lax

BLOCK = 128
REACH = 2
OLD_BLK = 64
CAP_PEER = 16
HALO = 256
OLD_NODES = 8192
NEW_NODES = 512
ELEMS = 2560
PEERS = 10
N_MAPX = 8
N_MAPY = 2
N_LAYER = 2


def draw_old_state(key, part):
    first, second, third = jax.random.split(key, 3)
    dims_flow = (N_MAPX, N_MAPY, N_LAYER, 4, OLD_NODES)
    dims_one = (N_MAPX, N_MAPY, N_LAYER, 1, OLD_NODES)
    flow = jax.random.normal(first, dims_flow, jnp.float32)
    temper = jax.random.uniform(second, dims_one, jnp.float32, -1.0, 0.0)
    damage = jax.random.uniform(third, dims_one, jnp.float32, 0.0, 0.9)
    return jnp.concatenate([flow, temper, damage], axis=3)


def draw_node_slots(key, part):
    first, second, third, fourth = jax.random.split(jax.random.fold_in(key, 7), 4)
    dims_all = (N_MAPX, N_MAPY, N_LAYER, 4, NEW_NODES)
    column = jnp.arange(N_MAPX, dtype=jnp.int32).reshape(N_MAPX, 1, 1, 1, 1)
    lowest = jnp.maximum(-REACH, -column)
    highest = jnp.minimum(REACH, N_MAPX - 1 - column)
    lowest = jnp.broadcast_to(lowest, dims_all)
    highest = jnp.broadcast_to(highest, dims_all)
    offset = jax.random.randint(first, dims_all, lowest, highest + 1)
    source_layer = jax.random.randint(second, dims_all, 0, N_LAYER)
    slot = jax.random.randint(third, dims_all, 0, CAP_PEER)
    within = jax.random.randint(fourth, dims_all, 0, BLOCK)
    return ((((offset + REACH) * N_LAYER + source_layer) * CAP_PEER + slot) * BLOCK + within).astype(jnp.int32)


def draw_node_weights(key, part):
    dims_all = (N_MAPX, N_MAPY, N_LAYER, 4, NEW_NODES)
    raw = jax.random.uniform(key, dims_all, jnp.float32, 0.2, 1.0)
    return raw / jnp.sum(raw, axis=3, keepdims=True)


def draw_shape_grads(key, part):
    dims_three = (N_MAPX, N_MAPY, N_LAYER, 3, 3, ELEMS)
    three = jax.random.normal(key, dims_three, jnp.float32)
    fourth = -(three[:, :, :, 0:1] + three[:, :, :, 1:2] + three[:, :, :, 2:3])
    return jnp.concatenate([three, fourth], axis=3).reshape(N_MAPX, N_MAPY, N_LAYER, 12, ELEMS)


def touch_ends(values, own_key, smallest, top_value):
    shape = values.shape
    spot = [jax.random.randint(jax.random.fold_in(own_key, axis), (), 0, shape[axis]) for axis in range(len(shape))]
    values = values.at[tuple(spot)].set(smallest)
    longest = shape.index(max(shape))
    spot[longest] = (spot[longest] + 1) % shape[longest]
    return values.at[tuple(spot)].set(top_value)


def shard_levels(rng, dims, cuts, least, largest):
    factor_of, own = 1.0, jax.random.fold_in(rng, 6)
    for axis_at, parts in cuts:
        heights = jnp.exp(jax.random.uniform(jax.random.fold_in(own, axis_at), (parts,), jnp.float32, least / len(cuts), largest / len(cuts)))
        factor_of = factor_of * jnp.repeat(heights, dims[axis_at] // parts).reshape([-1 if axis == axis_at else 1 for axis in range(len(dims))])
    return factor_of


def setup_inputs(seed: int = 0) -> dict:
    key_of = jax.random.split(jax.random.key(seed), 10)
    old_state = draw_old_state(jax.random.fold_in(key_of[9], 71), 0)
    send_blocks = touch_ends(jax.random.randint(key_of[1], (N_MAPX, N_MAPY, N_LAYER, PEERS, CAP_PEER), 0, OLD_BLK), jax.random.fold_in(key_of[1], 1), 0, OLD_BLK - 1).astype(jnp.int32)
    node_slots = draw_node_slots(jax.random.fold_in(key_of[9], 71), 0)
    node_weights = draw_node_weights(jax.random.fold_in(key_of[9], 71), 0)
    front_mask = touch_ends((jax.random.randint(key_of[4], (N_MAPX, N_MAPY, N_LAYER, NEW_NODES), 0, 8) < 1).astype(jnp.int32), jax.random.fold_in(key_of[4], 1), 0, 1)
    halo_lists = touch_ends(jax.random.randint(key_of[5], (N_MAPX, N_MAPY, N_LAYER, 6, HALO), 0, NEW_NODES), jax.random.fold_in(key_of[5], 1), 0, NEW_NODES - 1).astype(jnp.int32)
    elem_nodes = touch_ends(jax.random.randint(key_of[6], (N_MAPX, N_MAPY, N_LAYER, 4, ELEMS), 0, NEW_NODES + 6 * HALO), jax.random.fold_in(key_of[6], 1), 0, (NEW_NODES + 6 * HALO) - 1).astype(jnp.int32)
    shape_grads = draw_shape_grads(jax.random.fold_in(key_of[9], 71), 0)
    elem_volume = jnp.clip(jnp.exp(math.log(2.0) - 1.3862944 * jax.random.uniform(key_of[8], (N_MAPX, N_MAPY, N_LAYER, ELEMS), jnp.float32) ** shard_levels(key_of[8], (N_MAPX, N_MAPY, N_LAYER, ELEMS), ((0, 8), (1, 2), (2, 2)), -0.2, 0.2)), 0.5, 2.0)
    return dict(old_state=old_state, send_blocks=send_blocks, node_slots=node_slots, node_weights=node_weights, front_mask=front_mask, halo_lists=halo_lists, elem_nodes=elem_nodes, shape_grads=shape_grads, elem_volume=elem_volume)


ocean_temp = 0.0
strain_reg = 0.01
gravity = 0.5


def element_residual(node_table, elem_nodes, shape_grads, elem_volume):
    values = jnp.take(node_table, elem_nodes, axis=1)
    grads = shape_grads.reshape(4, 3, -1)
    velgrad = jnp.sum(values[:3, :, None, :] * grads[None, :, :, :], axis=1)
    strain = 0.5 * (velgrad + jnp.transpose(velgrad, (1, 0, 2)))
    second = 0.5 * jnp.sum(strain * strain, axis=(0, 1))
    means = jnp.mean(values[3:], axis=1)
    viscosity = 0.5 * (1.0 - means[2]) * jnp.exp(-means[1]) * (second + strain_reg) ** (-1.0 / 3.0)
    stress = 2.0 * viscosity * strain - means[0] * jnp.eye(3, dtype=strain.dtype)[:, :, None]
    momentum = elem_volume * jnp.sum(stress[None, :, :, :] * grads[:, None, :, :], axis=2)
    upward = jnp.array([0.0, 0.0, 1.0], dtype=momentum.dtype)
    momentum = momentum + (0.25 * gravity * elem_volume)[None, None, :] * upward[None, :, None]
    divergence = velgrad[0, 0] + velgrad[1, 1] + velgrad[2, 2]
    continuity = 0.25 * elem_volume * divergence
    cont_rows = jnp.broadcast_to(continuity[None, None, :], (4, 1, continuity.shape[0]))
    return jnp.concatenate([momentum, cont_rows], axis=1)


def assemble(contrib, elem_nodes, width):
    total = jnp.zeros((4, width), contrib.dtype)
    for corner in range(4):
        total = total.at[:, elem_nodes[corner]].add(contrib[corner])
    return total


def shift_grid(grid, dim, step):
    extent = grid.shape[dim]
    zero_part = jnp.zeros_like(lax.slice_in_dim(grid, 0, 1, axis=dim))
    if step > 0:
        return jnp.concatenate([zero_part, lax.slice_in_dim(grid, 0, extent - 1, axis=dim)], axis=dim)
    return jnp.concatenate([lax.slice_in_dim(grid, 1, extent, axis=dim), zero_part], axis=dim)


def pull_columns(grid, offset):
    extent = grid.shape[0]
    if offset == 0:
        return grid
    if offset > 0:
        zero_part = jnp.zeros_like(grid[:offset])
        return jnp.concatenate([grid[offset:], zero_part], axis=0)
    zero_part = jnp.zeros_like(grid[:(-offset)])
    return jnp.concatenate([zero_part, grid[:extent + offset]], axis=0)


def take_cols(table, picks):
    return jnp.take(table, picks, axis=1)


def add_cols(target, picks, addend):
    return target.at[:, picks].add(addend)


def interpolate(table, slot_ids, weights):
    return jnp.sum(jnp.take(table, slot_ids, axis=1) * weights[None], axis=1)


def reference(old_state, send_blocks, node_slots, node_weights, front_mask, halo_lists, elem_nodes, shape_grads, elem_volume):
    devices = N_MAPX * N_MAPY * N_LAYER
    spread = 2 * REACH + 1
    directions = [(0, 1), (0, -1), (1, 1), (1, -1), (2, 1), (2, -1)]
    blocks = old_state.reshape(devices, 6, OLD_BLK, BLOCK)
    picks = send_blocks.reshape(devices, PEERS, CAP_PEER)
    outgoing = jax.vmap(take_cols)(blocks, picks)
    outgoing = outgoing.reshape(N_MAPX, N_MAPY, N_LAYER, 6, spread, N_LAYER, CAP_PEER, BLOCK)
    columns = []
    for source in range(spread):
        offset = source - REACH
        slab = outgoing[:, :, :, :, spread - 1 - source]
        slab = pull_columns(slab, offset)
        columns.append(jnp.transpose(slab, (0, 1, 4, 3, 2, 5, 6)))
    received = jnp.stack(columns, axis=4).reshape(devices, 6, PEERS * CAP_PEER * BLOCK)
    slot_ids = node_slots.reshape(devices, 4, NEW_NODES)
    weights = node_weights.reshape(devices, 4, NEW_NODES)
    interpolated = jax.vmap(interpolate)(received, slot_ids, weights)
    temp_row = (jnp.arange(6) == 4)[None, :, None]
    front = (front_mask.reshape(devices, NEW_NODES) == 1)[:, None, :]
    new_state = jnp.where(temp_row & front, ocean_temp, interpolated)
    halos = halo_lists.reshape(devices, 6, HALO)
    pieces = [new_state]
    for index in range(6):
        dim, step = directions[index]
        portion = jax.vmap(take_cols)(new_state, halos[:, index])
        grid = portion.reshape(N_MAPX, N_MAPY, N_LAYER, 6, HALO)
        pieces.append(shift_grid(grid, dim, step).reshape(devices, 6, HALO))
    node_table = jnp.concatenate(pieces, axis=2)
    width = NEW_NODES + 6 * HALO

    def device_residual(inputs):
        table, nodes, grads, volume = inputs
        contrib = element_residual(table, nodes, grads, volume)
        return assemble(contrib, nodes, width)

    assembled = lax.map(device_residual, (node_table, elem_nodes.reshape(devices, 4, ELEMS), shape_grads.reshape(devices, 12, ELEMS), elem_volume.reshape(devices, ELEMS)))
    residual = assembled[:, :, :NEW_NODES]
    for index in range(6):
        dim, step = directions[index]
        start = NEW_NODES + index * HALO
        portion = assembled[:, :, start:start + HALO]
        grid = portion.reshape(N_MAPX, N_MAPY, N_LAYER, 4, HALO)
        arrived = shift_grid(grid, dim, -step).reshape(devices, 4, HALO)
        residual = jax.vmap(add_cols)(residual, halos[:, index], arrived)
    return (new_state.reshape(N_MAPX, N_MAPY, N_LAYER, 6, NEW_NODES), residual.reshape(N_MAPX, N_MAPY, N_LAYER, 4, NEW_NODES))
```

```python
import functools

import jax
import jax.numpy as jnp
from jax import lax
from jax.experimental import pallas as pl
from jax.experimental.pallas import tpu as pltpu
from jax.sharding import PartitionSpec as P

BLOCK = 128
REACH = 2
FIELDS = 6
SPLITS = 3

ocean_temp = 0.0
strain_reg = 0.01
gravity = 0.5

AXES = ("mapx", "mapy", "layer")
VMEM = pl.BlockSpec(memory_space=pltpu.VMEM)
SMEM = pl.BlockSpec(memory_space=pltpu.SMEM)


def params():
    return pltpu.CompilerParams(vmem_limit_bytes=32 * 1024 * 1024)


def place(axis, count):
    return lax.rem(lax.axis_index(axis), 2)


def spread_groups(sizes, base):
    nx, ny, nl = sizes
    number = lambda x, y, l: (x * ny + y) * nl + l
    groups = []
    for first in range(base, nx - 3, 4):
        for y in range(ny):
            groups.append([number(first + i, y, l) for i in range(4) for l in range(nl)])
    if base:
        for first in (0, nx - 2):
            for y in range(0, ny, 2):
                groups.append([number(first + i, y + j, l) for i in range(2) for j in range(2) for l in range(nl)])
    return groups


def pair_groups(sizes):
    nx, ny, nl = sizes
    number = lambda x, y, l: (x * ny + y) * nl + l
    return [
        [number(x + i, y + j, l) for i in range(2) for j in range(2) for l in range(2)]
        for x in range(0, nx, 2)
        for y in range(0, ny, 2)
    ]


def group_swap(chunks, groups):
    return lax.all_to_all(chunks, AXES, split_axis=0, concat_axis=0, axis_index_groups=groups)


def far_swap(value, axis, count):
    pairs = []
    for first in range(1, count - 1, 2):
        pairs += [(first, first + 1), (first + 1, first)]
    return lax.ppermute(value, axis, pairs)


def pack_kernel(blocks_ref, old_ref, near_ref, far_ref):
    slots = blocks_ref.shape[1]
    column = lax.axis_index("mapx")

    def put(out_ref, chunk, peer):
        for c in range(slots):
            start = pl.multiple_of(blocks_ref[peer, c] * BLOCK, BLOCK)
            out_ref[chunk, FIELDS * c : FIELDS * (c + 1), :] = old_ref[:, pl.ds(start, BLOCK)]

    here = lax.rem(column, 4)

    def near(chunk, carry):
        offset = chunk // 2 - here

        @pl.when(jnp.abs(offset) <= REACH)
        def _():
            put(near_ref, chunk, (offset + REACH) * 2 + lax.rem(chunk, 2))

        return carry

    lax.fori_loop(0, 8, near, 0)
    place_far = lax.rem(column + 2, 4)
    other = jnp.where(place_far < 2, 4, 0)

    def far(step, carry):
        chunk = other + step
        offset = chunk // 2 - place_far

        @pl.when(jnp.abs(offset) <= REACH)
        def _():
            put(far_ref, chunk, (offset + REACH) * 2 + lax.rem(chunk, 2))

        return carry

    lax.fori_loop(0, 4, far, 0)


def pick(row, lanes):
    return jnp.take_along_axis(jnp.broadcast_to(row, lanes.shape), lanes, axis=1)


def add_blocks(chunk_ref, chunk, first_block, slots, blocks, lanes, found):
    parts = len(blocks)
    local = [blocks[v] - first_block for v in range(parts)]
    found = list(found)
    for c in range(slots):
        hit = [local[v] == c for v in range(parts)]
        for f in range(FIELDS):
            row = chunk_ref[chunk, FIELDS * c + f : FIELDS * c + f + 1, :]
            for v in range(parts):
                found[f * parts + v] = jnp.where(hit[v], pick(row, lanes[v]), found[f * parts + v])
    return tuple(found)


def near_kernel(near_ref, slots_ref, found_ref):
    slots = near_ref.shape[1] // FIELDS
    parts = slots_ref.shape[0] // 8
    ids = [slots_ref[8 * v : 8 * v + 8, :] for v in range(parts)]
    blocks = [i >> 7 for i in ids]
    lanes = [i & (BLOCK - 1) for i in ids]
    here = lax.rem(lax.axis_index("mapx"), 4)

    def step(chunk, found):
        source = (chunk // 2 - here + REACH) * 2 + lax.rem(chunk, 2)
        return add_blocks(near_ref, chunk, source * slots, slots, blocks, lanes, found)

    start = tuple(jnp.zeros((8, BLOCK), jnp.float32) for _ in range(FIELDS * parts))
    found = lax.fori_loop(0, 8, step, start)
    for f in range(FIELDS):
        for v in range(parts):
            found_ref[f, 8 * v : 8 * v + 8, :] = found[f * parts + v]


def state_kernel(
    far_ref, slots_ref, found_ref, weights_ref, mask_ref, halos_ref, state_ref, table_ref, group_ref, far_x_ref, far_y_ref, cut_ref
):
    slots = far_ref.shape[1] // FIELDS
    parts = slots_ref.shape[0] // 8
    ids = [slots_ref[8 * v : 8 * v + 8, :] for v in range(parts)]
    blocks = [i >> 7 for i in ids]
    lanes = [i & (BLOCK - 1) for i in ids]
    place_far = lax.rem(lax.axis_index("mapx") + 2, 4)
    other = jnp.where(place_far < 2, 4, 0)

    def step(i, found):
        chunk = other + i
        source = (chunk // 2 - place_far + REACH) * 2 + lax.rem(chunk, 2)
        return add_blocks(far_ref, chunk, source * slots, slots, blocks, lanes, found)

    start = tuple(found_ref[f, 8 * v : 8 * v + 8, :] for f in range(FIELDS) for v in range(parts))
    found = lax.fori_loop(0, 4, step, start)
    front = mask_ref[...] == 1
    rows = mask_ref.shape[0]
    for f in range(FIELDS):
        total = jnp.zeros((rows, BLOCK), jnp.float32)
        for v in range(parts):
            term = found[f * parts + v] * weights_ref[8 * v : 8 * v + 8, :]
            for k in range(8 // rows):
                total = total + term[k * rows : (k + 1) * rows, :]
        if f == 4:
            total = jnp.where(front, ocean_temp, total)
        for r in range(rows):
            state_ref[f : f + 1, r * BLOCK : (r + 1) * BLOCK] = total[r : r + 1, :]
        for s in range(rows // 2):
            table_ref[s, 2 * f : 2 * f + 2, :] = total[2 * s : 2 * s + 2, :]
    halo_parts = halos_ref.shape[0] // 8
    halo = [halos_ref[8 * v : 8 * v + 8, :] for v in range(halo_parts)]
    halo_blocks = [i >> 7 for i in halo]
    halo_lanes = [i & (BLOCK - 1) for i in halo]
    for f in range(FIELDS):
        cut = [jnp.zeros((8, BLOCK), jnp.float32) for _ in range(halo_parts)]
        for b in range(rows):
            row = table_ref[b // 2, 2 * f + b % 2 : 2 * f + b % 2 + 1, :]
            for v in range(halo_parts):
                cut[v] = jnp.where(halo_blocks[v] == b, pick(row, halo_lanes[v]), cut[v])
        for k in range(6):
            v, r = (2 * k) // 8, (2 * k) % 8
            cut_ref[k, 2 * f : 2 * f + 2, :] = cut[v][r : r + 2, :]
    send_pairs(cut_ref, group_ref, far_x_ref, far_y_ref, [(0, 1), (2, 3), (4, 5)])


def pair_places():
    return [lax.rem(lax.axis_index(axis), 2) for axis in AXES]


def partner(px, py, pz, axis):
    flip = [px, py, pz]
    flip[axis] = 1 - flip[axis]
    return flip[0] * 4 + flip[1] * 2 + flip[2]


def send_pairs(cut_ref, group_ref, far_x_ref, far_y_ref, order):
    places = pair_places()
    for axis in range(3):
        even, odd = order[axis]
        inside = jnp.where(places[axis] == 0, even, odd)
        outside = jnp.where(places[axis] == 0, odd, even)
        group_ref[partner(*places, axis)] = cut_ref[inside]
        if axis == 0:
            far_x_ref[...] = cut_ref[outside]
        if axis == 1:
            far_y_ref[...] = cut_ref[outside]


def arrivals(group_ref, far_refs, counts):
    places = pair_places()
    result = []
    for axis in range(3):
        inside = group_ref[partner(*places, axis)]
        at = lax.axis_index(AXES[axis])
        edge = jnp.where(places[axis] == 0, at == 0, at == counts[axis] - 1)
        if far_refs[axis] is None:
            outside = jnp.zeros_like(inside)
        else:
            outside = jnp.where(edge, 0.0, far_refs[axis][...])
        result.append((places[axis], inside, outside))
    return result


def one_hot_sum(values, ids, block_count):
    rows = lax.broadcasted_iota(jnp.int32, (block_count, BLOCK), 0)
    hit = rows == jnp.broadcast_to(ids >> 7, rows.shape)
    left = [jnp.where(hit, jnp.broadcast_to(v, rows.shape), 0.0) for v in values]
    left = jnp.concatenate(left, axis=0).astype(jnp.bfloat16)
    lanes = lax.broadcasted_iota(jnp.int32, (BLOCK, BLOCK), 0)
    right = jnp.where(lanes == jnp.broadcast_to(ids & (BLOCK - 1), lanes.shape), 1.0, 0.0).astype(jnp.bfloat16)
    return left, right


def cut_parts(value):
    parts = []
    for _ in range(SPLITS - 1):
        part = value.astype(jnp.bfloat16).astype(jnp.float32)
        parts.append(part)
        value = value - part
    return parts + [value]


def nt_dot(left, right):
    return lax.dot_general(left, right, (((1,), (1,)), ((), ())), preferred_element_type=jnp.float32)


def element_kernel(
    counts,
    elem_rows,
    table_in_ref,
    group_ref,
    far_x_ref,
    far_y_ref,
    nodes_ref,
    grads_ref,
    volume_ref,
    own_ref,
    back_ref,
    back_x_ref,
    back_y_ref,
    table_ref,
    parts_ref,
    cut_ref,
):
    owned_slots = table_in_ref.shape[0]
    table_ref[0:owned_slots] = table_in_ref[...]
    far_refs = [far_x_ref, far_y_ref if counts[1] > 2 else None, None]
    for axis, (place_at, inside, outside) in enumerate(arrivals(group_ref, far_refs, counts)):
        table_ref[owned_slots + 2 * axis + 1 - place_at] = inside
        table_ref[owned_slots + 2 * axis + place_at] = outside
    block_count = 2 * table_ref.shape[0]
    padded = nodes_ref.shape[1]
    for t in range(padded // 8):
        at = slice(8 * t, 8 * t + 8)
        values = []
        for a in range(4):
            ids = nodes_ref[a, at, :]
            blocks, lanes = ids >> 7, ids & (BLOCK - 1)
            found = [jnp.zeros((8, BLOCK), jnp.float32) for _ in range(FIELDS)]
            for b in range(block_count):
                hit = blocks == b
                for f in range(FIELDS):
                    row = table_ref[b // 2, 2 * f + b % 2 : 2 * f + b % 2 + 1, :]
                    found[f] = jnp.where(hit, pick(row, lanes), found[f])
            values.append(found)
        grads = [[grads_ref[3 * a + j, at, :] for j in range(3)] for a in range(4)]
        volume = volume_ref[at, :]
        velgrad = [[sum(values[a][i] * grads[a][j] for a in range(4)) for j in range(3)] for i in range(3)]
        strain = [[0.5 * (velgrad[i][j] + velgrad[j][i]) if i <= j else None for j in range(3)] for i in range(3)]
        diagonal = sum(strain[i][i] * strain[i][i] for i in range(3))
        corner = sum(strain[i][j] * strain[i][j] for i, j in ((0, 1), (0, 2), (1, 2)))
        second = 0.5 * diagonal + corner
        pressure, temper, damage = [0.25 * (values[0][f] + values[1][f] + values[2][f] + values[3][f]) for f in (3, 4, 5)]
        root = jnp.exp(jnp.log(second + strain_reg) * (-1.0 / 3.0))
        twice = (1.0 - damage) * jnp.exp(-temper) * root
        stress = [[None] * 3 for _ in range(3)]
        for i in range(3):
            for j in range(i, 3):
                stress[i][j] = twice * strain[i][j] - (pressure if i == j else 0.0)
                stress[j][i] = stress[i][j]
        lift = (0.25 * gravity) * volume
        flow = 0.25 * volume * (velgrad[0][0] + velgrad[1][1] + velgrad[2][2])
        for s, part in enumerate(cut_parts(flow)):
            for a in range(4):
                parts_ref[3 * SPLITS + s, a * padded + 8 * t : a * padded + 8 * t + 8, :] = part
        for a in range(4):
            for i in range(3):
                force = volume * sum(stress[i][j] * grads[a][j] for j in range(3))
                if i == 2:
                    force = force + lift
                for s, part in enumerate(cut_parts(force)):
                    parts_ref[i * SPLITS + s, a * padded + 8 * t : a * padded + 8 * t + 8, :] = part

    group = 10

    def gather_terms(step, total):
        a = step // (elem_rows // group)
        first = lax.rem(step, elem_rows // group) * group
        lefts, rights = [], []
        for r in range(group):
            ids = nodes_ref[a, pl.ds(first + r, 1), :]
            terms = [
                parts_ref[c * SPLITS + s, pl.ds(a * padded + first + r, 1), :] for s in range(SPLITS) for c in range(4)
            ]
            left, right = one_hot_sum(terms, ids, block_count)
            lefts.append(left)
            rights.append(right)
        return total + nt_dot(jnp.concatenate(lefts, axis=1), jnp.concatenate(rights, axis=1))

    width = 4 * block_count
    total = lax.fori_loop(
        0, 4 * (elem_rows // group), gather_terms, jnp.zeros((SPLITS * width, BLOCK), jnp.float32)
    )
    total = sum(total[s * width : (s + 1) * width, :] for s in range(SPLITS))
    owned = 2 * owned_slots
    for c in range(4):
        own_ref[c * owned : (c + 1) * owned, :] = total[c * block_count : c * block_count + owned, :]
        for k in range(6):
            first = c * block_count + owned + 2 * k
            cut_ref[k, 2 * c : 2 * c + 2, :] = total[first : first + 2, :]
    send_pairs(cut_ref, back_ref, back_x_ref, back_y_ref, [(1, 0), (3, 2), (5, 4)])


def residual_kernel(counts, back_ref, far_x_ref, far_y_ref, own_ref, halos_ref, out_ref, came_ref):
    far_refs = [far_x_ref, far_y_ref if counts[1] > 2 else None, None]
    for axis, (place_at, inside, outside) in enumerate(arrivals(back_ref, far_refs, counts)):
        came_ref[2 * axis + place_at] = inside
        came_ref[2 * axis + 1 - place_at] = outside
    owned = own_ref.shape[0] // 4
    lefts, rights = [], []
    for k in range(6):
        parts = cut_parts(came_ref[k])
        for h in range(2):
            ids = halos_ref[2 * k + h : 2 * k + h + 1, :]
            terms = [parts[s][2 * c + h : 2 * c + h + 1, :] for s in range(SPLITS) for c in range(4)]
            left, right = one_hot_sum(terms, ids, owned)
            lefts.append(left)
            rights.append(right)
    total = nt_dot(jnp.concatenate(lefts, axis=1), jnp.concatenate(rights, axis=1))
    width = 4 * owned
    total = sum(total[s * width : (s + 1) * width, :] for s in range(SPLITS)) + own_ref[...]
    for c in range(4):
        for b in range(owned):
            r = c * owned + b
            out_ref[c : c + 1, b * BLOCK : (b + 1) * BLOCK] = total[r : r + 1, :]


def shaped(*shape):
    return jax.ShapeDtypeStruct(shape, jnp.float32)


def per_device(
    sizes,
    old_state,
    send_blocks,
    node_slots,
    node_weights,
    front_mask,
    halo_lists,
    elem_nodes,
    shape_grads,
    elem_volume,
):
    old_state, send_blocks = old_state[0, 0, 0], send_blocks[0, 0, 0]
    slots = send_blocks.shape[1]
    rows = FIELDS * slots
    near, far = pl.pallas_call(
        pack_kernel,
        out_shape=(shaped(8, rows, BLOCK), shaped(8, rows, BLOCK)),
        in_specs=[SMEM, VMEM],
        out_specs=(VMEM, VMEM),
        compiler_params=params(),
    )(send_blocks, old_state)
    near = group_swap(near, spread_groups(sizes, 0))
    far = group_swap(far, spread_groups(sizes, 2))

    owned = node_slots.shape[-1]
    slot_rows = node_slots.reshape(-1, BLOCK)
    weight_rows = node_weights.reshape(-1, BLOCK)
    found = pl.pallas_call(
        near_kernel,
        out_shape=shaped(FIELDS, slot_rows.shape[0], BLOCK),
        in_specs=[VMEM, VMEM],
        out_specs=VMEM,
        compiler_params=params(),
    )(near, slot_rows)
    halo_rows = halo_lists.reshape(-1, BLOCK)
    halo_rows = jnp.pad(halo_rows, ((0, -halo_rows.shape[0] % 8), (0, 0)))
    chunk = (2 * FIELDS, BLOCK)
    new_state, table, group, far_x, far_y = pl.pallas_call(
        state_kernel,
        out_shape=(
            shaped(FIELDS, owned),
            shaped(owned // (2 * BLOCK), *chunk),
            shaped(8, *chunk),
            shaped(*chunk),
            shaped(*chunk),
        ),
        in_specs=[VMEM] * 6,
        out_specs=(VMEM,) * 5,
        scratch_shapes=[pltpu.VMEM((6, *chunk), jnp.float32)],
        compiler_params=params(),
    )(far, slot_rows, found, weight_rows, front_mask.reshape(-1, BLOCK), halo_rows)

    far_x = far_swap(far_x, "mapx", sizes[0])
    if sizes[1] > 2:
        far_y = far_swap(far_y, "mapy", sizes[1])
    group = group_swap(group, pair_groups(sizes))

    elems = elem_nodes.shape[-1]
    elem_rows = elems // BLOCK
    more = -elem_rows % 8
    nodes = jnp.pad(elem_nodes.reshape(4, elem_rows, BLOCK), ((0, 0), (0, more), (0, 0)))
    grads = jnp.pad(shape_grads.reshape(12, elem_rows, BLOCK), ((0, 0), (0, more), (0, 0)))
    volume = jnp.pad(elem_volume.reshape(elem_rows, BLOCK), ((0, more), (0, 0)))
    slots_all = table.shape[0] + 6
    own, back, back_x, back_y = pl.pallas_call(
        functools.partial(element_kernel, sizes, elem_rows),
        out_shape=(shaped(4 * owned // BLOCK, BLOCK), shaped(8, 8, BLOCK), shaped(8, BLOCK), shaped(8, BLOCK)),
        in_specs=[VMEM] * 7,
        out_specs=(VMEM,) * 4,
        scratch_shapes=[
            pltpu.VMEM((slots_all, *chunk), jnp.float32),
            pltpu.VMEM((4 * SPLITS, 4 * (elem_rows + more), BLOCK), jnp.float32),
            pltpu.VMEM((6, 8, BLOCK), jnp.float32),
        ],
        compiler_params=params(),
    )(table, group, far_x, far_y, nodes, grads, volume)

    back_x = far_swap(back_x, "mapx", sizes[0])
    if sizes[1] > 2:
        back_y = far_swap(back_y, "mapy", sizes[1])
    back = group_swap(back, pair_groups(sizes))
    residual = pl.pallas_call(
        functools.partial(residual_kernel, sizes),
        out_shape=shaped(4, owned),
        in_specs=[VMEM] * 5,
        out_specs=VMEM,
        scratch_shapes=[pltpu.VMEM((6, 8, BLOCK), jnp.float32)],
        compiler_params=params(),
    )(back, back_x, back_y, own, halo_rows)
    return (new_state[None, None, None], residual[None, None, None])


def solution(mesh):
    sizes = tuple(mesh.shape[axis] for axis in AXES)
    row = P("mapx", "mapy", "layer", None)
    table = P("mapx", "mapy", "layer", None, None)
    return jax.shard_map(
        functools.partial(per_device, sizes),
        mesh=mesh,
        in_specs=(table, table, table, table, row, table, table, table, row),
        out_specs=(table, table),
        check_vma=False,
    )
```

```python
import functools

import jax
import jax.numpy as jnp
from jax import lax
from jax.experimental import pallas as pl
from jax.experimental.pallas import tpu as pltpu
from jax.sharding import PartitionSpec as P

BLOCK = 128
REACH = 2
FIELDS = 6
SPLITS = 3

ocean_temp = 0.0
strain_reg = 0.01
gravity = 0.5

AXES = ("mapx", "mapy", "layer")
VMEM = pl.BlockSpec(memory_space=pltpu.VMEM)
SMEM = pl.BlockSpec(memory_space=pltpu.SMEM)


def params():
    return pltpu.CompilerParams(vmem_limit_bytes=32 * 1024 * 1024)


def near_groups(sizes):
    nx, ny, nl = sizes
    number = lambda x, y, l: (x * ny + y) * nl + l
    return [
        [number(first + i, y, l) for i in range(4) for l in range(nl)] for first in range(0, nx, 4) for y in range(ny)
    ]


def both_ways(pairs):
    return [way for one, other in pairs for way in ((one, other), (other, one))]


def far_pairs(count):
    two, one = [], []
    for first in range(2, count - 3, 4):
        two += [(first, first + 2), (first + 1, first + 3)]
        one += [(first + 1, first + 2)]
    return both_ways(two), both_ways(one)


def pair_groups(sizes):
    nx, ny, nl = sizes
    number = lambda x, y, l: (x * ny + y) * nl + l
    return [
        [number(x + i, y + j, l) for i in range(2) for j in range(2) for l in range(2)]
        for x in range(0, nx, 2)
        for y in range(0, ny, 2)
    ]


def group_swap(chunks, groups):
    return lax.all_to_all(chunks, AXES, split_axis=0, concat_axis=0, axis_index_groups=groups)


def far_swap(value, axis, count):
    pairs = []
    for first in range(1, count - 1, 2):
        pairs += [(first, first + 1), (first + 1, first)]
    return lax.ppermute(value, axis, pairs)


def put_blocks(blocks_ref, old_ref, out_ref, chunk, peer):
    slots = blocks_ref.shape[1]
    count = old_ref.shape[0] // FIELDS
    for c in range(slots):
        rows = pl.ds(blocks_ref[peer, c], FIELDS, stride=count)
        out_ref[chunk, FIELDS * c : FIELDS * (c + 1), :] = old_ref[rows, :]


def far_place():
    at = lax.rem(lax.axis_index("mapx") + 2, 4)
    return at, jnp.where(at < 2, 1, -1)


def pack_far_kernel(blocks_ref, old_ref, swap_ref, own_ref):
    layer = lax.axis_index("layer")
    _, way = far_place()
    for i in range(2):
        peer = ((REACH - i) * way + REACH) * 2
        put_blocks(blocks_ref, old_ref, swap_ref, i, peer + 1 - layer)
    for i in range(2):
        peer = ((REACH - i) * way + REACH) * 2
        put_blocks(blocks_ref, old_ref, own_ref, i, peer + layer)


def pack_near_kernel(blocks_ref, old_ref, near_ref):
    here = lax.rem(lax.axis_index("mapx"), 4)

    def near(chunk, carry):
        offset = chunk // 2 - here

        @pl.when(jnp.abs(offset) <= REACH)
        def _():
            put_blocks(blocks_ref, old_ref, near_ref, chunk, (offset + REACH) * 2 + lax.rem(chunk, 2))

        return carry

    lax.fori_loop(0, 8, near, 0)


def pick(row, lanes):
    return jnp.take_along_axis(jnp.broadcast_to(row, lanes.shape), lanes, axis=1)


def add_blocks(chunk_ref, chunk, first_block, slots, blocks, lanes, found):
    parts = len(blocks)
    local = [blocks[v] - first_block for v in range(parts)]
    found = list(found)
    for c in range(slots):
        hit = [local[v] == c for v in range(parts)]
        for f in range(FIELDS):
            row = chunk_ref[chunk, FIELDS * c + f : FIELDS * c + f + 1, :]
            for v in range(parts):
                found[f * parts + v] = jnp.where(hit[v], pick(row, lanes[v]), found[f * parts + v])
    return tuple(found)


def near_kernel(near_ref, slots_ref, found_ref):
    slots = near_ref.shape[1] // FIELDS
    parts = slots_ref.shape[0] // 8
    ids = [slots_ref[8 * v : 8 * v + 8, :] for v in range(parts)]
    blocks = [i >> 7 for i in ids]
    lanes = [i & (BLOCK - 1) for i in ids]
    here = lax.rem(lax.axis_index("mapx"), 4)

    def step(chunk, found):
        source = (chunk // 2 - here + REACH) * 2 + lax.rem(chunk, 2)
        return add_blocks(near_ref, chunk, source * slots, slots, blocks, lanes, found)

    start = tuple(jnp.zeros((8, BLOCK), jnp.float32) for _ in range(FIELDS * parts))
    found = lax.fori_loop(0, 8, step, start)
    for f in range(FIELDS):
        for v in range(parts):
            found_ref[f, 8 * v : 8 * v + 8, :] = found[f * parts + v]


def state_kernel(
    two_ref, one_ref, slots_ref, found_ref, weights_ref, mask_ref, halos_ref, state_ref, table_ref, group_ref, far_x_ref, far_y_ref, cut_ref
):
    slots = two_ref.shape[1] // FIELDS
    parts = slots_ref.shape[0] // 8
    ids = [slots_ref[8 * v : 8 * v + 8, :] for v in range(parts)]
    blocks = [i >> 7 for i in ids]
    lanes = [i & (BLOCK - 1) for i in ids]
    at, way = far_place()
    found = tuple(found_ref[f, 8 * v : 8 * v + 8, :] for f in range(FIELDS) for v in range(parts))
    first_two = (2 * way + REACH) * 2 * slots
    first_one = jnp.where((at == 1) | (at == 2), (way + REACH) * 2 * slots, -(1 << 20))
    for ref, first in ((two_ref, first_two), (one_ref, first_one)):

        def step(chunk, found, ref=ref, first=first):
            return add_blocks(ref, chunk, first + chunk * slots, slots, blocks, lanes, found)

        found = lax.fori_loop(0, 2, step, found)
    front = mask_ref[...] == 1
    rows = mask_ref.shape[0]
    for f in range(FIELDS):
        total = jnp.zeros((rows, BLOCK), jnp.float32)
        for v in range(parts):
            term = found[f * parts + v] * weights_ref[8 * v : 8 * v + 8, :]
            for k in range(8 // rows):
                total = total + term[k * rows : (k + 1) * rows, :]
        if f == 4:
            total = jnp.where(front, ocean_temp, total)
        for r in range(rows):
            state_ref[f : f + 1, r * BLOCK : (r + 1) * BLOCK] = total[r : r + 1, :]
        for s in range(rows // 2):
            table_ref[s, 2 * f : 2 * f + 2, :] = total[2 * s : 2 * s + 2, :]
    halo_parts = halos_ref.shape[0] // 8
    halo = [halos_ref[8 * v : 8 * v + 8, :] for v in range(halo_parts)]
    halo_blocks = [i >> 7 for i in halo]
    halo_lanes = [i & (BLOCK - 1) for i in halo]
    for f in range(FIELDS):
        cut = [jnp.zeros((8, BLOCK), jnp.float32) for _ in range(halo_parts)]
        for b in range(rows):
            row = table_ref[b // 2, 2 * f + b % 2 : 2 * f + b % 2 + 1, :]
            for v in range(halo_parts):
                cut[v] = jnp.where(halo_blocks[v] == b, pick(row, halo_lanes[v]), cut[v])
        for k in range(6):
            v, r = (2 * k) // 8, (2 * k) % 8
            cut_ref[k, 2 * f : 2 * f + 2, :] = cut[v][r : r + 2, :]
    send_pairs(cut_ref, group_ref, far_x_ref, far_y_ref, [(0, 1), (2, 3), (4, 5)])


def pair_places():
    return [lax.rem(lax.axis_index(axis), 2) for axis in AXES]


def partner(px, py, pz, axis):
    flip = [px, py, pz]
    flip[axis] = 1 - flip[axis]
    return flip[0] * 4 + flip[1] * 2 + flip[2]


def send_pairs(cut_ref, group_ref, far_x_ref, far_y_ref, order):
    places = pair_places()
    for axis in range(3):
        even, odd = order[axis]
        inside = jnp.where(places[axis] == 0, even, odd)
        outside = jnp.where(places[axis] == 0, odd, even)
        group_ref[partner(*places, axis)] = cut_ref[inside]
        if axis == 0:
            far_x_ref[...] = cut_ref[outside]
        if axis == 1:
            far_y_ref[...] = cut_ref[outside]


def arrivals(group_ref, far_refs, counts):
    places = pair_places()
    result = []
    for axis in range(3):
        inside = group_ref[partner(*places, axis)]
        at = lax.axis_index(AXES[axis])
        edge = jnp.where(places[axis] == 0, at == 0, at == counts[axis] - 1)
        if far_refs[axis] is None:
            outside = jnp.zeros_like(inside)
        else:
            outside = jnp.where(edge, 0.0, far_refs[axis][...])
        result.append((places[axis], inside, outside))
    return result


def one_hot_sum(values, ids, block_count):
    rows = lax.broadcasted_iota(jnp.int32, (block_count, BLOCK), 0)
    hit = rows == jnp.broadcast_to(ids >> 7, rows.shape)
    left = [jnp.where(hit, jnp.broadcast_to(v, rows.shape), 0.0) for v in values]
    left = jnp.concatenate(left, axis=0).astype(jnp.bfloat16)
    lanes = lax.broadcasted_iota(jnp.int32, (BLOCK, BLOCK), 0)
    right = jnp.where(lanes == jnp.broadcast_to(ids & (BLOCK - 1), lanes.shape), 1.0, 0.0).astype(jnp.bfloat16)
    return left, right


def cut_parts(value):
    parts = []
    for _ in range(SPLITS - 1):
        part = value.astype(jnp.bfloat16).astype(jnp.float32)
        parts.append(part)
        value = value - part
    return parts + [value]


def nt_dot(left, right):
    return lax.dot_general(left, right, (((1,), (1,)), ((), ())), preferred_element_type=jnp.float32)


def element_kernel(
    counts,
    elem_rows,
    table_in_ref,
    group_ref,
    far_x_ref,
    far_y_ref,
    nodes_ref,
    grads_ref,
    volume_ref,
    own_ref,
    back_ref,
    back_x_ref,
    back_y_ref,
    table_ref,
    parts_ref,
    cut_ref,
):
    owned_slots = table_in_ref.shape[0]
    table_ref[0:owned_slots] = table_in_ref[...]
    far_refs = [far_x_ref, far_y_ref if counts[1] > 2 else None, None]
    for axis, (place_at, inside, outside) in enumerate(arrivals(group_ref, far_refs, counts)):
        table_ref[owned_slots + 2 * axis + 1 - place_at] = inside
        table_ref[owned_slots + 2 * axis + place_at] = outside
    block_count = 2 * table_ref.shape[0]
    padded = nodes_ref.shape[1]
    for t in range(padded // 8):
        at = slice(8 * t, 8 * t + 8)
        values = []
        for a in range(4):
            ids = nodes_ref[a, at, :]
            blocks, lanes = ids >> 7, ids & (BLOCK - 1)
            found = [jnp.zeros((8, BLOCK), jnp.float32) for _ in range(FIELDS)]
            for b in range(block_count):
                hit = blocks == b
                for f in range(FIELDS):
                    row = table_ref[b // 2, 2 * f + b % 2 : 2 * f + b % 2 + 1, :]
                    found[f] = jnp.where(hit, pick(row, lanes), found[f])
            values.append(found)
        grads = [[grads_ref[3 * a + j, at, :] for j in range(3)] for a in range(4)]
        volume = volume_ref[at, :]
        velgrad = [[sum(values[a][i] * grads[a][j] for a in range(4)) for j in range(3)] for i in range(3)]
        strain = [[0.5 * (velgrad[i][j] + velgrad[j][i]) if i <= j else None for j in range(3)] for i in range(3)]
        diagonal = sum(strain[i][i] * strain[i][i] for i in range(3))
        corner = sum(strain[i][j] * strain[i][j] for i, j in ((0, 1), (0, 2), (1, 2)))
        second = 0.5 * diagonal + corner
        pressure, temper, damage = [0.25 * (values[0][f] + values[1][f] + values[2][f] + values[3][f]) for f in (3, 4, 5)]
        root = jnp.exp(jnp.log(second + strain_reg) * (-1.0 / 3.0))
        twice = (1.0 - damage) * jnp.exp(-temper) * root
        stress = [[None] * 3 for _ in range(3)]
        for i in range(3):
            for j in range(i, 3):
                stress[i][j] = twice * strain[i][j] - (pressure if i == j else 0.0)
                stress[j][i] = stress[i][j]
        lift = (0.25 * gravity) * volume
        flow = 0.25 * volume * (velgrad[0][0] + velgrad[1][1] + velgrad[2][2])
        for s, part in enumerate(cut_parts(flow)):
            for a in range(4):
                parts_ref[3 * SPLITS + s, a * padded + 8 * t : a * padded + 8 * t + 8, :] = part
        for a in range(4):
            for i in range(3):
                force = volume * sum(stress[i][j] * grads[a][j] for j in range(3))
                if i == 2:
                    force = force + lift
                for s, part in enumerate(cut_parts(force)):
                    parts_ref[i * SPLITS + s, a * padded + 8 * t : a * padded + 8 * t + 8, :] = part

    group = 10

    def gather_terms(step, total):
        a = step // (elem_rows // group)
        first = lax.rem(step, elem_rows // group) * group
        lefts, rights = [], []
        for r in range(group):
            ids = nodes_ref[a, pl.ds(first + r, 1), :]
            terms = [
                parts_ref[c * SPLITS + s, pl.ds(a * padded + first + r, 1), :] for s in range(SPLITS) for c in range(4)
            ]
            left, right = one_hot_sum(terms, ids, block_count)
            lefts.append(left)
            rights.append(right)
        return total + nt_dot(jnp.concatenate(lefts, axis=1), jnp.concatenate(rights, axis=1))

    width = 4 * block_count
    total = lax.fori_loop(
        0, 4 * (elem_rows // group), gather_terms, jnp.zeros((SPLITS * width, BLOCK), jnp.float32)
    )
    total = sum(total[s * width : (s + 1) * width, :] for s in range(SPLITS))
    owned = 2 * owned_slots
    for c in range(4):
        own_ref[c * owned : (c + 1) * owned, :] = total[c * block_count : c * block_count + owned, :]
        for k in range(6):
            first = c * block_count + owned + 2 * k
            cut_ref[k, 2 * c : 2 * c + 2, :] = total[first : first + 2, :]
    send_pairs(cut_ref, back_ref, back_x_ref, back_y_ref, [(1, 0), (3, 2), (5, 4)])


def residual_kernel(counts, back_ref, far_x_ref, far_y_ref, own_ref, halos_ref, out_ref, came_ref):
    far_refs = [far_x_ref, far_y_ref if counts[1] > 2 else None, None]
    for axis, (place_at, inside, outside) in enumerate(arrivals(back_ref, far_refs, counts)):
        came_ref[2 * axis + place_at] = inside
        came_ref[2 * axis + 1 - place_at] = outside
    owned = own_ref.shape[0] // 4
    lefts, rights = [], []
    for k in range(6):
        parts = cut_parts(came_ref[k])
        for h in range(2):
            ids = halos_ref[2 * k + h : 2 * k + h + 1, :]
            terms = [parts[s][2 * c + h : 2 * c + h + 1, :] for s in range(SPLITS) for c in range(4)]
            left, right = one_hot_sum(terms, ids, owned)
            lefts.append(left)
            rights.append(right)
    total = nt_dot(jnp.concatenate(lefts, axis=1), jnp.concatenate(rights, axis=1))
    width = 4 * owned
    total = sum(total[s * width : (s + 1) * width, :] for s in range(SPLITS)) + own_ref[...]
    for c in range(4):
        for b in range(owned):
            r = c * owned + b
            out_ref[c : c + 1, b * BLOCK : (b + 1) * BLOCK] = total[r : r + 1, :]


def shaped(*shape):
    return jax.ShapeDtypeStruct(shape, jnp.float32)


def per_device(
    sizes,
    old_state,
    send_blocks,
    node_slots,
    node_weights,
    front_mask,
    halo_lists,
    elem_nodes,
    shape_grads,
    elem_volume,
):
    old_state, send_blocks = old_state[0, 0, 0], send_blocks[0, 0, 0]
    slots = send_blocks.shape[1]
    rows = FIELDS * slots
    old_rows = old_state.reshape(-1, BLOCK)
    swap, mine = pl.pallas_call(
        pack_far_kernel,
        out_shape=(shaped(2, rows, BLOCK), shaped(2, rows, BLOCK)),
        in_specs=[SMEM, VMEM],
        out_specs=(VMEM, VMEM),
        compiler_params=params(),
    )(send_blocks, old_rows)
    swap = lax.ppermute(swap, "layer", both_ways([(0, 1)]))
    near = pl.pallas_call(
        pack_near_kernel,
        out_shape=shaped(8, rows, BLOCK),
        in_specs=[SMEM, VMEM],
        out_specs=VMEM,
        compiler_params=params(),
    )(send_blocks, old_rows)
    near = group_swap(near, near_groups(sizes))
    first = lax.axis_index("layer") == 0
    pairs_two, pairs_one = far_pairs(sizes[0])
    sorted_far = [jnp.where(first, jnp.stack([mine[i], swap[i]]), jnp.stack([swap[i], mine[i]])) for i in range(2)]
    two = lax.ppermute(sorted_far[0], "mapx", pairs_two)
    one = lax.ppermute(sorted_far[1], "mapx", pairs_one)

    owned = node_slots.shape[-1]
    slot_rows = node_slots.reshape(-1, BLOCK)
    weight_rows = node_weights.reshape(-1, BLOCK)
    found = pl.pallas_call(
        near_kernel,
        out_shape=shaped(FIELDS, slot_rows.shape[0], BLOCK),
        in_specs=[VMEM, VMEM],
        out_specs=VMEM,
        compiler_params=params(),
    )(near, slot_rows)
    halo_rows = halo_lists.reshape(-1, BLOCK)
    halo_rows = jnp.pad(halo_rows, ((0, -halo_rows.shape[0] % 8), (0, 0)))
    chunk = (2 * FIELDS, BLOCK)
    new_state, table, group, far_x, far_y = pl.pallas_call(
        state_kernel,
        out_shape=(
            shaped(FIELDS, owned),
            shaped(owned // (2 * BLOCK), *chunk),
            shaped(8, *chunk),
            shaped(*chunk),
            shaped(*chunk),
        ),
        in_specs=[VMEM] * 7,
        out_specs=(VMEM,) * 5,
        scratch_shapes=[pltpu.VMEM((6, *chunk), jnp.float32)],
        compiler_params=params(),
    )(two, one, slot_rows, found, weight_rows, front_mask.reshape(-1, BLOCK), halo_rows)

    far_x = far_swap(far_x, "mapx", sizes[0])
    if sizes[1] > 2:
        far_y = far_swap(far_y, "mapy", sizes[1])
    group = group_swap(group, pair_groups(sizes))

    elems = elem_nodes.shape[-1]
    elem_rows = elems // BLOCK
    more = -elem_rows % 8
    nodes = jnp.pad(elem_nodes.reshape(4, elem_rows, BLOCK), ((0, 0), (0, more), (0, 0)))
    grads = jnp.pad(shape_grads.reshape(12, elem_rows, BLOCK), ((0, 0), (0, more), (0, 0)))
    volume = jnp.pad(elem_volume.reshape(elem_rows, BLOCK), ((0, more), (0, 0)))
    slots_all = table.shape[0] + 6
    own, back, back_x, back_y = pl.pallas_call(
        functools.partial(element_kernel, sizes, elem_rows),
        out_shape=(shaped(4 * owned // BLOCK, BLOCK), shaped(8, 8, BLOCK), shaped(8, BLOCK), shaped(8, BLOCK)),
        in_specs=[VMEM] * 7,
        out_specs=(VMEM,) * 4,
        scratch_shapes=[
            pltpu.VMEM((slots_all, *chunk), jnp.float32),
            pltpu.VMEM((4 * SPLITS, 4 * (elem_rows + more), BLOCK), jnp.float32),
            pltpu.VMEM((6, 8, BLOCK), jnp.float32),
        ],
        compiler_params=params(),
    )(table, group, far_x, far_y, nodes, grads, volume)

    back_x = far_swap(back_x, "mapx", sizes[0])
    if sizes[1] > 2:
        back_y = far_swap(back_y, "mapy", sizes[1])
    back = group_swap(back, pair_groups(sizes))
    residual = pl.pallas_call(
        functools.partial(residual_kernel, sizes),
        out_shape=shaped(4, owned),
        in_specs=[VMEM] * 5,
        out_specs=VMEM,
        scratch_shapes=[pltpu.VMEM((6, 8, BLOCK), jnp.float32)],
        compiler_params=params(),
    )(back, back_x, back_y, own, halo_rows)
    return (new_state[None, None, None], residual[None, None, None])


def solution(mesh):
    sizes = tuple(mesh.shape[axis] for axis in AXES)
    row = P("mapx", "mapy", "layer", None)
    table = P("mapx", "mapy", "layer", None, None)
    return jax.shard_map(
        functools.partial(per_device, sizes),
        mesh=mesh,
        in_specs=(table, table, table, table, row, table, table, table, row),
        out_specs=(table, table),
        check_vma=False,
    )
```

```python
import functools

import jax
import jax.numpy as jnp
from jax import lax
from jax.experimental import pallas as pl
from jax.experimental.pallas import tpu as pltpu
from jax.sharding import PartitionSpec as P

BLOCK = 128
REACH = 2
FIELDS = 6
SPLITS = 3

ocean_temp = 0.0
strain_reg = 0.01
gravity = 0.5

AXES = ("mapx", "mapy", "layer")
VMEM = pl.BlockSpec(memory_space=pltpu.VMEM)
SMEM = pl.BlockSpec(memory_space=pltpu.SMEM)


def params():
    return pltpu.CompilerParams(vmem_limit_bytes=32 * 1024 * 1024)


def near_groups(sizes):
    nx, ny, nl = sizes
    number = lambda x, y, l: (x * ny + y) * nl + l
    return [
        [number(first + i, y, l) for i in range(4) for l in range(nl)] for first in range(0, nx, 4) for y in range(ny)
    ]


def both_ways(pairs):
    return [way for one, other in pairs for way in ((one, other), (other, one))]


def far_pairs(count):
    two, one = [], []
    for first in range(2, count - 3, 4):
        two += [(first, first + 2), (first + 1, first + 3)]
        one += [(first + 1, first + 2)]
    return both_ways(two), both_ways(one)


def pair_groups(sizes):
    nx, ny, nl = sizes
    number = lambda x, y, l: (x * ny + y) * nl + l
    return [
        [number(x + i, y + j, l) for i in range(2) for j in range(2) for l in range(2)]
        for x in range(0, nx, 2)
        for y in range(0, ny, 2)
    ]


def group_gather(portions, groups):
    return lax.all_gather(portions, AXES, axis_index_groups=groups)


def group_swap(chunks, groups):
    return lax.all_to_all(chunks, AXES, split_axis=0, concat_axis=0, axis_index_groups=groups)


def far_swap(value, axis, count):
    pairs = []
    for first in range(1, count - 1, 2):
        pairs += [(first, first + 1), (first + 1, first)]
    return lax.ppermute(value, axis, pairs)


def put_blocks(blocks_ref, old_ref, out_ref, chunk, peer):
    slots = blocks_ref.shape[2]
    count = old_ref.shape[0] // FIELDS
    for c in range(slots):
        rows = pl.ds(blocks_ref[peer, 0, c], FIELDS, stride=count)
        out_ref[chunk, FIELDS * c : FIELDS * (c + 1), :] = old_ref[rows, :]


def far_place():
    at = lax.rem(lax.axis_index("mapx") + 2, 4)
    return at, jnp.where(at < 2, 1, -1)


def pack_far_kernel(blocks_ref, old_ref, swap_ref, own_ref):
    layer = lax.axis_index("layer")
    _, way = far_place()
    for i in range(2):
        peer = ((REACH - i) * way + REACH) * 2
        put_blocks(blocks_ref, old_ref, swap_ref, i, peer + 1 - layer)
    for i in range(2):
        peer = ((REACH - i) * way + REACH) * 2
        put_blocks(blocks_ref, old_ref, own_ref, i, peer + layer)


def pack_near_kernel(blocks_ref, old_ref, near_ref):
    here = lax.rem(lax.axis_index("mapx"), 4)

    def near(chunk, carry):
        offset = chunk // 2 - here

        @pl.when(jnp.abs(offset) <= REACH)
        def _():
            put_blocks(blocks_ref, old_ref, near_ref, chunk, (offset + REACH) * 2 + lax.rem(chunk, 2))

        return carry

    lax.fori_loop(0, 8, near, 0)


def pick(row, lanes):
    return jnp.take_along_axis(jnp.broadcast_to(row, lanes.shape), lanes, axis=1)


def add_blocks(chunk_ref, chunk, first_block, slots, blocks, lanes, found):
    parts = len(blocks)
    local = [blocks[v] - first_block for v in range(parts)]
    found = list(found)
    for c in range(slots):
        hit = [local[v] == c for v in range(parts)]
        for f in range(FIELDS):
            row = chunk_ref[chunk, FIELDS * c + f : FIELDS * c + f + 1, :]
            for v in range(parts):
                found[f * parts + v] = jnp.where(hit[v], pick(row, lanes[v]), found[f * parts + v])
    return tuple(found)


def near_kernel(near_ref, slots_ref, found_ref):
    slots = near_ref.shape[1] // FIELDS
    parts = slots_ref.shape[0] // 8
    ids = [slots_ref[8 * v : 8 * v + 8, :] for v in range(parts)]
    blocks = [i >> 7 for i in ids]
    lanes = [i & (BLOCK - 1) for i in ids]
    here = lax.rem(lax.axis_index("mapx"), 4)

    def step(chunk, found):
        source = (chunk // 2 - here + REACH) * 2 + lax.rem(chunk, 2)
        return add_blocks(near_ref, chunk, source * slots, slots, blocks, lanes, found)

    start = tuple(jnp.zeros((8, BLOCK), jnp.float32) for _ in range(FIELDS * parts))
    found = lax.fori_loop(0, 8, step, start)
    for f in range(FIELDS):
        for v in range(parts):
            found_ref[f, 8 * v : 8 * v + 8, :] = found[f * parts + v]


def state_kernel(
    two_ref, one_ref, slots_ref, found_ref, weights_ref, mask_ref, halos_ref, state_ref, table_ref, group_ref, far_x_ref, far_y_ref, cut_ref
):
    slots = two_ref.shape[1] // FIELDS
    parts = slots_ref.shape[0] // 8
    ids = [slots_ref[8 * v : 8 * v + 8, :] for v in range(parts)]
    blocks = [i >> 7 for i in ids]
    lanes = [i & (BLOCK - 1) for i in ids]
    at, way = far_place()
    found = tuple(found_ref[f, 8 * v : 8 * v + 8, :] for f in range(FIELDS) for v in range(parts))
    first_two = (2 * way + REACH) * 2 * slots
    first_one = jnp.where((at == 1) | (at == 2), (way + REACH) * 2 * slots, -(1 << 20))
    for ref, first in ((two_ref, first_two), (one_ref, first_one)):

        def step(chunk, found, ref=ref, first=first):
            return add_blocks(ref, chunk, first + chunk * slots, slots, blocks, lanes, found)

        found = lax.fori_loop(0, 2, step, found)
    front = mask_ref[...] == 1
    rows = mask_ref.shape[0]
    for f in range(FIELDS):
        total = jnp.zeros((rows, BLOCK), jnp.float32)
        for v in range(parts):
            term = found[f * parts + v] * weights_ref[8 * v : 8 * v + 8, :]
            for k in range(8 // rows):
                total = total + term[k * rows : (k + 1) * rows, :]
        if f == 4:
            total = jnp.where(front, ocean_temp, total)
        for r in range(rows):
            state_ref[f : f + 1, r * BLOCK : (r + 1) * BLOCK] = total[r : r + 1, :]
        for s in range(rows // 2):
            table_ref[s, 2 * f : 2 * f + 2, :] = total[2 * s : 2 * s + 2, :]
    halo_parts = halos_ref.shape[0] // 8
    halo = [halos_ref[8 * v : 8 * v + 8, :] for v in range(halo_parts)]
    halo_blocks = [i >> 7 for i in halo]
    halo_lanes = [i & (BLOCK - 1) for i in halo]
    for f in range(FIELDS):
        cut = [jnp.zeros((8, BLOCK), jnp.float32) for _ in range(halo_parts)]
        for b in range(rows):
            row = table_ref[b // 2, 2 * f + b % 2 : 2 * f + b % 2 + 1, :]
            for v in range(halo_parts):
                cut[v] = jnp.where(halo_blocks[v] == b, pick(row, halo_lanes[v]), cut[v])
        for k in range(6):
            v, r = (2 * k) // 8, (2 * k) % 8
            cut_ref[k, 2 * f : 2 * f + 2, :] = cut[v][r : r + 2, :]
    send_pairs(cut_ref, group_ref, far_x_ref, far_y_ref, [(0, 1), (2, 3), (4, 5)])


def pair_places():
    return [lax.rem(lax.axis_index(axis), 2) for axis in AXES]


def partner(px, py, pz, axis):
    flip = [px, py, pz]
    flip[axis] = 1 - flip[axis]
    return flip[0] * 4 + flip[1] * 2 + flip[2]


def send_pairs(cut_ref, group_ref, far_x_ref, far_y_ref, order):
    places = pair_places()
    for axis in range(3):
        even, odd = order[axis]
        inside = jnp.where(places[axis] == 0, even, odd)
        outside = jnp.where(places[axis] == 0, odd, even)
        group_ref[axis] = cut_ref[inside]
        if axis == 0:
            far_x_ref[...] = cut_ref[outside]
        if axis == 1:
            far_y_ref[...] = cut_ref[outside]


def arrivals(group_ref, far_refs, counts):
    places = pair_places()
    result = []
    for axis in range(3):
        inside = group_ref[partner(*places, axis), axis]
        at = lax.axis_index(AXES[axis])
        edge = jnp.where(places[axis] == 0, at == 0, at == counts[axis] - 1)
        if far_refs[axis] is None:
            outside = jnp.zeros_like(inside)
        else:
            outside = jnp.where(edge, 0.0, far_refs[axis][...])
        result.append((places[axis], inside, outside))
    return result


def one_hot_sum(values, ids, block_count):
    rows = lax.broadcasted_iota(jnp.int32, (block_count, BLOCK), 0)
    hit = rows == jnp.broadcast_to(ids >> 7, rows.shape)
    left = [jnp.where(hit, jnp.broadcast_to(v, rows.shape), 0.0) for v in values]
    left = jnp.concatenate(left, axis=0).astype(jnp.bfloat16)
    lanes = lax.broadcasted_iota(jnp.int32, (BLOCK, BLOCK), 0)
    right = jnp.where(lanes == jnp.broadcast_to(ids & (BLOCK - 1), lanes.shape), 1.0, 0.0).astype(jnp.bfloat16)
    return left, right


def cut_parts(value):
    parts = []
    for _ in range(SPLITS - 1):
        part = value.astype(jnp.bfloat16).astype(jnp.float32)
        parts.append(part)
        value = value - part
    return parts + [value]


def nt_dot(left, right):
    return lax.dot_general(left, right, (((1,), (1,)), ((), ())), preferred_element_type=jnp.float32)


def element_kernel(
    counts,
    elem_rows,
    table_in_ref,
    group_ref,
    far_x_ref,
    far_y_ref,
    nodes_ref,
    grads_ref,
    volume_ref,
    own_ref,
    back_ref,
    back_x_ref,
    back_y_ref,
    table_ref,
    parts_ref,
    cut_ref,
):
    owned_slots = table_in_ref.shape[0]
    table_ref[0:owned_slots] = table_in_ref[...]
    far_refs = [far_x_ref, far_y_ref if counts[1] > 2 else None, None]
    for axis, (place_at, inside, outside) in enumerate(arrivals(group_ref, far_refs, counts)):
        table_ref[owned_slots + 2 * axis + 1 - place_at] = inside
        table_ref[owned_slots + 2 * axis + place_at] = outside
    block_count = 2 * table_ref.shape[0]
    padded = nodes_ref.shape[1]
    for t in range(padded // 8):
        at = slice(8 * t, 8 * t + 8)
        values = []
        for a in range(4):
            ids = nodes_ref[a, at, :]
            blocks, lanes = ids >> 7, ids & (BLOCK - 1)
            found = [jnp.zeros((8, BLOCK), jnp.float32) for _ in range(FIELDS)]
            for b in range(block_count):
                hit = blocks == b
                for f in range(FIELDS):
                    row = table_ref[b // 2, 2 * f + b % 2 : 2 * f + b % 2 + 1, :]
                    found[f] = jnp.where(hit, pick(row, lanes), found[f])
            values.append(found)
        grads = [[grads_ref[3 * a + j, at, :] for j in range(3)] for a in range(4)]
        volume = volume_ref[at, :]
        velgrad = [[sum(values[a][i] * grads[a][j] for a in range(4)) for j in range(3)] for i in range(3)]
        strain = [[0.5 * (velgrad[i][j] + velgrad[j][i]) if i <= j else None for j in range(3)] for i in range(3)]
        diagonal = sum(strain[i][i] * strain[i][i] for i in range(3))
        corner = sum(strain[i][j] * strain[i][j] for i, j in ((0, 1), (0, 2), (1, 2)))
        second = 0.5 * diagonal + corner
        pressure, temper, damage = [0.25 * (values[0][f] + values[1][f] + values[2][f] + values[3][f]) for f in (3, 4, 5)]
        root = jnp.exp(jnp.log(second + strain_reg) * (-1.0 / 3.0))
        twice = (1.0 - damage) * jnp.exp(-temper) * root
        stress = [[None] * 3 for _ in range(3)]
        for i in range(3):
            for j in range(i, 3):
                stress[i][j] = twice * strain[i][j] - (pressure if i == j else 0.0)
                stress[j][i] = stress[i][j]
        lift = (0.25 * gravity) * volume
        flow = 0.25 * volume * (velgrad[0][0] + velgrad[1][1] + velgrad[2][2])
        for s, part in enumerate(cut_parts(flow)):
            for a in range(4):
                parts_ref[3 * SPLITS + s, a * padded + 8 * t : a * padded + 8 * t + 8, :] = part
        for a in range(4):
            for i in range(3):
                force = volume * sum(stress[i][j] * grads[a][j] for j in range(3))
                if i == 2:
                    force = force + lift
                for s, part in enumerate(cut_parts(force)):
                    parts_ref[i * SPLITS + s, a * padded + 8 * t : a * padded + 8 * t + 8, :] = part

    group = 10

    def gather_terms(step, total):
        a = step // (elem_rows // group)
        first = lax.rem(step, elem_rows // group) * group
        lefts, rights = [], []
        for r in range(group):
            ids = nodes_ref[a, pl.ds(first + r, 1), :]
            terms = [
                parts_ref[c * SPLITS + s, pl.ds(a * padded + first + r, 1), :] for s in range(SPLITS) for c in range(4)
            ]
            left, right = one_hot_sum(terms, ids, block_count)
            lefts.append(left)
            rights.append(right)
        return total + nt_dot(jnp.concatenate(lefts, axis=1), jnp.concatenate(rights, axis=1))

    width = 4 * block_count
    total = lax.fori_loop(
        0, 4 * (elem_rows // group), gather_terms, jnp.zeros((SPLITS * width, BLOCK), jnp.float32)
    )
    total = sum(total[s * width : (s + 1) * width, :] for s in range(SPLITS))
    owned = 2 * owned_slots
    for c in range(4):
        own_ref[c * owned : (c + 1) * owned, :] = total[c * block_count : c * block_count + owned, :]
        for k in range(6):
            first = c * block_count + owned + 2 * k
            cut_ref[k, 2 * c : 2 * c + 2, :] = total[first : first + 2, :]
    send_pairs(cut_ref, back_ref, back_x_ref, back_y_ref, [(1, 0), (3, 2), (5, 4)])


def residual_kernel(counts, back_ref, far_x_ref, far_y_ref, own_ref, halos_ref, out_ref, came_ref):
    far_refs = [far_x_ref, far_y_ref if counts[1] > 2 else None, None]
    for axis, (place_at, inside, outside) in enumerate(arrivals(back_ref, far_refs, counts)):
        came_ref[2 * axis + place_at] = inside
        came_ref[2 * axis + 1 - place_at] = outside
    owned = own_ref.shape[0] // 4
    lefts, rights = [], []
    for k in range(6):
        parts = cut_parts(came_ref[k])
        for h in range(2):
            ids = halos_ref[2 * k + h : 2 * k + h + 1, :]
            terms = [parts[s][2 * c + h : 2 * c + h + 1, :] for s in range(SPLITS) for c in range(4)]
            left, right = one_hot_sum(terms, ids, owned)
            lefts.append(left)
            rights.append(right)
    total = nt_dot(jnp.concatenate(lefts, axis=1), jnp.concatenate(rights, axis=1))
    width = 4 * owned
    total = sum(total[s * width : (s + 1) * width, :] for s in range(SPLITS)) + own_ref[...]
    for c in range(4):
        for b in range(owned):
            r = c * owned + b
            out_ref[c : c + 1, b * BLOCK : (b + 1) * BLOCK] = total[r : r + 1, :]


def shaped(*shape):
    return jax.ShapeDtypeStruct(shape, jnp.float32)


def per_device(
    sizes,
    old_state,
    send_blocks,
    node_slots,
    node_weights,
    front_mask,
    halo_lists,
    elem_nodes,
    shape_grads,
    elem_volume,
):
    old_state, send_blocks = old_state[0, 0, 0], send_blocks[0, 0, 0]
    slots = send_blocks.shape[1]
    send_blocks = send_blocks.reshape(-1, 1, slots)
    rows = FIELDS * slots
    old_rows = old_state.reshape(-1, BLOCK)
    swap, mine = pl.pallas_call(
        pack_far_kernel,
        out_shape=(shaped(2, rows, BLOCK), shaped(2, rows, BLOCK)),
        in_specs=[SMEM, VMEM],
        out_specs=(VMEM, VMEM),
        compiler_params=params(),
    )(send_blocks, old_rows)
    swap = lax.ppermute(swap, "layer", both_ways([(0, 1)]))
    near = pl.pallas_call(
        pack_near_kernel,
        out_shape=shaped(8, rows, BLOCK),
        in_specs=[SMEM, VMEM],
        out_specs=VMEM,
        compiler_params=params(),
    )(send_blocks, old_rows)
    near = group_swap(near, near_groups(sizes))
    first = lax.axis_index("layer") == 0
    pairs_two, pairs_one = far_pairs(sizes[0])
    sorted_far = [jnp.where(first, jnp.stack([mine[i], swap[i]]), jnp.stack([swap[i], mine[i]])) for i in range(2)]
    two = lax.ppermute(sorted_far[0], "mapx", pairs_two)
    one = lax.ppermute(sorted_far[1], "mapx", pairs_one)

    owned = node_slots.shape[-1]
    slot_rows = node_slots.reshape(-1, BLOCK)
    weight_rows = node_weights.reshape(-1, BLOCK)
    found = pl.pallas_call(
        near_kernel,
        out_shape=shaped(FIELDS, slot_rows.shape[0], BLOCK),
        in_specs=[VMEM, VMEM],
        out_specs=VMEM,
        compiler_params=params(),
    )(near, slot_rows)
    halo_rows = halo_lists.reshape(-1, BLOCK)
    halo_rows = jnp.pad(halo_rows, ((0, -halo_rows.shape[0] % 8), (0, 0)))
    chunk = (2 * FIELDS, BLOCK)
    new_state, table, group, far_x, far_y = pl.pallas_call(
        state_kernel,
        out_shape=(
            shaped(FIELDS, owned),
            shaped(owned // (2 * BLOCK), *chunk),
            shaped(3, *chunk),
            shaped(*chunk),
            shaped(*chunk),
        ),
        in_specs=[VMEM] * 7,
        out_specs=(VMEM,) * 5,
        scratch_shapes=[pltpu.VMEM((6, *chunk), jnp.float32)],
        compiler_params=params(),
    )(two, one, slot_rows, found, weight_rows, front_mask.reshape(-1, BLOCK), halo_rows)

    far_x = far_swap(far_x, "mapx", sizes[0])
    if sizes[1] > 2:
        far_y = far_swap(far_y, "mapy", sizes[1])
    group = group_gather(group, pair_groups(sizes))

    elems = elem_nodes.shape[-1]
    elem_rows = elems // BLOCK
    more = -elem_rows % 8
    nodes = jnp.pad(elem_nodes.reshape(4, elem_rows, BLOCK), ((0, 0), (0, more), (0, 0)))
    grads = jnp.pad(shape_grads.reshape(12, elem_rows, BLOCK), ((0, 0), (0, more), (0, 0)))
    volume = jnp.pad(elem_volume.reshape(elem_rows, BLOCK), ((0, more), (0, 0)))
    slots_all = table.shape[0] + 6
    own, back, back_x, back_y = pl.pallas_call(
        functools.partial(element_kernel, sizes, elem_rows),
        out_shape=(shaped(4 * owned // BLOCK, BLOCK), shaped(3, 8, BLOCK), shaped(8, BLOCK), shaped(8, BLOCK)),
        in_specs=[VMEM] * 7,
        out_specs=(VMEM,) * 4,
        scratch_shapes=[
            pltpu.VMEM((slots_all, *chunk), jnp.float32),
            pltpu.VMEM((4 * SPLITS, 4 * (elem_rows + more), BLOCK), jnp.float32),
            pltpu.VMEM((6, 8, BLOCK), jnp.float32),
        ],
        compiler_params=params(),
    )(table, group, far_x, far_y, nodes, grads, volume)

    back_x = far_swap(back_x, "mapx", sizes[0])
    if sizes[1] > 2:
        back_y = far_swap(back_y, "mapy", sizes[1])
    back = group_gather(back, pair_groups(sizes))
    residual = pl.pallas_call(
        functools.partial(residual_kernel, sizes),
        out_shape=shaped(4, owned),
        in_specs=[VMEM] * 5,
        out_specs=VMEM,
        scratch_shapes=[pltpu.VMEM((6, 8, BLOCK), jnp.float32)],
        compiler_params=params(),
    )(back, back_x, back_y, own, halo_rows)
    return (new_state[None, None, None], residual[None, None, None])


def solution(mesh):
    sizes = tuple(mesh.shape[axis] for axis in AXES)
    row = P("mapx", "mapy", "layer", None)
    table = P("mapx", "mapy", "layer", None, None)
    return jax.shard_map(
        functools.partial(per_device, sizes),
        mesh=mesh,
        in_specs=(table, table, table, table, row, table, table, table, row),
        out_specs=(table, table),
        check_vma=False,
    )
```

```python
import functools

import jax
import jax.numpy as jnp
from jax import lax
from jax.experimental import pallas as pl
from jax.experimental.pallas import tpu as pltpu
from jax.sharding import PartitionSpec as P

BLOCK = 128
REACH = 2
FIELDS = 6
SPLITS = 3

ocean_temp = 0.0
strain_reg = 0.01
gravity = 0.5

AXES = ("mapx", "mapy", "layer")
VMEM = pl.BlockSpec(memory_space=pltpu.VMEM)
SMEM = pl.BlockSpec(memory_space=pltpu.SMEM)


def params():
    return pltpu.CompilerParams(vmem_limit_bytes=32 * 1024 * 1024)


def near_groups(sizes):
    nx, ny, nl = sizes
    number = lambda x, y, l: (x * ny + y) * nl + l
    return [
        [number(first + i, y, l) for i in range(4) for l in range(nl)] for first in range(0, nx, 4) for y in range(ny)
    ]


def both_ways(pairs):
    return [way for one, other in pairs for way in ((one, other), (other, one))]


def far_pairs(count):
    two, one = [], []
    for first in range(2, count - 3, 4):
        two += [(first, first + 2), (first + 1, first + 3)]
        one += [(first + 1, first + 2)]
    return both_ways(two), both_ways(one)


def group_swap(chunks, groups):
    return lax.all_to_all(chunks, AXES, split_axis=0, concat_axis=0, axis_index_groups=groups)


def pair_swap(value, axis, count, first):
    return lax.ppermute(value, axis, both_ways([(at, at + 1) for at in range(first, count - 1, 2)]))


def swap_all(values, sizes):
    long = [axis for axis in range(3) if sizes[axis] > 2]
    steps = [(axis, 1) for axis in long] + [(axis, 0) for axis in range(3)]
    return [pair_swap(value, AXES[axis], sizes[axis], first) for value, (axis, first) in zip(values, steps)]


def put_blocks(blocks_ref, old_ref, out_ref, chunk, peer):
    slots = blocks_ref.shape[2]
    count = old_ref.shape[0] // FIELDS
    for c in range(slots):
        rows = pl.ds(blocks_ref[peer, 0, c], FIELDS, stride=count)
        out_ref[chunk, FIELDS * c : FIELDS * (c + 1), :] = old_ref[rows, :]


def far_place():
    at = lax.rem(lax.axis_index("mapx") + 2, 4)
    return at, jnp.where(at < 2, 1, -1)


def pack_far_kernel(blocks_ref, old_ref, swap_ref, own_ref):
    layer = lax.axis_index("layer")
    _, way = far_place()
    for i in range(2):
        peer = ((REACH - i) * way + REACH) * 2
        put_blocks(blocks_ref, old_ref, swap_ref, i, peer + 1 - layer)
    for i in range(2):
        peer = ((REACH - i) * way + REACH) * 2
        put_blocks(blocks_ref, old_ref, own_ref, i, peer + layer)


def pack_near_kernel(blocks_ref, old_ref, near_ref):
    here = lax.rem(lax.axis_index("mapx"), 4)

    def near(chunk, carry):
        offset = chunk // 2 - here

        @pl.when(jnp.abs(offset) <= REACH)
        def _():
            put_blocks(blocks_ref, old_ref, near_ref, chunk, (offset + REACH) * 2 + lax.rem(chunk, 2))

        return carry

    lax.fori_loop(0, 8, near, 0)


def pick(row, lanes):
    return jnp.take_along_axis(jnp.broadcast_to(row, lanes.shape), lanes, axis=1)


def add_blocks(chunk_ref, chunk, first_block, slots, blocks, lanes, found):
    parts = len(blocks)
    local = [blocks[v] - first_block for v in range(parts)]
    found = list(found)
    for c in range(slots):
        hit = [local[v] == c for v in range(parts)]
        for f in range(FIELDS):
            row = chunk_ref[chunk, FIELDS * c + f : FIELDS * c + f + 1, :]
            for v in range(parts):
                found[f * parts + v] = jnp.where(hit[v], pick(row, lanes[v]), found[f * parts + v])
    return tuple(found)


def cut_rows(from_ref, to_ref):
    count = from_ref.shape[1] // BLOCK
    for r in range(from_ref.shape[0]):
        for i in range(count):
            to_ref[r * count + i : r * count + i + 1, :] = from_ref[r : r + 1, i * BLOCK : (i + 1) * BLOCK]


def near_kernel(near_ref, slots_in_ref, weights_in_ref, found_ref, slots_ref, weights_ref):
    cut_rows(slots_in_ref, slots_ref)
    cut_rows(weights_in_ref, weights_ref)
    slots = near_ref.shape[1] // FIELDS
    parts = slots_ref.shape[0] // 8
    ids = [slots_ref[8 * v : 8 * v + 8, :] for v in range(parts)]
    blocks = [i >> 7 for i in ids]
    lanes = [i & (BLOCK - 1) for i in ids]
    here = lax.rem(lax.axis_index("mapx"), 4)

    def step(chunk, found):
        source = (chunk // 2 - here + REACH) * 2 + lax.rem(chunk, 2)
        return add_blocks(near_ref, chunk, source * slots, slots, blocks, lanes, found)

    start = tuple(jnp.zeros((8, BLOCK), jnp.float32) for _ in range(FIELDS * parts))
    found = lax.fori_loop(0, 8, step, start)
    for f in range(FIELDS):
        for v in range(parts):
            found_ref[f, 8 * v : 8 * v + 8, :] = found[f * parts + v]


def state_kernel(
    counts, two_ref, one_ref, slots_ref, found_ref, weights_ref, mask_ref, halos_ref, state_ref, table_ref, *more_refs
):
    send_refs, cut_ref = more_refs[:-1], more_refs[-1]
    slots = two_ref.shape[1] // FIELDS
    parts = slots_ref.shape[0] // 8
    ids = [slots_ref[8 * v : 8 * v + 8, :] for v in range(parts)]
    blocks = [i >> 7 for i in ids]
    lanes = [i & (BLOCK - 1) for i in ids]
    at, way = far_place()
    found = tuple(found_ref[f, 8 * v : 8 * v + 8, :] for f in range(FIELDS) for v in range(parts))
    first_two = (2 * way + REACH) * 2 * slots
    first_one = jnp.where((at == 1) | (at == 2), (way + REACH) * 2 * slots, -(1 << 20))
    for ref, first in ((two_ref, first_two), (one_ref, first_one)):

        def step(chunk, found, ref=ref, first=first):
            return add_blocks(ref, chunk, first + chunk * slots, slots, blocks, lanes, found)

        found = lax.fori_loop(0, 2, step, found)
    front = mask_ref[...] == 1
    rows = mask_ref.shape[0]
    for f in range(FIELDS):
        total = jnp.zeros((rows, BLOCK), jnp.float32)
        for v in range(parts):
            term = found[f * parts + v] * weights_ref[8 * v : 8 * v + 8, :]
            for k in range(8 // rows):
                total = total + term[k * rows : (k + 1) * rows, :]
        if f == 4:
            total = jnp.where(front, ocean_temp, total)
        for r in range(rows):
            state_ref[f : f + 1, r * BLOCK : (r + 1) * BLOCK] = total[r : r + 1, :]
        for s in range(rows // 2):
            table_ref[s, 2 * f : 2 * f + 2, :] = total[2 * s : 2 * s + 2, :]
    starts = (0, halos_ref.shape[0] - 8)
    halo = [halos_ref[first : first + 8, :] for first in starts]
    halo_blocks = [i >> 7 for i in halo]
    halo_lanes = [i & (BLOCK - 1) for i in halo]
    for f in range(FIELDS):
        cut = [jnp.zeros((8, BLOCK), jnp.float32) for _ in starts]
        for b in range(rows):
            row = table_ref[b // 2, 2 * f + b % 2 : 2 * f + b % 2 + 1, :]
            for v in range(2):
                cut[v] = jnp.where(halo_blocks[v] == b, pick(row, halo_lanes[v]), cut[v])
        for k in range(6):
            v = 0 if 2 * k + 2 <= 8 else 1
            r = 2 * k - starts[v]
            cut_ref[k, 2 * f : 2 * f + 2, :] = cut[v][r : r + 2, :]
    send_pairs(counts, cut_ref, send_refs, [(0, 1), (2, 3), (4, 5)])


def pair_places():
    return [lax.rem(lax.axis_index(axis), 2) for axis in AXES]


def send_pairs(counts, cut_ref, send_refs, order):
    places = pair_places()
    long = [axis for axis in range(3) if counts[axis] > 2]
    for axis in range(3):
        even, odd = order[axis]
        send_refs[len(long) + axis][...] = cut_ref[jnp.where(places[axis] == 0, even, odd)]
        if axis in long:
            send_refs[long.index(axis)][...] = cut_ref[jnp.where(places[axis] == 0, odd, even)]


def arrivals(counts, came_refs):
    places = pair_places()
    long = [axis for axis in range(3) if counts[axis] > 2]
    result = []
    for axis in range(3):
        inside = came_refs[len(long) + axis][...]
        at = lax.axis_index(AXES[axis])
        edge = jnp.where(places[axis] == 0, at == 0, at == counts[axis] - 1)
        outside = jnp.zeros_like(inside)
        if axis in long:
            outside = jnp.where(edge, 0.0, came_refs[long.index(axis)][...])
        result.append((places[axis], inside, outside))
    return result


def one_hot_sum(values, ids, block_count):
    rows = lax.broadcasted_iota(jnp.int32, (block_count, BLOCK), 0)
    hit = rows == jnp.broadcast_to(ids >> 7, rows.shape)
    left = [jnp.where(hit, jnp.broadcast_to(v, rows.shape), 0.0) for v in values]
    left = jnp.concatenate(left, axis=0).astype(jnp.bfloat16)
    lanes = lax.broadcasted_iota(jnp.int32, (BLOCK, BLOCK), 0)
    right = jnp.where(lanes == jnp.broadcast_to(ids & (BLOCK - 1), lanes.shape), 1.0, 0.0).astype(jnp.bfloat16)
    return left, right


def cut_parts(value):
    parts = []
    for _ in range(SPLITS - 1):
        part = value.astype(jnp.bfloat16).astype(jnp.float32)
        parts.append(part)
        value = value - part
    return parts + [value]


def nt_dot(left, right):
    return lax.dot_general(left, right, (((1,), (1,)), ((), ())), preferred_element_type=jnp.float32)


def element_kernel(counts, moves, *refs):
    table_in_ref, nodes_in_ref, grads_ref, volume_ref = refs[:4]
    came_refs = refs[4 : 4 + moves]
    own_ref = refs[4 + moves]
    send_refs = refs[5 + moves : 5 + 2 * moves]
    table_ref, nodes_ref, values_ref, parts_ref, cut_ref = refs[5 + 2 * moves :]
    owned_slots = table_in_ref.shape[0]
    table_ref[0:owned_slots] = table_in_ref[...]
    for axis, (place_at, inside, outside) in enumerate(arrivals(counts, came_refs)):
        table_ref[owned_slots + 2 * axis + 1 - place_at] = inside
        table_ref[owned_slots + 2 * axis + place_at] = outside
    cut_rows(nodes_in_ref, nodes_ref)
    block_count = 2 * table_ref.shape[0]
    all_rows = nodes_ref.shape[0]
    elem_rows = all_rows // 4
    ids = [nodes_ref[first : first + 8, :] for first in range(0, all_rows, 8)]
    blocks = [i >> 7 for i in ids]
    lanes = [i & (BLOCK - 1) for i in ids]
    for f in range(FIELDS):
        found = [jnp.zeros((8, BLOCK), jnp.float32) for _ in ids]
        for b in range(block_count):
            row = table_ref[b // 2, 2 * f + b % 2 : 2 * f + b % 2 + 1, :]
            for v in range(len(ids)):
                found[v] = jnp.where(blocks[v] == b, pick(row, lanes[v]), found[v])
        for v in range(len(ids)):
            values_ref[f, 8 * v : 8 * v + 8, :] = found[v]
    for first in [*range(0, elem_rows - 7, 8)] + ([elem_rows - 8] if elem_rows % 8 else []):
        at = [slice(r * elem_rows + first, r * elem_rows + first + 8) for r in range(12)]
        values = [[values_ref[f, at[a], :] for f in range(FIELDS)] for a in range(4)]
        grads = [[grads_ref[at[3 * a + j], :] for j in range(3)] for a in range(4)]
        volume = volume_ref[at[0], :]
        velgrad = [[sum(values[a][i] * grads[a][j] for a in range(4)) for j in range(3)] for i in range(3)]
        strain = [[0.5 * (velgrad[i][j] + velgrad[j][i]) if i <= j else None for j in range(3)] for i in range(3)]
        diagonal = sum(strain[i][i] * strain[i][i] for i in range(3))
        corner = sum(strain[i][j] * strain[i][j] for i, j in ((0, 1), (0, 2), (1, 2)))
        second = 0.5 * diagonal + corner
        pressure, temper, damage = [0.25 * (values[0][f] + values[1][f] + values[2][f] + values[3][f]) for f in (3, 4, 5)]
        root = jnp.exp(jnp.log(second + strain_reg) * (-1.0 / 3.0))
        twice = (1.0 - damage) * jnp.exp(-temper) * root
        stress = [[None] * 3 for _ in range(3)]
        for i in range(3):
            for j in range(i, 3):
                stress[i][j] = twice * strain[i][j] - (pressure if i == j else 0.0)
                stress[j][i] = stress[i][j]
        lift = (0.25 * gravity) * volume
        flow = 0.25 * volume * (velgrad[0][0] + velgrad[1][1] + velgrad[2][2])
        for s, part in enumerate(cut_parts(flow)):
            for a in range(4):
                parts_ref[3 * SPLITS + s, at[a], :] = part
        for a in range(4):
            for i in range(3):
                force = volume * sum(stress[i][j] * grads[a][j] for j in range(3))
                if i == 2:
                    force = force + lift
                for s, part in enumerate(cut_parts(force)):
                    parts_ref[i * SPLITS + s, at[a], :] = part

    group = 10

    def gather_terms(step, total):
        lefts, rights = [], []
        for r in range(group):
            at = pl.ds(step * group + r, 1)
            terms = [parts_ref[c * SPLITS + s, at, :] for s in range(SPLITS) for c in range(4)]
            left, right = one_hot_sum(terms, nodes_ref[at, :], block_count)
            lefts.append(left)
            rights.append(right)
        return total + nt_dot(jnp.concatenate(lefts, axis=1), jnp.concatenate(rights, axis=1))

    width = 4 * block_count
    total = lax.fori_loop(0, all_rows // group, gather_terms, jnp.zeros((SPLITS * width, BLOCK), jnp.float32))
    total = sum(total[s * width : (s + 1) * width, :] for s in range(SPLITS))
    owned = 2 * owned_slots
    for c in range(4):
        own_ref[c * owned : (c + 1) * owned, :] = total[c * block_count : c * block_count + owned, :]
        for k in range(6):
            first = c * block_count + owned + 2 * k
            cut_ref[k, 2 * c : 2 * c + 2, :] = total[first : first + 2, :]
    send_pairs(counts, cut_ref, send_refs, [(1, 0), (3, 2), (5, 4)])


def residual_kernel(counts, moves, *refs):
    own_ref, halos_ref = refs[:2]
    out_ref, came_ref = refs[2 + moves :]
    for axis, (place_at, inside, outside) in enumerate(arrivals(counts, refs[2 : 2 + moves])):
        came_ref[2 * axis + place_at] = inside
        came_ref[2 * axis + 1 - place_at] = outside
    owned = own_ref.shape[0] // 4
    lefts, rights = [], []
    for k in range(6):
        parts = cut_parts(came_ref[k])
        for h in range(2):
            ids = halos_ref[2 * k + h : 2 * k + h + 1, :]
            terms = [parts[s][2 * c + h : 2 * c + h + 1, :] for s in range(SPLITS) for c in range(4)]
            left, right = one_hot_sum(terms, ids, owned)
            lefts.append(left)
            rights.append(right)
    total = nt_dot(jnp.concatenate(lefts, axis=1), jnp.concatenate(rights, axis=1))
    width = 4 * owned
    total = sum(total[s * width : (s + 1) * width, :] for s in range(SPLITS)) + own_ref[...]
    for c in range(4):
        for b in range(owned):
            r = c * owned + b
            out_ref[c : c + 1, b * BLOCK : (b + 1) * BLOCK] = total[r : r + 1, :]


def shaped(*shape):
    return jax.ShapeDtypeStruct(shape, jnp.float32)


def per_device(
    sizes,
    old_state,
    send_blocks,
    node_slots,
    node_weights,
    front_mask,
    halo_lists,
    elem_nodes,
    shape_grads,
    elem_volume,
):
    old_state, send_blocks = old_state[0, 0, 0], send_blocks[0, 0, 0]
    slots = send_blocks.shape[1]
    send_blocks = send_blocks.reshape(-1, 1, slots)
    rows = FIELDS * slots
    old_rows = old_state.reshape(-1, BLOCK)
    swap, mine = pl.pallas_call(
        pack_far_kernel,
        out_shape=(shaped(2, rows, BLOCK), shaped(2, rows, BLOCK)),
        in_specs=[SMEM, VMEM],
        out_specs=(VMEM, VMEM),
        compiler_params=params(),
    )(send_blocks, old_rows)
    swap = lax.ppermute(swap, "layer", both_ways([(0, 1)]))
    near = pl.pallas_call(
        pack_near_kernel,
        out_shape=shaped(8, rows, BLOCK),
        in_specs=[SMEM, VMEM],
        out_specs=VMEM,
        compiler_params=params(),
    )(send_blocks, old_rows)
    near = group_swap(near, near_groups(sizes))
    first = lax.axis_index("layer") == 0
    pairs_two, pairs_one = far_pairs(sizes[0])
    sorted_far = [jnp.where(first, jnp.stack([mine[i], swap[i]]), jnp.stack([swap[i], mine[i]])) for i in range(2)]
    two = lax.ppermute(sorted_far[0], "mapx", pairs_two)
    one = lax.ppermute(sorted_far[1], "mapx", pairs_one)

    owned = node_slots.shape[-1]
    slot_rows = node_slots.size // BLOCK
    found, node_rows, weight_rows = pl.pallas_call(
        near_kernel,
        out_shape=(
            shaped(FIELDS, slot_rows, BLOCK),
            jax.ShapeDtypeStruct((slot_rows, BLOCK), jnp.int32),
            shaped(slot_rows, BLOCK),
        ),
        in_specs=[VMEM] * 3,
        out_specs=(VMEM,) * 3,
        compiler_params=params(),
    )(near, node_slots[0, 0, 0], node_weights[0, 0, 0])
    halo_rows = halo_lists.reshape(-1, BLOCK)
    moves = 3 + sum(size > 2 for size in sizes)
    chunk = (2 * FIELDS, BLOCK)
    new_state, table, *ghosts = pl.pallas_call(
        functools.partial(state_kernel, sizes),
        out_shape=(shaped(FIELDS, owned), shaped(owned // (2 * BLOCK), *chunk)) + (shaped(*chunk),) * moves,
        in_specs=[VMEM] * 7,
        out_specs=(VMEM,) * (2 + moves),
        scratch_shapes=[pltpu.VMEM((6, *chunk), jnp.float32)],
        compiler_params=params(),
    )(two, one, node_rows, found, weight_rows, front_mask.reshape(-1, BLOCK), halo_rows)
    ghosts = swap_all(ghosts, sizes)

    all_rows = elem_nodes.size // BLOCK
    slots_all = table.shape[0] + 6
    own, *sums = pl.pallas_call(
        functools.partial(element_kernel, sizes, moves),
        out_shape=(shaped(4 * owned // BLOCK, BLOCK),) + (shaped(8, BLOCK),) * moves,
        in_specs=[VMEM] * (4 + moves),
        out_specs=(VMEM,) * (1 + moves),
        scratch_shapes=[
            pltpu.VMEM((slots_all, *chunk), jnp.float32),
            pltpu.VMEM((all_rows, BLOCK), jnp.int32),
            pltpu.VMEM((FIELDS, all_rows, BLOCK), jnp.float32),
            pltpu.VMEM((4 * SPLITS, all_rows, BLOCK), jnp.float32),
            pltpu.VMEM((6, 8, BLOCK), jnp.float32),
        ],
        compiler_params=params(),
    )(table, elem_nodes[0, 0, 0], shape_grads.reshape(-1, BLOCK), elem_volume.reshape(-1, BLOCK), *ghosts)
    sums = swap_all(sums, sizes)
    residual = pl.pallas_call(
        functools.partial(residual_kernel, sizes, moves),
        out_shape=shaped(4, owned),
        in_specs=[VMEM] * (2 + moves),
        out_specs=VMEM,
        scratch_shapes=[pltpu.VMEM((6, 8, BLOCK), jnp.float32)],
        compiler_params=params(),
    )(own, halo_rows, *sums)
    return (new_state[None, None, None], residual[None, None, None])


def solution(mesh):
    sizes = tuple(mesh.shape[axis] for axis in AXES)
    row = P("mapx", "mapy", "layer", None)
    table = P("mapx", "mapy", "layer", None, None)
    return jax.shard_map(
        functools.partial(per_device, sizes),
        mesh=mesh,
        in_specs=(table, table, table, table, row, table, table, table, row),
        out_specs=(table, table),
        check_vma=False,
    )
```

```python
import functools

import jax
import jax.numpy as jnp
from jax import lax
from jax.experimental import pallas as pl
from jax.experimental.pallas import tpu as pltpu
from jax.sharding import PartitionSpec as P

BLOCK = 128
REACH = 2
FIELDS = 6
SPLITS = 3

ocean_temp = 0.0
strain_reg = 0.01
gravity = 0.5

AXES = ("mapx", "mapy", "layer")
VMEM = pl.BlockSpec(memory_space=pltpu.VMEM)
SMEM = pl.BlockSpec(memory_space=pltpu.SMEM)


def params():
    return pltpu.CompilerParams(vmem_limit_bytes=32 * 1024 * 1024)


def both_ways(pairs):
    return [way for one, other in pairs for way in ((one, other), (other, one))]


def column_moves(count):
    return [
        both_ways([(at, at + 1) for at in range(1, count - 1, 2)]),
        both_ways([(at + i, at + i + 2) for at in range(0, count - 3, 4) for i in range(2)]),
        both_ways([(at + i, at + i + 2) for at in range(2, count - 3, 4) for i in range(2)]),
        both_ways([(at, at + 1) for at in range(0, count - 1, 2)]),
    ]


def column_offsets():
    at = lax.axis_index("mapx")
    near = jnp.where(lax.rem(at, 2) == 0, 1, -1)
    two = jnp.where(lax.rem(at, 4) < 2, 2, -2)
    return [-near, two, -two, near, 0]


def pair_swap(value, axis, count, first):
    return lax.ppermute(value, axis, both_ways([(at, at + 1) for at in range(first, count - 1, 2)]))


def swap_all(values, sizes):
    long = [axis for axis in range(3) if sizes[axis] > 2]
    steps = [(axis, 1) for axis in long] + [(axis, 0) for axis in range(3)]
    return [pair_swap(value, AXES[axis], sizes[axis], first) for value, (axis, first) in zip(values, steps)]


def pack_kernel(count, *refs):
    blocks_in_ref, old_in_ref = refs[:2]
    cross_ref, mine_ref = refs[2 + count : 4 + count]
    blocks_ref, old_ref, sems = refs[4 + 2 * count :]
    first = [pltpu.make_async_copy(blocks_in_ref, blocks_ref, sems.at[0])]
    first += [pltpu.make_async_copy(old_in_ref, old_ref, sems.at[1])]
    rest = [
        pltpu.make_async_copy(refs[2 + i], refs[4 + count + i], sems.at[2 + i]) for i in range(count)
    ]
    for copy in first + rest:
        copy.start()
    for copy in first:
        copy.wait()
    slots = blocks_ref.shape[2]
    stride = old_ref.shape[0] // FIELDS
    layer = lax.axis_index("layer")
    offsets = column_offsets()
    for out_ref, to_layer in ((cross_ref, 1 - layer), (mine_ref, layer)):
        for q, offset in enumerate(offsets):
            peer = (offset + REACH) * 2 + to_layer
            for c in range(slots):
                rows = pl.ds(blocks_ref[peer, 0, c], FIELDS, stride=stride)
                out_ref[q, FIELDS * c : FIELDS * (c + 1), :] = old_ref[rows, :]
    for copy in rest:
        copy.wait()


def pick(row, lanes):
    return jnp.take_along_axis(jnp.broadcast_to(row, lanes.shape), lanes, axis=1)


def pick_fields(table_ref, block_count, blocks, lanes):
    found = [jnp.zeros((8, BLOCK), jnp.float32) for _ in range(FIELDS)]
    for b in range(block_count):
        hit = blocks == b
        for f in range(FIELDS):
            row = table_ref[b // 2, 2 * f + b % 2 : 2 * f + b % 2 + 1, :]
            found[f] = jnp.where(hit, pick(row, lanes), found[f])
    return found


def add_blocks(ref, chunk, first_block, blocks, lanes, found):
    local = blocks - first_block
    found = list(found)
    for c in range(ref.shape[1] // FIELDS):
        hit = local == c
        for f in range(FIELDS):
            row = ref[chunk, FIELDS * c + f : FIELDS * c + f + 1, :]
            found[f] = jnp.where(hit, pick(row, lanes), found[f])
    return tuple(found)


def first_block(offset, other_layer, slots):
    layer = lax.axis_index("layer")
    return ((offset + REACH) * 2 + (1 - layer if other_layer else layer)) * slots


def cut_rows(from_ref, to_ref):
    count = from_ref.shape[1] // BLOCK
    for r in range(from_ref.shape[0]):
        for i in range(count):
            to_ref[r * count + i : r * count + i + 1, :] = from_ref[r : r + 1, i * BLOCK : (i + 1) * BLOCK]


def near_kernel(
    mine_ref, swap_ref, next_ref, slots_in_ref, weights_in_ref, halos_in_ref, found_ref, slots_ref, weights_ref, halos_ref
):
    for k in range(halos_in_ref.shape[0]):
        cut_rows(halos_in_ref.at[k], halos_ref.at[2 * k : 2 * k + 2])
    cut_rows(slots_in_ref, slots_ref)
    cut_rows(weights_in_ref, weights_ref)
    slots = mine_ref.shape[1] // FIELDS
    offsets = column_offsets()
    for v in range(slots_ref.shape[0] // 8):
        ids = slots_ref[8 * v : 8 * v + 8, :]
        blocks, lanes = ids >> 7, ids & (BLOCK - 1)
        found = tuple(jnp.zeros((8, BLOCK), jnp.float32) for _ in range(FIELDS))
        for ref, chunk, q, other in ((mine_ref, 4, 4, 0), (swap_ref, 4, 4, 1), (next_ref, 0, 0, 0), (next_ref, 1, 0, 1)):
            found = add_blocks(ref, chunk, first_block(offsets[q], other, slots), blocks, lanes, found)
        for f in range(FIELDS):
            found_ref[f, 8 * v : 8 * v + 8, :] = found[f]


def state_kernel(
    counts, two_ref, across_ref, pair_ref, slots_ref, found_ref, weights_ref, mask_ref, halos_ref, state_ref, table_ref, *more_refs
):
    send_refs, cut_ref = more_refs[:-1], more_refs[-1]
    slots = two_ref.shape[1] // FIELDS
    offsets = column_offsets()
    parts = slots_ref.shape[0] // 8
    found = []
    for v in range(parts):
        ids = slots_ref[8 * v : 8 * v + 8, :]
        blocks, lanes = ids >> 7, ids & (BLOCK - 1)
        fields = tuple(found_ref[f, 8 * v : 8 * v + 8, :] for f in range(FIELDS))
        for q, ref in ((1, two_ref), (2, across_ref), (3, pair_ref)):
            for other in range(2):
                fields = add_blocks(ref, other, first_block(offsets[q], other, slots), blocks, lanes, fields)
        found.append(fields)
    front = mask_ref[...] == 1
    rows = mask_ref.shape[0]
    for f in range(FIELDS):
        total = jnp.zeros((rows, BLOCK), jnp.float32)
        for v in range(parts):
            term = found[v][f] * weights_ref[8 * v : 8 * v + 8, :]
            for k in range(8 // rows):
                total = total + term[k * rows : (k + 1) * rows, :]
        if f == 4:
            total = jnp.where(front, ocean_temp, total)
        for r in range(rows):
            state_ref[f : f + 1, r * BLOCK : (r + 1) * BLOCK] = total[r : r + 1, :]
        for s in range(rows // 2):
            table_ref[s, 2 * f : 2 * f + 2, :] = total[2 * s : 2 * s + 2, :]
    starts = (0, halos_ref.shape[0] - 8)
    halo = [halos_ref[first : first + 8, :] for first in starts]
    halo_blocks = [i >> 7 for i in halo]
    halo_lanes = [i & (BLOCK - 1) for i in halo]
    for v in range(2):
        cut = pick_fields(table_ref, rows, halo_blocks[v], halo_lanes[v])
        for k in range(6):
            r = 2 * k - starts[v]
            if 0 <= r <= 6:
                for f in range(FIELDS):
                    cut_ref[k, 2 * f : 2 * f + 2, :] = cut[f][r : r + 2, :]
    send_pairs(counts, cut_ref, send_refs, [(0, 1), (2, 3), (4, 5)])


def pair_places():
    return [lax.rem(lax.axis_index(axis), 2) for axis in AXES]


def send_pairs(counts, cut_ref, send_refs, order):
    places = pair_places()
    long = [axis for axis in range(3) if counts[axis] > 2]
    for axis in range(3):
        even, odd = order[axis]
        send_refs[len(long) + axis][...] = cut_ref[jnp.where(places[axis] == 0, even, odd)]
        if axis in long:
            send_refs[long.index(axis)][...] = cut_ref[jnp.where(places[axis] == 0, odd, even)]


def arrivals(counts, came_refs):
    places = pair_places()
    long = [axis for axis in range(3) if counts[axis] > 2]
    result = []
    for axis in range(3):
        inside = came_refs[len(long) + axis][...]
        at = lax.axis_index(AXES[axis])
        edge = jnp.where(places[axis] == 0, at == 0, at == counts[axis] - 1)
        outside = jnp.zeros_like(inside)
        if axis in long:
            outside = jnp.where(edge, 0.0, came_refs[long.index(axis)][...])
        result.append((places[axis], inside, outside))
    return result


def one_hot_sum(values, ids, block_count):
    rows = lax.broadcasted_iota(jnp.int32, (block_count, BLOCK), 0)
    hit = rows == jnp.broadcast_to(ids >> 7, rows.shape)
    left = [jnp.where(hit, jnp.broadcast_to(v, rows.shape), 0.0) for v in values]
    left = jnp.concatenate(left, axis=0).astype(jnp.bfloat16)
    lanes = lax.broadcasted_iota(jnp.int32, (BLOCK, BLOCK), 0)
    right = jnp.where(lanes == jnp.broadcast_to(ids & (BLOCK - 1), lanes.shape), 1.0, 0.0).astype(jnp.bfloat16)
    return left, right


def cut_parts(value):
    parts = []
    for _ in range(SPLITS - 1):
        part = value.astype(jnp.bfloat16).astype(jnp.float32)
        parts.append(part)
        value = value - part
    return parts + [value]


def nt_dot(left, right):
    return lax.dot_general(left, right, (((1,), (1,)), ((), ())), preferred_element_type=jnp.float32)


def element_kernel(counts, moves, *refs):
    table_in_ref, nodes_in_ref, grads_ref, volume_in_ref = refs[:4]
    came_refs = refs[4 : 4 + moves]
    own_ref = refs[4 + moves]
    send_refs = refs[5 + moves : 5 + 2 * moves]
    table_ref, nodes_ref, volume_ref, values_ref, parts_ref, cut_ref = refs[5 + 2 * moves :]
    owned_slots = table_in_ref.shape[0]
    table_ref[0:owned_slots] = table_in_ref[...]
    for axis, (place_at, inside, outside) in enumerate(arrivals(counts, came_refs)):
        table_ref[owned_slots + 2 * axis + 1 - place_at] = inside
        table_ref[owned_slots + 2 * axis + place_at] = outside
    cut_rows(nodes_in_ref, nodes_ref)
    cut_rows(volume_in_ref, volume_ref)
    block_count = 2 * table_ref.shape[0]
    all_rows = nodes_ref.shape[0]
    elem_rows = all_rows // 4
    for first in range(0, all_rows, 8):
        ids = nodes_ref[first : first + 8, :]
        found = pick_fields(table_ref, block_count, ids >> 7, ids & (BLOCK - 1))
        for f in range(FIELDS):
            values_ref[f, first : first + 8, :] = found[f]
    for first in [*range(0, elem_rows - 7, 8)] + ([elem_rows - 8] if elem_rows % 8 else []):
        at = [slice(r * elem_rows + first, r * elem_rows + first + 8) for r in range(12)]
        values = [[values_ref[f, at[a], :] for f in range(FIELDS)] for a in range(4)]
        grads = [[grads_ref[at[3 * a + j], :] for j in range(3)] for a in range(4)]
        volume = volume_ref[at[0], :]
        velgrad = [[sum(values[a][i] * grads[a][j] for a in range(4)) for j in range(3)] for i in range(3)]
        strain = [[0.5 * (velgrad[i][j] + velgrad[j][i]) if i <= j else None for j in range(3)] for i in range(3)]
        diagonal = sum(strain[i][i] * strain[i][i] for i in range(3))
        corner = sum(strain[i][j] * strain[i][j] for i, j in ((0, 1), (0, 2), (1, 2)))
        second = 0.5 * diagonal + corner
        pressure, temper, damage = [0.25 * (values[0][f] + values[1][f] + values[2][f] + values[3][f]) for f in (3, 4, 5)]
        root = jnp.exp(jnp.log(second + strain_reg) * (-1.0 / 3.0))
        twice = (1.0 - damage) * jnp.exp(-temper) * root
        stress = [[None] * 3 for _ in range(3)]
        for i in range(3):
            for j in range(i, 3):
                stress[i][j] = twice * strain[i][j] - (pressure if i == j else 0.0)
                stress[j][i] = stress[i][j]
        lift = (0.25 * gravity) * volume
        flow = 0.25 * volume * (velgrad[0][0] + velgrad[1][1] + velgrad[2][2])
        for s, part in enumerate(cut_parts(flow)):
            for a in range(4):
                parts_ref[3 * SPLITS + s, at[a], :] = part
        for a in range(4):
            for i in range(3):
                force = volume * sum(stress[i][j] * grads[a][j] for j in range(3))
                if i == 2:
                    force = force + lift
                for s, part in enumerate(cut_parts(force)):
                    parts_ref[i * SPLITS + s, at[a], :] = part

    group = 10

    def gather_terms(step, total):
        lefts, rights = [], []
        for r in range(group):
            at = pl.ds(step * group + r, 1)
            terms = [parts_ref[c * SPLITS + s, at, :] for s in range(SPLITS) for c in range(4)]
            left, right = one_hot_sum(terms, nodes_ref[at, :], block_count)
            lefts.append(left)
            rights.append(right)
        return total + nt_dot(jnp.concatenate(lefts, axis=1), jnp.concatenate(rights, axis=1))

    width = 4 * block_count
    total = lax.fori_loop(0, all_rows // group, gather_terms, jnp.zeros((SPLITS * width, BLOCK), jnp.float32))
    total = sum(total[s * width : (s + 1) * width, :] for s in range(SPLITS))
    owned = 2 * owned_slots
    for c in range(4):
        own_ref[c * owned : (c + 1) * owned, :] = total[c * block_count : c * block_count + owned, :]
        for k in range(6):
            first = c * block_count + owned + 2 * k
            cut_ref[k, 2 * c : 2 * c + 2, :] = total[first : first + 2, :]
    send_pairs(counts, cut_ref, send_refs, [(1, 0), (3, 2), (5, 4)])


def residual_kernel(counts, moves, *refs):
    own_ref, halos_ref = refs[:2]
    out_ref, came_ref = refs[2 + moves :]
    for axis, (place_at, inside, outside) in enumerate(arrivals(counts, refs[2 : 2 + moves])):
        came_ref[2 * axis + place_at] = inside
        came_ref[2 * axis + 1 - place_at] = outside
    owned = own_ref.shape[0] // 4
    lefts, rights = [], []
    for k in range(6):
        parts = cut_parts(came_ref[k])
        for h in range(2):
            ids = halos_ref[2 * k + h : 2 * k + h + 1, :]
            terms = [parts[s][2 * c + h : 2 * c + h + 1, :] for s in range(SPLITS) for c in range(4)]
            left, right = one_hot_sum(terms, ids, owned)
            lefts.append(left)
            rights.append(right)
    total = nt_dot(jnp.concatenate(lefts, axis=1), jnp.concatenate(rights, axis=1))
    width = 4 * owned
    total = sum(total[s * width : (s + 1) * width, :] for s in range(SPLITS)) + own_ref[...]
    for c in range(4):
        for b in range(owned):
            r = c * owned + b
            out_ref[c : c + 1, b * BLOCK : (b + 1) * BLOCK] = total[r : r + 1, :]


def shaped(*shape):
    return jax.ShapeDtypeStruct(shape, jnp.float32)


def per_device(
    sizes,
    old_state,
    send_blocks,
    node_slots,
    node_weights,
    front_mask,
    halo_lists,
    elem_nodes,
    shape_grads,
    elem_volume,
):
    old_state, send_blocks = old_state[0, 0, 0], send_blocks[0, 0, 0]
    slots = send_blocks.shape[1]
    send_blocks = send_blocks.reshape(-1, 1, slots)
    rows = FIELDS * slots
    arguments = [
        node_slots[0, 0, 0],
        node_weights[0, 0, 0],
        front_mask.reshape(-1, BLOCK),
        halo_lists.reshape(halo_lists.shape[-2], 1, -1),
        elem_nodes[0, 0, 0],
        shape_grads.reshape(-1, BLOCK),
        elem_volume[0, 0],
    ]
    old_rows = old_state.reshape(-1, BLOCK)
    count = len(arguments)
    cross, mine, *held = pl.pallas_call(
        functools.partial(pack_kernel, count),
        out_shape=[shaped(5, rows, BLOCK)] * 2 + [jax.ShapeDtypeStruct(a.shape, a.dtype) for a in arguments],
        in_specs=[pl.BlockSpec(memory_space=pltpu.HBM)] * (2 + count),
        out_specs=[VMEM] * (2 + count),
        scratch_shapes=[
            pltpu.SMEM(send_blocks.shape, jnp.int32),
            pltpu.VMEM(old_rows.shape, jnp.float32),
            pltpu.SemaphoreType.DMA((2 + count,)),
        ],
        compiler_params=params(),
    )(*(pltpu.with_memory_space_constraint(a, pltpu.HBM) for a in (send_blocks, old_rows, *arguments)))
    node_slots, node_weights, mask_rows, halos, elem_nodes, grad_rows, volume = held
    swap = lax.ppermute(cross, "layer", both_ways([(0, 1)]))
    moved = [
        lax.ppermute(jnp.stack([mine[q], swap[q]]), "mapx", pairs) for q, pairs in enumerate(column_moves(sizes[0]))
    ]

    owned = node_slots.shape[-1]
    slot_rows = node_slots.size // BLOCK
    found, node_rows, weight_rows, halo_rows = pl.pallas_call(
        near_kernel,
        out_shape=(
            shaped(FIELDS, slot_rows, BLOCK),
            jax.ShapeDtypeStruct((slot_rows, BLOCK), jnp.int32),
            shaped(slot_rows, BLOCK),
            jax.ShapeDtypeStruct((halos.size // BLOCK, BLOCK), jnp.int32),
        ),
        in_specs=[VMEM] * 6,
        out_specs=(VMEM,) * 4,
        compiler_params=params(),
    )(mine, swap, moved[0], node_slots, node_weights, halos)
    moves = 3 + sum(size > 2 for size in sizes)
    chunk = (2 * FIELDS, BLOCK)
    new_state, table, *ghosts = pl.pallas_call(
        functools.partial(state_kernel, sizes),
        out_shape=(shaped(FIELDS, owned), shaped(owned // (2 * BLOCK), *chunk)) + (shaped(*chunk),) * moves,
        in_specs=[VMEM] * 8,
        out_specs=(VMEM,) * (2 + moves),
        scratch_shapes=[pltpu.VMEM((6, *chunk), jnp.float32)],
        compiler_params=params(),
    )(*moved[1:], node_rows, found, weight_rows, mask_rows, halo_rows)
    ghosts = swap_all(ghosts, sizes)

    all_rows = elem_nodes.size // BLOCK
    slots_all = table.shape[0] + 6
    own, *sums = pl.pallas_call(
        functools.partial(element_kernel, sizes, moves),
        out_shape=(shaped(4 * owned // BLOCK, BLOCK),) + (shaped(8, BLOCK),) * moves,
        in_specs=[VMEM] * (4 + moves),
        out_specs=(VMEM,) * (1 + moves),
        scratch_shapes=[
            pltpu.VMEM((slots_all, *chunk), jnp.float32),
            pltpu.VMEM((all_rows, BLOCK), jnp.int32),
            pltpu.VMEM((all_rows // 4, BLOCK), jnp.float32),
            pltpu.VMEM((FIELDS, all_rows, BLOCK), jnp.float32),
            pltpu.VMEM((4 * SPLITS, all_rows, BLOCK), jnp.float32),
            pltpu.VMEM((6, 8, BLOCK), jnp.float32),
        ],
        compiler_params=params(),
    )(table, elem_nodes, grad_rows, volume, *ghosts)
    sums = swap_all(sums, sizes)
    residual = pl.pallas_call(
        functools.partial(residual_kernel, sizes, moves),
        out_shape=shaped(4, owned),
        in_specs=[VMEM] * (2 + moves),
        out_specs=VMEM,
        scratch_shapes=[pltpu.VMEM((6, 8, BLOCK), jnp.float32)],
        compiler_params=params(),
    )(own, halo_rows, *sums)
    return (new_state[None, None, None], residual[None, None, None])


def solution(mesh):
    sizes = tuple(mesh.shape[axis] for axis in AXES)
    row = P("mapx", "mapy", "layer", None)
    table = P("mapx", "mapy", "layer", None, None)
    return jax.shard_map(
        functools.partial(per_device, sizes),
        mesh=mesh,
        in_specs=(table, table, table, table, row, table, table, table, row),
        out_specs=(table, table),
        check_vma=False,
    )
```

```python
import functools

import jax
import jax.numpy as jnp
from jax import lax
from jax.experimental import pallas as pl
from jax.experimental.pallas import tpu as pltpu
from jax.sharding import PartitionSpec as P

BLOCK = 128
REACH = 2
FIELDS = 6
SPLITS = 3

ocean_temp = 0.0
strain_reg = 0.01
gravity = 0.5

AXES = ("mapx", "mapy", "layer")
VMEM = pl.BlockSpec(memory_space=pltpu.VMEM)
SMEM = pl.BlockSpec(memory_space=pltpu.SMEM)


def params():
    return pltpu.CompilerParams(vmem_limit_bytes=32 * 1024 * 1024)


def both_ways(pairs):
    return [way for one, other in pairs for way in ((one, other), (other, one))]


def column_moves(count):
    return [
        both_ways([(at, at + 1) for at in range(1, count - 1, 2)]),
        both_ways([(at + i, at + i + 2) for at in range(0, count - 3, 4) for i in range(2)]),
        both_ways([(at + i, at + i + 2) for at in range(2, count - 3, 4) for i in range(2)]),
        both_ways([(at, at + 1) for at in range(0, count - 1, 2)]),
    ]


def column_offsets():
    at = lax.axis_index("mapx")
    near = jnp.where(lax.rem(at, 2) == 0, 1, -1)
    two = jnp.where(lax.rem(at, 4) < 2, 2, -2)
    return [-near, two, -two, near, 0]


def pair_swap(value, axis, count, first):
    return lax.ppermute(value, axis, both_ways([(at, at + 1) for at in range(first, count - 1, 2)]))


def swap_all(values, sizes):
    long = [axis for axis in range(3) if sizes[axis] > 2]
    steps = [(axis, 1) for axis in long] + [(axis, 0) for axis in range(3)]
    return [pair_swap(value, AXES[axis], sizes[axis], first) for value, (axis, first) in zip(values, steps)]


def pack_kernel(count, *refs):
    blocks_in_ref, old_in_ref = refs[:2]
    cross_first_ref, cross_ref, mine_first_ref, mine_ref = refs[2 + count : 6 + count]
    blocks_ref, old_ref, sems = refs[6 + 2 * count :]
    first = [pltpu.make_async_copy(blocks_in_ref, blocks_ref, sems.at[0])]
    first += [pltpu.make_async_copy(old_in_ref, old_ref, sems.at[1])]
    rest = [
        pltpu.make_async_copy(refs[2 + i], refs[6 + count + i], sems.at[2 + i]) for i in range(count)
    ]
    for copy in first + rest:
        copy.start()
    for copy in first:
        copy.wait()
    slots = blocks_ref.shape[2]
    stride = old_ref.shape[0] // FIELDS
    layer = lax.axis_index("layer")
    offsets = column_offsets()
    for first_ref, out_ref, to_layer in ((cross_first_ref, cross_ref, 1 - layer), (mine_first_ref, mine_ref, layer)):
        for q, offset in enumerate(offsets):
            peer = (offset + REACH) * 2 + to_layer
            chunk_ref = first_ref.at[0] if q == 0 else out_ref.at[q - 1]
            for c in range(slots):
                rows = pl.ds(blocks_ref[peer, 0, c], FIELDS, stride=stride)
                chunk_ref[FIELDS * c : FIELDS * (c + 1), :] = old_ref[rows, :]
    for copy in rest:
        copy.wait()


def pick(row, lanes):
    return jnp.take_along_axis(jnp.broadcast_to(row, lanes.shape), lanes, axis=1)


def pick_fields(table_ref, block_count, blocks, lanes):
    found = [jnp.zeros((8, BLOCK), jnp.float32) for _ in range(FIELDS)]
    for b in range(block_count):
        hit = blocks == b
        for f in range(FIELDS):
            row = table_ref[b // 2, 2 * f + b % 2 : 2 * f + b % 2 + 1, :]
            found[f] = jnp.where(hit, pick(row, lanes), found[f])
    return found


def add_blocks(ref, chunk, first_block, blocks, lanes, found):
    local = blocks - first_block
    found = list(found)
    for c in range(ref.shape[1] // FIELDS):
        hit = local == c
        for f in range(FIELDS):
            row = ref[chunk, FIELDS * c + f : FIELDS * c + f + 1, :]
            found[f] = jnp.where(hit, pick(row, lanes), found[f])
    return tuple(found)


def first_block(offset, other_layer, slots):
    layer = lax.axis_index("layer")
    return ((offset + REACH) * 2 + (1 - layer if other_layer else layer)) * slots


def cut_rows(from_ref, to_ref):
    count = from_ref.shape[1] // BLOCK
    for r in range(from_ref.shape[0]):
        for i in range(count):
            to_ref[r * count + i : r * count + i + 1, :] = from_ref[r : r + 1, i * BLOCK : (i + 1) * BLOCK]


def lane_one_hot(ids):
    lanes = (ids & (BLOCK - 1)).astype(jnp.float32).astype(jnp.bfloat16)
    rows = lax.broadcasted_iota(jnp.int32, (BLOCK, BLOCK), 0).astype(jnp.float32).astype(jnp.bfloat16)
    hit = rows == jnp.broadcast_to(lanes, rows.shape)
    return jnp.where(hit, jnp.ones_like(rows), jnp.zeros_like(rows))


def near_kernel(
    mine_ref,
    swap_ref,
    slots_in_ref,
    weights_in_ref,
    halos_in_ref,
    nodes_in_ref,
    volume_in_ref,
    found_ref,
    slots_ref,
    weights_ref,
    halos_ref,
    nodes_ref,
    volume_ref,
    halo_hot_ref,
    node_hot_ref,
):
    for k in range(halos_in_ref.shape[0]):
        cut_rows(halos_in_ref.at[k], halos_ref.at[2 * k : 2 * k + 2])
    cut_rows(slots_in_ref, slots_ref)
    cut_rows(weights_in_ref, weights_ref)
    cut_rows(nodes_in_ref, nodes_ref)
    cut_rows(volume_in_ref, volume_ref)
    slots = mine_ref.shape[1] // FIELDS
    for v in range(slots_ref.shape[0] // 8):
        ids = slots_ref[8 * v : 8 * v + 8, :]
        blocks, lanes = ids >> 7, ids & (BLOCK - 1)
        found = tuple(jnp.zeros((8, BLOCK), jnp.float32) for _ in range(FIELDS))
        for ref, other in ((mine_ref, 0), (swap_ref, 1)):
            found = add_blocks(ref, 3, first_block(0, other, slots), blocks, lanes, found)
        for f in range(FIELDS):
            found_ref[f, 8 * v : 8 * v + 8, :] = found[f]
    for r in range(halos_ref.shape[0]):
        halo_hot_ref[:, r * BLOCK : (r + 1) * BLOCK] = lane_one_hot(halos_ref[r : r + 1, :])
    steps, _, width = node_hot_ref.shape
    group = width // BLOCK

    def hot(step, carry):
        for r in range(group):
            ids = nodes_ref[pl.ds(step * group + r, 1), :]
            node_hot_ref[step, :, r * BLOCK : (r + 1) * BLOCK] = lane_one_hot(ids)
        return carry

    lax.fori_loop(0, steps, hot, 0)


def state_kernel(
    counts, next_ref, two_ref, across_ref, pair_ref, slots_ref, found_ref, weights_ref, mask_ref, halos_ref, state_ref, table_ref, *more_refs
):
    send_refs, cut_ref = more_refs[:-1], more_refs[-1]
    slots = two_ref.shape[1] // FIELDS
    offsets = column_offsets()
    parts = slots_ref.shape[0] // 8
    found = []
    for v in range(parts):
        ids = slots_ref[8 * v : 8 * v + 8, :]
        blocks, lanes = ids >> 7, ids & (BLOCK - 1)
        fields = tuple(found_ref[f, 8 * v : 8 * v + 8, :] for f in range(FIELDS))
        for q, ref in enumerate((next_ref, two_ref, across_ref, pair_ref)):
            for other in range(2):
                fields = add_blocks(ref, other, first_block(offsets[q], other, slots), blocks, lanes, fields)
        found.append(fields)
    front = mask_ref[...] == 1
    rows = mask_ref.shape[0]
    for f in range(FIELDS):
        total = jnp.zeros((rows, BLOCK), jnp.float32)
        for v in range(parts):
            term = found[v][f] * weights_ref[8 * v : 8 * v + 8, :]
            for k in range(8 // rows):
                total = total + term[k * rows : (k + 1) * rows, :]
        if f == 4:
            total = jnp.where(front, ocean_temp, total)
        state_ref[f * rows : (f + 1) * rows, :] = total
        for s in range(rows // 2):
            table_ref[s, 2 * f : 2 * f + 2, :] = total[2 * s : 2 * s + 2, :]
    starts = (0, halos_ref.shape[0] - 8)
    halo = [halos_ref[first : first + 8, :] for first in starts]
    halo_blocks = [i >> 7 for i in halo]
    halo_lanes = [i & (BLOCK - 1) for i in halo]
    for v in range(2):
        cut = pick_fields(table_ref, rows, halo_blocks[v], halo_lanes[v])
        for k in range(6):
            r = 2 * k - starts[v]
            if 0 <= r <= 6:
                for f in range(FIELDS):
                    cut_ref[k, 2 * f : 2 * f + 2, :] = cut[f][r : r + 2, :]
    send_pairs(counts, cut_ref, send_refs, [(0, 1), (2, 3), (4, 5)])


def pair_places():
    return [lax.rem(lax.axis_index(axis), 2) for axis in AXES]


def send_pairs(counts, cut_ref, send_refs, order):
    places = pair_places()
    long = [axis for axis in range(3) if counts[axis] > 2]
    for axis in range(3):
        even, odd = order[axis]
        send_refs[len(long) + axis][...] = cut_ref[jnp.where(places[axis] == 0, even, odd)]
        if axis in long:
            send_refs[long.index(axis)][...] = cut_ref[jnp.where(places[axis] == 0, odd, even)]


def arrivals(counts, came_refs):
    places = pair_places()
    long = [axis for axis in range(3) if counts[axis] > 2]
    result = []
    for axis in range(3):
        inside = came_refs[len(long) + axis][...]
        at = lax.axis_index(AXES[axis])
        edge = jnp.where(places[axis] == 0, at == 0, at == counts[axis] - 1)
        outside = jnp.zeros_like(inside)
        if axis in long:
            outside = jnp.where(edge, 0.0, came_refs[long.index(axis)][...])
        result.append((places[axis], inside, outside))
    return result


def placed(values, ids, block_count):
    rows = lax.broadcasted_iota(jnp.int32, (block_count, BLOCK), 0)
    hit = rows == jnp.broadcast_to(ids >> 7, rows.shape)
    left = [jnp.where(hit, jnp.broadcast_to(v, rows.shape), 0.0) for v in values]
    return jnp.concatenate(left, axis=0).astype(jnp.bfloat16)


def cut_parts(value):
    parts = []
    for _ in range(SPLITS - 1):
        part = value.astype(jnp.bfloat16).astype(jnp.float32)
        parts.append(part)
        value = value - part
    return parts + [value]


def nt_dot(left, right):
    return lax.dot_general(left, right, (((1,), (1,)), ((), ())), preferred_element_type=jnp.float32)


def element_kernel(counts, moves, *refs):
    table_in_ref, nodes_ref, node_hot_ref, grads_ref, volume_ref = refs[:5]
    came_refs = refs[5 : 5 + moves]
    own_ref = refs[5 + moves]
    send_refs = refs[6 + moves : 6 + 2 * moves]
    table_ref, values_ref, parts_ref, cut_ref = refs[6 + 2 * moves :]
    owned_slots = table_in_ref.shape[0]
    table_ref[0:owned_slots] = table_in_ref[...]
    for axis, (place_at, inside, outside) in enumerate(arrivals(counts, came_refs)):
        table_ref[owned_slots + 2 * axis + 1 - place_at] = inside
        table_ref[owned_slots + 2 * axis + place_at] = outside
    block_count = 2 * table_ref.shape[0]
    all_rows = nodes_ref.shape[0]
    elem_rows = all_rows // 4
    for first in range(0, all_rows, 8):
        ids = nodes_ref[first : first + 8, :]
        found = pick_fields(table_ref, block_count, ids >> 7, ids & (BLOCK - 1))
        for f in range(FIELDS):
            values_ref[f, first : first + 8, :] = found[f]
    for first in [*range(0, elem_rows - 7, 8)] + ([elem_rows - 8] if elem_rows % 8 else []):
        at = [slice(r * elem_rows + first, r * elem_rows + first + 8) for r in range(12)]
        values = [[values_ref[f, at[a], :] for f in range(FIELDS)] for a in range(4)]
        grads = [[grads_ref[at[3 * a + j], :] for j in range(3)] for a in range(4)]
        volume = volume_ref[at[0], :]
        velgrad = [[sum(values[a][i] * grads[a][j] for a in range(4)) for j in range(3)] for i in range(3)]
        strain = [[0.5 * (velgrad[i][j] + velgrad[j][i]) if i <= j else None for j in range(3)] for i in range(3)]
        diagonal = sum(strain[i][i] * strain[i][i] for i in range(3))
        corner = sum(strain[i][j] * strain[i][j] for i, j in ((0, 1), (0, 2), (1, 2)))
        second = 0.5 * diagonal + corner
        pressure, temper, damage = [0.25 * (values[0][f] + values[1][f] + values[2][f] + values[3][f]) for f in (3, 4, 5)]
        root = jnp.exp(jnp.log(second + strain_reg) * (-1.0 / 3.0))
        twice = (1.0 - damage) * jnp.exp(-temper) * root
        stress = [[None] * 3 for _ in range(3)]
        for i in range(3):
            for j in range(i, 3):
                stress[i][j] = twice * strain[i][j] - (pressure if i == j else 0.0)
                stress[j][i] = stress[i][j]
        lift = (0.25 * gravity) * volume
        flow = 0.25 * volume * (velgrad[0][0] + velgrad[1][1] + velgrad[2][2])
        for s, part in enumerate(cut_parts(flow)):
            for a in range(4):
                parts_ref[3 * SPLITS + s, at[a], :] = part
        for a in range(4):
            for i in range(3):
                force = volume * sum(stress[i][j] * grads[a][j] for j in range(3))
                if i == 2:
                    force = force + lift
                for s, part in enumerate(cut_parts(force)):
                    parts_ref[i * SPLITS + s, at[a], :] = part

    group = node_hot_ref.shape[2] // BLOCK

    def gather_terms(step, total):
        lefts = []
        for r in range(group):
            at = pl.ds(step * group + r, 1)
            terms = [parts_ref[c * SPLITS + s, at, :] for s in range(SPLITS) for c in range(4)]
            lefts.append(placed(terms, nodes_ref[at, :], block_count))
        return total + nt_dot(jnp.concatenate(lefts, axis=1), node_hot_ref[step])

    width = 4 * block_count
    total = lax.fori_loop(0, all_rows // group, gather_terms, jnp.zeros((SPLITS * width, BLOCK), jnp.float32))
    total = sum(total[s * width : (s + 1) * width, :] for s in range(SPLITS))
    owned = 2 * owned_slots
    for c in range(4):
        own_ref[c * owned : (c + 1) * owned, :] = total[c * block_count : c * block_count + owned, :]
        for k in range(6):
            first = c * block_count + owned + 2 * k
            cut_ref[k, 2 * c : 2 * c + 2, :] = total[first : first + 2, :]
    send_pairs(counts, cut_ref, send_refs, [(1, 0), (3, 2), (5, 4)])


def residual_kernel(counts, moves, *refs):
    own_ref, halos_ref, halo_hot_ref = refs[:3]
    out_ref, came_ref = refs[3 + moves :]
    for axis, (place_at, inside, outside) in enumerate(arrivals(counts, refs[3 : 3 + moves])):
        came_ref[2 * axis + place_at] = inside
        came_ref[2 * axis + 1 - place_at] = outside
    owned = own_ref.shape[0] // 4
    lefts = []
    for k in range(6):
        parts = cut_parts(came_ref[k])
        for h in range(2):
            ids = halos_ref[2 * k + h : 2 * k + h + 1, :]
            terms = [parts[s][2 * c + h : 2 * c + h + 1, :] for s in range(SPLITS) for c in range(4)]
            lefts.append(placed(terms, ids, owned))
    total = nt_dot(jnp.concatenate(lefts, axis=1), halo_hot_ref[...])
    width = 4 * owned
    total = sum(total[s * width : (s + 1) * width, :] for s in range(SPLITS)) + own_ref[...]
    for c in range(4):
        for b in range(owned):
            r = c * owned + b
            out_ref[c : c + 1, b * BLOCK : (b + 1) * BLOCK] = total[r : r + 1, :]


def shaped(*shape):
    return jax.ShapeDtypeStruct(shape, jnp.float32)


def per_device(
    sizes,
    old_state,
    send_blocks,
    node_slots,
    node_weights,
    front_mask,
    halo_lists,
    elem_nodes,
    shape_grads,
    elem_volume,
):
    old_state, send_blocks = old_state[0, 0, 0], send_blocks[0, 0, 0]
    slots = send_blocks.shape[1]
    send_blocks = send_blocks.reshape(-1, 1, slots)
    rows = FIELDS * slots
    arguments = [
        node_slots[0, 0, 0],
        node_weights[0, 0, 0],
        front_mask.reshape(-1, BLOCK),
        halo_lists.reshape(halo_lists.shape[-2], 1, -1),
        elem_nodes[0, 0, 0],
        shape_grads.reshape(-1, BLOCK),
        elem_volume[0, 0],
    ]
    old_rows = old_state.reshape(-1, BLOCK)
    count = len(arguments)
    cross_first, cross, mine_first, mine, *held = pl.pallas_call(
        functools.partial(pack_kernel, count),
        out_shape=[shaped(1, rows, BLOCK), shaped(4, rows, BLOCK)] * 2 + [jax.ShapeDtypeStruct(a.shape, a.dtype) for a in arguments],
        in_specs=[pl.BlockSpec(memory_space=pltpu.HBM)] * (2 + count),
        out_specs=[VMEM] * (4 + count),
        scratch_shapes=[
            pltpu.SMEM(send_blocks.shape, jnp.int32),
            pltpu.VMEM(old_rows.shape, jnp.float32),
            pltpu.SemaphoreType.DMA((2 + count,)),
        ],
        compiler_params=params(),
    )(*(pltpu.with_memory_space_constraint(a, pltpu.HBM) for a in (send_blocks, old_rows, *arguments)))
    node_slots, node_weights, mask_rows, halos, elem_nodes, grad_rows, volume = held
    layers = both_ways([(0, 1)])
    swap_first = lax.ppermute(cross_first, "layer", layers)
    swap = lax.ppermute(cross, "layer", layers)
    both = [jnp.concatenate([mine_first, swap_first])] + [jnp.stack([mine[q], swap[q]]) for q in range(3)]
    moved = [lax.ppermute(pair, "mapx", pairs) for pair, pairs in zip(both, column_moves(sizes[0]))]

    owned = node_slots.shape[-1]
    slot_rows = node_slots.size // BLOCK
    all_rows = elem_nodes.size // BLOCK
    halo_count = halos.size // BLOCK
    hot_steps = next(n for n in (8, 4, 2, 1) if all_rows % n == 0)
    whole = lambda *shape: jax.ShapeDtypeStruct(shape, jnp.int32)
    found, slots_cut, weights_cut, halos_cut, nodes_cut, volume_cut, halo_hot, node_hot = pl.pallas_call(
        near_kernel,
        out_shape=(
            shaped(FIELDS, slot_rows, BLOCK),
            whole(slot_rows, BLOCK),
            shaped(slot_rows, BLOCK),
            whole(halo_count, BLOCK),
            whole(all_rows, BLOCK),
            shaped(all_rows // 4, BLOCK),
            jax.ShapeDtypeStruct((BLOCK, halo_count * BLOCK), jnp.bfloat16),
            jax.ShapeDtypeStruct((hot_steps, BLOCK, all_rows // hot_steps * BLOCK), jnp.bfloat16),
        ),
        in_specs=[VMEM] * 7,
        out_specs=(VMEM,) * 8,
        compiler_params=params(),
    )(mine, swap, node_slots, node_weights, halos, elem_nodes, volume)
    moves = 3 + sum(size > 2 for size in sizes)
    chunk = (2 * FIELDS, BLOCK)
    new_state, table, *ghosts = pl.pallas_call(
        functools.partial(state_kernel, sizes),
        out_shape=(shaped(FIELDS * owned // BLOCK, BLOCK), shaped(owned // (2 * BLOCK), *chunk)) + (shaped(*chunk),) * moves,
        in_specs=[VMEM] * 9,
        out_specs=(VMEM,) * (2 + moves),
        scratch_shapes=[pltpu.VMEM((6, *chunk), jnp.float32)],
        compiler_params=params(),
    )(*moved, slots_cut, found, weights_cut, mask_rows, halos_cut)
    ghosts = swap_all(ghosts, sizes)

    slots_all = table.shape[0] + 6
    own, *sums = pl.pallas_call(
        functools.partial(element_kernel, sizes, moves),
        out_shape=(shaped(4 * owned // BLOCK, BLOCK),) + (shaped(8, BLOCK),) * moves,
        in_specs=[VMEM] * (5 + moves),
        out_specs=(VMEM,) * (1 + moves),
        scratch_shapes=[
            pltpu.VMEM((slots_all, *chunk), jnp.float32),
            pltpu.VMEM((FIELDS, all_rows, BLOCK), jnp.float32),
            pltpu.VMEM((4 * SPLITS, all_rows, BLOCK), jnp.float32),
            pltpu.VMEM((6, 8, BLOCK), jnp.float32),
        ],
        compiler_params=params(),
    )(table, nodes_cut, node_hot, grad_rows, volume_cut, *ghosts)
    sums = swap_all(sums, sizes)
    residual = pl.pallas_call(
        functools.partial(residual_kernel, sizes, moves),
        out_shape=shaped(4, owned),
        in_specs=[VMEM] * (3 + moves),
        out_specs=VMEM,
        scratch_shapes=[pltpu.VMEM((6, 8, BLOCK), jnp.float32)],
        compiler_params=params(),
    )(own, halos_cut, halo_hot, *sums)
    return (new_state.reshape(1, 1, 1, FIELDS, owned), residual[None, None, None])


def solution(mesh):
    sizes = tuple(mesh.shape[axis] for axis in AXES)
    row = P("mapx", "mapy", "layer", None)
    table = P("mapx", "mapy", "layer", None, None)
    return jax.shard_map(
        functools.partial(per_device, sizes),
        mesh=mesh,
        in_specs=(table, table, table, table, row, table, table, table, row),
        out_specs=(table, table),
        check_vma=False,
    )
```

```python
import functools

import jax
import jax.numpy as jnp
from jax import lax
from jax.experimental import pallas as pl
from jax.experimental.pallas import tpu as pltpu
from jax.sharding import PartitionSpec as P

BLOCK = 128
REACH = 2
FIELDS = 6
SPLITS = 3

ocean_temp = 0.0
strain_reg = 0.01
gravity = 0.5

AXES = ("mapx", "mapy", "layer")
VMEM = pl.BlockSpec(memory_space=pltpu.VMEM)
SMEM = pl.BlockSpec(memory_space=pltpu.SMEM)


def params():
    return pltpu.CompilerParams(vmem_limit_bytes=32 * 1024 * 1024)


def both_ways(pairs):
    return [way for one, other in pairs for way in ((one, other), (other, one))]


def column_moves(count):
    outside = [(at, at + 1) for at in range(1, count - 1, 2)]
    inside = [(at, at + 1) for at in range(0, count - 1, 2)]
    within = [(at + i, at + i + 2) for at in range(0, count - 3, 4) for i in range(2)]
    across = [(at + i, at + i + 2) for at in range(2, count - 3, 4) for i in range(2)]
    number = lambda pairs, layer: [(one * 2 + layer, other * 2 + layer) for one, other in pairs]
    return [
        both_ways(number(outside, 0) + number(inside, 1)),
        both_ways(number(within, 0) + number(across, 1)),
    ]


def column_offsets(layer):
    at = lax.axis_index("mapx")
    near = jnp.where(lax.rem(at, 2) == 0, 1, -1)
    two = jnp.where(lax.rem(at, 4) < 2, 2, -2)
    return [jnp.where(layer == 0, -near, near), jnp.where(layer == 0, two, -two)]


def pair_swap(value, axis, count, first):
    return lax.ppermute(value, axis, both_ways([(at, at + 1) for at in range(first, count - 1, 2)]))


def swap_all(values, sizes):
    long = [axis for axis in range(3) if sizes[axis] > 2]
    steps = [(axis, 1) for axis in long] + [(axis, 0) for axis in range(3)]
    return [pair_swap(value, AXES[axis], sizes[axis], first) for value, (axis, first) in zip(values, steps)]


def pack_kernel(count, *refs):
    blocks_in_ref, old_in_ref = refs[:2]
    give_ref, first_ref, second_ref, own_ref = refs[2 + count : 6 + count]
    held = refs[6 + count : 6 + 2 * count]
    blocks_ref, old_ref, sems = refs[6 + 2 * count :]
    first = [pltpu.make_async_copy(blocks_in_ref, blocks_ref, sems.at[0])]
    first += [pltpu.make_async_copy(old_in_ref, old_ref, sems.at[1])]
    rest = [pltpu.make_async_copy(refs[2 + i], held[i], sems.at[2 + i]) for i in range(count)]
    for copy in first + rest:
        copy.start()
    for copy in first:
        copy.wait()
    slots = blocks_ref.shape[2]
    stride = old_ref.shape[0] // FIELDS
    layer = lax.axis_index("layer")
    mine, other = column_offsets(layer), column_offsets(1 - layer)
    size = FIELDS * slots
    for ref, chunk, offset in (
        (give_ref, 0, other[0]),
        (give_ref, 2, other[1]),
        (first_ref, 0, mine[0]),
        (second_ref, 0, mine[1]),
        (own_ref, 0, 0),
    ):
        for to_layer in range(2):
            peer = (offset + REACH) * 2 + to_layer
            start = (chunk + to_layer) * size
            for c in range(slots):
                rows = pl.ds(blocks_ref[peer, 0, c], FIELDS, stride=stride)
                ref[start + FIELDS * c : start + FIELDS * (c + 1), :] = old_ref[rows, :]
    for copy in rest:
        copy.wait()
    slots_ref, weights_ref = held[0], held[1]
    slot_rows = slots_ref.shape[0] * slots_ref.shape[1] // BLOCK
    cut_rows(slots_ref, give_ref.at[4 * size : 4 * size + slot_rows])
    cut_rows(weights_ref, give_ref.at[4 * size + slot_rows : 4 * size + 2 * slot_rows])


def pick(row, lanes):
    return jnp.take_along_axis(jnp.broadcast_to(row, lanes.shape), lanes, axis=1)


def pick_fields(table_ref, block_count, blocks, lanes):
    found = [jnp.zeros((8, BLOCK), jnp.float32) for _ in range(FIELDS)]
    for b in range(block_count):
        hit = blocks == b
        for f in range(FIELDS):
            row = table_ref[b // 2, 2 * f + b % 2 : 2 * f + b % 2 + 1, :]
            found[f] = jnp.where(hit, pick(row, lanes), found[f])
    return found


def add_blocks(ref, chunk, first_block, blocks, lanes, found):
    local = blocks - first_block
    found = list(found)
    for c in range(ref.shape[1] // FIELDS):
        hit = local == c
        for f in range(FIELDS):
            row = ref[chunk, FIELDS * c + f : FIELDS * c + f + 1, :]
            found[f] = jnp.where(hit, pick(row, lanes), found[f])
    return tuple(found)


def add_chunks(ref, numbers, offset, ids, found):
    blocks, lanes = ids >> 7, ids & (BLOCK - 1)
    for chunk, layer in numbers:
        first = ((offset + REACH) * 2 + layer) * (ref.shape[1] // FIELDS)
        found = add_blocks(ref, chunk, first, blocks, lanes, found)
    return found


def load_fields(found_ref, owner, v):
    return tuple(found_ref[owner, f, 8 * v : 8 * v + 8, :] for f in range(FIELDS))


def save_fields(found_ref, owner, v, found):
    for f in range(FIELDS):
        found_ref[owner, f, 8 * v : 8 * v + 8, :] = found[f]


def arrived_chunks(ref, move, ids, found, owner):
    layer = lax.axis_index("layer")
    to_layer = 1 - layer if owner else layer
    numbers = [(to_layer, layer), (2 + to_layer, 1 - layer)]
    return add_chunks(ref, numbers, column_offsets(layer)[move], ids, found)


def cut_rows(from_ref, to_ref):
    count = from_ref.shape[1] // BLOCK
    for r in range(from_ref.shape[0]):
        for i in range(count):
            to_ref[r * count + i : r * count + i + 1, :] = from_ref[
                r : r + 1, i * BLOCK : (i + 1) * BLOCK
            ].astype(to_ref.dtype)


def lane_one_hot(ids, count):
    lanes = (ids & (count - 1)).astype(jnp.float32).astype(jnp.bfloat16)
    rows = lax.broadcasted_iota(jnp.int32, (count, BLOCK), 0).astype(jnp.float32).astype(jnp.bfloat16)
    hit = rows == jnp.broadcast_to(lanes, rows.shape)
    return jnp.where(hit, jnp.ones_like(rows), jnp.zeros_like(rows))


def own_kernel(
    own_ref,
    other_slots_ref,
    slots_in_ref,
    weights_in_ref,
    halos_in_ref,
    nodes_in_ref,
    volume_in_ref,
    found_ref,
    slots_ref,
    weights_ref,
    halos_ref,
    nodes_ref,
    volume_ref,
    halo_hot_ref,
    node_hot_ref,
):
    for k in range(halos_in_ref.shape[0]):
        cut_rows(halos_in_ref.at[k], halos_ref.at[2 * k : 2 * k + 2])
    cut_rows(slots_in_ref, slots_ref.at[0])
    slots_ref[1] = other_slots_ref[...].astype(jnp.int32)
    cut_rows(weights_in_ref, weights_ref)
    cut_rows(nodes_in_ref, nodes_ref)
    cut_rows(volume_in_ref, volume_ref)
    layer = lax.axis_index("layer")
    for owner in range(2):
        for v in range(slots_ref.shape[1] // 8):
            ids = slots_ref[owner, 8 * v : 8 * v + 8, :]
            found = tuple(jnp.zeros((8, BLOCK), jnp.float32) for _ in range(FIELDS))
            numbers = [(1 - layer if owner else layer, layer)]
            save_fields(found_ref, owner, v, add_chunks(own_ref, numbers, 0, ids, found))
    for r in range(halos_ref.shape[0]):
        halo_hot_ref[:, r * BLOCK : (r + 1) * BLOCK] = lane_one_hot(halos_ref[r : r + 1, :], BLOCK)
    steps, lanes, width = node_hot_ref.shape
    group = width // BLOCK

    def hot(step, carry):
        for r in range(group):
            ids = nodes_ref[pl.ds(step * group + r, 1), :]
            node_hot_ref[step, :, r * BLOCK : (r + 1) * BLOCK] = lane_one_hot(ids, lanes)
        return carry

    lax.fori_loop(0, steps, hot, 0)


def first_kernel(came_ref, slots_ref, found_in_ref, found_ref):
    for owner in range(2):
        for v in range(slots_ref.shape[1] // 8):
            ids = slots_ref[owner, 8 * v : 8 * v + 8, :]
            found = arrived_chunks(came_ref, 0, ids, load_fields(found_in_ref, owner, v), owner)
            save_fields(found_ref, owner, v, found)


def second_kernel(rows, came_ref, slots_ref, found_ref, weights_ref, other_weights_ref, mine_ref, other_ref):
    for owner, out_ref, weight_ref in ((1, other_ref, other_weights_ref), (0, mine_ref, weights_ref)):
        totals = [jnp.zeros((rows, BLOCK), jnp.float32) for _ in range(FIELDS)]
        for v in range(slots_ref.shape[1] // 8):
            ids = slots_ref[owner, 8 * v : 8 * v + 8, :]
            found = arrived_chunks(came_ref, 1, ids, load_fields(found_ref, owner, v), owner)
            for f in range(FIELDS):
                term = found[f] * weight_ref[8 * v : 8 * v + 8, :]
                for k in range(8 // rows):
                    totals[f] = totals[f] + term[k * rows : (k + 1) * rows, :]
        for f in range(FIELDS):
            out_ref[f * rows : (f + 1) * rows, :] = totals[f]


def state_kernel(counts, mine_ref, came_ref, mask_ref, halos_ref, state_ref, table_ref, *more_refs):
    send_refs, cut_ref = more_refs[:-1], more_refs[-1]
    front = mask_ref[...] == 1
    rows = mask_ref.shape[0]
    for f in range(FIELDS):
        at = slice(f * rows, (f + 1) * rows)
        total = mine_ref[at, :] + came_ref[at, :]
        if f == 4:
            total = jnp.where(front, ocean_temp, total)
        state_ref[f * rows : (f + 1) * rows, :] = total
        for s in range(rows // 2):
            table_ref[s, 2 * f : 2 * f + 2, :] = total[2 * s : 2 * s + 2, :]
    starts = (0, halos_ref.shape[0] - 8)
    halo = [halos_ref[first : first + 8, :] for first in starts]
    halo_blocks = [i >> 7 for i in halo]
    halo_lanes = [i & (BLOCK - 1) for i in halo]
    for v in range(2):
        cut = pick_fields(table_ref, rows, halo_blocks[v], halo_lanes[v])
        for k in range(6):
            r = 2 * k - starts[v]
            if 0 <= r <= 6:
                for f in range(FIELDS):
                    cut_ref[k, 2 * f : 2 * f + 2, :] = cut[f][r : r + 2, :]
    send_pairs(counts, cut_ref, send_refs, [(0, 1), (2, 3), (4, 5)])


def pair_places():
    return [lax.rem(lax.axis_index(axis), 2) for axis in AXES]


def send_pairs(counts, cut_ref, send_refs, order):
    places = pair_places()
    long = [axis for axis in range(3) if counts[axis] > 2]
    for axis in range(3):
        even, odd = order[axis]
        send_refs[len(long) + axis][...] = cut_ref[jnp.where(places[axis] == 0, even, odd)]
        if axis in long:
            send_refs[long.index(axis)][...] = cut_ref[jnp.where(places[axis] == 0, odd, even)]


def arrivals(counts, came_refs):
    places = pair_places()
    long = [axis for axis in range(3) if counts[axis] > 2]
    result = []
    for axis in range(3):
        inside = came_refs[len(long) + axis][...]
        at = lax.axis_index(AXES[axis])
        edge = jnp.where(places[axis] == 0, at == 0, at == counts[axis] - 1)
        outside = jnp.zeros_like(inside)
        if axis in long:
            outside = jnp.where(edge, 0.0, came_refs[long.index(axis)][...])
        result.append((places[axis], inside, outside))
    return result


def placed(values, ids, shift, block_count):
    rows = lax.broadcasted_iota(jnp.int32, (block_count, BLOCK), 0)
    hit = rows == jnp.broadcast_to(ids >> shift, rows.shape)
    left = [jnp.where(hit, jnp.broadcast_to(v, rows.shape), 0.0) for v in values]
    return jnp.concatenate(left, axis=0).astype(jnp.bfloat16)


def cut_parts(value):
    parts = []
    for _ in range(SPLITS - 1):
        part = value.astype(jnp.bfloat16).astype(jnp.float32)
        parts.append(part)
        value = value - part
    return parts + [value]


def nt_dot(left, right):
    return lax.dot_general(left, right, (((1,), (1,)), ((), ())), preferred_element_type=jnp.float32)


def element_kernel(counts, moves, *refs):
    table_in_ref, nodes_ref, node_hot_ref, grads_ref, volume_ref = refs[:5]
    came_refs = refs[5 : 5 + moves]
    own_ref = refs[5 + moves]
    send_refs = refs[6 + moves : 6 + 2 * moves]
    table_ref, values_ref, parts_ref, cut_ref = refs[6 + 2 * moves :]
    owned_slots = table_in_ref.shape[0]
    table_ref[0:owned_slots] = table_in_ref[...]
    for axis, (place_at, inside, outside) in enumerate(arrivals(counts, came_refs)):
        table_ref[owned_slots + 2 * axis + 1 - place_at] = inside
        table_ref[owned_slots + 2 * axis + place_at] = outside
    slot_count = table_ref.shape[0]
    block_count = 2 * slot_count
    all_rows = nodes_ref.shape[0]
    elem_rows = all_rows // 4
    for first in range(0, all_rows, 8):
        ids = nodes_ref[first : first + 8, :]
        found = pick_fields(table_ref, block_count, ids >> 7, ids & (BLOCK - 1))
        for f in range(FIELDS):
            values_ref[f, first : first + 8, :] = found[f]
    for first in [*range(0, elem_rows - 7, 8)] + ([elem_rows - 8] if elem_rows % 8 else []):
        at = [slice(r * elem_rows + first, r * elem_rows + first + 8) for r in range(12)]
        values = [[values_ref[f, at[a], :] for f in range(FIELDS)] for a in range(4)]
        grads = [[grads_ref[at[3 * a + j], :] for j in range(3)] for a in range(4)]
        volume = volume_ref[at[0], :]
        velgrad = [[sum(values[a][i] * grads[a][j] for a in range(4)) for j in range(3)] for i in range(3)]
        strain = [[0.5 * (velgrad[i][j] + velgrad[j][i]) if i <= j else None for j in range(3)] for i in range(3)]
        diagonal = sum(strain[i][i] * strain[i][i] for i in range(3))
        corner = sum(strain[i][j] * strain[i][j] for i, j in ((0, 1), (0, 2), (1, 2)))
        second = 0.5 * diagonal + corner
        pressure, temper, damage = [0.25 * (values[0][f] + values[1][f] + values[2][f] + values[3][f]) for f in (3, 4, 5)]
        root = jnp.exp(jnp.log(second + strain_reg) * (-1.0 / 3.0))
        twice = (1.0 - damage) * jnp.exp(-temper) * root
        stress = [[None] * 3 for _ in range(3)]
        for i in range(3):
            for j in range(i, 3):
                stress[i][j] = twice * strain[i][j] - (pressure if i == j else 0.0)
                stress[j][i] = stress[i][j]
        lift = (0.25 * gravity) * volume
        flow = 0.25 * volume * (velgrad[0][0] + velgrad[1][1] + velgrad[2][2])
        for s, part in enumerate(cut_parts(flow)):
            for a in range(4):
                parts_ref[3 * SPLITS + s, at[a], :] = part
        for a in range(4):
            for i in range(3):
                force = volume * sum(stress[i][j] * grads[a][j] for j in range(3))
                if i == 2:
                    force = force + lift
                for s, part in enumerate(cut_parts(force)):
                    parts_ref[i * SPLITS + s, at[a], :] = part

    group = node_hot_ref.shape[2] // BLOCK

    def gather_terms(step, total):
        lefts = []
        for r in range(group):
            at = pl.ds(step * group + r, 1)
            terms = [parts_ref[c * SPLITS + s, at, :] for s in range(SPLITS) for c in range(4)]
            lefts.append(placed(terms, nodes_ref[at, :], 8, slot_count))
        return total + nt_dot(jnp.concatenate(lefts, axis=1), node_hot_ref[step])

    width = 4 * slot_count
    total = lax.fori_loop(0, all_rows // group, gather_terms, jnp.zeros((SPLITS * width, 2 * BLOCK), jnp.float32))
    total = sum(total[s * width : (s + 1) * width, :] for s in range(SPLITS))
    for c in range(4):
        for h in range(2):
            half = total[c * slot_count : (c + 1) * slot_count, h * BLOCK : (h + 1) * BLOCK]
            for s in range(owned_slots):
                at = c * 2 * owned_slots + 2 * s + h
                own_ref[at : at + 1, :] = half[s : s + 1, :]
            for k in range(6):
                cut_ref[k, 2 * c + h : 2 * c + h + 1, :] = half[owned_slots + k : owned_slots + k + 1, :]
    send_pairs(counts, cut_ref, send_refs, [(1, 0), (3, 2), (5, 4)])


def residual_kernel(counts, moves, *refs):
    own_ref, halos_ref, halo_hot_ref = refs[:3]
    out_ref, came_ref = refs[3 + moves :]
    for axis, (place_at, inside, outside) in enumerate(arrivals(counts, refs[3 : 3 + moves])):
        came_ref[2 * axis + place_at] = inside
        came_ref[2 * axis + 1 - place_at] = outside
    owned = own_ref.shape[0] // 4
    lefts = []
    for k in range(6):
        parts = cut_parts(came_ref[k])
        for h in range(2):
            ids = halos_ref[2 * k + h : 2 * k + h + 1, :]
            terms = [parts[s][2 * c + h : 2 * c + h + 1, :] for s in range(SPLITS) for c in range(4)]
            lefts.append(placed(terms, ids, 7, owned))
    total = nt_dot(jnp.concatenate(lefts, axis=1), halo_hot_ref[...])
    width = 4 * owned
    total = sum(total[s * width : (s + 1) * width, :] for s in range(SPLITS)) + own_ref[...]
    for c in range(4):
        for b in range(owned):
            r = c * owned + b
            out_ref[c : c + 1, b * BLOCK : (b + 1) * BLOCK] = total[r : r + 1, :]


def shaped(*shape):
    return jax.ShapeDtypeStruct(shape, jnp.float32)


def per_device(
    sizes,
    old_state,
    send_blocks,
    node_slots,
    node_weights,
    front_mask,
    halo_lists,
    elem_nodes,
    shape_grads,
    elem_volume,
):
    old_state, send_blocks = old_state[0, 0, 0], send_blocks[0, 0, 0]
    slots = send_blocks.shape[1]
    send_blocks = send_blocks.reshape(-1, 1, slots)
    rows = FIELDS * slots
    arguments = [
        node_slots[0, 0, 0],
        node_weights[0, 0, 0],
        front_mask.reshape(-1, BLOCK),
        halo_lists.reshape(halo_lists.shape[-2], 1, -1),
        elem_nodes[0, 0, 0],
        shape_grads.reshape(-1, BLOCK),
        elem_volume[0, 0],
    ]
    old_rows = old_state.reshape(-1, BLOCK)
    count = len(arguments)
    owned = node_slots.shape[-1]
    slot_rows = node_slots.size // BLOCK
    give_rows = 4 * rows + 2 * slot_rows
    give, first, second, own, *held = pl.pallas_call(
        functools.partial(pack_kernel, count),
        out_shape=[shaped(give_rows, BLOCK)]
        + [shaped(2 * rows, BLOCK)] * 3
        + [jax.ShapeDtypeStruct(a.shape, a.dtype) for a in arguments],
        in_specs=[pl.BlockSpec(memory_space=pltpu.HBM)] * (2 + count),
        out_specs=[VMEM] * (4 + count),
        scratch_shapes=[
            pltpu.SMEM(send_blocks.shape, jnp.int32),
            pltpu.VMEM(old_rows.shape, jnp.float32),
            pltpu.SemaphoreType.DMA((2 + count,)),
        ],
        compiler_params=params(),
    )(*(pltpu.with_memory_space_constraint(a, pltpu.HBM) for a in (send_blocks, old_rows, *arguments)))
    node_slots, node_weights, mask_rows, halos, elem_nodes, grad_rows, volume = held
    layers = both_ways([(0, 1)])
    got = lax.ppermute(give, "layer", layers)
    full = [jnp.concatenate([first, got[: 2 * rows]]), jnp.concatenate([second, got[2 * rows : 4 * rows]])]
    first, second = [
        lax.ppermute(part, ("mapx", "layer"), pairs).reshape(4, rows, BLOCK)
        for part, pairs in zip(full, column_moves(sizes[0]))
    ]
    other_slots, other_weights = got[4 * rows : 4 * rows + slot_rows], got[4 * rows + slot_rows :]

    all_rows = elem_nodes.size // BLOCK
    halo_count = halos.size // BLOCK
    hot_steps = next(n for n in (8, 4, 2, 1) if all_rows % n == 0)
    whole = lambda *shape: jax.ShapeDtypeStruct(shape, jnp.int32)
    found, slots_cut, weights_cut, halos_cut, nodes_cut, volume_cut, halo_hot, node_hot = pl.pallas_call(
        own_kernel,
        out_shape=(
            shaped(2, FIELDS, slot_rows, BLOCK),
            whole(2, slot_rows, BLOCK),
            shaped(slot_rows, BLOCK),
            whole(halo_count, BLOCK),
            whole(all_rows, BLOCK),
            shaped(all_rows // 4, BLOCK),
            jax.ShapeDtypeStruct((BLOCK, halo_count * BLOCK), jnp.bfloat16),
            jax.ShapeDtypeStruct((hot_steps, 2 * BLOCK, all_rows // hot_steps * BLOCK), jnp.bfloat16),
        ),
        in_specs=[VMEM] * 7,
        out_specs=(VMEM,) * 8,
        compiler_params=params(),
    )(own.reshape(2, rows, BLOCK), other_slots, node_slots, node_weights, halos, elem_nodes, volume)
    found = pl.pallas_call(
        first_kernel,
        out_shape=shaped(2, FIELDS, slot_rows, BLOCK),
        in_specs=[VMEM] * 3,
        out_specs=VMEM,
        compiler_params=params(),
    )(first, slots_cut, found)
    state_rows = FIELDS * owned // BLOCK
    mine, other = pl.pallas_call(
        functools.partial(second_kernel, owned // BLOCK),
        out_shape=(shaped(state_rows, BLOCK),) * 2,
        in_specs=[VMEM] * 5,
        out_specs=(VMEM,) * 2,
        compiler_params=params(),
    )(second, slots_cut, found, weights_cut, other_weights)
    other = lax.ppermute(other, "layer", layers)
    moves = 3 + sum(size > 2 for size in sizes)
    chunk = (2 * FIELDS, BLOCK)
    new_state, table, *ghosts = pl.pallas_call(
        functools.partial(state_kernel, sizes),
        out_shape=(shaped(state_rows, BLOCK), shaped(owned // (2 * BLOCK), *chunk)) + (shaped(*chunk),) * moves,
        in_specs=[VMEM] * 4,
        out_specs=(VMEM,) * (2 + moves),
        scratch_shapes=[pltpu.VMEM((6, *chunk), jnp.float32)],
        compiler_params=params(),
    )(mine, other, mask_rows, halos_cut)
    ghosts = swap_all(ghosts, sizes)

    slots_all = table.shape[0] + 6
    own, *sums = pl.pallas_call(
        functools.partial(element_kernel, sizes, moves),
        out_shape=(shaped(4 * owned // BLOCK, BLOCK),) + (shaped(8, BLOCK),) * moves,
        in_specs=[VMEM] * (5 + moves),
        out_specs=(VMEM,) * (1 + moves),
        scratch_shapes=[
            pltpu.VMEM((slots_all, *chunk), jnp.float32),
            pltpu.VMEM((FIELDS, all_rows, BLOCK), jnp.float32),
            pltpu.VMEM((4 * SPLITS, all_rows, BLOCK), jnp.float32),
            pltpu.VMEM((6, 8, BLOCK), jnp.float32),
        ],
        compiler_params=params(),
    )(table, nodes_cut, node_hot, grad_rows, volume_cut, *ghosts)
    sums = swap_all(sums, sizes)
    residual = pl.pallas_call(
        functools.partial(residual_kernel, sizes, moves),
        out_shape=shaped(4, owned),
        in_specs=[VMEM] * (3 + moves),
        out_specs=VMEM,
        scratch_shapes=[pltpu.VMEM((6, 8, BLOCK), jnp.float32)],
        compiler_params=params(),
    )(own, halos_cut, halo_hot, *sums)
    return (new_state.reshape(1, 1, 1, FIELDS, owned), residual[None, None, None])


def solution(mesh):
    sizes = tuple(mesh.shape[axis] for axis in AXES)
    row = P("mapx", "mapy", "layer", None)
    table = P("mapx", "mapy", "layer", None, None)
    return jax.shard_map(
        functools.partial(per_device, sizes),
        mesh=mesh,
        in_specs=(table, table, table, table, row, table, table, table, row),
        out_specs=(table, table),
        check_vma=False,
    )
```

```python
import functools

import jax
import jax.numpy as jnp
from jax import lax
from jax.experimental import pallas as pl
from jax.experimental.pallas import tpu as pltpu
from jax.sharding import PartitionSpec as P

BLOCK = 128
REACH = 2
FIELDS = 6
SPLITS = 3

ocean_temp = 0.0
strain_reg = 0.01
gravity = 0.5

AXES = ("mapx", "mapy", "layer")
VMEM = pl.BlockSpec(memory_space=pltpu.VMEM)
SMEM = pl.BlockSpec(memory_space=pltpu.SMEM)


def params():
    return pltpu.CompilerParams(vmem_limit_bytes=32 * 1024 * 1024)


def both_ways(pairs):
    return [way for one, other in pairs for way in ((one, other), (other, one))]


def column_moves(count):
    outside = [(at, at + 1) for at in range(1, count - 1, 2)]
    inside = [(at, at + 1) for at in range(0, count - 1, 2)]
    within = [(at + i, at + i + 2) for at in range(0, count - 3, 4) for i in range(2)]
    across = [(at + i, at + i + 2) for at in range(2, count - 3, 4) for i in range(2)]
    number = lambda pairs, layer: [(one * 2 + layer, other * 2 + layer) for one, other in pairs]
    return [
        both_ways(number(outside, 0) + number(inside, 1)),
        both_ways(number(within, 0) + number(across, 1)),
    ]


def column_offsets(layer):
    at = lax.axis_index("mapx")
    near = jnp.where(lax.rem(at, 2) == 0, 1, -1)
    two = jnp.where(lax.rem(at, 4) < 2, 2, -2)
    return [jnp.where(layer == 0, -near, near), jnp.where(layer == 0, two, -two)]


def pair_swap(value, axis, count, first):
    return lax.ppermute(value, axis, both_ways([(at, at + 1) for at in range(first, count - 1, 2)]))


def swap_all(values, sizes):
    long = [axis for axis in range(3) if sizes[axis] > 2]
    steps = [(axis, 1) for axis in long] + [(axis, 0) for axis in range(3)]
    return [pair_swap(value, AXES[axis], sizes[axis], first) for value, (axis, first) in zip(values, steps)]


def pack_kernel(count, *refs):
    blocks_in_ref, old_in_ref = refs[:2]
    give_first_ref, give_ref, first_ref, second_ref, own_ref = refs[2 + count : 7 + count]
    held = refs[7 + count : 7 + 2 * count]
    blocks_ref, old_ref, sems = refs[7 + 2 * count :]
    first = [pltpu.make_async_copy(blocks_in_ref, blocks_ref, sems.at[0])]
    first += [pltpu.make_async_copy(old_in_ref, old_ref, sems.at[1])]
    rest = [pltpu.make_async_copy(refs[2 + i], held[i], sems.at[2 + i]) for i in range(count)]
    for copy in first + rest:
        copy.start()
    for copy in first:
        copy.wait()
    slots = blocks_ref.shape[2]
    stride = old_ref.shape[0] // FIELDS
    layer = lax.axis_index("layer")
    mine, other = column_offsets(layer), column_offsets(1 - layer)
    size = FIELDS * slots
    for ref, offset in (
        (give_first_ref, other[0]),
        (give_ref, other[1]),
        (first_ref, mine[0]),
        (second_ref, mine[1]),
        (own_ref, 0),
    ):
        for to_layer in range(2):
            peer = (offset + REACH) * 2 + to_layer
            start = to_layer * size
            for c in range(slots):
                rows = pl.ds(blocks_ref[peer, 0, c], FIELDS, stride=stride)
                ref[start + FIELDS * c : start + FIELDS * (c + 1), :] = old_ref[rows, :]
    for copy in rest:
        copy.wait()
    slots_ref, weights_ref = held[0], held[1]
    slot_rows = slots_ref.shape[0] * slots_ref.shape[1] // BLOCK
    cut_rows(slots_ref, give_ref.at[2 * size : 2 * size + slot_rows])
    cut_rows(weights_ref, give_ref.at[2 * size + slot_rows : 2 * size + 2 * slot_rows])


def pick(row, lanes):
    return jnp.take_along_axis(jnp.broadcast_to(row, lanes.shape), lanes, axis=1)


def pick_fields(table_ref, block_count, blocks, lanes):
    found = [jnp.zeros((8, BLOCK), jnp.float32) for _ in range(FIELDS)]
    for b in range(block_count):
        hit = blocks == b
        for f in range(FIELDS):
            row = table_ref[b // 2, 2 * f + b % 2 : 2 * f + b % 2 + 1, :]
            found[f] = jnp.where(hit, pick(row, lanes), found[f])
    return found


def add_blocks(ref, chunk, first_block, blocks, lanes, found):
    local = blocks - first_block
    found = list(found)
    for c in range(ref.shape[1] // FIELDS):
        hit = local == c
        for f in range(FIELDS):
            row = ref[chunk, FIELDS * c + f : FIELDS * c + f + 1, :]
            found[f] = jnp.where(hit, pick(row, lanes), found[f])
    return tuple(found)


def add_chunks(ref, numbers, offset, ids, found):
    blocks, lanes = ids >> 7, ids & (BLOCK - 1)
    for chunk, layer in numbers:
        first = ((offset + REACH) * 2 + layer) * (ref.shape[1] // FIELDS)
        found = add_blocks(ref, chunk, first, blocks, lanes, found)
    return found


def load_fields(found_ref, owner, v):
    return tuple(found_ref[owner, f, 8 * v : 8 * v + 8, :] for f in range(FIELDS))


def save_fields(found_ref, owner, v, found):
    for f in range(FIELDS):
        found_ref[owner, f, 8 * v : 8 * v + 8, :] = found[f]


def arrived_chunks(ref, move, ids, found, owner):
    layer = lax.axis_index("layer")
    to_layer = 1 - layer if owner else layer
    numbers = [(to_layer, layer), (2 + to_layer, 1 - layer)]
    return add_chunks(ref, numbers, column_offsets(layer)[move], ids, found)


def cut_rows(from_ref, to_ref):
    count = from_ref.shape[1] // BLOCK
    for r in range(from_ref.shape[0]):
        for i in range(count):
            to_ref[r * count + i : r * count + i + 1, :] = from_ref[
                r : r + 1, i * BLOCK : (i + 1) * BLOCK
            ].astype(to_ref.dtype)


def lane_one_hot(ids):
    rows = lax.broadcasted_iota(jnp.int32, (BLOCK, BLOCK), 0)
    hit = rows == jnp.broadcast_to(ids & (BLOCK - 1), rows.shape)
    return jnp.where(hit, 1.0, 0.0).T.astype(jnp.bfloat16)


def own_kernel(
    own_ref,
    other_slots_ref,
    slots_in_ref,
    weights_in_ref,
    halos_in_ref,
    nodes_in_ref,
    volume_in_ref,
    found_ref,
    slots_ref,
    weights_ref,
    halos_ref,
    nodes_ref,
    volume_ref,
    halo_hot_ref,
    node_hot_ref,
):
    for k in range(halos_in_ref.shape[0]):
        cut_rows(halos_in_ref.at[k], halos_ref.at[2 * k : 2 * k + 2])
    cut_rows(slots_in_ref, slots_ref.at[0])
    slots_ref[1] = other_slots_ref[...].astype(jnp.int32)
    cut_rows(weights_in_ref, weights_ref)
    cut_rows(nodes_in_ref, nodes_ref)
    cut_rows(volume_in_ref, volume_ref)
    layer = lax.axis_index("layer")
    for owner in range(2):
        for v in range(slots_ref.shape[1] // 8):
            ids = slots_ref[owner, 8 * v : 8 * v + 8, :]
            found = tuple(jnp.zeros((8, BLOCK), jnp.float32) for _ in range(FIELDS))
            numbers = [(1 - layer if owner else layer, layer)]
            save_fields(found_ref, owner, v, add_chunks(own_ref, numbers, 0, ids, found))
    for r in range(halos_ref.shape[0]):
        halo_hot_ref[r * BLOCK : (r + 1) * BLOCK, :] = lane_one_hot(halos_ref[r : r + 1, :])
    steps, width, _ = node_hot_ref.shape
    group = width // BLOCK

    def hot(step, carry):
        for r in range(group):
            ids = nodes_ref[pl.ds(step * group + r, 1), :]
            node_hot_ref[step, r * BLOCK : (r + 1) * BLOCK, :] = lane_one_hot(ids)
        return carry

    lax.fori_loop(0, steps, hot, 0)


def early_kernel(came_ref, slots_ref, found_in_ref, found_ref):
    for owner in range(2):
        for v in range(slots_ref.shape[1] // 8):
            ids = slots_ref[owner, 8 * v : 8 * v + 8, :]
            found = arrived_chunks(came_ref, 1, ids, load_fields(found_in_ref, owner, v), owner)
            save_fields(found_ref, owner, v, found)


def late_kernel(rows, came_ref, slots_ref, found_ref, weights_ref, other_weights_ref, mine_ref, other_ref):
    for owner, out_ref, weight_ref in ((1, other_ref, other_weights_ref), (0, mine_ref, weights_ref)):
        totals = [jnp.zeros((rows, BLOCK), jnp.float32) for _ in range(FIELDS)]
        for v in range(slots_ref.shape[1] // 8):
            ids = slots_ref[owner, 8 * v : 8 * v + 8, :]
            found = arrived_chunks(came_ref, 0, ids, load_fields(found_ref, owner, v), owner)
            for f in range(FIELDS):
                term = found[f] * weight_ref[8 * v : 8 * v + 8, :]
                for k in range(8 // rows):
                    totals[f] = totals[f] + term[k * rows : (k + 1) * rows, :]
        for f in range(FIELDS):
            out_ref[f * rows : (f + 1) * rows, :] = totals[f]


def state_kernel(counts, mine_ref, came_ref, mask_ref, halos_ref, state_ref, table_ref, *more_refs):
    send_refs, cut_ref = more_refs[:-1], more_refs[-1]
    front = mask_ref[...] == 1
    rows = mask_ref.shape[0]
    for f in range(FIELDS):
        at = slice(f * rows, (f + 1) * rows)
        total = mine_ref[at, :] + came_ref[at, :]
        if f == 4:
            total = jnp.where(front, ocean_temp, total)
        state_ref[f * rows : (f + 1) * rows, :] = total
        for s in range(rows // 2):
            table_ref[s, 2 * f : 2 * f + 2, :] = total[2 * s : 2 * s + 2, :]
    starts = (0, halos_ref.shape[0] - 8)
    halo = [halos_ref[first : first + 8, :] for first in starts]
    halo_blocks = [i >> 7 for i in halo]
    halo_lanes = [i & (BLOCK - 1) for i in halo]
    for v in range(2):
        cut = pick_fields(table_ref, rows, halo_blocks[v], halo_lanes[v])
        for k in range(6):
            r = 2 * k - starts[v]
            if 0 <= r <= 6:
                for f in range(FIELDS):
                    cut_ref[k, 2 * f : 2 * f + 2, :] = cut[f][r : r + 2, :]
    send_pairs(counts, cut_ref, send_refs, [(0, 1), (2, 3), (4, 5)])


def pair_places():
    return [lax.rem(lax.axis_index(axis), 2) for axis in AXES]


def send_pairs(counts, cut_ref, send_refs, order):
    places = pair_places()
    long = [axis for axis in range(3) if counts[axis] > 2]
    for axis in range(3):
        even, odd = order[axis]
        send_refs[len(long) + axis][...] = cut_ref[jnp.where(places[axis] == 0, even, odd)]
        if axis in long:
            send_refs[long.index(axis)][...] = cut_ref[jnp.where(places[axis] == 0, odd, even)]


def arrivals(counts, came_refs):
    places = pair_places()
    long = [axis for axis in range(3) if counts[axis] > 2]
    result = []
    for axis in range(3):
        inside = came_refs[len(long) + axis][...]
        at = lax.axis_index(AXES[axis])
        edge = jnp.where(places[axis] == 0, at == 0, at == counts[axis] - 1)
        outside = jnp.zeros_like(inside)
        if axis in long:
            outside = jnp.where(edge, 0.0, came_refs[long.index(axis)][...])
        result.append((places[axis], inside, outside))
    return result


def placed(values, ids, block_count):
    rows = lax.broadcasted_iota(jnp.int32, (block_count, BLOCK), 0)
    hit = rows == jnp.broadcast_to(ids >> 7, rows.shape)
    left = [jnp.where(hit, jnp.broadcast_to(v, rows.shape), 0.0) for v in values]
    return jnp.concatenate(left, axis=0).astype(jnp.bfloat16)


def cut_parts(value):
    parts = []
    for _ in range(SPLITS - 1):
        part = value.astype(jnp.bfloat16).astype(jnp.float32)
        parts.append(part)
        value = value - part
    return parts + [value]


def hot_dot(left, right):
    return jnp.dot(left, right, preferred_element_type=jnp.float32)


def element_kernel(counts, moves, *refs):
    table_in_ref, nodes_ref, node_hot_ref, grads_ref, volume_ref = refs[:5]
    came_refs = refs[5 : 5 + moves]
    own_ref = refs[5 + moves]
    send_refs = refs[6 + moves : 6 + 2 * moves]
    table_ref, values_ref, parts_ref, cut_ref = refs[6 + 2 * moves :]
    owned_slots = table_in_ref.shape[0]
    table_ref[0:owned_slots] = table_in_ref[...]
    for axis, (place_at, inside, outside) in enumerate(arrivals(counts, came_refs)):
        table_ref[owned_slots + 2 * axis + 1 - place_at] = inside
        table_ref[owned_slots + 2 * axis + place_at] = outside
    block_count = 2 * table_ref.shape[0]
    all_rows = nodes_ref.shape[0]
    elem_rows = all_rows // 4
    for first in range(0, all_rows, 8):
        ids = nodes_ref[first : first + 8, :]
        found = pick_fields(table_ref, block_count, ids >> 7, ids & (BLOCK - 1))
        for f in range(FIELDS):
            values_ref[f, first : first + 8, :] = found[f]
    for first in [*range(0, elem_rows - 7, 8)] + ([elem_rows - 8] if elem_rows % 8 else []):
        at = [slice(r * elem_rows + first, r * elem_rows + first + 8) for r in range(12)]
        values = [[values_ref[f, at[a], :] for f in range(FIELDS)] for a in range(4)]
        grads = [[grads_ref[at[3 * a + j], :] for j in range(3)] for a in range(4)]
        volume = volume_ref[at[0], :]
        velgrad = [[sum(values[a][i] * grads[a][j] for a in range(4)) for j in range(3)] for i in range(3)]
        strain = [[0.5 * (velgrad[i][j] + velgrad[j][i]) if i <= j else None for j in range(3)] for i in range(3)]
        diagonal = sum(strain[i][i] * strain[i][i] for i in range(3))
        corner = sum(strain[i][j] * strain[i][j] for i, j in ((0, 1), (0, 2), (1, 2)))
        second = 0.5 * diagonal + corner
        pressure, temper, damage = [0.25 * (values[0][f] + values[1][f] + values[2][f] + values[3][f]) for f in (3, 4, 5)]
        root = jnp.exp(jnp.log(second + strain_reg) * (-1.0 / 3.0))
        twice = (1.0 - damage) * jnp.exp(-temper) * root
        stress = [[None] * 3 for _ in range(3)]
        for i in range(3):
            for j in range(i, 3):
                stress[i][j] = twice * strain[i][j] - (pressure if i == j else 0.0)
                stress[j][i] = stress[i][j]
        lift = (0.25 * gravity) * volume
        flow = 0.25 * volume * (velgrad[0][0] + velgrad[1][1] + velgrad[2][2])
        for s, part in enumerate(cut_parts(flow)):
            for a in range(4):
                parts_ref[3 * SPLITS + s, at[a], :] = part
        for a in range(4):
            for i in range(3):
                force = volume * sum(stress[i][j] * grads[a][j] for j in range(3))
                if i == 2:
                    force = force + lift
                for s, part in enumerate(cut_parts(force)):
                    parts_ref[i * SPLITS + s, at[a], :] = part

    group = node_hot_ref.shape[1] // BLOCK

    def gather_terms(step, total):
        lefts = []
        for r in range(group):
            at = pl.ds(step * group + r, 1)
            terms = [parts_ref[c * SPLITS + s, at, :] for s in range(SPLITS) for c in range(4)]
            lefts.append(placed(terms, nodes_ref[at, :], block_count))
        return total + hot_dot(jnp.concatenate(lefts, axis=1), node_hot_ref[step])

    width = 4 * block_count
    total = lax.fori_loop(0, all_rows // group, gather_terms, jnp.zeros((SPLITS * width, BLOCK), jnp.float32))
    total = sum(total[s * width : (s + 1) * width, :] for s in range(SPLITS))
    owned = 2 * owned_slots
    for c in range(4):
        own_ref[c * owned : (c + 1) * owned, :] = total[c * block_count : c * block_count + owned, :]
        for k in range(6):
            first = c * block_count + owned + 2 * k
            cut_ref[k, 2 * c : 2 * c + 2, :] = total[first : first + 2, :]
    send_pairs(counts, cut_ref, send_refs, [(1, 0), (3, 2), (5, 4)])


def residual_kernel(counts, moves, *refs):
    own_ref, halos_ref, halo_hot_ref = refs[:3]
    out_ref, came_ref = refs[3 + moves :]
    for axis, (place_at, inside, outside) in enumerate(arrivals(counts, refs[3 : 3 + moves])):
        came_ref[2 * axis + place_at] = inside
        came_ref[2 * axis + 1 - place_at] = outside
    owned = own_ref.shape[0] // 4
    lefts = []
    for k in range(6):
        parts = cut_parts(came_ref[k])
        for h in range(2):
            ids = halos_ref[2 * k + h : 2 * k + h + 1, :]
            terms = [parts[s][2 * c + h : 2 * c + h + 1, :] for s in range(SPLITS) for c in range(4)]
            lefts.append(placed(terms, ids, owned))
    total = hot_dot(jnp.concatenate(lefts, axis=1), halo_hot_ref[...])
    width = 4 * owned
    total = sum(total[s * width : (s + 1) * width, :] for s in range(SPLITS)) + own_ref[...]
    for c in range(4):
        for b in range(owned):
            r = c * owned + b
            out_ref[c : c + 1, b * BLOCK : (b + 1) * BLOCK] = total[r : r + 1, :]


def shaped(*shape):
    return jax.ShapeDtypeStruct(shape, jnp.float32)


def per_device(
    sizes,
    old_state,
    send_blocks,
    node_slots,
    node_weights,
    front_mask,
    halo_lists,
    elem_nodes,
    shape_grads,
    elem_volume,
):
    old_state, send_blocks = old_state[0, 0, 0], send_blocks[0, 0, 0]
    slots = send_blocks.shape[1]
    send_blocks = send_blocks.reshape(-1, 1, slots)
    rows = FIELDS * slots
    arguments = [
        node_slots[0, 0, 0],
        node_weights[0, 0, 0],
        front_mask.reshape(-1, BLOCK),
        halo_lists.reshape(halo_lists.shape[-2], 1, -1),
        elem_nodes[0, 0, 0],
        shape_grads.reshape(-1, BLOCK),
        elem_volume[0, 0],
    ]
    old_rows = old_state.reshape(-1, BLOCK)
    count = len(arguments)
    owned = node_slots.shape[-1]
    slot_rows = node_slots.size // BLOCK
    give_rows = 2 * rows + 2 * slot_rows
    give_first, give, first, second, own, *held = pl.pallas_call(
        functools.partial(pack_kernel, count),
        out_shape=[shaped(2 * rows, BLOCK), shaped(give_rows, BLOCK)]
        + [shaped(2 * rows, BLOCK)] * 3
        + [jax.ShapeDtypeStruct(a.shape, a.dtype) for a in arguments],
        in_specs=[pl.BlockSpec(memory_space=pltpu.HBM)] * (2 + count),
        out_specs=[VMEM] * (5 + count),
        scratch_shapes=[
            pltpu.SMEM(send_blocks.shape, jnp.int32),
            pltpu.VMEM(old_rows.shape, jnp.float32),
            pltpu.SemaphoreType.DMA((2 + count,)),
        ],
        compiler_params=params(),
    )(*(pltpu.with_memory_space_constraint(a, pltpu.HBM) for a in (send_blocks, old_rows, *arguments)))
    node_slots, node_weights, mask_rows, halos, elem_nodes, grad_rows, volume = held
    layers = both_ways([(0, 1)])
    got_first = lax.ppermute(give_first, "layer", layers)
    got = lax.ppermute(give, "layer", layers)
    full = [jnp.concatenate([first, got_first]), jnp.concatenate([second, got[: 2 * rows]])]
    first, second = [
        lax.ppermute(part, ("mapx", "layer"), pairs).reshape(4, rows, BLOCK)
        for part, pairs in zip(full, column_moves(sizes[0]))
    ]
    other_slots, other_weights = got[2 * rows : 2 * rows + slot_rows], got[2 * rows + slot_rows :]

    all_rows = elem_nodes.size // BLOCK
    halo_count = halos.size // BLOCK
    hot_steps = next(n for n in (8, 4, 2, 1) if all_rows % n == 0)
    whole = lambda *shape: jax.ShapeDtypeStruct(shape, jnp.int32)
    found, slots_cut, weights_cut, halos_cut, nodes_cut, volume_cut, halo_hot, node_hot = pl.pallas_call(
        own_kernel,
        out_shape=(
            shaped(2, FIELDS, slot_rows, BLOCK),
            whole(2, slot_rows, BLOCK),
            shaped(slot_rows, BLOCK),
            whole(halo_count, BLOCK),
            whole(all_rows, BLOCK),
            shaped(all_rows // 4, BLOCK),
            jax.ShapeDtypeStruct((halo_count * BLOCK, BLOCK), jnp.bfloat16),
            jax.ShapeDtypeStruct((hot_steps, all_rows // hot_steps * BLOCK, BLOCK), jnp.bfloat16),
        ),
        in_specs=[VMEM] * 7,
        out_specs=(VMEM,) * 8,
        compiler_params=params(),
    )(own.reshape(2, rows, BLOCK), other_slots, node_slots, node_weights, halos, elem_nodes, volume)
    found = pl.pallas_call(
        early_kernel,
        out_shape=shaped(2, FIELDS, slot_rows, BLOCK),
        in_specs=[VMEM] * 3,
        out_specs=VMEM,
        compiler_params=params(),
    )(second, slots_cut, found)
    state_rows = FIELDS * owned // BLOCK
    mine, other = pl.pallas_call(
        functools.partial(late_kernel, owned // BLOCK),
        out_shape=(shaped(state_rows, BLOCK),) * 2,
        in_specs=[VMEM] * 5,
        out_specs=(VMEM,) * 2,
        compiler_params=params(),
    )(first, slots_cut, found, weights_cut, other_weights)
    other = lax.ppermute(other, "layer", layers)
    moves = 3 + sum(size > 2 for size in sizes)
    chunk = (2 * FIELDS, BLOCK)
    new_state, table, *ghosts = pl.pallas_call(
        functools.partial(state_kernel, sizes),
        out_shape=(shaped(state_rows, BLOCK), shaped(owned // (2 * BLOCK), *chunk)) + (shaped(*chunk),) * moves,
        in_specs=[VMEM] * 4,
        out_specs=(VMEM,) * (2 + moves),
        scratch_shapes=[pltpu.VMEM((6, *chunk), jnp.float32)],
        compiler_params=params(),
    )(mine, other, mask_rows, halos_cut)
    ghosts = swap_all(ghosts, sizes)

    slots_all = table.shape[0] + 6
    own, *sums = pl.pallas_call(
        functools.partial(element_kernel, sizes, moves),
        out_shape=(shaped(4 * owned // BLOCK, BLOCK),) + (shaped(8, BLOCK),) * moves,
        in_specs=[VMEM] * (5 + moves),
        out_specs=(VMEM,) * (1 + moves),
        scratch_shapes=[
            pltpu.VMEM((slots_all, *chunk), jnp.float32),
            pltpu.VMEM((FIELDS, all_rows, BLOCK), jnp.float32),
            pltpu.VMEM((4 * SPLITS, all_rows, BLOCK), jnp.float32),
            pltpu.VMEM((6, 8, BLOCK), jnp.float32),
        ],
        compiler_params=params(),
    )(table, nodes_cut, node_hot, grad_rows, volume_cut, *ghosts)
    sums = swap_all(sums, sizes)
    residual = pl.pallas_call(
        functools.partial(residual_kernel, sizes, moves),
        out_shape=shaped(4, owned),
        in_specs=[VMEM] * (3 + moves),
        out_specs=VMEM,
        scratch_shapes=[pltpu.VMEM((6, 8, BLOCK), jnp.float32)],
        compiler_params=params(),
    )(own, halos_cut, halo_hot, *sums)
    return (new_state.reshape(1, 1, 1, FIELDS, owned), residual[None, None, None])


def solution(mesh):
    sizes = tuple(mesh.shape[axis] for axis in AXES)
    row = P("mapx", "mapy", "layer", None)
    table = P("mapx", "mapy", "layer", None, None)
    return jax.shard_map(
        functools.partial(per_device, sizes),
        mesh=mesh,
        in_specs=(table, table, table, table, row, table, table, table, row),
        out_specs=(table, table),
        check_vma=False,
    )
```

```python
import functools

import jax
import jax.numpy as jnp
from jax import lax
from jax.experimental import pallas as pl
from jax.experimental.pallas import tpu as pltpu
from jax.sharding import PartitionSpec as P

BLOCK = 128
REACH = 2
FIELDS = 6
SPLITS = 3

ocean_temp = 0.0
strain_reg = 0.01
gravity = 0.5

AXES = ("mapx", "mapy", "layer")
VMEM = pl.BlockSpec(memory_space=pltpu.VMEM)
SMEM = pl.BlockSpec(memory_space=pltpu.SMEM)


def params():
    return pltpu.CompilerParams(vmem_limit_bytes=32 * 1024 * 1024)


def both_ways(pairs):
    return [way for one, other in pairs for way in ((one, other), (other, one))]


def column_moves(count):
    outside = [(at, at + 1) for at in range(1, count - 1, 2)]
    inside = [(at, at + 1) for at in range(0, count - 1, 2)]
    within = [(at + i, at + i + 2) for at in range(0, count - 3, 4) for i in range(2)]
    across = [(at + i, at + i + 2) for at in range(2, count - 3, 4) for i in range(2)]
    number = lambda pairs, layer: [(one * 2 + layer, other * 2 + layer) for one, other in pairs]
    return [
        both_ways(number(outside, 0) + number(inside, 1)),
        both_ways(number(within, 0) + number(across, 1)),
    ]


def column_offsets(layer):
    at = lax.axis_index("mapx")
    near = jnp.where(lax.rem(at, 2) == 0, 1, -1)
    two = jnp.where(lax.rem(at, 4) < 2, 2, -2)
    return [jnp.where(layer == 0, -near, near), jnp.where(layer == 0, two, -two)]


def pair_swap(value, axis, count, first):
    return lax.ppermute(value, axis, both_ways([(at, at + 1) for at in range(first, count - 1, 2)]))


def swap_all(values, sizes):
    long = [axis for axis in range(3) if sizes[axis] > 2]
    steps = [(axis, 1) for axis in long] + [(axis, 0) for axis in range(3)]
    return [pair_swap(value, AXES[axis], sizes[axis], first) for value, (axis, first) in zip(values, steps)]


def pack_kernel(count, *refs):
    blocks_in_ref, old_in_ref = refs[:2]
    give_first_ref, give_ref, first_ref, second_ref, own_ref = refs[2 + count : 7 + count]
    held = refs[7 + count : 7 + 2 * count]
    blocks_ref, old_ref, sems = refs[7 + 2 * count :]
    first = [pltpu.make_async_copy(blocks_in_ref, blocks_ref, sems.at[0])]
    first += [pltpu.make_async_copy(old_in_ref, old_ref, sems.at[1])]
    rest = [pltpu.make_async_copy(refs[2 + i], held[i], sems.at[2 + i]) for i in range(count)]
    for copy in first + rest:
        copy.start()
    for copy in first:
        copy.wait()
    slots = blocks_ref.shape[2]
    stride = old_ref.shape[0] // FIELDS
    layer = lax.axis_index("layer")
    mine, other = column_offsets(layer), column_offsets(1 - layer)
    size = FIELDS * slots
    for ref, offset in (
        (give_first_ref, other[0]),
        (give_ref, other[1]),
        (first_ref, mine[0]),
        (second_ref, mine[1]),
        (own_ref, 0),
    ):
        for to_layer in range(2):
            peer = (offset + REACH) * 2 + to_layer
            start = to_layer * size
            for c in range(slots):
                rows = pl.ds(blocks_ref[peer, 0, c], FIELDS, stride=stride)
                ref[start + FIELDS * c : start + FIELDS * (c + 1), :] = old_ref[rows, :]
    for copy in rest:
        copy.wait()
    slots_ref, weights_ref = held[0], held[1]
    slot_rows = slots_ref.shape[0] * slots_ref.shape[1] // BLOCK
    cut_rows(slots_ref, give_ref.at[2 * size : 2 * size + slot_rows])
    cut_rows(weights_ref, give_ref.at[2 * size + slot_rows : 2 * size + 2 * slot_rows])


def pick(row, lanes):
    return jnp.take_along_axis(jnp.broadcast_to(row, lanes.shape), lanes, axis=1)


def pick_fields(table_ref, block_count, blocks, lanes):
    found = [jnp.zeros((8, BLOCK), jnp.float32) for _ in range(FIELDS)]
    for b in range(block_count):
        hit = blocks == b
        for f in range(FIELDS):
            row = table_ref[b // 2, 2 * f + b % 2 : 2 * f + b % 2 + 1, :]
            found[f] = jnp.where(hit, pick(row, lanes), found[f])
    return found


def add_blocks(ref, chunk, first_block, blocks, lanes, found):
    local = blocks - first_block
    found = list(found)
    for c in range(ref.shape[1] // FIELDS):
        hit = local == c
        for f in range(FIELDS):
            row = ref[chunk, FIELDS * c + f : FIELDS * c + f + 1, :]
            found[f] = jnp.where(hit, pick(row, lanes), found[f])
    return tuple(found)


def add_chunks(ref, numbers, offset, ids, found):
    blocks, lanes = ids >> 7, ids & (BLOCK - 1)
    for chunk, layer in numbers:
        first = ((offset + REACH) * 2 + layer) * (ref.shape[1] // FIELDS)
        found = add_blocks(ref, chunk, first, blocks, lanes, found)
    return found


def load_fields(found_ref, owner, v):
    return tuple(found_ref[owner, f, 8 * v : 8 * v + 8, :] for f in range(FIELDS))


def save_fields(found_ref, owner, v, found):
    for f in range(FIELDS):
        found_ref[owner, f, 8 * v : 8 * v + 8, :] = found[f]


def arrived_chunks(ref, move, ids, found, owner):
    layer = lax.axis_index("layer")
    to_layer = 1 - layer if owner else layer
    numbers = [(to_layer, layer), (2 + to_layer, 1 - layer)]
    return add_chunks(ref, numbers, column_offsets(layer)[move], ids, found)


def cut_rows(from_ref, to_ref):
    count = from_ref.shape[1] // BLOCK
    for r in range(from_ref.shape[0]):
        for i in range(count):
            to_ref[r * count + i : r * count + i + 1, :] = from_ref[
                r : r + 1, i * BLOCK : (i + 1) * BLOCK
            ].astype(to_ref.dtype)


def lane_one_hot(ids):
    rows = lax.broadcasted_iota(jnp.int32, (BLOCK, BLOCK), 0)
    hit = rows == jnp.broadcast_to(ids & (BLOCK - 1), rows.shape)
    return jnp.where(hit, 1.0, 0.0).T.astype(jnp.bfloat16)


def own_kernel(
    own_ref,
    other_slots_ref,
    slots_in_ref,
    weights_in_ref,
    halos_in_ref,
    nodes_in_ref,
    volume_in_ref,
    found_ref,
    slots_ref,
    weights_ref,
    halos_ref,
    nodes_ref,
    volume_ref,
    halo_hot_ref,
    node_hot_ref,
):
    for k in range(halos_in_ref.shape[0]):
        cut_rows(halos_in_ref.at[k], halos_ref.at[2 * k : 2 * k + 2])
    cut_rows(slots_in_ref, slots_ref.at[0])
    slots_ref[1] = other_slots_ref[...].astype(jnp.int32)
    cut_rows(weights_in_ref, weights_ref)
    cut_rows(nodes_in_ref, nodes_ref)
    cut_rows(volume_in_ref, volume_ref)
    layer = lax.axis_index("layer")
    for owner in range(2):
        for v in range(slots_ref.shape[1] // 8):
            ids = slots_ref[owner, 8 * v : 8 * v + 8, :]
            found = tuple(jnp.zeros((8, BLOCK), jnp.float32) for _ in range(FIELDS))
            numbers = [(1 - layer if owner else layer, layer)]
            save_fields(found_ref, owner, v, add_chunks(own_ref, numbers, 0, ids, found))
    for r in range(halos_ref.shape[0]):
        halo_hot_ref[r * BLOCK : (r + 1) * BLOCK, :] = lane_one_hot(halos_ref[r : r + 1, :])
    steps, width, _ = node_hot_ref.shape
    group = width // BLOCK

    def hot(step, carry):
        for r in range(group):
            ids = nodes_ref[pl.ds(step * group + r, 1), :]
            node_hot_ref[step, r * BLOCK : (r + 1) * BLOCK, :] = lane_one_hot(ids)
        return carry

    lax.fori_loop(0, steps, hot, 0)


def early_kernel(came_ref, slots_ref, found_in_ref, found_ref):
    for owner in range(2):
        for v in range(slots_ref.shape[1] // 8):
            ids = slots_ref[owner, 8 * v : 8 * v + 8, :]
            found = arrived_chunks(came_ref, 0, ids, load_fields(found_in_ref, owner, v), owner)
            save_fields(found_ref, owner, v, found)


def late_kernel(rows, came_ref, slots_ref, found_ref, weights_ref, other_weights_ref, mine_ref, other_ref):
    for owner, out_ref, weight_ref in ((1, other_ref, other_weights_ref), (0, mine_ref, weights_ref)):
        totals = [jnp.zeros((rows, BLOCK), jnp.float32) for _ in range(FIELDS)]
        for v in range(slots_ref.shape[1] // 8):
            ids = slots_ref[owner, 8 * v : 8 * v + 8, :]
            found = arrived_chunks(came_ref, 1, ids, load_fields(found_ref, owner, v), owner)
            for f in range(FIELDS):
                term = found[f] * weight_ref[8 * v : 8 * v + 8, :]
                for k in range(8 // rows):
                    totals[f] = totals[f] + term[k * rows : (k + 1) * rows, :]
        for f in range(FIELDS):
            out_ref[f * rows : (f + 1) * rows, :] = totals[f]


def state_kernel(counts, mine_ref, came_ref, mask_ref, halos_ref, state_ref, table_ref, *more_refs):
    send_refs, cut_ref = more_refs[:-1], more_refs[-1]
    front = mask_ref[...] == 1
    rows = mask_ref.shape[0]
    for f in range(FIELDS):
        at = slice(f * rows, (f + 1) * rows)
        total = mine_ref[at, :] + came_ref[at, :]
        if f == 4:
            total = jnp.where(front, ocean_temp, total)
        state_ref[f * rows : (f + 1) * rows, :] = total
        for s in range(rows // 2):
            table_ref[s, 2 * f : 2 * f + 2, :] = total[2 * s : 2 * s + 2, :]
    starts = (0, halos_ref.shape[0] - 8)
    halo = [halos_ref[first : first + 8, :] for first in starts]
    halo_blocks = [i >> 7 for i in halo]
    halo_lanes = [i & (BLOCK - 1) for i in halo]
    for v in range(2):
        cut = pick_fields(table_ref, rows, halo_blocks[v], halo_lanes[v])
        for k in range(6):
            r = 2 * k - starts[v]
            if 0 <= r <= 6:
                for f in range(FIELDS):
                    cut_ref[k, 2 * f : 2 * f + 2, :] = cut[f][r : r + 2, :]
    send_pairs(counts, cut_ref, send_refs, [(0, 1), (2, 3), (4, 5)])


def pair_places():
    return [lax.rem(lax.axis_index(axis), 2) for axis in AXES]


def send_pairs(counts, cut_ref, send_refs, order):
    places = pair_places()
    long = [axis for axis in range(3) if counts[axis] > 2]
    for axis in range(3):
        even, odd = order[axis]
        send_refs[len(long) + axis][...] = cut_ref[jnp.where(places[axis] == 0, even, odd)]
        if axis in long:
            send_refs[long.index(axis)][...] = cut_ref[jnp.where(places[axis] == 0, odd, even)]


def arrivals(counts, came_refs):
    places = pair_places()
    long = [axis for axis in range(3) if counts[axis] > 2]
    result = []
    for axis in range(3):
        inside = came_refs[len(long) + axis][...]
        at = lax.axis_index(AXES[axis])
        edge = jnp.where(places[axis] == 0, at == 0, at == counts[axis] - 1)
        outside = jnp.zeros_like(inside)
        if axis in long:
            outside = jnp.where(edge, 0.0, came_refs[long.index(axis)][...])
        result.append((places[axis], inside, outside))
    return result


def placed(values, ids, block_count):
    kind = jnp.bfloat16 if block_count % 16 == 0 else jnp.float32
    rows = lax.broadcasted_iota(jnp.int32, (block_count, BLOCK), 0).astype(jnp.float32).astype(kind)
    wide = lambda value: jnp.broadcast_to(value, rows.shape).astype(kind)
    hit = rows == wide((ids >> 7).astype(jnp.float32))
    left = jnp.concatenate([jnp.where(hit, wide(v), jnp.zeros_like(rows)) for v in values], axis=0)
    return left.astype(jnp.bfloat16)


def cut_parts(value):
    parts = []
    for _ in range(SPLITS - 1):
        part = value.astype(jnp.bfloat16).astype(jnp.float32)
        parts.append(part)
        value = value - part
    return parts + [value]


def hot_dot(left, right):
    return jnp.dot(left, right, preferred_element_type=jnp.float32)


def element_kernel(counts, moves, *refs):
    table_in_ref, nodes_ref, node_hot_ref, grads_ref, volume_ref = refs[:5]
    came_refs = refs[5 : 5 + moves]
    own_ref = refs[5 + moves]
    send_refs = refs[6 + moves : 6 + 2 * moves]
    table_ref, values_ref, parts_ref, cut_ref = refs[6 + 2 * moves :]
    owned_slots = table_in_ref.shape[0]
    table_ref[0:owned_slots] = table_in_ref[...]
    for axis, (place_at, inside, outside) in enumerate(arrivals(counts, came_refs)):
        table_ref[owned_slots + 2 * axis + 1 - place_at] = inside
        table_ref[owned_slots + 2 * axis + place_at] = outside
    block_count = 2 * table_ref.shape[0]
    all_rows = nodes_ref.shape[0]
    elem_rows = all_rows // 4
    for first in range(0, all_rows, 8):
        ids = nodes_ref[first : first + 8, :]
        found = pick_fields(table_ref, block_count, ids >> 7, ids & (BLOCK - 1))
        for f in range(FIELDS):
            values_ref[f, first : first + 8, :] = found[f]
    for first in [*range(0, elem_rows - 7, 8)] + ([elem_rows - 8] if elem_rows % 8 else []):
        at = [slice(r * elem_rows + first, r * elem_rows + first + 8) for r in range(12)]
        values = [[values_ref[f, at[a], :] for f in range(FIELDS)] for a in range(4)]
        grads = [[grads_ref[at[3 * a + j], :] for j in range(3)] for a in range(4)]
        volume = volume_ref[at[0], :]
        velgrad = [[sum(values[a][i] * grads[a][j] for a in range(4)) for j in range(3)] for i in range(3)]
        strain = [[0.5 * (velgrad[i][j] + velgrad[j][i]) if i <= j else None for j in range(3)] for i in range(3)]
        diagonal = sum(strain[i][i] * strain[i][i] for i in range(3))
        corner = sum(strain[i][j] * strain[i][j] for i, j in ((0, 1), (0, 2), (1, 2)))
        second = 0.5 * diagonal + corner
        pressure, temper, damage = [0.25 * (values[0][f] + values[1][f] + values[2][f] + values[3][f]) for f in (3, 4, 5)]
        root = jnp.exp(jnp.log(second + strain_reg) * (-1.0 / 3.0))
        twice = (1.0 - damage) * jnp.exp(-temper) * root
        stress = [[None] * 3 for _ in range(3)]
        for i in range(3):
            for j in range(i, 3):
                stress[i][j] = twice * strain[i][j] - (pressure if i == j else 0.0)
                stress[j][i] = stress[i][j]
        lift = (0.25 * gravity) * volume
        flow = 0.25 * volume * (velgrad[0][0] + velgrad[1][1] + velgrad[2][2])
        for s, part in enumerate(cut_parts(flow)):
            for a in range(4):
                parts_ref[3 * SPLITS + s, at[a], :] = part
        for a in range(4):
            for i in range(3):
                force = volume * sum(stress[i][j] * grads[a][j] for j in range(3))
                if i == 2:
                    force = force + lift
                for s, part in enumerate(cut_parts(force)):
                    parts_ref[i * SPLITS + s, at[a], :] = part

    group = node_hot_ref.shape[1] // BLOCK

    def gather_terms(step, total):
        lefts = []
        for r in range(group):
            at = pl.ds(step * group + r, 1)
            terms = [parts_ref[c * SPLITS + s, at, :] for s in range(SPLITS) for c in range(4)]
            lefts.append(placed(terms, nodes_ref[at, :], block_count))
        return total + hot_dot(jnp.concatenate(lefts, axis=1), node_hot_ref[step])

    width = 4 * block_count
    total = lax.fori_loop(0, all_rows // group, gather_terms, jnp.zeros((SPLITS * width, BLOCK), jnp.float32))
    total = sum(total[s * width : (s + 1) * width, :] for s in range(SPLITS))
    owned = 2 * owned_slots
    for c in range(4):
        own_ref[c * owned : (c + 1) * owned, :] = total[c * block_count : c * block_count + owned, :]
        for k in range(6):
            first = c * block_count + owned + 2 * k
            cut_ref[k, 2 * c : 2 * c + 2, :] = total[first : first + 2, :]
    send_pairs(counts, cut_ref, send_refs, [(1, 0), (3, 2), (5, 4)])


def residual_kernel(counts, moves, *refs):
    own_ref, halos_ref, halo_hot_ref = refs[:3]
    out_ref, came_ref = refs[3 + moves :]
    for axis, (place_at, inside, outside) in enumerate(arrivals(counts, refs[3 : 3 + moves])):
        came_ref[2 * axis + place_at] = inside
        came_ref[2 * axis + 1 - place_at] = outside
    owned = own_ref.shape[0] // 4
    lefts = []
    for k in range(6):
        parts = cut_parts(came_ref[k])
        for h in range(2):
            ids = halos_ref[2 * k + h : 2 * k + h + 1, :]
            terms = [parts[s][2 * c + h : 2 * c + h + 1, :] for s in range(SPLITS) for c in range(4)]
            lefts.append(placed(terms, ids, owned))
    total = hot_dot(jnp.concatenate(lefts, axis=1), halo_hot_ref[...])
    width = 4 * owned
    total = sum(total[s * width : (s + 1) * width, :] for s in range(SPLITS)) + own_ref[...]
    for c in range(4):
        for b in range(owned):
            r = c * owned + b
            out_ref[c : c + 1, b * BLOCK : (b + 1) * BLOCK] = total[r : r + 1, :]


def shaped(*shape):
    return jax.ShapeDtypeStruct(shape, jnp.float32)


def per_device(
    sizes,
    old_state,
    send_blocks,
    node_slots,
    node_weights,
    front_mask,
    halo_lists,
    elem_nodes,
    shape_grads,
    elem_volume,
):
    old_state, send_blocks = old_state[0, 0, 0], send_blocks[0, 0, 0]
    slots = send_blocks.shape[1]
    send_blocks = send_blocks.reshape(-1, 1, slots)
    rows = FIELDS * slots
    arguments = [
        node_slots[0, 0, 0],
        node_weights[0, 0, 0],
        front_mask.reshape(-1, BLOCK),
        halo_lists.reshape(halo_lists.shape[-2], 1, -1),
        elem_nodes[0, 0, 0],
        shape_grads.reshape(-1, BLOCK),
        elem_volume[0, 0],
    ]
    old_rows = old_state.reshape(-1, BLOCK)
    count = len(arguments)
    owned = node_slots.shape[-1]
    slot_rows = node_slots.size // BLOCK
    give_rows = 2 * rows + 2 * slot_rows
    give_first, give, first, second, own, *held = pl.pallas_call(
        functools.partial(pack_kernel, count),
        out_shape=[shaped(2 * rows, BLOCK), shaped(give_rows, BLOCK)]
        + [shaped(2 * rows, BLOCK)] * 3
        + [jax.ShapeDtypeStruct(a.shape, a.dtype) for a in arguments],
        in_specs=[pl.BlockSpec(memory_space=pltpu.HBM)] * (2 + count),
        out_specs=[VMEM] * (5 + count),
        scratch_shapes=[
            pltpu.SMEM(send_blocks.shape, jnp.int32),
            pltpu.VMEM(old_rows.shape, jnp.float32),
            pltpu.SemaphoreType.DMA((2 + count,)),
        ],
        compiler_params=params(),
    )(*(pltpu.with_memory_space_constraint(a, pltpu.HBM) for a in (send_blocks, old_rows, *arguments)))
    node_slots, node_weights, mask_rows, halos, elem_nodes, grad_rows, volume = held
    layers = both_ways([(0, 1)])
    got_first = lax.ppermute(give_first, "layer", layers)
    got = lax.ppermute(give, "layer", layers)
    full = [jnp.concatenate([first, got_first]), jnp.concatenate([second, got[: 2 * rows]])]
    first, second = [
        lax.ppermute(part, ("mapx", "layer"), pairs).reshape(4, rows, BLOCK)
        for part, pairs in zip(full, column_moves(sizes[0]))
    ]
    other_slots, other_weights = got[2 * rows : 2 * rows + slot_rows], got[2 * rows + slot_rows :]

    all_rows = elem_nodes.size // BLOCK
    halo_count = halos.size // BLOCK
    hot_steps = next(n for n in (8, 4, 2, 1) if all_rows % n == 0)
    whole = lambda *shape: jax.ShapeDtypeStruct(shape, jnp.int32)
    found, slots_cut, weights_cut, halos_cut, nodes_cut, volume_cut, halo_hot, node_hot = pl.pallas_call(
        own_kernel,
        out_shape=(
            shaped(2, FIELDS, slot_rows, BLOCK),
            whole(2, slot_rows, BLOCK),
            shaped(slot_rows, BLOCK),
            whole(halo_count, BLOCK),
            whole(all_rows, BLOCK),
            shaped(all_rows // 4, BLOCK),
            jax.ShapeDtypeStruct((halo_count * BLOCK, BLOCK), jnp.bfloat16),
            jax.ShapeDtypeStruct((hot_steps, all_rows // hot_steps * BLOCK, BLOCK), jnp.bfloat16),
        ),
        in_specs=[VMEM] * 7,
        out_specs=(VMEM,) * 8,
        compiler_params=params(),
    )(own.reshape(2, rows, BLOCK), other_slots, node_slots, node_weights, halos, elem_nodes, volume)
    found = pl.pallas_call(
        early_kernel,
        out_shape=shaped(2, FIELDS, slot_rows, BLOCK),
        in_specs=[VMEM] * 3,
        out_specs=VMEM,
        compiler_params=params(),
    )(first, slots_cut, found)
    state_rows = FIELDS * owned // BLOCK
    mine, other = pl.pallas_call(
        functools.partial(late_kernel, owned // BLOCK),
        out_shape=(shaped(state_rows, BLOCK),) * 2,
        in_specs=[VMEM] * 5,
        out_specs=(VMEM,) * 2,
        compiler_params=params(),
    )(second, slots_cut, found, weights_cut, other_weights)
    other = lax.ppermute(other, "layer", layers)
    moves = 3 + sum(size > 2 for size in sizes)
    chunk = (2 * FIELDS, BLOCK)
    new_state, table, *ghosts = pl.pallas_call(
        functools.partial(state_kernel, sizes),
        out_shape=(shaped(state_rows, BLOCK), shaped(owned // (2 * BLOCK), *chunk)) + (shaped(*chunk),) * moves,
        in_specs=[VMEM] * 4,
        out_specs=(VMEM,) * (2 + moves),
        scratch_shapes=[pltpu.VMEM((6, *chunk), jnp.float32)],
        compiler_params=params(),
    )(mine, other, mask_rows, halos_cut)
    ghosts = swap_all(ghosts, sizes)

    slots_all = table.shape[0] + 6
    own, *sums = pl.pallas_call(
        functools.partial(element_kernel, sizes, moves),
        out_shape=(shaped(4 * owned // BLOCK, BLOCK),) + (shaped(8, BLOCK),) * moves,
        in_specs=[VMEM] * (5 + moves),
        out_specs=(VMEM,) * (1 + moves),
        scratch_shapes=[
            pltpu.VMEM((slots_all, *chunk), jnp.float32),
            pltpu.VMEM((FIELDS, all_rows, BLOCK), jnp.float32),
            pltpu.VMEM((4 * SPLITS, all_rows, BLOCK), jnp.float32),
            pltpu.VMEM((6, 8, BLOCK), jnp.float32),
        ],
        compiler_params=params(),
    )(table, nodes_cut, node_hot, grad_rows, volume_cut, *ghosts)
    sums = swap_all(sums, sizes)
    residual = pl.pallas_call(
        functools.partial(residual_kernel, sizes, moves),
        out_shape=shaped(4, owned),
        in_specs=[VMEM] * (3 + moves),
        out_specs=VMEM,
        scratch_shapes=[pltpu.VMEM((6, 8, BLOCK), jnp.float32)],
        compiler_params=params(),
    )(own, halos_cut, halo_hot, *sums)
    return (new_state.reshape(1, 1, 1, FIELDS, owned), residual[None, None, None])


def solution(mesh):
    sizes = tuple(mesh.shape[axis] for axis in AXES)
    row = P("mapx", "mapy", "layer", None)
    table = P("mapx", "mapy", "layer", None, None)
    return jax.shard_map(
        functools.partial(per_device, sizes),
        mesh=mesh,
        in_specs=(table, table, table, table, row, table, table, table, row),
        out_specs=(table, table),
        check_vma=False,
    )
```

```python
import functools

import jax
import jax.numpy as jnp
from jax import lax
from jax.experimental import pallas as pl
from jax.experimental.pallas import tpu as pltpu
from jax.sharding import PartitionSpec as P

BLOCK = 128
REACH = 2
FIELDS = 6
SPLITS = 3

ocean_temp = 0.0
strain_reg = 0.01
gravity = 0.5

AXES = ("mapx", "mapy", "layer")
VMEM = pl.BlockSpec(memory_space=pltpu.VMEM)
SMEM = pl.BlockSpec(memory_space=pltpu.SMEM)


def params():
    return pltpu.CompilerParams(vmem_limit_bytes=32 * 1024 * 1024)


def both_ways(pairs):
    return [way for one, other in pairs for way in ((one, other), (other, one))]


def column_moves(count):
    outside = [(at, at + 1) for at in range(1, count - 1, 2)]
    inside = [(at, at + 1) for at in range(0, count - 1, 2)]
    within = [(at + i, at + i + 2) for at in range(0, count - 3, 4) for i in range(2)]
    across = [(at + i, at + i + 2) for at in range(2, count - 3, 4) for i in range(2)]
    number = lambda pairs, layer: [(one * 2 + layer, other * 2 + layer) for one, other in pairs]
    return [
        both_ways(number(outside, 0) + number(inside, 1)),
        both_ways(number(within, 0) + number(across, 1)),
    ]


def column_offsets(layer):
    at = lax.axis_index("mapx")
    near = jnp.where(lax.rem(at, 2) == 0, 1, -1)
    two = jnp.where(lax.rem(at, 4) < 2, 2, -2)
    return [jnp.where(layer == 0, -near, near), jnp.where(layer == 0, two, -two)]


def pair_swap(value, axis, count, first):
    return lax.ppermute(value, axis, both_ways([(at, at + 1) for at in range(first, count - 1, 2)]))


def swap_all(values, sizes):
    long = [axis for axis in range(3) if sizes[axis] > 2]
    steps = [(axis, 1) for axis in long] + [(axis, 0) for axis in range(3)]
    return [pair_swap(value, AXES[axis], sizes[axis], first) for value, (axis, first) in zip(values, steps)]


def pack_kernel(count, *refs):
    blocks_in_ref, old_in_ref = refs[:2]
    give_first_ref, give_ref, first_ref, second_ref, own_ref = refs[2 + count : 7 + count]
    held = refs[7 + count : 7 + 2 * count]
    blocks_ref, old_ref, sems = refs[7 + 2 * count :]
    first = [pltpu.make_async_copy(blocks_in_ref, blocks_ref, sems.at[0])]
    first += [pltpu.make_async_copy(old_in_ref, old_ref, sems.at[1])]
    rest = [pltpu.make_async_copy(refs[2 + i], held[i], sems.at[2 + i]) for i in range(count)]
    for copy in first + rest:
        copy.start()
    for copy in first:
        copy.wait()
    slots = blocks_ref.shape[2]
    stride = old_ref.shape[0] // FIELDS
    layer = lax.axis_index("layer")
    mine, other = column_offsets(layer), column_offsets(1 - layer)
    size = FIELDS * slots
    for ref, offset in (
        (give_first_ref, other[0]),
        (give_ref, other[1]),
        (first_ref, mine[0]),
        (second_ref, mine[1]),
        (own_ref, 0),
    ):
        for to_layer in range(2):
            peer = (offset + REACH) * 2 + to_layer
            start = to_layer * size
            for c in range(slots):
                rows = pl.ds(blocks_ref[peer, 0, c], FIELDS, stride=stride)
                ref[start + FIELDS * c : start + FIELDS * (c + 1), :] = old_ref[rows, :]
    for copy in rest:
        copy.wait()
    slots_ref, weights_ref = held[0], held[1]
    slot_rows = slots_ref.shape[0] * slots_ref.shape[1] // BLOCK
    cut_rows(slots_ref, give_ref.at[2 * size : 2 * size + slot_rows])
    cut_rows(weights_ref, give_ref.at[2 * size + slot_rows : 2 * size + 2 * slot_rows])


def pick(row, lanes):
    return jnp.take_along_axis(jnp.broadcast_to(row, lanes.shape), lanes, axis=1)


def pick_fields(table_ref, block_count, blocks, lanes):
    found = [jnp.zeros((8, BLOCK), jnp.float32) for _ in range(FIELDS)]
    for b in range(block_count):
        hit = blocks == b
        for f in range(FIELDS):
            row = table_ref[b // 2, 2 * f + b % 2 : 2 * f + b % 2 + 1, :]
            found[f] = jnp.where(hit, pick(row, lanes), found[f])
    return found


def add_blocks(ref, chunk, first_block, blocks, lanes, found):
    local = blocks - first_block
    found = list(found)
    for c in range(ref.shape[1] // FIELDS):
        hit = local == c
        for f in range(FIELDS):
            row = ref[chunk, FIELDS * c + f : FIELDS * c + f + 1, :]
            found[f] = jnp.where(hit, pick(row, lanes), found[f])
    return tuple(found)


def add_chunks(ref, numbers, offset, ids, found):
    blocks, lanes = ids >> 7, ids & (BLOCK - 1)
    for chunk, layer in numbers:
        first = ((offset + REACH) * 2 + layer) * (ref.shape[1] // FIELDS)
        found = add_blocks(ref, chunk, first, blocks, lanes, found)
    return found


def load_fields(found_ref, owner, v):
    return tuple(found_ref[owner, f, 8 * v : 8 * v + 8, :] for f in range(FIELDS))


def save_fields(found_ref, owner, v, found):
    for f in range(FIELDS):
        found_ref[owner, f, 8 * v : 8 * v + 8, :] = found[f]


def arrived_chunks(ref, move, ids, found, owner):
    layer = lax.axis_index("layer")
    to_layer = 1 - layer if owner else layer
    numbers = [(to_layer, layer), (2 + to_layer, 1 - layer)]
    return add_chunks(ref, numbers, column_offsets(layer)[move], ids, found)


def cut_rows(from_ref, to_ref):
    count = from_ref.shape[1] // BLOCK
    for r in range(from_ref.shape[0]):
        for i in range(count):
            to_ref[r * count + i : r * count + i + 1, :] = from_ref[
                r : r + 1, i * BLOCK : (i + 1) * BLOCK
            ].astype(to_ref.dtype)


def lane_one_hot(ids):
    rows = lax.broadcasted_iota(jnp.int32, (BLOCK, BLOCK), 0)
    hit = rows == jnp.broadcast_to(ids & (BLOCK - 1), rows.shape)
    return jnp.where(hit, 1.0, 0.0).T.astype(jnp.bfloat16)


def own_kernel(
    own_ref,
    other_slots_ref,
    slots_in_ref,
    weights_in_ref,
    halos_in_ref,
    nodes_in_ref,
    volume_in_ref,
    found_ref,
    slots_ref,
    weights_ref,
    halos_ref,
    nodes_ref,
    volume_ref,
    halo_hot_ref,
    node_hot_ref,
):
    for k in range(halos_in_ref.shape[0]):
        cut_rows(halos_in_ref.at[k], halos_ref.at[2 * k : 2 * k + 2])
    cut_rows(slots_in_ref, slots_ref.at[0])
    slots_ref[1] = other_slots_ref[...].astype(jnp.int32)
    cut_rows(weights_in_ref, weights_ref)
    cut_rows(nodes_in_ref, nodes_ref)
    cut_rows(volume_in_ref, volume_ref)
    layer = lax.axis_index("layer")
    for owner in range(2):
        for v in range(slots_ref.shape[1] // 8):
            ids = slots_ref[owner, 8 * v : 8 * v + 8, :]
            found = tuple(jnp.zeros((8, BLOCK), jnp.float32) for _ in range(FIELDS))
            numbers = [(1 - layer if owner else layer, layer)]
            save_fields(found_ref, owner, v, add_chunks(own_ref, numbers, 0, ids, found))
    for r in range(halos_ref.shape[0]):
        halo_hot_ref[r * BLOCK : (r + 1) * BLOCK, :] = lane_one_hot(halos_ref[r : r + 1, :])
    steps, width, _ = node_hot_ref.shape
    group = width // BLOCK

    def hot(step, carry):
        for r in range(group):
            ids = nodes_ref[pl.ds(step * group + r, 1), :]
            node_hot_ref[step, r * BLOCK : (r + 1) * BLOCK, :] = lane_one_hot(ids)
        return carry

    lax.fori_loop(0, steps, hot, 0)


def early_kernel(came_ref, slots_ref, found_in_ref, found_ref):
    for owner in range(2):
        for v in range(slots_ref.shape[1] // 8):
            ids = slots_ref[owner, 8 * v : 8 * v + 8, :]
            found = arrived_chunks(came_ref, 0, ids, load_fields(found_in_ref, owner, v), owner)
            save_fields(found_ref, owner, v, found)


def late_kernel(rows, came_ref, slots_ref, found_ref, weights_ref, other_weights_ref, mine_ref, other_ref):
    for owner, out_ref, weight_ref in ((1, other_ref, other_weights_ref), (0, mine_ref, weights_ref)):
        totals = [jnp.zeros((rows, BLOCK), jnp.float32) for _ in range(FIELDS)]
        for v in range(slots_ref.shape[1] // 8):
            ids = slots_ref[owner, 8 * v : 8 * v + 8, :]
            found = arrived_chunks(came_ref, 1, ids, load_fields(found_ref, owner, v), owner)
            for f in range(FIELDS):
                term = found[f] * weight_ref[8 * v : 8 * v + 8, :]
                for k in range(8 // rows):
                    totals[f] = totals[f] + term[k * rows : (k + 1) * rows, :]
        for f in range(FIELDS):
            out_ref[f * rows : (f + 1) * rows, :] = totals[f]


def state_kernel(counts, mine_ref, came_ref, mask_ref, halos_ref, state_ref, table_ref, *more_refs):
    send_refs, cut_ref = more_refs[:-1], more_refs[-1]
    front = mask_ref[...] == 1
    rows = mask_ref.shape[0]
    for f in range(FIELDS):
        at = slice(f * rows, (f + 1) * rows)
        total = mine_ref[at, :] + came_ref[at, :]
        if f == 4:
            total = jnp.where(front, ocean_temp, total)
        state_ref[f * rows : (f + 1) * rows, :] = total
        for s in range(rows // 2):
            table_ref[s, 2 * f : 2 * f + 2, :] = total[2 * s : 2 * s + 2, :]
    starts = (0, halos_ref.shape[0] - 8)
    halo = [halos_ref[first : first + 8, :] for first in starts]
    halo_blocks = [i >> 7 for i in halo]
    halo_lanes = [i & (BLOCK - 1) for i in halo]
    for v in range(2):
        cut = pick_fields(table_ref, rows, halo_blocks[v], halo_lanes[v])
        for k in range(6):
            r = 2 * k - starts[v]
            if 0 <= r <= 6:
                for f in range(FIELDS):
                    cut_ref[k, 2 * f : 2 * f + 2, :] = cut[f][r : r + 2, :]
    send_pairs(counts, cut_ref, send_refs, [(0, 1), (2, 3), (4, 5)])


def pair_places():
    return [lax.rem(lax.axis_index(axis), 2) for axis in AXES]


def send_pairs(counts, cut_ref, send_refs, order):
    places = pair_places()
    long = [axis for axis in range(3) if counts[axis] > 2]
    for axis in range(3):
        even, odd = order[axis]
        send_refs[len(long) + axis][...] = cut_ref[jnp.where(places[axis] == 0, even, odd)]
        if axis in long:
            send_refs[long.index(axis)][...] = cut_ref[jnp.where(places[axis] == 0, odd, even)]


def arrivals(counts, came_refs):
    places = pair_places()
    long = [axis for axis in range(3) if counts[axis] > 2]
    result = []
    for axis in range(3):
        inside = came_refs[len(long) + axis][...]
        at = lax.axis_index(AXES[axis])
        edge = jnp.where(places[axis] == 0, at == 0, at == counts[axis] - 1)
        outside = jnp.zeros_like(inside)
        if axis in long:
            outside = jnp.where(edge, 0.0, came_refs[long.index(axis)][...])
        result.append((places[axis], inside, outside))
    return result


def placed(values, ids, block_count):
    rows = lax.broadcasted_iota(jnp.int32, (block_count, BLOCK), 0)
    hit = rows == jnp.broadcast_to(ids >> 7, rows.shape)
    left = [jnp.where(hit, jnp.broadcast_to(v, rows.shape), 0.0) for v in values]
    return jnp.concatenate(left, axis=0).astype(jnp.bfloat16)


def cut_parts(value):
    parts = []
    for _ in range(SPLITS - 1):
        part = value.astype(jnp.bfloat16).astype(jnp.float32)
        parts.append(part)
        value = value - part
    return parts + [value]


def hot_dot(left, right):
    return jnp.dot(left, right, preferred_element_type=jnp.float32)


def element_kernel(counts, moves, *refs):
    table_in_ref, nodes_ref, node_hot_ref, grads_ref, volume_ref = refs[:5]
    came_refs = refs[5 : 5 + moves]
    own_ref = refs[5 + moves]
    send_refs = refs[6 + moves : 6 + 2 * moves]
    table_ref, values_ref, parts_ref, cut_ref = refs[6 + 2 * moves :]
    owned_slots = table_in_ref.shape[0]
    table_ref[0:owned_slots] = table_in_ref[...]
    for axis, (place_at, inside, outside) in enumerate(arrivals(counts, came_refs)):
        table_ref[owned_slots + 2 * axis + 1 - place_at] = inside
        table_ref[owned_slots + 2 * axis + place_at] = outside
    block_count = 2 * table_ref.shape[0]
    all_rows = nodes_ref.shape[0]
    elem_rows = all_rows // 4
    for first in range(0, all_rows, 8):
        ids = nodes_ref[first : first + 8, :]
        found = pick_fields(table_ref, block_count, ids >> 7, ids & (BLOCK - 1))
        for f in range(FIELDS):
            values_ref[f, first : first + 8, :] = found[f]
    for first in [*range(0, elem_rows - 7, 8)] + ([elem_rows - 8] if elem_rows % 8 else []):
        at = [slice(r * elem_rows + first, r * elem_rows + first + 8) for r in range(12)]
        values = [[values_ref[f, at[a], :] for f in range(FIELDS)] for a in range(4)]
        grads = [[grads_ref[at[3 * a + j], :] for j in range(3)] for a in range(4)]
        volume = volume_ref[at[0], :]
        velgrad = [[sum(values[a][i] * grads[a][j] for a in range(4)) for j in range(3)] for i in range(3)]
        strain = [[0.5 * (velgrad[i][j] + velgrad[j][i]) if i <= j else None for j in range(3)] for i in range(3)]
        diagonal = sum(strain[i][i] * strain[i][i] for i in range(3))
        corner = sum(strain[i][j] * strain[i][j] for i, j in ((0, 1), (0, 2), (1, 2)))
        second = 0.5 * diagonal + corner
        pressure, temper, damage = [0.25 * (values[0][f] + values[1][f] + values[2][f] + values[3][f]) for f in (3, 4, 5)]
        root = jnp.exp(jnp.log(second + strain_reg) * (-1.0 / 3.0))
        twice = (1.0 - damage) * jnp.exp(-temper) * root
        stress = [[None] * 3 for _ in range(3)]
        for i in range(3):
            for j in range(i, 3):
                stress[i][j] = twice * strain[i][j] - (pressure if i == j else 0.0)
                stress[j][i] = stress[i][j]
        lift = (0.25 * gravity) * volume
        flow = 0.25 * volume * (velgrad[0][0] + velgrad[1][1] + velgrad[2][2])
        for s, part in enumerate(cut_parts(flow)):
            for a in range(4):
                parts_ref[3 * SPLITS + s, at[a], :] = part
        for a in range(4):
            for i in range(3):
                force = volume * sum(stress[i][j] * grads[a][j] for j in range(3))
                if i == 2:
                    force = force + lift
                for s, part in enumerate(cut_parts(force)):
                    parts_ref[i * SPLITS + s, at[a], :] = part

    group = node_hot_ref.shape[1] // BLOCK

    width = 4 * block_count
    total = jnp.zeros((SPLITS * width, BLOCK), jnp.float32)
    for step in range(all_rows // group):
        lefts = []
        for r in range(step * group, (step + 1) * group):
            terms = [parts_ref[c * SPLITS + s, r : r + 1, :] for s in range(SPLITS) for c in range(4)]
            lefts.append(placed(terms, nodes_ref[r : r + 1, :], block_count))
        total = total + hot_dot(jnp.concatenate(lefts, axis=1), node_hot_ref[step])
    total = sum(total[s * width : (s + 1) * width, :] for s in range(SPLITS))
    owned = 2 * owned_slots
    for c in range(4):
        own_ref[c * owned : (c + 1) * owned, :] = total[c * block_count : c * block_count + owned, :]
        for k in range(6):
            first = c * block_count + owned + 2 * k
            cut_ref[k, 2 * c : 2 * c + 2, :] = total[first : first + 2, :]
    send_pairs(counts, cut_ref, send_refs, [(1, 0), (3, 2), (5, 4)])


def residual_kernel(counts, moves, *refs):
    own_ref, halos_ref, halo_hot_ref = refs[:3]
    out_ref, came_ref = refs[3 + moves :]
    for axis, (place_at, inside, outside) in enumerate(arrivals(counts, refs[3 : 3 + moves])):
        came_ref[2 * axis + place_at] = inside
        came_ref[2 * axis + 1 - place_at] = outside
    owned = own_ref.shape[0] // 4
    lefts = []
    for k in range(6):
        parts = cut_parts(came_ref[k])
        for h in range(2):
            ids = halos_ref[2 * k + h : 2 * k + h + 1, :]
            terms = [parts[s][2 * c + h : 2 * c + h + 1, :] for s in range(SPLITS) for c in range(4)]
            lefts.append(placed(terms, ids, owned))
    total = hot_dot(jnp.concatenate(lefts, axis=1), halo_hot_ref[...])
    width = 4 * owned
    total = sum(total[s * width : (s + 1) * width, :] for s in range(SPLITS)) + own_ref[...]
    for c in range(4):
        for b in range(owned):
            r = c * owned + b
            out_ref[c : c + 1, b * BLOCK : (b + 1) * BLOCK] = total[r : r + 1, :]


def shaped(*shape):
    return jax.ShapeDtypeStruct(shape, jnp.float32)


def per_device(
    sizes,
    old_state,
    send_blocks,
    node_slots,
    node_weights,
    front_mask,
    halo_lists,
    elem_nodes,
    shape_grads,
    elem_volume,
):
    old_state, send_blocks = old_state[0, 0, 0], send_blocks[0, 0, 0]
    slots = send_blocks.shape[1]
    send_blocks = send_blocks.reshape(-1, 1, slots)
    rows = FIELDS * slots
    arguments = [
        node_slots[0, 0, 0],
        node_weights[0, 0, 0],
        front_mask.reshape(-1, BLOCK),
        halo_lists.reshape(halo_lists.shape[-2], 1, -1),
        elem_nodes[0, 0, 0],
        shape_grads.reshape(-1, BLOCK),
        elem_volume[0, 0],
    ]
    old_rows = old_state.reshape(-1, BLOCK)
    count = len(arguments)
    owned = node_slots.shape[-1]
    slot_rows = node_slots.size // BLOCK
    give_rows = 2 * rows + 2 * slot_rows
    give_first, give, first, second, own, *held = pl.pallas_call(
        functools.partial(pack_kernel, count),
        out_shape=[shaped(2 * rows, BLOCK), shaped(give_rows, BLOCK)]
        + [shaped(2 * rows, BLOCK)] * 3
        + [jax.ShapeDtypeStruct(a.shape, a.dtype) for a in arguments],
        in_specs=[pl.BlockSpec(memory_space=pltpu.HBM)] * (2 + count),
        out_specs=[VMEM] * (5 + count),
        scratch_shapes=[
            pltpu.SMEM(send_blocks.shape, jnp.int32),
            pltpu.VMEM(old_rows.shape, jnp.float32),
            pltpu.SemaphoreType.DMA((2 + count,)),
        ],
        compiler_params=params(),
    )(*(pltpu.with_memory_space_constraint(a, pltpu.HBM) for a in (send_blocks, old_rows, *arguments)))
    node_slots, node_weights, mask_rows, halos, elem_nodes, grad_rows, volume = held
    layers = both_ways([(0, 1)])
    got_first = lax.ppermute(give_first, "layer", layers)
    got = lax.ppermute(give, "layer", layers)
    full = [jnp.concatenate([first, got_first]), jnp.concatenate([second, got[: 2 * rows]])]
    first, second = [
        lax.ppermute(part, ("mapx", "layer"), pairs).reshape(4, rows, BLOCK)
        for part, pairs in zip(full, column_moves(sizes[0]))
    ]
    other_slots, other_weights = got[2 * rows : 2 * rows + slot_rows], got[2 * rows + slot_rows :]

    all_rows = elem_nodes.size // BLOCK
    halo_count = halos.size // BLOCK
    hot_steps = next(n for n in (8, 4, 2, 1) if all_rows % n == 0)
    whole = lambda *shape: jax.ShapeDtypeStruct(shape, jnp.int32)
    found, slots_cut, weights_cut, halos_cut, nodes_cut, volume_cut, halo_hot, node_hot = pl.pallas_call(
        own_kernel,
        out_shape=(
            shaped(2, FIELDS, slot_rows, BLOCK),
            whole(2, slot_rows, BLOCK),
            shaped(slot_rows, BLOCK),
            whole(halo_count, BLOCK),
            whole(all_rows, BLOCK),
            shaped(all_rows // 4, BLOCK),
            jax.ShapeDtypeStruct((halo_count * BLOCK, BLOCK), jnp.bfloat16),
            jax.ShapeDtypeStruct((hot_steps, all_rows // hot_steps * BLOCK, BLOCK), jnp.bfloat16),
        ),
        in_specs=[VMEM] * 7,
        out_specs=(VMEM,) * 8,
        compiler_params=params(),
    )(own.reshape(2, rows, BLOCK), other_slots, node_slots, node_weights, halos, elem_nodes, volume)
    found = pl.pallas_call(
        early_kernel,
        out_shape=shaped(2, FIELDS, slot_rows, BLOCK),
        in_specs=[VMEM] * 3,
        out_specs=VMEM,
        compiler_params=params(),
    )(first, slots_cut, found)
    state_rows = FIELDS * owned // BLOCK
    mine, other = pl.pallas_call(
        functools.partial(late_kernel, owned // BLOCK),
        out_shape=(shaped(state_rows, BLOCK),) * 2,
        in_specs=[VMEM] * 5,
        out_specs=(VMEM,) * 2,
        compiler_params=params(),
    )(second, slots_cut, found, weights_cut, other_weights)
    other = lax.ppermute(other, "layer", layers)
    moves = 3 + sum(size > 2 for size in sizes)
    chunk = (2 * FIELDS, BLOCK)
    new_state, table, *ghosts = pl.pallas_call(
        functools.partial(state_kernel, sizes),
        out_shape=(shaped(state_rows, BLOCK), shaped(owned // (2 * BLOCK), *chunk)) + (shaped(*chunk),) * moves,
        in_specs=[VMEM] * 4,
        out_specs=(VMEM,) * (2 + moves),
        scratch_shapes=[pltpu.VMEM((6, *chunk), jnp.float32)],
        compiler_params=params(),
    )(mine, other, mask_rows, halos_cut)
    ghosts = swap_all(ghosts, sizes)

    slots_all = table.shape[0] + 6
    own, *sums = pl.pallas_call(
        functools.partial(element_kernel, sizes, moves),
        out_shape=(shaped(4 * owned // BLOCK, BLOCK),) + (shaped(8, BLOCK),) * moves,
        in_specs=[VMEM] * (5 + moves),
        out_specs=(VMEM,) * (1 + moves),
        scratch_shapes=[
            pltpu.VMEM((slots_all, *chunk), jnp.float32),
            pltpu.VMEM((FIELDS, all_rows, BLOCK), jnp.float32),
            pltpu.VMEM((4 * SPLITS, all_rows, BLOCK), jnp.float32),
            pltpu.VMEM((6, 8, BLOCK), jnp.float32),
        ],
        compiler_params=params(),
    )(table, nodes_cut, node_hot, grad_rows, volume_cut, *ghosts)
    sums = swap_all(sums, sizes)
    residual = pl.pallas_call(
        functools.partial(residual_kernel, sizes, moves),
        out_shape=shaped(4, owned),
        in_specs=[VMEM] * (3 + moves),
        out_specs=VMEM,
        scratch_shapes=[pltpu.VMEM((6, 8, BLOCK), jnp.float32)],
        compiler_params=params(),
    )(own, halos_cut, halo_hot, *sums)
    return (new_state.reshape(1, 1, 1, FIELDS, owned), residual[None, None, None])


def solution(mesh):
    sizes = tuple(mesh.shape[axis] for axis in AXES)
    row = P("mapx", "mapy", "layer", None)
    table = P("mapx", "mapy", "layer", None, None)
    return jax.shard_map(
        functools.partial(per_device, sizes),
        mesh=mesh,
        in_specs=(table, table, table, table, row, table, table, table, row),
        out_specs=(table, table),
        check_vma=False,
    )
```

```python
import functools

import jax
import jax.numpy as jnp
from jax import lax
from jax.experimental import pallas as pl
from jax.experimental.pallas import tpu as pltpu
from jax.sharding import PartitionSpec as P

BLOCK = 128
REACH = 2
FIELDS = 6
SPLITS = 3

ocean_temp = 0.0
strain_reg = 0.01
gravity = 0.5

AXES = ("mapx", "mapy", "layer")
VMEM = pl.BlockSpec(memory_space=pltpu.VMEM)
SMEM = pl.BlockSpec(memory_space=pltpu.SMEM)


def params():
    return pltpu.CompilerParams(vmem_limit_bytes=32 * 1024 * 1024)


def both_ways(pairs):
    return [way for one, other in pairs for way in ((one, other), (other, one))]


def column_moves(count):
    outside = [(at, at + 1) for at in range(1, count - 1, 2)]
    inside = [(at, at + 1) for at in range(0, count - 1, 2)]
    within = [(at + i, at + i + 2) for at in range(0, count - 3, 4) for i in range(2)]
    across = [(at + i, at + i + 2) for at in range(2, count - 3, 4) for i in range(2)]
    number = lambda pairs, layer: [(one * 2 + layer, other * 2 + layer) for one, other in pairs]
    return [
        both_ways(number(outside, 1) + number(inside, 0)),
        both_ways(number(within, 0) + number(across, 1)),
    ]


def column_offsets(layer):
    at = lax.axis_index("mapx")
    near = jnp.where(lax.rem(at, 2) == 0, 1, -1)
    two = jnp.where(lax.rem(at, 4) < 2, 2, -2)
    return [jnp.where(layer == 0, near, -near), jnp.where(layer == 0, two, -two)]


def pair_swap(value, axis, count, first):
    return lax.ppermute(value, axis, both_ways([(at, at + 1) for at in range(first, count - 1, 2)]))


def swap_all(values, sizes):
    long = [axis for axis in range(3) if sizes[axis] > 2]
    steps = [(axis, 1) for axis in long] + [(axis, 0) for axis in range(3)]
    return [pair_swap(value, AXES[axis], sizes[axis], first) for value, (axis, first) in zip(values, steps)]


def pack_kernel(count, *refs):
    blocks_in_ref, old_in_ref = refs[:2]
    give_first_ref, give_ref, first_ref, second_ref, own_ref = refs[2 + count : 7 + count]
    held = refs[7 + count : 7 + 2 * count]
    blocks_ref, old_ref, sems = refs[7 + 2 * count :]
    first = [pltpu.make_async_copy(blocks_in_ref, blocks_ref, sems.at[0])]
    first += [pltpu.make_async_copy(old_in_ref, old_ref, sems.at[1])]
    rest = [pltpu.make_async_copy(refs[2 + i], held[i], sems.at[2 + i]) for i in range(count)]
    for copy in first + rest:
        copy.start()
    for copy in first:
        copy.wait()
    slots = blocks_ref.shape[2]
    stride = old_ref.shape[0] // FIELDS
    layer = lax.axis_index("layer")
    mine, other = column_offsets(layer), column_offsets(1 - layer)
    size = FIELDS * slots
    for ref, offset in (
        (give_first_ref, other[0]),
        (give_ref, other[1]),
        (first_ref, mine[0]),
        (second_ref, mine[1]),
        (own_ref, 0),
    ):
        for to_layer in range(2):
            peer = (offset + REACH) * 2 + to_layer
            start = to_layer * size
            for c in range(slots):
                rows = pl.ds(blocks_ref[peer, 0, c], FIELDS, stride=stride)
                ref[start + FIELDS * c : start + FIELDS * (c + 1), :] = old_ref[rows, :]
    for copy in rest:
        copy.wait()
    slots_ref, weights_ref = held[0], held[1]
    slot_rows = slots_ref.shape[0] * slots_ref.shape[1] // BLOCK
    cut_rows(slots_ref, give_ref.at[2 * size : 2 * size + slot_rows])
    cut_rows(weights_ref, give_ref.at[2 * size + slot_rows : 2 * size + 2 * slot_rows])


def pick(row, lanes):
    return jnp.take_along_axis(jnp.broadcast_to(row, lanes.shape), lanes, axis=1)


def pick_fields(table_ref, block_count, blocks, lanes):
    found = [jnp.zeros((8, BLOCK), jnp.float32) for _ in range(FIELDS)]
    for b in range(block_count):
        hit = blocks == b
        for f in range(FIELDS):
            row = table_ref[b // 2, 2 * f + b % 2 : 2 * f + b % 2 + 1, :]
            found[f] = jnp.where(hit, pick(row, lanes), found[f])
    return found


def add_blocks(ref, chunk, first_block, blocks, lanes, found):
    local = blocks - first_block
    found = list(found)
    for c in range(ref.shape[1] // FIELDS):
        hit = local == c
        for f in range(FIELDS):
            row = ref[chunk, FIELDS * c + f : FIELDS * c + f + 1, :]
            found[f] = jnp.where(hit, pick(row, lanes), found[f])
    return tuple(found)


def add_chunks(ref, numbers, offset, ids, found):
    blocks, lanes = ids >> 7, ids & (BLOCK - 1)
    for chunk, layer in numbers:
        first = ((offset + REACH) * 2 + layer) * (ref.shape[1] // FIELDS)
        found = add_blocks(ref, chunk, first, blocks, lanes, found)
    return found


def load_fields(found_ref, owner, v):
    return tuple(found_ref[owner, f, 8 * v : 8 * v + 8, :] for f in range(FIELDS))


def save_fields(found_ref, owner, v, found):
    for f in range(FIELDS):
        found_ref[owner, f, 8 * v : 8 * v + 8, :] = found[f]


def arrived_chunks(ref, move, ids, found, owner):
    layer = lax.axis_index("layer")
    to_layer = 1 - layer if owner else layer
    numbers = [(to_layer, layer), (2 + to_layer, 1 - layer)]
    return add_chunks(ref, numbers, column_offsets(layer)[move], ids, found)


def cut_rows(from_ref, to_ref):
    count = from_ref.shape[1] // BLOCK
    for r in range(from_ref.shape[0]):
        for i in range(count):
            to_ref[r * count + i : r * count + i + 1, :] = from_ref[
                r : r + 1, i * BLOCK : (i + 1) * BLOCK
            ].astype(to_ref.dtype)


def lane_one_hot(ids):
    rows = lax.broadcasted_iota(jnp.int32, (BLOCK, BLOCK), 0)
    hit = rows == jnp.broadcast_to(ids & (BLOCK - 1), rows.shape)
    return jnp.where(hit, 1.0, 0.0).T.astype(jnp.bfloat16)


def own_kernel(
    own_ref,
    other_slots_ref,
    slots_in_ref,
    weights_in_ref,
    halos_in_ref,
    nodes_in_ref,
    volume_in_ref,
    found_ref,
    slots_ref,
    weights_ref,
    halos_ref,
    nodes_ref,
    volume_ref,
    halo_hot_ref,
    node_hot_ref,
):
    for k in range(halos_in_ref.shape[0]):
        cut_rows(halos_in_ref.at[k], halos_ref.at[2 * k : 2 * k + 2])
    cut_rows(slots_in_ref, slots_ref.at[0])
    slots_ref[1] = other_slots_ref[...].astype(jnp.int32)
    cut_rows(weights_in_ref, weights_ref)
    cut_rows(nodes_in_ref, nodes_ref)
    cut_rows(volume_in_ref, volume_ref)
    layer = lax.axis_index("layer")
    for owner in range(2):
        for v in range(slots_ref.shape[1] // 8):
            ids = slots_ref[owner, 8 * v : 8 * v + 8, :]
            found = tuple(jnp.zeros((8, BLOCK), jnp.float32) for _ in range(FIELDS))
            numbers = [(1 - layer if owner else layer, layer)]
            save_fields(found_ref, owner, v, add_chunks(own_ref, numbers, 0, ids, found))
    for r in range(halos_ref.shape[0]):
        halo_hot_ref[r * BLOCK : (r + 1) * BLOCK, :] = lane_one_hot(halos_ref[r : r + 1, :])
    steps, width, _ = node_hot_ref.shape
    group = width // BLOCK

    def hot(step, carry):
        for r in range(group):
            ids = nodes_ref[pl.ds(step * group + r, 1), :]
            node_hot_ref[step, r * BLOCK : (r + 1) * BLOCK, :] = lane_one_hot(ids)
        return carry

    lax.fori_loop(0, steps, hot, 0)


def early_kernel(came_ref, slots_ref, found_in_ref, found_ref):
    for owner in range(2):
        for v in range(slots_ref.shape[1] // 8):
            ids = slots_ref[owner, 8 * v : 8 * v + 8, :]
            found = arrived_chunks(came_ref, 0, ids, load_fields(found_in_ref, owner, v), owner)
            save_fields(found_ref, owner, v, found)


def late_kernel(rows, came_ref, slots_ref, found_ref, weights_ref, other_weights_ref, mine_ref, other_ref):
    for owner, out_ref, weight_ref in ((1, other_ref, other_weights_ref), (0, mine_ref, weights_ref)):
        totals = [jnp.zeros((rows, BLOCK), jnp.float32) for _ in range(FIELDS)]
        for v in range(slots_ref.shape[1] // 8):
            ids = slots_ref[owner, 8 * v : 8 * v + 8, :]
            found = arrived_chunks(came_ref, 1, ids, load_fields(found_ref, owner, v), owner)
            for f in range(FIELDS):
                term = found[f] * weight_ref[8 * v : 8 * v + 8, :]
                for k in range(8 // rows):
                    totals[f] = totals[f] + term[k * rows : (k + 1) * rows, :]
        for f in range(FIELDS):
            out_ref[f * rows : (f + 1) * rows, :] = totals[f]


def state_kernel(counts, mine_ref, came_ref, mask_ref, halos_ref, state_ref, table_ref, *more_refs):
    send_refs, cut_ref = more_refs[:-1], more_refs[-1]
    front = mask_ref[...] == 1
    rows = mask_ref.shape[0]
    for f in range(FIELDS):
        at = slice(f * rows, (f + 1) * rows)
        total = mine_ref[at, :] + came_ref[at, :]
        if f == 4:
            total = jnp.where(front, ocean_temp, total)
        state_ref[f * rows : (f + 1) * rows, :] = total
        for s in range(rows // 2):
            table_ref[s, 2 * f : 2 * f + 2, :] = total[2 * s : 2 * s + 2, :]
    starts = (0, halos_ref.shape[0] - 8)
    halo = [halos_ref[first : first + 8, :] for first in starts]
    halo_blocks = [i >> 7 for i in halo]
    halo_lanes = [i & (BLOCK - 1) for i in halo]
    for v in range(2):
        cut = pick_fields(table_ref, rows, halo_blocks[v], halo_lanes[v])
        for k in range(6):
            r = 2 * k - starts[v]
            if 0 <= r <= 6:
                for f in range(FIELDS):
                    cut_ref[k, 2 * f : 2 * f + 2, :] = cut[f][r : r + 2, :]
    send_pairs(counts, cut_ref, send_refs, [(0, 1), (2, 3), (4, 5)])


def pair_places():
    return [lax.rem(lax.axis_index(axis), 2) for axis in AXES]


def send_pairs(counts, cut_ref, send_refs, order):
    places = pair_places()
    long = [axis for axis in range(3) if counts[axis] > 2]
    for axis in range(3):
        even, odd = order[axis]
        send_refs[len(long) + axis][...] = cut_ref[jnp.where(places[axis] == 0, even, odd)]
        if axis in long:
            send_refs[long.index(axis)][...] = cut_ref[jnp.where(places[axis] == 0, odd, even)]


def arrivals(counts, came_refs):
    places = pair_places()
    long = [axis for axis in range(3) if counts[axis] > 2]
    result = []
    for axis in range(3):
        inside = came_refs[len(long) + axis][...]
        at = lax.axis_index(AXES[axis])
        edge = jnp.where(places[axis] == 0, at == 0, at == counts[axis] - 1)
        outside = jnp.zeros_like(inside)
        if axis in long:
            outside = jnp.where(edge, 0.0, came_refs[long.index(axis)][...])
        result.append((places[axis], inside, outside))
    return result


def placed(values, ids, block_count):
    rows = lax.broadcasted_iota(jnp.int32, (block_count, BLOCK), 0)
    hit = rows == jnp.broadcast_to(ids >> 7, rows.shape)
    left = [jnp.where(hit, jnp.broadcast_to(v, rows.shape), 0.0) for v in values]
    return jnp.concatenate(left, axis=0).astype(jnp.bfloat16)


def cut_parts(value):
    parts = []
    for _ in range(SPLITS - 1):
        part = value.astype(jnp.bfloat16).astype(jnp.float32)
        parts.append(part)
        value = value - part
    return parts + [value]


def hot_dot(left, right):
    return jnp.dot(left, right, preferred_element_type=jnp.float32)


def came_slots(counts):
    places = pair_places()
    long = [axis for axis in range(3) if counts[axis] > 2]
    slots = []
    for axis in long:
        at = lax.axis_index(AXES[axis])
        edge = jnp.where(places[axis] == 0, at == 0, at == counts[axis] - 1)
        slots.append(jnp.where(edge, -(1 << 10), 2 * axis + places[axis]))
    return slots + [2 * axis + 1 - places[axis] for axis in range(3)]


def moved_axes(counts):
    return [axis for axis in range(3) if counts[axis] > 2] + [0, 1, 2]


def add_slot(read, slot, ids, found):
    blocks, lanes = (ids >> 7) - 2 * slot, ids & (BLOCK - 1)
    found = list(found)
    for h in range(2):
        hit = blocks == h
        for f in range(FIELDS):
            found[f] = jnp.where(hit, pick(read(2 * f + h), lanes), found[f])
    return found


def values_kernel(counts, table_ref, nodes_ref, *refs):
    came_refs, values_ref = refs[:-1], refs[-1]
    owned_slots = table_ref.shape[0]
    slots = [slot for slot, axis in zip(came_slots(counts), moved_axes(counts)) if axis == 0]
    for first in range(0, nodes_ref.shape[0], 8):
        ids = nodes_ref[first : first + 8, :]
        found = [jnp.zeros((8, BLOCK), jnp.float32) for _ in range(FIELDS)]
        for s in range(owned_slots):
            found = add_slot(lambda r: table_ref[s, r : r + 1, :], s, ids, found)
        for ref, slot in zip(came_refs, slots):
            found = add_slot(lambda r: ref[r : r + 1, :], owned_slots + slot, ids, found)
        for f in range(FIELDS):
            values_ref[f, first : first + 8, :] = found[f]


def element_kernel(counts, moves, owned_slots, *refs):
    values_in_ref, nodes_ref, node_hot_ref, grads_ref, volume_ref = refs[:5]
    last = [slot for slot, axis in zip(came_slots(counts), moved_axes(counts)) if axis != 0]
    came_refs, refs = refs[5 : 5 + len(last)], refs[5 + len(last) :]
    own_ref, send_refs = refs[0], refs[1 : 1 + moves]
    values_ref, parts_ref, cut_ref = refs[1 + moves :]
    block_count = 2 * (owned_slots + 6)
    all_rows = nodes_ref.shape[0]
    elem_rows = all_rows // 4
    for first in range(0, all_rows, 8):
        ids = nodes_ref[first : first + 8, :]
        found = [values_in_ref[f, first : first + 8, :] for f in range(FIELDS)]
        for ref, slot in zip(came_refs, last):
            found = add_slot(lambda r: ref[r : r + 1, :], owned_slots + slot, ids, found)
        for f in range(FIELDS):
            values_ref[f, first : first + 8, :] = found[f]
    for first in [*range(0, elem_rows - 7, 8)] + ([elem_rows - 8] if elem_rows % 8 else []):
        at = [slice(r * elem_rows + first, r * elem_rows + first + 8) for r in range(12)]
        values = [[values_ref[f, at[a], :] for f in range(FIELDS)] for a in range(4)]
        grads = [[grads_ref[at[3 * a + j], :] for j in range(3)] for a in range(4)]
        volume = volume_ref[at[0], :]
        velgrad = [[sum(values[a][i] * grads[a][j] for a in range(4)) for j in range(3)] for i in range(3)]
        strain = [[0.5 * (velgrad[i][j] + velgrad[j][i]) if i <= j else None for j in range(3)] for i in range(3)]
        diagonal = sum(strain[i][i] * strain[i][i] for i in range(3))
        corner = sum(strain[i][j] * strain[i][j] for i, j in ((0, 1), (0, 2), (1, 2)))
        second = 0.5 * diagonal + corner
        pressure, temper, damage = [0.25 * (values[0][f] + values[1][f] + values[2][f] + values[3][f]) for f in (3, 4, 5)]
        root = jnp.exp(jnp.log(second + strain_reg) * (-1.0 / 3.0))
        twice = (1.0 - damage) * jnp.exp(-temper) * root
        stress = [[None] * 3 for _ in range(3)]
        for i in range(3):
            for j in range(i, 3):
                stress[i][j] = twice * strain[i][j] - (pressure if i == j else 0.0)
                stress[j][i] = stress[i][j]
        lift = (0.25 * gravity) * volume
        flow = 0.25 * volume * (velgrad[0][0] + velgrad[1][1] + velgrad[2][2])
        for s, part in enumerate(cut_parts(flow)):
            for a in range(4):
                parts_ref[3 * SPLITS + s, at[a], :] = part
        for a in range(4):
            for i in range(3):
                force = volume * sum(stress[i][j] * grads[a][j] for j in range(3))
                if i == 2:
                    force = force + lift
                for s, part in enumerate(cut_parts(force)):
                    parts_ref[i * SPLITS + s, at[a], :] = part

    group = node_hot_ref.shape[1] // BLOCK

    width = 4 * block_count
    total = jnp.zeros((SPLITS * width, BLOCK), jnp.float32)
    for step in range(all_rows // group):
        lefts = []
        for r in range(step * group, (step + 1) * group):
            terms = [parts_ref[c * SPLITS + s, r : r + 1, :] for s in range(SPLITS) for c in range(4)]
            lefts.append(placed(terms, nodes_ref[r : r + 1, :], block_count))
        total = total + hot_dot(jnp.concatenate(lefts, axis=1), node_hot_ref[step])
    total = sum(total[s * width : (s + 1) * width, :] for s in range(SPLITS))
    owned = 2 * owned_slots
    for c in range(4):
        own_ref[c * owned : (c + 1) * owned, :] = total[c * block_count : c * block_count + owned, :]
        for k in range(6):
            first = c * block_count + owned + 2 * k
            cut_ref[k, 2 * c : 2 * c + 2, :] = total[first : first + 2, :]
    send_pairs(counts, cut_ref, send_refs, [(1, 0), (3, 2), (5, 4)])


def residual_kernel(counts, moves, *refs):
    own_ref, halos_ref, halo_hot_ref = refs[:3]
    out_ref, came_ref = refs[3 + moves :]
    for axis, (place_at, inside, outside) in enumerate(arrivals(counts, refs[3 : 3 + moves])):
        came_ref[2 * axis + place_at] = inside
        came_ref[2 * axis + 1 - place_at] = outside
    owned = own_ref.shape[0] // 4
    lefts = []
    for k in range(6):
        parts = cut_parts(came_ref[k])
        for h in range(2):
            ids = halos_ref[2 * k + h : 2 * k + h + 1, :]
            terms = [parts[s][2 * c + h : 2 * c + h + 1, :] for s in range(SPLITS) for c in range(4)]
            lefts.append(placed(terms, ids, owned))
    total = hot_dot(jnp.concatenate(lefts, axis=1), halo_hot_ref[...])
    width = 4 * owned
    total = sum(total[s * width : (s + 1) * width, :] for s in range(SPLITS)) + own_ref[...]
    for c in range(4):
        for b in range(owned):
            r = c * owned + b
            out_ref[c : c + 1, b * BLOCK : (b + 1) * BLOCK] = total[r : r + 1, :]


def shaped(*shape):
    return jax.ShapeDtypeStruct(shape, jnp.float32)


def per_device(
    sizes,
    old_state,
    send_blocks,
    node_slots,
    node_weights,
    front_mask,
    halo_lists,
    elem_nodes,
    shape_grads,
    elem_volume,
):
    old_state, send_blocks = old_state[0, 0, 0], send_blocks[0, 0, 0]
    slots = send_blocks.shape[1]
    send_blocks = send_blocks.reshape(-1, 1, slots)
    rows = FIELDS * slots
    arguments = [
        node_slots[0, 0, 0],
        node_weights[0, 0, 0],
        front_mask.reshape(-1, BLOCK),
        halo_lists.reshape(halo_lists.shape[-2], 1, -1),
        elem_nodes[0, 0, 0],
        shape_grads.reshape(-1, BLOCK),
        elem_volume[0, 0],
    ]
    old_rows = old_state.reshape(-1, BLOCK)
    count = len(arguments)
    owned = node_slots.shape[-1]
    slot_rows = node_slots.size // BLOCK
    give_rows = 2 * rows + 2 * slot_rows
    give_first, give, first, second, own, *held = pl.pallas_call(
        functools.partial(pack_kernel, count),
        out_shape=[shaped(2 * rows, BLOCK), shaped(give_rows, BLOCK)]
        + [shaped(2 * rows, BLOCK)] * 3
        + [jax.ShapeDtypeStruct(a.shape, a.dtype) for a in arguments],
        in_specs=[pl.BlockSpec(memory_space=pltpu.HBM)] * (2 + count),
        out_specs=[VMEM] * (5 + count),
        scratch_shapes=[
            pltpu.SMEM(send_blocks.shape, jnp.int32),
            pltpu.VMEM(old_rows.shape, jnp.float32),
            pltpu.SemaphoreType.DMA((2 + count,)),
        ],
        compiler_params=params(),
    )(*(pltpu.with_memory_space_constraint(a, pltpu.HBM) for a in (send_blocks, old_rows, *arguments)))
    node_slots, node_weights, mask_rows, halos, elem_nodes, grad_rows, volume = held
    layers = both_ways([(0, 1)])
    got_first = lax.ppermute(give_first, "layer", layers)
    got = lax.ppermute(give, "layer", layers)
    full = [jnp.concatenate([first, got_first]), jnp.concatenate([second, got[: 2 * rows]])]
    first, second = [
        lax.ppermute(part, ("mapx", "layer"), pairs).reshape(4, rows, BLOCK)
        for part, pairs in zip(full, column_moves(sizes[0]))
    ]
    other_slots, other_weights = got[2 * rows : 2 * rows + slot_rows], got[2 * rows + slot_rows :]

    all_rows = elem_nodes.size // BLOCK
    halo_count = halos.size // BLOCK
    hot_steps = next(n for n in (8, 4, 2, 1) if all_rows % n == 0)
    whole = lambda *shape: jax.ShapeDtypeStruct(shape, jnp.int32)
    found, slots_cut, weights_cut, halos_cut, nodes_cut, volume_cut, halo_hot, node_hot = pl.pallas_call(
        own_kernel,
        out_shape=(
            shaped(2, FIELDS, slot_rows, BLOCK),
            whole(2, slot_rows, BLOCK),
            shaped(slot_rows, BLOCK),
            whole(halo_count, BLOCK),
            whole(all_rows, BLOCK),
            shaped(all_rows // 4, BLOCK),
            jax.ShapeDtypeStruct((halo_count * BLOCK, BLOCK), jnp.bfloat16),
            jax.ShapeDtypeStruct((hot_steps, all_rows // hot_steps * BLOCK, BLOCK), jnp.bfloat16),
        ),
        in_specs=[VMEM] * 7,
        out_specs=(VMEM,) * 8,
        compiler_params=params(),
    )(own.reshape(2, rows, BLOCK), other_slots, node_slots, node_weights, halos, elem_nodes, volume)
    found = pl.pallas_call(
        early_kernel,
        out_shape=shaped(2, FIELDS, slot_rows, BLOCK),
        in_specs=[VMEM] * 3,
        out_specs=VMEM,
        compiler_params=params(),
    )(first, slots_cut, found)
    state_rows = FIELDS * owned // BLOCK
    mine, other = pl.pallas_call(
        functools.partial(late_kernel, owned // BLOCK),
        out_shape=(shaped(state_rows, BLOCK),) * 2,
        in_specs=[VMEM] * 5,
        out_specs=(VMEM,) * 2,
        compiler_params=params(),
    )(second, slots_cut, found, weights_cut, other_weights)
    other = lax.ppermute(other, "layer", layers)
    moves = 3 + sum(size > 2 for size in sizes)
    chunk = (2 * FIELDS, BLOCK)
    new_state, table, *ghosts = pl.pallas_call(
        functools.partial(state_kernel, sizes),
        out_shape=(shaped(state_rows, BLOCK), shaped(owned // (2 * BLOCK), *chunk)) + (shaped(*chunk),) * moves,
        in_specs=[VMEM] * 4,
        out_specs=(VMEM,) * (2 + moves),
        scratch_shapes=[pltpu.VMEM((6, *chunk), jnp.float32)],
        compiler_params=params(),
    )(mine, other, mask_rows, halos_cut)
    ghosts = swap_all(ghosts, sizes)

    owned_slots = table.shape[0]
    early = [ghost for ghost, axis in zip(ghosts, moved_axes(sizes)) if axis == 0]
    late = [ghost for ghost, axis in zip(ghosts, moved_axes(sizes)) if axis != 0]
    values = pl.pallas_call(
        functools.partial(values_kernel, sizes),
        out_shape=shaped(FIELDS, all_rows, BLOCK),
        in_specs=[VMEM] * (2 + len(early)),
        out_specs=VMEM,
        compiler_params=params(),
    )(table, nodes_cut, *early)
    own, *sums = pl.pallas_call(
        functools.partial(element_kernel, sizes, moves, owned_slots),
        out_shape=(shaped(4 * owned // BLOCK, BLOCK),) + (shaped(8, BLOCK),) * moves,
        in_specs=[VMEM] * (5 + len(late)),
        out_specs=(VMEM,) * (1 + moves),
        scratch_shapes=[
            pltpu.VMEM((FIELDS, all_rows, BLOCK), jnp.float32),
            pltpu.VMEM((4 * SPLITS, all_rows, BLOCK), jnp.float32),
            pltpu.VMEM((6, 8, BLOCK), jnp.float32),
        ],
        compiler_params=params(),
    )(values, nodes_cut, node_hot, grad_rows, volume_cut, *late)
    sums = swap_all(sums, sizes)
    residual = pl.pallas_call(
        functools.partial(residual_kernel, sizes, moves),
        out_shape=shaped(4, owned),
        in_specs=[VMEM] * (3 + moves),
        out_specs=VMEM,
        scratch_shapes=[pltpu.VMEM((6, 8, BLOCK), jnp.float32)],
        compiler_params=params(),
    )(own, halos_cut, halo_hot, *sums)
    return (new_state.reshape(1, 1, 1, FIELDS, owned), residual[None, None, None])


def solution(mesh):
    sizes = tuple(mesh.shape[axis] for axis in AXES)
    row = P("mapx", "mapy", "layer", None)
    table = P("mapx", "mapy", "layer", None, None)
    return jax.shard_map(
        functools.partial(per_device, sizes),
        mesh=mesh,
        in_specs=(table, table, table, table, row, table, table, table, row),
        out_specs=(table, table),
        check_vma=False,
    )
```

```python
import functools

import jax
import jax.numpy as jnp
from jax import lax
from jax.experimental import pallas as pl
from jax.experimental.pallas import tpu as pltpu
from jax.sharding import PartitionSpec as P

BLOCK = 128
REACH = 2
FIELDS = 6
SPLITS = 3

ocean_temp = 0.0
strain_reg = 0.01
gravity = 0.5

AXES = ("mapx", "mapy", "layer")
VMEM = pl.BlockSpec(memory_space=pltpu.VMEM)
SMEM = pl.BlockSpec(memory_space=pltpu.SMEM)


def params():
    return pltpu.CompilerParams(vmem_limit_bytes=32 * 1024 * 1024)


def both_ways(pairs):
    return [way for one, other in pairs for way in ((one, other), (other, one))]


def column_moves(count):
    outside = [(at, at + 1) for at in range(1, count - 1, 2)]
    inside = [(at, at + 1) for at in range(0, count - 1, 2)]
    within = [(at + i, at + i + 2) for at in range(0, count - 3, 4) for i in range(2)]
    across = [(at + i, at + i + 2) for at in range(2, count - 3, 4) for i in range(2)]
    number = lambda pairs, layer: [(one * 2 + layer, other * 2 + layer) for one, other in pairs]
    return [
        both_ways(number(outside, 1) + number(inside, 0)),
        both_ways(number(within, 0) + number(across, 1)),
    ]


def column_offsets(layer):
    at = lax.axis_index("mapx")
    near = jnp.where(lax.rem(at, 2) == 0, 1, -1)
    two = jnp.where(lax.rem(at, 4) < 2, 2, -2)
    return [jnp.where(layer == 0, near, -near), jnp.where(layer == 0, two, -two)]


def pair_swap(value, axis, count, first):
    return lax.ppermute(value, axis, both_ways([(at, at + 1) for at in range(first, count - 1, 2)]))


def swap_all(values, sizes):
    long = [axis for axis in range(3) if sizes[axis] > 2]
    steps = [(axis, 1) for axis in long] + [(axis, 0) for axis in range(3)]
    return [pair_swap(value, AXES[axis], sizes[axis], first) for value, (axis, first) in zip(values, steps)]


def pack_blocks(blocks_ref, old_ref, ref, offset):
    slots = blocks_ref.shape[2]
    stride = old_ref.shape[0] // FIELDS
    for to_layer in range(2):
        peer = (offset + REACH) * 2 + to_layer
        start = to_layer * FIELDS * slots
        for c in range(slots):
            rows = pl.ds(blocks_ref[peer, 0, c], FIELDS, stride=stride)
            ref[start + FIELDS * c : start + FIELDS * (c + 1), :] = old_ref[rows, :]


def give_kernel(count, *refs):
    blocks_in_ref, old_in_ref = refs[:2]
    give_first_ref, give_ref, old_ref = refs[2 + count : 5 + count]
    held = refs[5 + count : 5 + 2 * count]
    blocks_ref, sems = refs[5 + 2 * count :]
    first = [pltpu.make_async_copy(blocks_in_ref, blocks_ref, sems.at[0])]
    first += [pltpu.make_async_copy(old_in_ref, old_ref, sems.at[1])]
    rest = [pltpu.make_async_copy(refs[2 + i], held[i], sems.at[2 + i]) for i in range(count)]
    for copy in first + rest:
        copy.start()
    for copy in first:
        copy.wait()
    offsets = column_offsets(1 - lax.axis_index("layer"))
    pack_blocks(blocks_ref, old_ref, give_first_ref, offsets[0])
    pack_blocks(blocks_ref, old_ref, give_ref, offsets[1])
    for copy in rest:
        copy.wait()
    size = give_first_ref.shape[0]
    slots_ref, weights_ref = held[0], held[1]
    slot_rows = slots_ref.shape[0] * slots_ref.shape[1] // BLOCK
    cut_rows(slots_ref, give_ref.at[size : size + slot_rows])
    cut_rows(weights_ref, give_ref.at[size + slot_rows : size + 2 * slot_rows])


def keep_kernel(blocks_ref, old_ref, first_ref, second_ref):
    offsets = column_offsets(lax.axis_index("layer"))
    pack_blocks(blocks_ref, old_ref, first_ref, offsets[0])
    pack_blocks(blocks_ref, old_ref, second_ref, offsets[1])


def pick(row, lanes):
    return jnp.take_along_axis(jnp.broadcast_to(row, lanes.shape), lanes, axis=1)


def pick_fields(table_ref, block_count, blocks, lanes):
    found = [jnp.zeros((8, BLOCK), jnp.float32) for _ in range(FIELDS)]
    for b in range(block_count):
        hit = blocks == b
        for f in range(FIELDS):
            row = table_ref[b // 2, 2 * f + b % 2 : 2 * f + b % 2 + 1, :]
            found[f] = jnp.where(hit, pick(row, lanes), found[f])
    return found


def add_blocks(ref, chunk, first_block, blocks, lanes, found):
    local = blocks - first_block
    found = list(found)
    for c in range(ref.shape[1] // FIELDS):
        hit = local == c
        for f in range(FIELDS):
            row = ref[chunk, FIELDS * c + f : FIELDS * c + f + 1, :]
            found[f] = jnp.where(hit, pick(row, lanes), found[f])
    return tuple(found)


def add_chunks(ref, numbers, offset, ids, found):
    blocks, lanes = ids >> 7, ids & (BLOCK - 1)
    for chunk, layer in numbers:
        first = ((offset + REACH) * 2 + layer) * (ref.shape[1] // FIELDS)
        found = add_blocks(ref, chunk, first, blocks, lanes, found)
    return found


def load_fields(found_ref, owner, v):
    return tuple(found_ref[owner, f, 8 * v : 8 * v + 8, :] for f in range(FIELDS))


def save_fields(found_ref, owner, v, found):
    for f in range(FIELDS):
        found_ref[owner, f, 8 * v : 8 * v + 8, :] = found[f]


def arrived_chunks(ref, move, ids, found, owner):
    layer = lax.axis_index("layer")
    to_layer = 1 - layer if owner else layer
    numbers = [(to_layer, layer), (2 + to_layer, 1 - layer)]
    return add_chunks(ref, numbers, column_offsets(layer)[move], ids, found)


def cut_rows(from_ref, to_ref):
    count = from_ref.shape[1] // BLOCK
    for r in range(from_ref.shape[0]):
        for i in range(count):
            to_ref[r * count + i : r * count + i + 1, :] = from_ref[
                r : r + 1, i * BLOCK : (i + 1) * BLOCK
            ].astype(to_ref.dtype)


def lane_one_hot(ids):
    rows = lax.broadcasted_iota(jnp.int32, (BLOCK, BLOCK), 0)
    hit = rows == jnp.broadcast_to(ids & (BLOCK - 1), rows.shape)
    return jnp.where(hit, 1.0, 0.0).T.astype(jnp.bfloat16)


def own_kernel(
    blocks_ref,
    old_ref,
    other_slots_ref,
    slots_in_ref,
    weights_in_ref,
    halos_in_ref,
    nodes_in_ref,
    volume_in_ref,
    found_ref,
    slots_ref,
    weights_ref,
    halos_ref,
    nodes_ref,
    volume_ref,
    halo_hot_ref,
    node_hot_ref,
    own_ref,
):
    for layer in range(2):
        chunk_ref = own_ref.at[layer]
        for c in range(blocks_ref.shape[2]):
            rows = pl.ds(blocks_ref[2 * REACH + layer, 0, c], FIELDS, stride=old_ref.shape[0] // FIELDS)
            chunk_ref[FIELDS * c : FIELDS * (c + 1), :] = old_ref[rows, :]
    for k in range(halos_in_ref.shape[0]):
        cut_rows(halos_in_ref.at[k], halos_ref.at[2 * k : 2 * k + 2])
    cut_rows(slots_in_ref, slots_ref.at[0])
    slots_ref[1] = other_slots_ref[...].astype(jnp.int32)
    cut_rows(weights_in_ref, weights_ref)
    cut_rows(nodes_in_ref, nodes_ref)
    cut_rows(volume_in_ref, volume_ref)
    layer = lax.axis_index("layer")
    for owner in range(2):
        for v in range(slots_ref.shape[1] // 8):
            ids = slots_ref[owner, 8 * v : 8 * v + 8, :]
            found = tuple(jnp.zeros((8, BLOCK), jnp.float32) for _ in range(FIELDS))
            numbers = [(1 - layer if owner else layer, layer)]
            save_fields(found_ref, owner, v, add_chunks(own_ref, numbers, 0, ids, found))
    for r in range(halos_ref.shape[0]):
        halo_hot_ref[r * BLOCK : (r + 1) * BLOCK, :] = lane_one_hot(halos_ref[r : r + 1, :])
    steps, width, _ = node_hot_ref.shape
    group = width // BLOCK

    def hot(step, carry):
        for r in range(group):
            ids = nodes_ref[pl.ds(step * group + r, 1), :]
            node_hot_ref[step, r * BLOCK : (r + 1) * BLOCK, :] = lane_one_hot(ids)
        return carry

    lax.fori_loop(0, steps, hot, 0)


def early_kernel(came_ref, slots_ref, found_in_ref, found_ref):
    for owner in range(2):
        for v in range(slots_ref.shape[1] // 8):
            ids = slots_ref[owner, 8 * v : 8 * v + 8, :]
            found = arrived_chunks(came_ref, 0, ids, load_fields(found_in_ref, owner, v), owner)
            save_fields(found_ref, owner, v, found)


def late_kernel(rows, came_ref, slots_ref, found_ref, weights_ref, other_weights_ref, mine_ref, other_ref):
    for owner, out_ref, weight_ref in ((1, other_ref, other_weights_ref), (0, mine_ref, weights_ref)):
        totals = [jnp.zeros((rows, BLOCK), jnp.float32) for _ in range(FIELDS)]
        for v in range(slots_ref.shape[1] // 8):
            ids = slots_ref[owner, 8 * v : 8 * v + 8, :]
            found = arrived_chunks(came_ref, 1, ids, load_fields(found_ref, owner, v), owner)
            for f in range(FIELDS):
                term = found[f] * weight_ref[8 * v : 8 * v + 8, :]
                for k in range(8 // rows):
                    totals[f] = totals[f] + term[k * rows : (k + 1) * rows, :]
        for f in range(FIELDS):
            out_ref[f * rows : (f + 1) * rows, :] = totals[f]


def state_kernel(counts, mine_ref, came_ref, mask_ref, halos_ref, state_ref, table_ref, *more_refs):
    send_refs, cut_ref = more_refs[:-1], more_refs[-1]
    front = mask_ref[...] == 1
    rows = mask_ref.shape[0]
    for f in range(FIELDS):
        at = slice(f * rows, (f + 1) * rows)
        total = mine_ref[at, :] + came_ref[at, :]
        if f == 4:
            total = jnp.where(front, ocean_temp, total)
        state_ref[f * rows : (f + 1) * rows, :] = total
        for s in range(rows // 2):
            table_ref[s, 2 * f : 2 * f + 2, :] = total[2 * s : 2 * s + 2, :]
    starts = (0, halos_ref.shape[0] - 8)
    halo = [halos_ref[first : first + 8, :] for first in starts]
    halo_blocks = [i >> 7 for i in halo]
    halo_lanes = [i & (BLOCK - 1) for i in halo]
    for v in range(2):
        cut = pick_fields(table_ref, rows, halo_blocks[v], halo_lanes[v])
        for k in range(6):
            r = 2 * k - starts[v]
            if 0 <= r <= 6:
                for f in range(FIELDS):
                    cut_ref[k, 2 * f : 2 * f + 2, :] = cut[f][r : r + 2, :]
    send_pairs(counts, cut_ref, send_refs, [(0, 1), (2, 3), (4, 5)])


def pair_places():
    return [lax.rem(lax.axis_index(axis), 2) for axis in AXES]


def send_pairs(counts, cut_ref, send_refs, order):
    places = pair_places()
    long = [axis for axis in range(3) if counts[axis] > 2]
    for axis in range(3):
        even, odd = order[axis]
        send_refs[len(long) + axis][...] = cut_ref[jnp.where(places[axis] == 0, even, odd)]
        if axis in long:
            send_refs[long.index(axis)][...] = cut_ref[jnp.where(places[axis] == 0, odd, even)]


def placed(values, ids, block_count):
    rows = lax.broadcasted_iota(jnp.int32, (block_count, BLOCK), 0)
    hit = rows == jnp.broadcast_to(ids >> 7, rows.shape)
    left = [jnp.where(hit, jnp.broadcast_to(v, rows.shape), 0.0) for v in values]
    return jnp.concatenate(left, axis=0).astype(jnp.bfloat16)


def cut_parts(value):
    parts = []
    for _ in range(SPLITS - 1):
        part = value.astype(jnp.bfloat16).astype(jnp.float32)
        parts.append(part)
        value = value - part
    return parts + [value]


def hot_dot(left, right):
    return jnp.dot(left, right, preferred_element_type=jnp.float32)


def came_slots(counts):
    places = pair_places()
    long = [axis for axis in range(3) if counts[axis] > 2]
    slots = []
    for axis in long:
        at = lax.axis_index(AXES[axis])
        edge = jnp.where(places[axis] == 0, at == 0, at == counts[axis] - 1)
        slots.append(jnp.where(edge, -(1 << 10), 2 * axis + places[axis]))
    return slots + [2 * axis + 1 - places[axis] for axis in range(3)]


def moved_axes(counts):
    return [axis for axis in range(3) if counts[axis] > 2] + [0, 1, 2]


def add_slot(read, slot, ids, found):
    blocks, lanes = (ids >> 7) - 2 * slot, ids & (BLOCK - 1)
    found = list(found)
    for h in range(2):
        hit = blocks == h
        for f in range(FIELDS):
            found[f] = jnp.where(hit, pick(read(2 * f + h), lanes), found[f])
    return found


def values_kernel(counts, table_ref, nodes_ref, *refs):
    came_refs, values_ref = refs[:-1], refs[-1]
    owned_slots = table_ref.shape[0]
    slots = [slot for slot, axis in zip(came_slots(counts), moved_axes(counts)) if axis == 0]
    for first in range(0, nodes_ref.shape[0], 8):
        ids = nodes_ref[first : first + 8, :]
        found = [jnp.zeros((8, BLOCK), jnp.float32) for _ in range(FIELDS)]
        for s in range(owned_slots):
            found = add_slot(lambda r: table_ref[s, r : r + 1, :], s, ids, found)
        for ref, slot in zip(came_refs, slots):
            found = add_slot(lambda r: ref[r : r + 1, :], owned_slots + slot, ids, found)
        for f in range(FIELDS):
            values_ref[f, first : first + 8, :] = found[f]


def element_kernel(counts, moves, owned_slots, *refs):
    values_in_ref, nodes_ref, node_hot_ref, grads_ref, volume_ref = refs[:5]
    last = [slot for slot, axis in zip(came_slots(counts), moved_axes(counts)) if axis != 0]
    came_refs, refs = refs[5 : 5 + len(last)], refs[5 + len(last) :]
    own_ref, send_refs = refs[0], refs[1 : 1 + moves]
    values_ref, parts_ref, cut_ref = refs[1 + moves :]
    block_count = 2 * (owned_slots + 6)
    all_rows = nodes_ref.shape[0]
    elem_rows = all_rows // 4
    for first in range(0, all_rows, 8):
        ids = nodes_ref[first : first + 8, :]
        found = [values_in_ref[f, first : first + 8, :] for f in range(FIELDS)]
        for ref, slot in zip(came_refs, last):
            found = add_slot(lambda r: ref[r : r + 1, :], owned_slots + slot, ids, found)
        for f in range(FIELDS):
            values_ref[f, first : first + 8, :] = found[f]
    for first in [*range(0, elem_rows - 7, 8)] + ([elem_rows - 8] if elem_rows % 8 else []):
        at = [slice(r * elem_rows + first, r * elem_rows + first + 8) for r in range(12)]
        values = [[values_ref[f, at[a], :] for f in range(FIELDS)] for a in range(4)]
        grads = [[grads_ref[at[3 * a + j], :] for j in range(3)] for a in range(4)]
        volume = volume_ref[at[0], :]
        velgrad = [[sum(values[a][i] * grads[a][j] for a in range(4)) for j in range(3)] for i in range(3)]
        strain = [[0.5 * (velgrad[i][j] + velgrad[j][i]) if i <= j else None for j in range(3)] for i in range(3)]
        diagonal = sum(strain[i][i] * strain[i][i] for i in range(3))
        corner = sum(strain[i][j] * strain[i][j] for i, j in ((0, 1), (0, 2), (1, 2)))
        second = 0.5 * diagonal + corner
        pressure, temper, damage = [0.25 * (values[0][f] + values[1][f] + values[2][f] + values[3][f]) for f in (3, 4, 5)]
        root = jnp.exp(jnp.log(second + strain_reg) * (-1.0 / 3.0))
        twice = (1.0 - damage) * jnp.exp(-temper) * root
        stress = [[None] * 3 for _ in range(3)]
        for i in range(3):
            for j in range(i, 3):
                stress[i][j] = twice * strain[i][j] - (pressure if i == j else 0.0)
                stress[j][i] = stress[i][j]
        lift = (0.25 * gravity) * volume
        flow = 0.25 * volume * (velgrad[0][0] + velgrad[1][1] + velgrad[2][2])
        for s, part in enumerate(cut_parts(flow)):
            for a in range(4):
                parts_ref[3 * SPLITS + s, at[a], :] = part
        for a in range(4):
            for i in range(3):
                force = volume * sum(stress[i][j] * grads[a][j] for j in range(3))
                if i == 2:
                    force = force + lift
                for s, part in enumerate(cut_parts(force)):
                    parts_ref[i * SPLITS + s, at[a], :] = part

    group = node_hot_ref.shape[1] // BLOCK

    width = 4 * block_count
    total = jnp.zeros((SPLITS * width, BLOCK), jnp.float32)
    for step in range(all_rows // group):
        lefts = []
        for r in range(step * group, (step + 1) * group):
            terms = [parts_ref[c * SPLITS + s, r : r + 1, :] for s in range(SPLITS) for c in range(4)]
            lefts.append(placed(terms, nodes_ref[r : r + 1, :], block_count))
        total = total + hot_dot(jnp.concatenate(lefts, axis=1), node_hot_ref[step])
    total = sum(total[s * width : (s + 1) * width, :] for s in range(SPLITS))
    owned = 2 * owned_slots
    for c in range(4):
        own_ref[c * owned : (c + 1) * owned, :] = total[c * block_count : c * block_count + owned, :]
        for k in range(6):
            first = c * block_count + owned + 2 * k
            cut_ref[k, 2 * c : 2 * c + 2, :] = total[first : first + 2, :]
    send_pairs(counts, cut_ref, send_refs, [(1, 0), (3, 2), (5, 4)])


def placed_few(values, ids, block_count):
    each = 8 // block_count
    rows = lax.broadcasted_iota(jnp.int32, (8, BLOCK), 0)
    hit = (rows & (block_count - 1)) == jnp.broadcast_to(ids >> 7, rows.shape)
    left = []
    for first in range(0, len(values), each):
        tile = jnp.broadcast_to(values[first], rows.shape)
        for i in range(1, each):
            tile = jnp.where(rows >= i * block_count, jnp.broadcast_to(values[first + i], rows.shape), tile)
        left.append(jnp.where(hit, tile, 0.0))
    return jnp.concatenate(left, axis=0).astype(jnp.bfloat16)


def add_returned(total, came_refs, directions, halos_ref, halo_hot_ref):
    owned = total.shape[0] // 4
    lefts, rights = [], []
    for ref, k in zip(came_refs, directions):
        parts = cut_parts(ref[...])
        for h in range(2):
            terms = [parts[s][2 * c + h : 2 * c + h + 1, :] for s in range(SPLITS) for c in range(4)]
            lefts.append(placed_few(terms, halos_ref[pl.ds(2 * k + h, 1), :], owned))
            rights.append(halo_hot_ref[pl.ds(pl.multiple_of((2 * k + h) * BLOCK, BLOCK), BLOCK), :])
    sums = hot_dot(jnp.concatenate(lefts, axis=1), jnp.concatenate(rights, axis=0))
    width = 4 * owned
    return total + sum(sums[s * width : (s + 1) * width, :] for s in range(SPLITS))


def back_directions(counts):
    places = pair_places()
    long = [axis for axis in range(3) if counts[axis] > 2]
    return [2 * axis + 1 - places[axis] for axis in long] + [2 * axis + places[axis] for axis in range(3)]


def early_residual_kernel(counts, own_ref, halos_ref, halo_hot_ref, *refs):
    directions = [k for k, axis in zip(back_directions(counts), moved_axes(counts)) if axis == 0][::-1]
    refs[-1][...] = add_returned(own_ref[...], refs[:-1], directions, halos_ref, halo_hot_ref)


def residual_kernel(counts, sums_ref, halos_ref, halo_hot_ref, *refs):
    directions = [k for k, axis in zip(back_directions(counts), moved_axes(counts)) if axis != 0]
    total = add_returned(sums_ref[...], refs[:-1], directions, halos_ref, halo_hot_ref)
    owned = total.shape[0] // 4
    for c in range(4):
        for b in range(owned):
            r = c * owned + b
            refs[-1][c : c + 1, b * BLOCK : (b + 1) * BLOCK] = total[r : r + 1, :]


def shaped(*shape):
    return jax.ShapeDtypeStruct(shape, jnp.float32)


def per_device(
    sizes,
    old_state,
    send_blocks,
    node_slots,
    node_weights,
    front_mask,
    halo_lists,
    elem_nodes,
    shape_grads,
    elem_volume,
):
    old_state, send_blocks = old_state[0, 0, 0], send_blocks[0, 0, 0]
    slots = send_blocks.shape[1]
    send_blocks = send_blocks.reshape(-1, 1, slots)
    rows = FIELDS * slots
    arguments = [
        node_slots[0, 0, 0],
        node_weights[0, 0, 0],
        front_mask.reshape(-1, BLOCK),
        halo_lists.reshape(halo_lists.shape[-2], 1, -1),
        elem_nodes[0, 0, 0],
        shape_grads.reshape(-1, BLOCK),
        elem_volume[0, 0],
        send_blocks,
    ]
    old_rows = old_state.reshape(-1, BLOCK)
    count = len(arguments)
    owned = node_slots.shape[-1]
    slot_rows = node_slots.size // BLOCK
    give_rows = 2 * rows + 2 * slot_rows
    give_first, give, old_rows, *held = pl.pallas_call(
        functools.partial(give_kernel, count),
        out_shape=[shaped(2 * rows, BLOCK), shaped(give_rows, BLOCK), shaped(*old_rows.shape)]
        + [jax.ShapeDtypeStruct(a.shape, a.dtype) for a in arguments],
        in_specs=[pl.BlockSpec(memory_space=pltpu.HBM)] * (2 + count),
        out_specs=[VMEM] * (3 + count),
        scratch_shapes=[pltpu.SMEM(send_blocks.shape, jnp.int32), pltpu.SemaphoreType.DMA((2 + count,))],
        compiler_params=params(),
    )(*(pltpu.with_memory_space_constraint(a, pltpu.HBM) for a in (send_blocks, old_rows, *arguments)))
    node_slots, node_weights, mask_rows, halos, elem_nodes, grad_rows, volume, held_blocks = held
    first, second = pl.pallas_call(
        keep_kernel,
        out_shape=(shaped(2 * rows, BLOCK),) * 2,
        in_specs=[SMEM, VMEM],
        out_specs=(VMEM,) * 2,
        compiler_params=params(),
    )(held_blocks, old_rows)
    layers = both_ways([(0, 1)])
    got_first = lax.ppermute(give_first, "layer", layers)
    got = lax.ppermute(give, "layer", layers)
    full = [jnp.concatenate([first, got_first]), jnp.concatenate([second, got[: 2 * rows]])]
    first, second = [
        lax.ppermute(part, ("mapx", "layer"), pairs).reshape(4, rows, BLOCK)
        for part, pairs in zip(full, column_moves(sizes[0]))
    ]
    other_slots, other_weights = got[2 * rows : 2 * rows + slot_rows], got[2 * rows + slot_rows :]

    all_rows = elem_nodes.size // BLOCK
    halo_count = halos.size // BLOCK
    hot_steps = next(n for n in (8, 4, 2, 1) if all_rows % n == 0)
    whole = lambda *shape: jax.ShapeDtypeStruct(shape, jnp.int32)
    found, slots_cut, weights_cut, halos_cut, nodes_cut, volume_cut, halo_hot, node_hot = pl.pallas_call(
        own_kernel,
        out_shape=(
            shaped(2, FIELDS, slot_rows, BLOCK),
            whole(2, slot_rows, BLOCK),
            shaped(slot_rows, BLOCK),
            whole(halo_count, BLOCK),
            whole(all_rows, BLOCK),
            shaped(all_rows // 4, BLOCK),
            jax.ShapeDtypeStruct((halo_count * BLOCK, BLOCK), jnp.bfloat16),
            jax.ShapeDtypeStruct((hot_steps, all_rows // hot_steps * BLOCK, BLOCK), jnp.bfloat16),
        ),
        in_specs=[SMEM] + [VMEM] * 7,
        out_specs=(VMEM,) * 8,
        scratch_shapes=[pltpu.VMEM((2, rows, BLOCK), jnp.float32)],
        compiler_params=params(),
    )(held_blocks, old_rows, other_slots, node_slots, node_weights, halos, elem_nodes, volume)
    found = pl.pallas_call(
        early_kernel,
        out_shape=shaped(2, FIELDS, slot_rows, BLOCK),
        in_specs=[VMEM] * 3,
        out_specs=VMEM,
        compiler_params=params(),
    )(first, slots_cut, found)
    state_rows = FIELDS * owned // BLOCK
    mine, other = pl.pallas_call(
        functools.partial(late_kernel, owned // BLOCK),
        out_shape=(shaped(state_rows, BLOCK),) * 2,
        in_specs=[VMEM] * 5,
        out_specs=(VMEM,) * 2,
        compiler_params=params(),
    )(second, slots_cut, found, weights_cut, other_weights)
    other = lax.ppermute(other, "layer", layers)
    moves = 3 + sum(size > 2 for size in sizes)
    chunk = (2 * FIELDS, BLOCK)
    new_state, table, *ghosts = pl.pallas_call(
        functools.partial(state_kernel, sizes),
        out_shape=(shaped(state_rows, BLOCK), shaped(owned // (2 * BLOCK), *chunk)) + (shaped(*chunk),) * moves,
        in_specs=[VMEM] * 4,
        out_specs=(VMEM,) * (2 + moves),
        scratch_shapes=[pltpu.VMEM((6, *chunk), jnp.float32)],
        compiler_params=params(),
    )(mine, other, mask_rows, halos_cut)
    ghosts = swap_all(ghosts, sizes)

    owned_slots = table.shape[0]
    early = [ghost for ghost, axis in zip(ghosts, moved_axes(sizes)) if axis == 0]
    late = [ghost for ghost, axis in zip(ghosts, moved_axes(sizes)) if axis != 0]
    values = pl.pallas_call(
        functools.partial(values_kernel, sizes),
        out_shape=shaped(FIELDS, all_rows, BLOCK),
        in_specs=[VMEM] * (2 + len(early)),
        out_specs=VMEM,
        compiler_params=params(),
    )(table, nodes_cut, *early)
    own, *sums = pl.pallas_call(
        functools.partial(element_kernel, sizes, moves, owned_slots),
        out_shape=(shaped(4 * owned // BLOCK, BLOCK),) + (shaped(8, BLOCK),) * moves,
        in_specs=[VMEM] * (5 + len(late)),
        out_specs=(VMEM,) * (1 + moves),
        scratch_shapes=[
            pltpu.VMEM((FIELDS, all_rows, BLOCK), jnp.float32),
            pltpu.VMEM((4 * SPLITS, all_rows, BLOCK), jnp.float32),
            pltpu.VMEM((6, 8, BLOCK), jnp.float32),
        ],
        compiler_params=params(),
    )(values, nodes_cut, node_hot, grad_rows, volume_cut, *late)
    sums = swap_all(sums, sizes)
    early = [came for came, axis in zip(sums, moved_axes(sizes)) if axis == 0][::-1]
    late = [came for came, axis in zip(sums, moved_axes(sizes)) if axis != 0]
    own = pl.pallas_call(
        functools.partial(early_residual_kernel, sizes),
        out_shape=shaped(*own.shape),
        in_specs=[VMEM] * (3 + len(early)),
        out_specs=VMEM,
        compiler_params=params(),
    )(own, halos_cut, halo_hot, *early)
    residual = pl.pallas_call(
        functools.partial(residual_kernel, sizes),
        out_shape=shaped(4, owned),
        in_specs=[VMEM] * (3 + len(late)),
        out_specs=VMEM,
        compiler_params=params(),
    )(own, halos_cut, halo_hot, *late)
    return (new_state.reshape(1, 1, 1, FIELDS, owned), residual[None, None, None])


def solution(mesh):
    sizes = tuple(mesh.shape[axis] for axis in AXES)
    row = P("mapx", "mapy", "layer", None)
    table = P("mapx", "mapy", "layer", None, None)
    return jax.shard_map(
        functools.partial(per_device, sizes),
        mesh=mesh,
        in_specs=(table, table, table, table, row, table, table, table, row),
        out_specs=(table, table),
        check_vma=False,
    )
```

```python
import functools

import jax
import jax.numpy as jnp
from jax import lax
from jax.experimental import pallas as pl
from jax.experimental.pallas import tpu as pltpu
from jax.sharding import PartitionSpec as P

BLOCK = 128
REACH = 2
FIELDS = 6
SPLITS = 3

ocean_temp = 0.0
strain_reg = 0.01
gravity = 0.5

AXES = ("mapx", "mapy", "layer")
VMEM = pl.BlockSpec(memory_space=pltpu.VMEM)
SMEM = pl.BlockSpec(memory_space=pltpu.SMEM)


def params():
    return pltpu.CompilerParams(vmem_limit_bytes=32 * 1024 * 1024)


def both_ways(pairs):
    return [way for one, other in pairs for way in ((one, other), (other, one))]


def column_moves(count):
    outside = [(at, at + 1) for at in range(1, count - 1, 2)]
    inside = [(at, at + 1) for at in range(0, count - 1, 2)]
    within = [(at + i, at + i + 2) for at in range(0, count - 3, 4) for i in range(2)]
    across = [(at + i, at + i + 2) for at in range(2, count - 3, 4) for i in range(2)]
    number = lambda pairs, layer: [(one * 2 + layer, other * 2 + layer) for one, other in pairs]
    return [
        both_ways(number(outside, 1) + number(inside, 0)),
        both_ways(number(within, 0) + number(across, 1)),
    ]


def column_offsets(layer):
    at = lax.axis_index("mapx")
    near = jnp.where(lax.rem(at, 2) == 0, 1, -1)
    two = jnp.where(lax.rem(at, 4) < 2, 2, -2)
    return [jnp.where(layer == 0, near, -near), jnp.where(layer == 0, two, -two)]


def pair_swap(value, axis, count, first):
    return lax.ppermute(value, axis, both_ways([(at, at + 1) for at in range(first, count - 1, 2)]))


def swap_all(values, sizes):
    long = [axis for axis in range(3) if sizes[axis] > 2]
    steps = [(axis, 1) for axis in long] + [(axis, 0) for axis in range(3)]
    return [pair_swap(value, AXES[axis], sizes[axis], first) for value, (axis, first) in zip(values, steps)]


def pack_blocks(blocks_ref, old_ref, ref, offset):
    slots = blocks_ref.shape[2]
    stride = old_ref.shape[0] // FIELDS
    for to_layer in range(2):
        peer = (offset + REACH) * 2 + to_layer
        start = to_layer * FIELDS * slots
        for c in range(slots):
            rows = pl.ds(blocks_ref[peer, 0, c], FIELDS, stride=stride)
            ref[start + FIELDS * c : start + FIELDS * (c + 1), :] = old_ref[rows, :]


def give_kernel(count, *refs):
    blocks_in_ref, old_in_ref = refs[:2]
    give_first_ref, give_ref, old_ref = refs[2 + count : 5 + count]
    held = refs[5 + count : 5 + 2 * count]
    blocks_ref, sems = refs[5 + 2 * count :]
    first = [pltpu.make_async_copy(blocks_in_ref, blocks_ref, sems.at[0])]
    first += [pltpu.make_async_copy(old_in_ref, old_ref, sems.at[1])]
    rest = [pltpu.make_async_copy(refs[2 + i], held[i], sems.at[2 + i]) for i in range(count)]
    for copy in first + rest:
        copy.start()
    for copy in first:
        copy.wait()
    offsets = column_offsets(1 - lax.axis_index("layer"))
    pack_blocks(blocks_ref, old_ref, give_first_ref, offsets[0])
    pack_blocks(blocks_ref, old_ref, give_ref, offsets[1])
    for copy in rest:
        copy.wait()
    size = give_first_ref.shape[0]
    slots_ref, weights_ref = held[0], held[1]
    slot_rows = slots_ref.shape[0] * slots_ref.shape[1] // BLOCK
    cut_rows(slots_ref, give_ref.at[size : size + slot_rows])
    cut_rows(weights_ref, give_ref.at[size + slot_rows : size + 2 * slot_rows])


def keep_kernel(blocks_ref, old_ref, first_ref, second_ref):
    offsets = column_offsets(lax.axis_index("layer"))
    pack_blocks(blocks_ref, old_ref, first_ref, offsets[0])
    pack_blocks(blocks_ref, old_ref, second_ref, offsets[1])


def pick(row, lanes):
    return jnp.take_along_axis(jnp.broadcast_to(row, lanes.shape), lanes, axis=1)


def pick_fields(table_ref, block_count, blocks, lanes):
    found = [jnp.zeros((8, BLOCK), jnp.float32) for _ in range(FIELDS)]
    for b in range(block_count):
        hit = blocks == b
        for f in range(FIELDS):
            row = table_ref[b // 2, 2 * f + b % 2 : 2 * f + b % 2 + 1, :]
            found[f] = jnp.where(hit, pick(row, lanes), found[f])
    return found


def add_blocks(ref, chunk, first_block, blocks, lanes, found):
    local = blocks - first_block
    found = list(found)
    for c in range(ref.shape[1] // FIELDS):
        hit = local == c
        for f in range(FIELDS):
            row = ref[chunk, FIELDS * c + f : FIELDS * c + f + 1, :]
            found[f] = jnp.where(hit, pick(row, lanes), found[f])
    return tuple(found)


def add_chunks(ref, numbers, offset, ids, found):
    blocks, lanes = ids >> 7, ids & (BLOCK - 1)
    for chunk, layer in numbers:
        first = ((offset + REACH) * 2 + layer) * (ref.shape[1] // FIELDS)
        found = add_blocks(ref, chunk, first, blocks, lanes, found)
    return found


def load_fields(found_ref, owner, v):
    return tuple(found_ref[owner, f, 8 * v : 8 * v + 8, :] for f in range(FIELDS))


def save_fields(found_ref, owner, v, found):
    for f in range(FIELDS):
        found_ref[owner, f, 8 * v : 8 * v + 8, :] = found[f]


def arrived_chunks(ref, move, ids, found, owner):
    layer = lax.axis_index("layer")
    to_layer = 1 - layer if owner else layer
    numbers = [(to_layer, layer), (2 + to_layer, 1 - layer)]
    return add_chunks(ref, numbers, column_offsets(layer)[move], ids, found)


def cut_rows(from_ref, to_ref):
    count = from_ref.shape[1] // BLOCK
    for r in range(from_ref.shape[0]):
        for i in range(count):
            to_ref[r * count + i : r * count + i + 1, :] = from_ref[
                r : r + 1, i * BLOCK : (i + 1) * BLOCK
            ].astype(to_ref.dtype)


def lane_one_hot(ids):
    rows = lax.broadcasted_iota(jnp.int32, (BLOCK, BLOCK), 0)
    hit = rows == jnp.broadcast_to(ids & (BLOCK - 1), rows.shape)
    return jnp.where(hit, 1.0, 0.0).T.astype(jnp.bfloat16)


def own_kernel(
    blocks_ref,
    old_ref,
    other_slots_ref,
    slots_in_ref,
    weights_in_ref,
    halos_in_ref,
    nodes_in_ref,
    volume_in_ref,
    found_ref,
    slots_ref,
    weights_ref,
    halos_ref,
    nodes_ref,
    volume_ref,
    halo_hot_ref,
    node_hot_ref,
    own_ref,
):
    for layer in range(2):
        chunk_ref = own_ref.at[layer]
        for c in range(blocks_ref.shape[2]):
            rows = pl.ds(blocks_ref[2 * REACH + layer, 0, c], FIELDS, stride=old_ref.shape[0] // FIELDS)
            chunk_ref[FIELDS * c : FIELDS * (c + 1), :] = old_ref[rows, :]
    for k in range(halos_in_ref.shape[0]):
        cut_rows(halos_in_ref.at[k], halos_ref.at[2 * k : 2 * k + 2])
    cut_rows(slots_in_ref, slots_ref.at[0])
    slots_ref[1] = other_slots_ref[...].astype(jnp.int32)
    cut_rows(weights_in_ref, weights_ref)
    cut_rows(nodes_in_ref, nodes_ref)
    cut_rows(volume_in_ref, volume_ref)
    layer = lax.axis_index("layer")
    for owner in range(2):
        for v in range(slots_ref.shape[1] // 8):
            ids = slots_ref[owner, 8 * v : 8 * v + 8, :]
            found = tuple(jnp.zeros((8, BLOCK), jnp.float32) for _ in range(FIELDS))
            numbers = [(1 - layer if owner else layer, layer)]
            save_fields(found_ref, owner, v, add_chunks(own_ref, numbers, 0, ids, found))
    for r in range(halos_ref.shape[0]):
        halo_hot_ref[r * BLOCK : (r + 1) * BLOCK, :] = lane_one_hot(halos_ref[r : r + 1, :])
    steps, width, _ = node_hot_ref.shape
    group = width // BLOCK

    def hot(step, carry):
        for r in range(group):
            ids = nodes_ref[pl.ds(step * group + r, 1), :]
            node_hot_ref[step, r * BLOCK : (r + 1) * BLOCK, :] = lane_one_hot(ids)
        return carry

    lax.fori_loop(0, steps, hot, 0)


def early_kernel(came_ref, slots_ref, found_in_ref, found_ref):
    for owner in range(2):
        for v in range(slots_ref.shape[1] // 8):
            ids = slots_ref[owner, 8 * v : 8 * v + 8, :]
            found = arrived_chunks(came_ref, 0, ids, load_fields(found_in_ref, owner, v), owner)
            save_fields(found_ref, owner, v, found)


def late_kernel(rows, came_ref, slots_ref, found_ref, weights_ref, other_weights_ref, mine_ref, other_ref):
    for owner, out_ref, weight_ref in ((1, other_ref, other_weights_ref), (0, mine_ref, weights_ref)):
        totals = [jnp.zeros((rows, BLOCK), jnp.float32) for _ in range(FIELDS)]
        for v in range(slots_ref.shape[1] // 8):
            ids = slots_ref[owner, 8 * v : 8 * v + 8, :]
            found = arrived_chunks(came_ref, 1, ids, load_fields(found_ref, owner, v), owner)
            for f in range(FIELDS):
                term = found[f] * weight_ref[8 * v : 8 * v + 8, :]
                for k in range(8 // rows):
                    totals[f] = totals[f] + term[k * rows : (k + 1) * rows, :]
        for f in range(FIELDS):
            out_ref[f * rows : (f + 1) * rows, :] = totals[f]


def state_kernel(counts, mine_ref, came_ref, mask_ref, halos_ref, state_ref, table_ref, *more_refs):
    send_refs, cut_ref = more_refs[:-1], more_refs[-1]
    front = mask_ref[...] == 1
    rows = mask_ref.shape[0]
    for f in range(FIELDS):
        at = slice(f * rows, (f + 1) * rows)
        total = mine_ref[at, :] + came_ref[at, :]
        if f == 4:
            total = jnp.where(front, ocean_temp, total)
        state_ref[f * rows : (f + 1) * rows, :] = total
        for s in range(rows // 2):
            table_ref[s, 2 * f : 2 * f + 2, :] = total[2 * s : 2 * s + 2, :]
    starts = (0, halos_ref.shape[0] - 8)
    halo = [halos_ref[first : first + 8, :] for first in starts]
    halo_blocks = [i >> 7 for i in halo]
    halo_lanes = [i & (BLOCK - 1) for i in halo]
    for v in range(2):
        cut = pick_fields(table_ref, rows, halo_blocks[v], halo_lanes[v])
        for k in range(6):
            r = 2 * k - starts[v]
            if 0 <= r <= 6:
                for f in range(FIELDS):
                    cut_ref[k, 2 * f : 2 * f + 2, :] = cut[f][r : r + 2, :]
    send_pairs(counts, cut_ref, send_refs, [(0, 1), (2, 3), (4, 5)])


def pair_places():
    return [lax.rem(lax.axis_index(axis), 2) for axis in AXES]


def send_pairs(counts, cut_ref, send_refs, order):
    places = pair_places()
    long = [axis for axis in range(3) if counts[axis] > 2]
    for axis in range(3):
        even, odd = order[axis]
        send_refs[len(long) + axis][...] = cut_ref[jnp.where(places[axis] == 0, even, odd)]
        if axis in long:
            send_refs[long.index(axis)][...] = cut_ref[jnp.where(places[axis] == 0, odd, even)]


def placed(values, ids, block_count):
    rows = lax.broadcasted_iota(jnp.int32, (block_count, BLOCK), 0)
    hit = rows == jnp.broadcast_to(ids >> 7, rows.shape)
    left = [jnp.where(hit, jnp.broadcast_to(v, rows.shape), 0.0) for v in values]
    return jnp.concatenate(left, axis=0).astype(jnp.bfloat16)


def cut_parts(value):
    parts = []
    for _ in range(SPLITS - 1):
        part = value.astype(jnp.bfloat16).astype(jnp.float32)
        parts.append(part)
        value = value - part
    return parts + [value]


def hot_dot(left, right):
    return jnp.dot(left, right, preferred_element_type=jnp.float32)


def came_slots(counts):
    places = pair_places()
    long = [axis for axis in range(3) if counts[axis] > 2]
    slots = []
    for axis in long:
        at = lax.axis_index(AXES[axis])
        edge = jnp.where(places[axis] == 0, at == 0, at == counts[axis] - 1)
        slots.append(jnp.where(edge, -(1 << 10), 2 * axis + places[axis]))
    return slots + [2 * axis + 1 - places[axis] for axis in range(3)]


def moved_axes(counts):
    return [axis for axis in range(3) if counts[axis] > 2] + [0, 1, 2]


def add_slot(read, slot, ids, found):
    blocks, lanes = (ids >> 7) - 2 * slot, ids & (BLOCK - 1)
    found = list(found)
    for h in range(2):
        hit = blocks == h
        for f in range(FIELDS):
            found[f] = jnp.where(hit, pick(read(2 * f + h), lanes), found[f])
    return found


def values_kernel(counts, table_ref, nodes_ref, *refs):
    came_refs, values_ref = refs[:-1], refs[-1]
    owned_slots = table_ref.shape[0]
    slots = [slot for slot, axis in zip(came_slots(counts), moved_axes(counts)) if axis == 0]
    for first in range(0, nodes_ref.shape[0], 8):
        ids = nodes_ref[first : first + 8, :]
        found = [jnp.zeros((8, BLOCK), jnp.float32) for _ in range(FIELDS)]
        for s in range(owned_slots):
            found = add_slot(lambda r: table_ref[s, r : r + 1, :], s, ids, found)
        for ref, slot in zip(came_refs, slots):
            found = add_slot(lambda r: ref[r : r + 1, :], owned_slots + slot, ids, found)
        for f in range(FIELDS):
            values_ref[f, first : first + 8, :] = found[f]


def element_kernel(counts, moves, owned_slots, *refs):
    values_in_ref, nodes_ref, node_hot_ref, grads_ref, volume_ref = refs[:5]
    last = [slot for slot, axis in zip(came_slots(counts), moved_axes(counts)) if axis != 0]
    came_refs, refs = refs[5 : 5 + len(last)], refs[5 + len(last) :]
    own_ref, send_refs = refs[0], refs[1 : 1 + moves]
    values_ref, parts_ref, cut_ref = refs[1 + moves :]
    block_count = 2 * (owned_slots + 6)
    all_rows = nodes_ref.shape[0]
    elem_rows = all_rows // 4
    for first in range(0, all_rows, 8):
        ids = nodes_ref[first : first + 8, :]
        found = [values_in_ref[f, first : first + 8, :] for f in range(FIELDS)]
        for ref, slot in zip(came_refs, last):
            found = add_slot(lambda r: ref[r : r + 1, :], owned_slots + slot, ids, found)
        for f in range(FIELDS):
            values_ref[f, first : first + 8, :] = found[f]
    for first in [*range(0, elem_rows - 7, 8)] + ([elem_rows - 8] if elem_rows % 8 else []):
        at = [slice(r * elem_rows + first, r * elem_rows + first + 8) for r in range(12)]
        values = [[values_ref[f, at[a], :] for f in range(FIELDS)] for a in range(4)]
        grads = [[grads_ref[at[3 * a + j], :] for j in range(3)] for a in range(4)]
        volume = volume_ref[at[0], :]
        velgrad = [[sum(values[a][i] * grads[a][j] for a in range(4)) for j in range(3)] for i in range(3)]
        strain = [[0.5 * (velgrad[i][j] + velgrad[j][i]) if i <= j else None for j in range(3)] for i in range(3)]
        diagonal = sum(strain[i][i] * strain[i][i] for i in range(3))
        corner = sum(strain[i][j] * strain[i][j] for i, j in ((0, 1), (0, 2), (1, 2)))
        second = 0.5 * diagonal + corner
        pressure, temper, damage = [0.25 * (values[0][f] + values[1][f] + values[2][f] + values[3][f]) for f in (3, 4, 5)]
        root = jnp.exp(jnp.log(second + strain_reg) * (-1.0 / 3.0))
        twice = (1.0 - damage) * jnp.exp(-temper) * root
        stress = [[None] * 3 for _ in range(3)]
        for i in range(3):
            for j in range(i, 3):
                stress[i][j] = twice * strain[i][j] - (pressure if i == j else 0.0)
                stress[j][i] = stress[i][j]
        lift = (0.25 * gravity) * volume
        flow = 0.25 * volume * (velgrad[0][0] + velgrad[1][1] + velgrad[2][2])
        for s, part in enumerate(cut_parts(flow)):
            for a in range(4):
                parts_ref[3 * SPLITS + s, at[a], :] = part
        for a in range(4):
            for i in range(3):
                force = volume * sum(stress[i][j] * grads[a][j] for j in range(3))
                if i == 2:
                    force = force + lift
                for s, part in enumerate(cut_parts(force)):
                    parts_ref[i * SPLITS + s, at[a], :] = part

    group = node_hot_ref.shape[1] // BLOCK

    width = 4 * block_count
    total = jnp.zeros((SPLITS * width, BLOCK), jnp.float32)
    for step in range(all_rows // group):
        lefts = []
        for r in range(step * group, (step + 1) * group):
            terms = [parts_ref[c * SPLITS + s, r : r + 1, :] for s in range(SPLITS) for c in range(4)]
            lefts.append(placed(terms, nodes_ref[r : r + 1, :], block_count))
        total = total + hot_dot(jnp.concatenate(lefts, axis=1), node_hot_ref[step])
    total = sum(total[s * width : (s + 1) * width, :] for s in range(SPLITS))
    owned = 2 * owned_slots
    for c in range(4):
        own_ref[c * owned : (c + 1) * owned, :] = total[c * block_count : c * block_count + owned, :]
        for k in range(6):
            first = c * block_count + owned + 2 * k
            cut_ref[k, 2 * c : 2 * c + 2, :] = total[first : first + 2, :]
    send_pairs(counts, cut_ref, send_refs, [(1, 0), (3, 2), (5, 4)])


def placed_few(values, ids, block_count):
    each = 8 // block_count
    rows = lax.broadcasted_iota(jnp.int32, (8, BLOCK), 0)
    hit = (rows & (block_count - 1)) == jnp.broadcast_to(ids >> 7, rows.shape)
    left = []
    for first in range(0, len(values), each):
        tile = jnp.broadcast_to(values[first], rows.shape)
        for i in range(1, each):
            tile = jnp.where(rows >= i * block_count, jnp.broadcast_to(values[first + i], rows.shape), tile)
        left.append(jnp.where(hit, tile, 0.0))
    return jnp.concatenate(left, axis=0).astype(jnp.bfloat16)


def add_returned(total, came_refs, directions, halos_ref, halo_hot_ref):
    owned = total.shape[0] // 4
    lefts, rights = [], []
    for ref, k in zip(came_refs, directions):
        parts = cut_parts(ref[...])
        for h in range(2):
            terms = [parts[s][2 * c + h : 2 * c + h + 1, :] for s in range(SPLITS) for c in range(4)]
            lefts.append(placed_few(terms, halos_ref[pl.ds(2 * k + h, 1), :], owned))
            rights.append(halo_hot_ref[pl.ds(pl.multiple_of((2 * k + h) * BLOCK, BLOCK), BLOCK), :])
    sums = hot_dot(jnp.concatenate(lefts, axis=1), jnp.concatenate(rights, axis=0))
    width = 4 * owned
    return total + sum(sums[s * width : (s + 1) * width, :] for s in range(SPLITS))


def back_directions(counts):
    places = pair_places()
    long = [axis for axis in range(3) if counts[axis] > 2]
    return [2 * axis + 1 - places[axis] for axis in long] + [2 * axis + places[axis] for axis in range(3)]


def early_residual_kernel(counts, own_ref, halos_ref, halo_hot_ref, state_in_ref, *refs):
    refs, state_ref = refs[:-1], refs[-1]
    state_ref[...] = state_in_ref[...]
    directions = [k for k, axis in zip(back_directions(counts), moved_axes(counts)) if axis == 0][::-1]
    refs[-1][...] = add_returned(own_ref[...], refs[:-1], directions, halos_ref, halo_hot_ref)


def residual_kernel(counts, sums_ref, halos_ref, halo_hot_ref, *refs):
    directions = [k for k, axis in zip(back_directions(counts), moved_axes(counts)) if axis != 0]
    total = add_returned(sums_ref[...], refs[:-1], directions, halos_ref, halo_hot_ref)
    owned = total.shape[0] // 4
    for c in range(4):
        for b in range(owned):
            r = c * owned + b
            refs[-1][c : c + 1, b * BLOCK : (b + 1) * BLOCK] = total[r : r + 1, :]


def shaped(*shape):
    return jax.ShapeDtypeStruct(shape, jnp.float32)


def per_device(
    sizes,
    old_state,
    send_blocks,
    node_slots,
    node_weights,
    front_mask,
    halo_lists,
    elem_nodes,
    shape_grads,
    elem_volume,
):
    old_state, send_blocks = old_state[0, 0, 0], send_blocks[0, 0, 0]
    slots = send_blocks.shape[1]
    send_blocks = send_blocks.reshape(-1, 1, slots)
    rows = FIELDS * slots
    arguments = [
        node_slots[0, 0, 0],
        node_weights[0, 0, 0],
        front_mask.reshape(-1, BLOCK),
        halo_lists.reshape(halo_lists.shape[-2], 1, -1),
        elem_nodes[0, 0, 0],
        shape_grads.reshape(-1, BLOCK),
        elem_volume[0, 0],
        send_blocks,
    ]
    old_rows = old_state.reshape(-1, BLOCK)
    count = len(arguments)
    owned = node_slots.shape[-1]
    slot_rows = node_slots.size // BLOCK
    give_rows = 2 * rows + 2 * slot_rows
    give_first, give, old_rows, *held = pl.pallas_call(
        functools.partial(give_kernel, count),
        out_shape=[shaped(2 * rows, BLOCK), shaped(give_rows, BLOCK), shaped(*old_rows.shape)]
        + [jax.ShapeDtypeStruct(a.shape, a.dtype) for a in arguments],
        in_specs=[pl.BlockSpec(memory_space=pltpu.HBM)] * (2 + count),
        out_specs=[VMEM] * (3 + count),
        scratch_shapes=[pltpu.SMEM(send_blocks.shape, jnp.int32), pltpu.SemaphoreType.DMA((2 + count,))],
        compiler_params=params(),
    )(*(pltpu.with_memory_space_constraint(a, pltpu.HBM) for a in (send_blocks, old_rows, *arguments)))
    node_slots, node_weights, mask_rows, halos, elem_nodes, grad_rows, volume, held_blocks = held
    first, second = pl.pallas_call(
        keep_kernel,
        out_shape=(shaped(2 * rows, BLOCK),) * 2,
        in_specs=[SMEM, VMEM],
        out_specs=(VMEM,) * 2,
        compiler_params=params(),
    )(held_blocks, old_rows)
    layers = both_ways([(0, 1)])
    got_first = lax.ppermute(give_first, "layer", layers)
    got = lax.ppermute(give, "layer", layers)
    full = [jnp.concatenate([first, got_first]), jnp.concatenate([second, got[: 2 * rows]])]
    first, second = [
        lax.ppermute(part, ("mapx", "layer"), pairs).reshape(4, rows, BLOCK)
        for part, pairs in zip(full, column_moves(sizes[0]))
    ]
    other_slots, other_weights = got[2 * rows : 2 * rows + slot_rows], got[2 * rows + slot_rows :]

    all_rows = elem_nodes.size // BLOCK
    halo_count = halos.size // BLOCK
    hot_steps = next(n for n in (8, 4, 2, 1) if all_rows % n == 0)
    whole = lambda *shape: jax.ShapeDtypeStruct(shape, jnp.int32)
    found, slots_cut, weights_cut, halos_cut, nodes_cut, volume_cut, halo_hot, node_hot = pl.pallas_call(
        own_kernel,
        out_shape=(
            shaped(2, FIELDS, slot_rows, BLOCK),
            whole(2, slot_rows, BLOCK),
            shaped(slot_rows, BLOCK),
            whole(halo_count, BLOCK),
            whole(all_rows, BLOCK),
            shaped(all_rows // 4, BLOCK),
            jax.ShapeDtypeStruct((halo_count * BLOCK, BLOCK), jnp.bfloat16),
            jax.ShapeDtypeStruct((hot_steps, all_rows // hot_steps * BLOCK, BLOCK), jnp.bfloat16),
        ),
        in_specs=[SMEM] + [VMEM] * 7,
        out_specs=(VMEM,) * 8,
        scratch_shapes=[pltpu.VMEM((2, rows, BLOCK), jnp.float32)],
        compiler_params=params(),
    )(held_blocks, old_rows, other_slots, node_slots, node_weights, halos, elem_nodes, volume)
    found = pl.pallas_call(
        early_kernel,
        out_shape=shaped(2, FIELDS, slot_rows, BLOCK),
        in_specs=[VMEM] * 3,
        out_specs=VMEM,
        compiler_params=params(),
    )(first, slots_cut, found)
    state_rows = FIELDS * owned // BLOCK
    mine, other = pl.pallas_call(
        functools.partial(late_kernel, owned // BLOCK),
        out_shape=(shaped(state_rows, BLOCK),) * 2,
        in_specs=[VMEM] * 5,
        out_specs=(VMEM,) * 2,
        compiler_params=params(),
    )(second, slots_cut, found, weights_cut, other_weights)
    other = lax.ppermute(other, "layer", layers)
    moves = 3 + sum(size > 2 for size in sizes)
    chunk = (2 * FIELDS, BLOCK)
    new_state, table, *ghosts = pl.pallas_call(
        functools.partial(state_kernel, sizes),
        out_shape=(shaped(state_rows, BLOCK), shaped(owned // (2 * BLOCK), *chunk)) + (shaped(*chunk),) * moves,
        in_specs=[VMEM] * 4,
        out_specs=(VMEM,) * (2 + moves),
        scratch_shapes=[pltpu.VMEM((6, *chunk), jnp.float32)],
        compiler_params=params(),
    )(mine, other, mask_rows, halos_cut)
    ghosts = swap_all(ghosts, sizes)

    owned_slots = table.shape[0]
    early = [ghost for ghost, axis in zip(ghosts, moved_axes(sizes)) if axis == 0]
    late = [ghost for ghost, axis in zip(ghosts, moved_axes(sizes)) if axis != 0]
    values = pl.pallas_call(
        functools.partial(values_kernel, sizes),
        out_shape=shaped(FIELDS, all_rows, BLOCK),
        in_specs=[VMEM] * (2 + len(early)),
        out_specs=VMEM,
        compiler_params=params(),
    )(table, nodes_cut, *early)
    own, *sums = pl.pallas_call(
        functools.partial(element_kernel, sizes, moves, owned_slots),
        out_shape=(shaped(4 * owned // BLOCK, BLOCK),) + (shaped(8, BLOCK),) * moves,
        in_specs=[VMEM] * (5 + len(late)),
        out_specs=(VMEM,) * (1 + moves),
        scratch_shapes=[
            pltpu.VMEM((FIELDS, all_rows, BLOCK), jnp.float32),
            pltpu.VMEM((4 * SPLITS, all_rows, BLOCK), jnp.float32),
            pltpu.VMEM((6, 8, BLOCK), jnp.float32),
        ],
        compiler_params=params(),
    )(values, nodes_cut, node_hot, grad_rows, volume_cut, *late)
    sums = swap_all(sums, sizes)
    early = [came for came, axis in zip(sums, moved_axes(sizes)) if axis == 0][::-1]
    late = [came for came, axis in zip(sums, moved_axes(sizes)) if axis != 0]
    own, new_state = pl.pallas_call(
        functools.partial(early_residual_kernel, sizes),
        out_shape=(shaped(*own.shape), shaped(*new_state.shape)),
        in_specs=[VMEM] * (4 + len(early)),
        out_specs=(VMEM,) * 2,
        compiler_params=params(),
    )(own, halos_cut, halo_hot, new_state, *early)
    residual = pl.pallas_call(
        functools.partial(residual_kernel, sizes),
        out_shape=shaped(4, owned),
        in_specs=[VMEM] * (3 + len(late)),
        out_specs=VMEM,
        compiler_params=params(),
    )(own, halos_cut, halo_hot, *late)
    return (new_state.reshape(1, 1, 1, FIELDS, owned), residual[None, None, None])


def solution(mesh):
    sizes = tuple(mesh.shape[axis] for axis in AXES)
    row = P("mapx", "mapy", "layer", None)
    table = P("mapx", "mapy", "layer", None, None)
    return jax.shard_map(
        functools.partial(per_device, sizes),
        mesh=mesh,
        in_specs=(table, table, table, table, row, table, table, table, row),
        out_specs=(table, table),
        check_vma=False,
    )
```

```python
import functools

import jax
import jax.numpy as jnp
from jax import lax
from jax.experimental import pallas as pl
from jax.experimental.pallas import tpu as pltpu
from jax.sharding import PartitionSpec as P

BLOCK = 128
REACH = 2
FIELDS = 6
SPLITS = 3

ocean_temp = 0.0
strain_reg = 0.01
gravity = 0.5

AXES = ("mapx", "mapy", "layer")
VMEM = pl.BlockSpec(memory_space=pltpu.VMEM)
SMEM = pl.BlockSpec(memory_space=pltpu.SMEM)


def params():
    return pltpu.CompilerParams(vmem_limit_bytes=32 * 1024 * 1024)


def both_ways(pairs):
    return [way for one, other in pairs for way in ((one, other), (other, one))]


def column_moves(count):
    outside = [(at, at + 1) for at in range(1, count - 1, 2)]
    inside = [(at, at + 1) for at in range(0, count - 1, 2)]
    within = [(at + i, at + i + 2) for at in range(0, count - 3, 4) for i in range(2)]
    across = [(at + i, at + i + 2) for at in range(2, count - 3, 4) for i in range(2)]
    number = lambda pairs, layer: [(one * 2 + layer, other * 2 + layer) for one, other in pairs]
    return [
        both_ways(number(outside, 1) + number(inside, 0)),
        both_ways(number(within, 0) + number(across, 1)),
    ]


def column_offsets(layer):
    at = lax.axis_index("mapx")
    near = jnp.where(lax.rem(at, 2) == 0, 1, -1)
    two = jnp.where(lax.rem(at, 4) < 2, 2, -2)
    return [jnp.where(layer == 0, near, -near), jnp.where(layer == 0, two, -two)]


def pair_swap(value, axis, count, first):
    return lax.ppermute(value, axis, both_ways([(at, at + 1) for at in range(first, count - 1, 2)]))


def swap_all(values, sizes):
    long = [axis for axis in range(3) if sizes[axis] > 2]
    steps = [(axis, 1) for axis in long] + [(axis, 0) for axis in range(3)]
    return [pair_swap(value, AXES[axis], sizes[axis], first) for value, (axis, first) in zip(values, steps)]


def pack_blocks(blocks_ref, old_ref, ref, offset):
    slots = blocks_ref.shape[2]
    stride = old_ref.shape[0] // FIELDS
    for to_layer in range(2):
        peer = (offset + REACH) * 2 + to_layer
        start = to_layer * FIELDS * slots
        for c in range(slots):
            rows = pl.ds(blocks_ref[peer, 0, c], FIELDS, stride=stride)
            ref[start + FIELDS * c : start + FIELDS * (c + 1), :] = old_ref[rows, :]


def give_kernel(count, *refs):
    blocks_in_ref, old_in_ref = refs[:2]
    give_first_ref, give_ref, old_ref = refs[2 + count : 5 + count]
    held = refs[5 + count : 5 + 2 * count]
    blocks_ref, sems = refs[5 + 2 * count :]
    first = [pltpu.make_async_copy(blocks_in_ref, blocks_ref, sems.at[0])]
    first += [pltpu.make_async_copy(old_in_ref, old_ref, sems.at[1])]
    rest = [pltpu.make_async_copy(refs[2 + i], held[i], sems.at[2 + i]) for i in range(count)]
    for copy in first + rest:
        copy.start()
    for copy in first:
        copy.wait()
    offsets = column_offsets(1 - lax.axis_index("layer"))
    pack_blocks(blocks_ref, old_ref, give_first_ref, offsets[0])
    pack_blocks(blocks_ref, old_ref, give_ref, offsets[1])
    for copy in rest:
        copy.wait()
    size = give_first_ref.shape[0]
    slots_ref, weights_ref = held[0], held[1]
    slot_rows = slots_ref.shape[0] * slots_ref.shape[1] // BLOCK
    cut_rows(slots_ref, give_ref.at[size : size + slot_rows])
    cut_rows(weights_ref, give_ref.at[size + slot_rows : size + 2 * slot_rows])


def keep_kernel(blocks_ref, old_ref, first_ref, second_ref):
    offsets = column_offsets(lax.axis_index("layer"))
    pack_blocks(blocks_ref, old_ref, first_ref, offsets[0])
    pack_blocks(blocks_ref, old_ref, second_ref, offsets[1])


def pick(row, lanes):
    return jnp.take_along_axis(jnp.broadcast_to(row, lanes.shape), lanes, axis=1)


def pick_fields(table_ref, block_count, blocks, lanes):
    found = [jnp.zeros((8, BLOCK), jnp.float32) for _ in range(FIELDS)]
    for b in range(block_count):
        hit = blocks == b
        for f in range(FIELDS):
            row = table_ref[b // 2, 2 * f + b % 2 : 2 * f + b % 2 + 1, :]
            found[f] = jnp.where(hit, pick(row, lanes), found[f])
    return found


def add_blocks(ref, chunk, first_block, blocks, lanes, found):
    local = blocks - first_block
    found = list(found)
    for c in range(ref.shape[1] // FIELDS):
        hit = local == c
        for f in range(FIELDS):
            row = ref[chunk, FIELDS * c + f : FIELDS * c + f + 1, :]
            found[f] = jnp.where(hit, pick(row, lanes), found[f])
    return tuple(found)


def add_chunks(ref, numbers, offset, ids, found):
    blocks, lanes = ids >> 7, ids & (BLOCK - 1)
    for chunk, layer in numbers:
        first = ((offset + REACH) * 2 + layer) * (ref.shape[1] // FIELDS)
        found = add_blocks(ref, chunk, first, blocks, lanes, found)
    return found


def load_fields(found_ref, owner, v):
    return tuple(found_ref[owner, f, 8 * v : 8 * v + 8, :] for f in range(FIELDS))


def save_fields(found_ref, owner, v, found):
    for f in range(FIELDS):
        found_ref[owner, f, 8 * v : 8 * v + 8, :] = found[f]


def arrived_chunks(ref, move, ids, found, owner):
    layer = lax.axis_index("layer")
    to_layer = 1 - layer if owner else layer
    numbers = [(to_layer, layer), (2 + to_layer, 1 - layer)]
    return add_chunks(ref, numbers, column_offsets(layer)[move], ids, found)


def cut_rows(from_ref, to_ref):
    count = from_ref.shape[1] // BLOCK
    for r in range(from_ref.shape[0]):
        for i in range(count):
            to_ref[r * count + i : r * count + i + 1, :] = from_ref[
                r : r + 1, i * BLOCK : (i + 1) * BLOCK
            ].astype(to_ref.dtype)


def lane_one_hot(ids):
    rows = lax.broadcasted_iota(jnp.int32, (BLOCK, BLOCK), 0)
    hit = rows == jnp.broadcast_to(ids & (BLOCK - 1), rows.shape)
    return jnp.where(hit, 1.0, 0.0).T.astype(jnp.bfloat16)


def own_kernel(
    blocks_ref,
    old_ref,
    other_slots_ref,
    slots_in_ref,
    weights_in_ref,
    halos_in_ref,
    nodes_in_ref,
    volume_in_ref,
    found_ref,
    slots_ref,
    weights_ref,
    halos_ref,
    nodes_ref,
    volume_ref,
    halo_hot_ref,
    node_hot_ref,
    own_ref,
):
    for layer in range(2):
        chunk_ref = own_ref.at[layer]
        for c in range(blocks_ref.shape[2]):
            rows = pl.ds(blocks_ref[2 * REACH + layer, 0, c], FIELDS, stride=old_ref.shape[0] // FIELDS)
            chunk_ref[FIELDS * c : FIELDS * (c + 1), :] = old_ref[rows, :]
    for k in range(halos_in_ref.shape[0]):
        cut_rows(halos_in_ref.at[k], halos_ref.at[2 * k : 2 * k + 2])
    cut_rows(slots_in_ref, slots_ref.at[0])
    slots_ref[1] = other_slots_ref[...].astype(jnp.int32)
    cut_rows(weights_in_ref, weights_ref)
    cut_rows(nodes_in_ref, nodes_ref)
    cut_rows(volume_in_ref, volume_ref)
    layer = lax.axis_index("layer")
    for owner in range(2):
        for v in range(slots_ref.shape[1] // 8):
            ids = slots_ref[owner, 8 * v : 8 * v + 8, :]
            found = tuple(jnp.zeros((8, BLOCK), jnp.float32) for _ in range(FIELDS))
            numbers = [(1 - layer if owner else layer, layer)]
            save_fields(found_ref, owner, v, add_chunks(own_ref, numbers, 0, ids, found))
    for r in range(halos_ref.shape[0]):
        halo_hot_ref[r * BLOCK : (r + 1) * BLOCK, :] = lane_one_hot(halos_ref[r : r + 1, :])
    steps, width, _ = node_hot_ref.shape
    group = width // BLOCK

    def hot(step, carry):
        for r in range(group):
            ids = nodes_ref[pl.ds(step * group + r, 1), :]
            node_hot_ref[step, r * BLOCK : (r + 1) * BLOCK, :] = lane_one_hot(ids)
        return carry

    lax.fori_loop(0, steps, hot, 0)


def early_kernel(came_ref, slots_ref, found_in_ref, found_ref):
    for owner in range(2):
        for v in range(slots_ref.shape[1] // 8):
            ids = slots_ref[owner, 8 * v : 8 * v + 8, :]
            found = arrived_chunks(came_ref, 0, ids, load_fields(found_in_ref, owner, v), owner)
            save_fields(found_ref, owner, v, found)


def late_kernel(rows, owner, came_ref, slots_ref, found_ref, weights_ref, out_ref):
    totals = [jnp.zeros((rows, BLOCK), jnp.float32) for _ in range(FIELDS)]
    for v in range(slots_ref.shape[1] // 8):
        ids = slots_ref[owner, 8 * v : 8 * v + 8, :]
        found = arrived_chunks(came_ref, 1, ids, load_fields(found_ref, owner, v), owner)
        for f in range(FIELDS):
            term = found[f] * weights_ref[8 * v : 8 * v + 8, :]
            for k in range(8 // rows):
                totals[f] = totals[f] + term[k * rows : (k + 1) * rows, :]
    for f in range(FIELDS):
        out_ref[f * rows : (f + 1) * rows, :] = totals[f]


def state_kernel(counts, mine_ref, came_ref, mask_ref, halos_ref, state_ref, table_ref, *more_refs):
    send_refs, cut_ref = more_refs[:-1], more_refs[-1]
    front = mask_ref[...] == 1
    rows = mask_ref.shape[0]
    for f in range(FIELDS):
        at = slice(f * rows, (f + 1) * rows)
        total = mine_ref[at, :] + came_ref[at, :]
        if f == 4:
            total = jnp.where(front, ocean_temp, total)
        state_ref[f * rows : (f + 1) * rows, :] = total
        for s in range(rows // 2):
            table_ref[s, 2 * f : 2 * f + 2, :] = total[2 * s : 2 * s + 2, :]
    starts = (0, halos_ref.shape[0] - 8)
    halo = [halos_ref[first : first + 8, :] for first in starts]
    halo_blocks = [i >> 7 for i in halo]
    halo_lanes = [i & (BLOCK - 1) for i in halo]
    for v in range(2):
        cut = pick_fields(table_ref, rows, halo_blocks[v], halo_lanes[v])
        for k in range(6):
            r = 2 * k - starts[v]
            if 0 <= r <= 6:
                for f in range(FIELDS):
                    cut_ref[k, 2 * f : 2 * f + 2, :] = cut[f][r : r + 2, :]
    send_pairs(counts, cut_ref, send_refs, [(0, 1), (2, 3), (4, 5)])


def pair_places():
    return [lax.rem(lax.axis_index(axis), 2) for axis in AXES]


def send_pairs(counts, cut_ref, send_refs, order):
    places = pair_places()
    long = [axis for axis in range(3) if counts[axis] > 2]
    for axis in range(3):
        even, odd = order[axis]
        send_refs[len(long) + axis][...] = cut_ref[jnp.where(places[axis] == 0, even, odd)]
        if axis in long:
            send_refs[long.index(axis)][...] = cut_ref[jnp.where(places[axis] == 0, odd, even)]


def placed(values, ids, block_count):
    rows = lax.broadcasted_iota(jnp.int32, (block_count, BLOCK), 0)
    hit = rows == jnp.broadcast_to(ids >> 7, rows.shape)
    left = [jnp.where(hit, jnp.broadcast_to(v, rows.shape), 0.0) for v in values]
    return jnp.concatenate(left, axis=0).astype(jnp.bfloat16)


def cut_parts(value):
    parts = []
    for _ in range(SPLITS - 1):
        part = value.astype(jnp.bfloat16).astype(jnp.float32)
        parts.append(part)
        value = value - part
    return parts + [value]


def hot_dot(left, right):
    return jnp.dot(left, right, preferred_element_type=jnp.float32)


def came_slots(counts):
    places = pair_places()
    long = [axis for axis in range(3) if counts[axis] > 2]
    slots = []
    for axis in long:
        at = lax.axis_index(AXES[axis])
        edge = jnp.where(places[axis] == 0, at == 0, at == counts[axis] - 1)
        slots.append(jnp.where(edge, -(1 << 10), 2 * axis + places[axis]))
    return slots + [2 * axis + 1 - places[axis] for axis in range(3)]


def moved_axes(counts):
    return [axis for axis in range(3) if counts[axis] > 2] + [0, 1, 2]


def add_slot(read, slot, ids, found):
    blocks, lanes = (ids >> 7) - 2 * slot, ids & (BLOCK - 1)
    found = list(found)
    for h in range(2):
        hit = blocks == h
        for f in range(FIELDS):
            found[f] = jnp.where(hit, pick(read(2 * f + h), lanes), found[f])
    return found


def values_kernel(counts, table_ref, nodes_ref, *refs):
    came_refs, values_ref = refs[:-1], refs[-1]
    owned_slots = table_ref.shape[0]
    slots = [slot for slot, axis in zip(came_slots(counts), moved_axes(counts)) if axis == 0]
    for first in range(0, nodes_ref.shape[0], 8):
        ids = nodes_ref[first : first + 8, :]
        found = [jnp.zeros((8, BLOCK), jnp.float32) for _ in range(FIELDS)]
        for s in range(owned_slots):
            found = add_slot(lambda r: table_ref[s, r : r + 1, :], s, ids, found)
        for ref, slot in zip(came_refs, slots):
            found = add_slot(lambda r: ref[r : r + 1, :], owned_slots + slot, ids, found)
        for f in range(FIELDS):
            values_ref[f, first : first + 8, :] = found[f]


def element_kernel(counts, moves, owned_slots, *refs):
    values_in_ref, nodes_ref, node_hot_ref, grads_ref, volume_ref = refs[:5]
    last = [slot for slot, axis in zip(came_slots(counts), moved_axes(counts)) if axis != 0]
    came_refs, refs = refs[5 : 5 + len(last)], refs[5 + len(last) :]
    own_ref, send_refs = refs[0], refs[1 : 1 + moves]
    values_ref, parts_ref, cut_ref = refs[1 + moves :]
    block_count = 2 * (owned_slots + 6)
    all_rows = nodes_ref.shape[0]
    elem_rows = all_rows // 4
    for first in range(0, all_rows, 8):
        ids = nodes_ref[first : first + 8, :]
        found = [values_in_ref[f, first : first + 8, :] for f in range(FIELDS)]
        for ref, slot in zip(came_refs, last):
            found = add_slot(lambda r: ref[r : r + 1, :], owned_slots + slot, ids, found)
        for f in range(FIELDS):
            values_ref[f, first : first + 8, :] = found[f]
    for first in [*range(0, elem_rows - 7, 8)] + ([elem_rows - 8] if elem_rows % 8 else []):
        at = [slice(r * elem_rows + first, r * elem_rows + first + 8) for r in range(12)]
        values = [[values_ref[f, at[a], :] for f in range(FIELDS)] for a in range(4)]
        grads = [[grads_ref[at[3 * a + j], :] for j in range(3)] for a in range(4)]
        volume = volume_ref[at[0], :]
        velgrad = [[sum(values[a][i] * grads[a][j] for a in range(4)) for j in range(3)] for i in range(3)]
        strain = [[0.5 * (velgrad[i][j] + velgrad[j][i]) if i <= j else None for j in range(3)] for i in range(3)]
        diagonal = sum(strain[i][i] * strain[i][i] for i in range(3))
        corner = sum(strain[i][j] * strain[i][j] for i, j in ((0, 1), (0, 2), (1, 2)))
        second = 0.5 * diagonal + corner
        pressure, temper, damage = [0.25 * (values[0][f] + values[1][f] + values[2][f] + values[3][f]) for f in (3, 4, 5)]
        root = jnp.exp(jnp.log(second + strain_reg) * (-1.0 / 3.0))
        twice = (1.0 - damage) * jnp.exp(-temper) * root
        stress = [[None] * 3 for _ in range(3)]
        for i in range(3):
            for j in range(i, 3):
                stress[i][j] = twice * strain[i][j] - (pressure if i == j else 0.0)
                stress[j][i] = stress[i][j]
        lift = (0.25 * gravity) * volume
        flow = 0.25 * volume * (velgrad[0][0] + velgrad[1][1] + velgrad[2][2])
        for s, part in enumerate(cut_parts(flow)):
            for a in range(4):
                parts_ref[3 * SPLITS + s, at[a], :] = part
        for a in range(4):
            for i in range(3):
                force = volume * sum(stress[i][j] * grads[a][j] for j in range(3))
                if i == 2:
                    force = force + lift
                for s, part in enumerate(cut_parts(force)):
                    parts_ref[i * SPLITS + s, at[a], :] = part

    group = node_hot_ref.shape[1] // BLOCK

    width = 4 * block_count
    total = jnp.zeros((SPLITS * width, BLOCK), jnp.float32)
    for step in range(all_rows // group):
        lefts = []
        for r in range(step * group, (step + 1) * group):
            terms = [parts_ref[c * SPLITS + s, r : r + 1, :] for s in range(SPLITS) for c in range(4)]
            lefts.append(placed(terms, nodes_ref[r : r + 1, :], block_count))
        total = total + hot_dot(jnp.concatenate(lefts, axis=1), node_hot_ref[step])
    total = sum(total[s * width : (s + 1) * width, :] for s in range(SPLITS))
    owned = 2 * owned_slots
    for c in range(4):
        own_ref[c * owned : (c + 1) * owned, :] = total[c * block_count : c * block_count + owned, :]
        for k in range(6):
            first = c * block_count + owned + 2 * k
            cut_ref[k, 2 * c : 2 * c + 2, :] = total[first : first + 2, :]
    send_pairs(counts, cut_ref, send_refs, [(1, 0), (3, 2), (5, 4)])


def placed_few(values, ids, block_count):
    each = 8 // block_count
    rows = lax.broadcasted_iota(jnp.int32, (8, BLOCK), 0)
    hit = (rows & (block_count - 1)) == jnp.broadcast_to(ids >> 7, rows.shape)
    left = []
    for first in range(0, len(values), each):
        tile = jnp.broadcast_to(values[first], rows.shape)
        for i in range(1, each):
            tile = jnp.where(rows >= i * block_count, jnp.broadcast_to(values[first + i], rows.shape), tile)
        left.append(jnp.where(hit, tile, 0.0))
    return jnp.concatenate(left, axis=0).astype(jnp.bfloat16)


def add_returned(total, came_refs, directions, halos_ref, halo_hot_ref):
    owned = total.shape[0] // 4
    lefts, rights = [], []
    for ref, k in zip(came_refs, directions):
        parts = cut_parts(ref[...])
        for h in range(2):
            terms = [parts[s][2 * c + h : 2 * c + h + 1, :] for s in range(SPLITS) for c in range(4)]
            lefts.append(placed_few(terms, halos_ref[pl.ds(2 * k + h, 1), :], owned))
            rights.append(halo_hot_ref[pl.ds(pl.multiple_of((2 * k + h) * BLOCK, BLOCK), BLOCK), :])
    sums = hot_dot(jnp.concatenate(lefts, axis=1), jnp.concatenate(rights, axis=0))
    width = 4 * owned
    return total + sum(sums[s * width : (s + 1) * width, :] for s in range(SPLITS))


def back_directions(counts):
    places = pair_places()
    long = [axis for axis in range(3) if counts[axis] > 2]
    return [2 * axis + 1 - places[axis] for axis in long] + [2 * axis + places[axis] for axis in range(3)]


def early_residual_kernel(counts, own_ref, halos_ref, halo_hot_ref, state_in_ref, *refs):
    refs, state_ref = refs[:-1], refs[-1]
    state_ref[...] = state_in_ref[...]
    directions = [k for k, axis in zip(back_directions(counts), moved_axes(counts)) if axis == 0][::-1]
    refs[-1][...] = add_returned(own_ref[...], refs[:-1], directions, halos_ref, halo_hot_ref)


def residual_kernel(counts, sums_ref, halos_ref, halo_hot_ref, *refs):
    directions = [k for k, axis in zip(back_directions(counts), moved_axes(counts)) if axis != 0]
    total = add_returned(sums_ref[...], refs[:-1], directions, halos_ref, halo_hot_ref)
    owned = total.shape[0] // 4
    for c in range(4):
        for b in range(owned):
            r = c * owned + b
            refs[-1][c : c + 1, b * BLOCK : (b + 1) * BLOCK] = total[r : r + 1, :]


def shaped(*shape):
    return jax.ShapeDtypeStruct(shape, jnp.float32)


def per_device(
    sizes,
    old_state,
    send_blocks,
    node_slots,
    node_weights,
    front_mask,
    halo_lists,
    elem_nodes,
    shape_grads,
    elem_volume,
):
    old_state, send_blocks = old_state[0, 0, 0], send_blocks[0, 0, 0]
    slots = send_blocks.shape[1]
    send_blocks = send_blocks.reshape(-1, 1, slots)
    rows = FIELDS * slots
    arguments = [
        node_slots[0, 0, 0],
        node_weights[0, 0, 0],
        front_mask.reshape(-1, BLOCK),
        halo_lists.reshape(halo_lists.shape[-2], 1, -1),
        elem_nodes[0, 0, 0],
        shape_grads.reshape(-1, BLOCK),
        elem_volume[0, 0],
        send_blocks,
    ]
    old_rows = old_state.reshape(-1, BLOCK)
    count = len(arguments)
    owned = node_slots.shape[-1]
    slot_rows = node_slots.size // BLOCK
    give_rows = 2 * rows + 2 * slot_rows
    give_first, give, old_rows, *held = pl.pallas_call(
        functools.partial(give_kernel, count),
        out_shape=[shaped(2 * rows, BLOCK), shaped(give_rows, BLOCK), shaped(*old_rows.shape)]
        + [jax.ShapeDtypeStruct(a.shape, a.dtype) for a in arguments],
        in_specs=[pl.BlockSpec(memory_space=pltpu.HBM)] * (2 + count),
        out_specs=[VMEM] * (3 + count),
        scratch_shapes=[pltpu.SMEM(send_blocks.shape, jnp.int32), pltpu.SemaphoreType.DMA((2 + count,))],
        compiler_params=params(),
    )(*(pltpu.with_memory_space_constraint(a, pltpu.HBM) for a in (send_blocks, old_rows, *arguments)))
    node_slots, node_weights, mask_rows, halos, elem_nodes, grad_rows, volume, held_blocks = held
    first, second = pl.pallas_call(
        keep_kernel,
        out_shape=(shaped(2 * rows, BLOCK),) * 2,
        in_specs=[SMEM, VMEM],
        out_specs=(VMEM,) * 2,
        compiler_params=params(),
    )(held_blocks, old_rows)
    layers = both_ways([(0, 1)])
    got_first = lax.ppermute(give_first, "layer", layers)
    got = lax.ppermute(give, "layer", layers)
    full = [jnp.concatenate([first, got_first]), jnp.concatenate([second, got[: 2 * rows]])]
    first, second = [
        lax.ppermute(part, ("mapx", "layer"), pairs).reshape(4, rows, BLOCK)
        for part, pairs in zip(full, column_moves(sizes[0]))
    ]
    other_slots, other_weights = got[2 * rows : 2 * rows + slot_rows], got[2 * rows + slot_rows :]

    all_rows = elem_nodes.size // BLOCK
    halo_count = halos.size // BLOCK
    hot_steps = next(n for n in (8, 4, 2, 1) if all_rows % n == 0)
    whole = lambda *shape: jax.ShapeDtypeStruct(shape, jnp.int32)
    found, slots_cut, weights_cut, halos_cut, nodes_cut, volume_cut, halo_hot, node_hot = pl.pallas_call(
        own_kernel,
        out_shape=(
            shaped(2, FIELDS, slot_rows, BLOCK),
            whole(2, slot_rows, BLOCK),
            shaped(slot_rows, BLOCK),
            whole(halo_count, BLOCK),
            whole(all_rows, BLOCK),
            shaped(all_rows // 4, BLOCK),
            jax.ShapeDtypeStruct((halo_count * BLOCK, BLOCK), jnp.bfloat16),
            jax.ShapeDtypeStruct((hot_steps, all_rows // hot_steps * BLOCK, BLOCK), jnp.bfloat16),
        ),
        in_specs=[SMEM] + [VMEM] * 7,
        out_specs=(VMEM,) * 8,
        scratch_shapes=[pltpu.VMEM((2, rows, BLOCK), jnp.float32)],
        compiler_params=params(),
    )(held_blocks, old_rows, other_slots, node_slots, node_weights, halos, elem_nodes, volume)
    found = pl.pallas_call(
        early_kernel,
        out_shape=shaped(2, FIELDS, slot_rows, BLOCK),
        in_specs=[VMEM] * 3,
        out_specs=VMEM,
        compiler_params=params(),
    )(first, slots_cut, found)
    state_rows = FIELDS * owned // BLOCK
    other, mine = [
        pl.pallas_call(
            functools.partial(late_kernel, owned // BLOCK, owner),
            out_shape=shaped(state_rows, BLOCK),
            in_specs=[VMEM] * 4,
            out_specs=VMEM,
            compiler_params=params(),
        )(second, slots_cut, found, weights)
        for owner, weights in ((1, other_weights), (0, weights_cut))
    ]
    other = lax.ppermute(other, "layer", layers)
    moves = 3 + sum(size > 2 for size in sizes)
    chunk = (2 * FIELDS, BLOCK)
    new_state, table, *ghosts = pl.pallas_call(
        functools.partial(state_kernel, sizes),
        out_shape=(shaped(state_rows, BLOCK), shaped(owned // (2 * BLOCK), *chunk)) + (shaped(*chunk),) * moves,
        in_specs=[VMEM] * 4,
        out_specs=(VMEM,) * (2 + moves),
        scratch_shapes=[pltpu.VMEM((6, *chunk), jnp.float32)],
        compiler_params=params(),
    )(mine, other, mask_rows, halos_cut)
    ghosts = swap_all(ghosts, sizes)

    owned_slots = table.shape[0]
    early = [ghost for ghost, axis in zip(ghosts, moved_axes(sizes)) if axis == 0]
    late = [ghost for ghost, axis in zip(ghosts, moved_axes(sizes)) if axis != 0]
    values = pl.pallas_call(
        functools.partial(values_kernel, sizes),
        out_shape=shaped(FIELDS, all_rows, BLOCK),
        in_specs=[VMEM] * (2 + len(early)),
        out_specs=VMEM,
        compiler_params=params(),
    )(table, nodes_cut, *early)
    own, *sums = pl.pallas_call(
        functools.partial(element_kernel, sizes, moves, owned_slots),
        out_shape=(shaped(4 * owned // BLOCK, BLOCK),) + (shaped(8, BLOCK),) * moves,
        in_specs=[VMEM] * (5 + len(late)),
        out_specs=(VMEM,) * (1 + moves),
        scratch_shapes=[
            pltpu.VMEM((FIELDS, all_rows, BLOCK), jnp.float32),
            pltpu.VMEM((4 * SPLITS, all_rows, BLOCK), jnp.float32),
            pltpu.VMEM((6, 8, BLOCK), jnp.float32),
        ],
        compiler_params=params(),
    )(values, nodes_cut, node_hot, grad_rows, volume_cut, *late)
    sums = swap_all(sums, sizes)
    early = [came for came, axis in zip(sums, moved_axes(sizes)) if axis == 0][::-1]
    late = [came for came, axis in zip(sums, moved_axes(sizes)) if axis != 0]
    own, new_state = pl.pallas_call(
        functools.partial(early_residual_kernel, sizes),
        out_shape=(shaped(*own.shape), shaped(*new_state.shape)),
        in_specs=[VMEM] * (4 + len(early)),
        out_specs=(VMEM,) * 2,
        compiler_params=params(),
    )(own, halos_cut, halo_hot, new_state, *early)
    residual = pl.pallas_call(
        functools.partial(residual_kernel, sizes),
        out_shape=shaped(4, owned),
        in_specs=[VMEM] * (3 + len(late)),
        out_specs=VMEM,
        compiler_params=params(),
    )(own, halos_cut, halo_hot, *late)
    return (new_state.reshape(1, 1, 1, FIELDS, owned), residual[None, None, None])


def solution(mesh):
    sizes = tuple(mesh.shape[axis] for axis in AXES)
    row = P("mapx", "mapy", "layer", None)
    table = P("mapx", "mapy", "layer", None, None)
    return jax.shard_map(
        functools.partial(per_device, sizes),
        mesh=mesh,
        in_specs=(table, table, table, table, row, table, table, table, row),
        out_specs=(table, table),
        check_vma=False,
    )
```

```python
import functools

import jax
import jax.numpy as jnp
from jax import lax
from jax.experimental import pallas as pl
from jax.experimental.pallas import tpu as pltpu
from jax.sharding import PartitionSpec as P

BLOCK = 128
REACH = 2
FIELDS = 6
SPLITS = 3

ocean_temp = 0.0
strain_reg = 0.01
gravity = 0.5

AXES = ("mapx", "mapy", "layer")
VMEM = pl.BlockSpec(memory_space=pltpu.VMEM)
SMEM = pl.BlockSpec(memory_space=pltpu.SMEM)


def params():
    return pltpu.CompilerParams(vmem_limit_bytes=32 * 1024 * 1024)


def both_ways(pairs):
    return [way for one, other in pairs for way in ((one, other), (other, one))]


def column_moves(count):
    outside = [(at, at + 1) for at in range(1, count - 1, 2)]
    inside = [(at, at + 1) for at in range(0, count - 1, 2)]
    within = [(at + i, at + i + 2) for at in range(0, count - 3, 4) for i in range(2)]
    across = [(at + i, at + i + 2) for at in range(2, count - 3, 4) for i in range(2)]
    number = lambda pairs, layer: [(one * 2 + layer, other * 2 + layer) for one, other in pairs]
    return [
        both_ways(number(outside, 1) + number(within, 0)),
        both_ways(number(inside, 0) + number(across, 1)),
    ]


def column_offsets(layer):
    at = lax.axis_index("mapx")
    near = jnp.where(lax.rem(at, 2) == 0, 1, -1)
    two = jnp.where(lax.rem(at, 4) < 2, 2, -2)
    return [jnp.where(layer == 0, two, -near), jnp.where(layer == 0, near, -two)]


def pair_swap(value, axis, count, first):
    return lax.ppermute(value, axis, both_ways([(at, at + 1) for at in range(first, count - 1, 2)]))


def swap_all(values, sizes):
    long = [axis for axis in range(3) if sizes[axis] > 2]
    steps = [(axis, 1) for axis in long] + [(axis, 0) for axis in range(3)]
    return [pair_swap(value, AXES[axis], sizes[axis], first) for value, (axis, first) in zip(values, steps)]


def pack_blocks(blocks_ref, old_ref, ref, offset):
    slots = blocks_ref.shape[2]
    stride = old_ref.shape[0] // FIELDS
    for to_layer in range(2):
        peer = (offset + REACH) * 2 + to_layer
        start = to_layer * FIELDS * slots
        for c in range(slots):
            rows = pl.ds(blocks_ref[peer, 0, c], FIELDS, stride=stride)
            ref[start + FIELDS * c : start + FIELDS * (c + 1), :] = old_ref[rows, :]


def give_kernel(count, *refs):
    blocks_in_ref, old_in_ref = refs[:2]
    give_first_ref, give_ref, old_ref = refs[2 + count : 5 + count]
    held = refs[5 + count : 5 + 2 * count]
    blocks_ref, sems = refs[5 + 2 * count :]
    first = [pltpu.make_async_copy(blocks_in_ref, blocks_ref, sems.at[0])]
    first += [pltpu.make_async_copy(old_in_ref, old_ref, sems.at[1])]
    rest = [pltpu.make_async_copy(refs[2 + i], held[i], sems.at[2 + i]) for i in range(count)]
    for copy in first + rest:
        copy.start()
    for copy in first:
        copy.wait()
    offsets = column_offsets(1 - lax.axis_index("layer"))
    pack_blocks(blocks_ref, old_ref, give_first_ref, offsets[0])
    pack_blocks(blocks_ref, old_ref, give_ref, offsets[1])
    for copy in rest:
        copy.wait()
    size = give_first_ref.shape[0]
    slots_ref, weights_ref = held[0], held[1]
    slot_rows = slots_ref.shape[0] * slots_ref.shape[1] // BLOCK
    cut_rows(slots_ref, give_ref.at[size : size + slot_rows])
    cut_rows(weights_ref, give_ref.at[size + slot_rows : size + 2 * slot_rows])


def keep_kernel(blocks_ref, old_ref, first_ref, second_ref):
    offsets = column_offsets(lax.axis_index("layer"))
    pack_blocks(blocks_ref, old_ref, first_ref, offsets[0])
    pack_blocks(blocks_ref, old_ref, second_ref, offsets[1])


def pick(row, lanes):
    return jnp.take_along_axis(jnp.broadcast_to(row, lanes.shape), lanes, axis=1)


def pick_fields(table_ref, block_count, blocks, lanes):
    found = [jnp.zeros((8, BLOCK), jnp.float32) for _ in range(FIELDS)]
    for b in range(block_count):
        hit = blocks == b
        for f in range(FIELDS):
            row = table_ref[b // 2, 2 * f + b % 2 : 2 * f + b % 2 + 1, :]
            found[f] = jnp.where(hit, pick(row, lanes), found[f])
    return found


def add_blocks(ref, chunk, first_block, blocks, lanes, found):
    local = blocks - first_block
    found = list(found)
    for c in range(ref.shape[1] // FIELDS):
        hit = local == c
        for f in range(FIELDS):
            row = ref[chunk, FIELDS * c + f : FIELDS * c + f + 1, :]
            found[f] = jnp.where(hit, pick(row, lanes), found[f])
    return tuple(found)


def add_chunks(ref, numbers, offset, ids, found):
    blocks, lanes = ids >> 7, ids & (BLOCK - 1)
    for chunk, layer in numbers:
        first = ((offset + REACH) * 2 + layer) * (ref.shape[1] // FIELDS)
        found = add_blocks(ref, chunk, first, blocks, lanes, found)
    return found


def load_fields(found_ref, owner, v):
    return tuple(found_ref[owner, f, 8 * v : 8 * v + 8, :] for f in range(FIELDS))


def save_fields(found_ref, owner, v, found):
    for f in range(FIELDS):
        found_ref[owner, f, 8 * v : 8 * v + 8, :] = found[f]


def arrived_chunks(ref, move, ids, found, owner):
    layer = lax.axis_index("layer")
    to_layer = 1 - layer if owner else layer
    numbers = [(to_layer, layer), (2 + to_layer, 1 - layer)]
    return add_chunks(ref, numbers, column_offsets(layer)[move], ids, found)


def cut_rows(from_ref, to_ref):
    count = from_ref.shape[1] // BLOCK
    for r in range(from_ref.shape[0]):
        for i in range(count):
            to_ref[r * count + i : r * count + i + 1, :] = from_ref[
                r : r + 1, i * BLOCK : (i + 1) * BLOCK
            ].astype(to_ref.dtype)


def lane_one_hot(ids):
    rows = lax.broadcasted_iota(jnp.int32, (BLOCK, BLOCK), 0)
    hit = rows == jnp.broadcast_to(ids & (BLOCK - 1), rows.shape)
    return jnp.where(hit, 1.0, 0.0).T.astype(jnp.bfloat16)


def own_kernel(
    blocks_ref,
    old_ref,
    other_slots_ref,
    slots_in_ref,
    weights_in_ref,
    halos_in_ref,
    nodes_in_ref,
    volume_in_ref,
    found_ref,
    slots_ref,
    weights_ref,
    halos_ref,
    nodes_ref,
    volume_ref,
    halo_hot_ref,
    node_hot_ref,
    own_ref,
):
    for layer in range(2):
        chunk_ref = own_ref.at[layer]
        for c in range(blocks_ref.shape[2]):
            rows = pl.ds(blocks_ref[2 * REACH + layer, 0, c], FIELDS, stride=old_ref.shape[0] // FIELDS)
            chunk_ref[FIELDS * c : FIELDS * (c + 1), :] = old_ref[rows, :]
    for k in range(halos_in_ref.shape[0]):
        cut_rows(halos_in_ref.at[k], halos_ref.at[2 * k : 2 * k + 2])
    cut_rows(slots_in_ref, slots_ref.at[0])
    slots_ref[1] = other_slots_ref[...].astype(jnp.int32)
    cut_rows(weights_in_ref, weights_ref)
    cut_rows(nodes_in_ref, nodes_ref)
    cut_rows(volume_in_ref, volume_ref)
    layer = lax.axis_index("layer")
    for owner in range(2):
        for v in range(slots_ref.shape[1] // 8):
            ids = slots_ref[owner, 8 * v : 8 * v + 8, :]
            found = tuple(jnp.zeros((8, BLOCK), jnp.float32) for _ in range(FIELDS))
            numbers = [(1 - layer if owner else layer, layer)]
            save_fields(found_ref, owner, v, add_chunks(own_ref, numbers, 0, ids, found))
    for r in range(halos_ref.shape[0]):
        halo_hot_ref[r * BLOCK : (r + 1) * BLOCK, :] = lane_one_hot(halos_ref[r : r + 1, :])
    steps, width, _ = node_hot_ref.shape
    group = width // BLOCK

    def hot(step, carry):
        for r in range(group):
            ids = nodes_ref[pl.ds(step * group + r, 1), :]
            node_hot_ref[step, r * BLOCK : (r + 1) * BLOCK, :] = lane_one_hot(ids)
        return carry

    lax.fori_loop(0, steps, hot, 0)


def early_kernel(came_ref, slots_ref, found_in_ref, found_ref):
    for owner in range(2):
        for v in range(slots_ref.shape[1] // 8):
            ids = slots_ref[owner, 8 * v : 8 * v + 8, :]
            found = arrived_chunks(came_ref, 0, ids, load_fields(found_in_ref, owner, v), owner)
            save_fields(found_ref, owner, v, found)


def late_kernel(rows, owner, came_ref, slots_ref, found_ref, weights_ref, out_ref):
    totals = [jnp.zeros((rows, BLOCK), jnp.float32) for _ in range(FIELDS)]
    for v in range(slots_ref.shape[1] // 8):
        ids = slots_ref[owner, 8 * v : 8 * v + 8, :]
        found = arrived_chunks(came_ref, 1, ids, load_fields(found_ref, owner, v), owner)
        for f in range(FIELDS):
            term = found[f] * weights_ref[8 * v : 8 * v + 8, :]
            for k in range(8 // rows):
                totals[f] = totals[f] + term[k * rows : (k + 1) * rows, :]
    for f in range(FIELDS):
        out_ref[f * rows : (f + 1) * rows, :] = totals[f]


def state_kernel(counts, mine_ref, came_ref, mask_ref, halos_ref, state_ref, table_ref, *more_refs):
    send_refs, cut_ref = more_refs[:-1], more_refs[-1]
    front = mask_ref[...] == 1
    rows = mask_ref.shape[0]
    for f in range(FIELDS):
        at = slice(f * rows, (f + 1) * rows)
        total = mine_ref[at, :] + came_ref[at, :]
        if f == 4:
            total = jnp.where(front, ocean_temp, total)
        state_ref[f * rows : (f + 1) * rows, :] = total
        for s in range(rows // 2):
            table_ref[s, 2 * f : 2 * f + 2, :] = total[2 * s : 2 * s + 2, :]
    starts = (0, halos_ref.shape[0] - 8)
    halo = [halos_ref[first : first + 8, :] for first in starts]
    halo_blocks = [i >> 7 for i in halo]
    halo_lanes = [i & (BLOCK - 1) for i in halo]
    for v in range(2):
        cut = pick_fields(table_ref, rows, halo_blocks[v], halo_lanes[v])
        for k in range(6):
            r = 2 * k - starts[v]
            if 0 <= r <= 6:
                for f in range(FIELDS):
                    cut_ref[k, 2 * f : 2 * f + 2, :] = cut[f][r : r + 2, :]
    send_pairs(counts, cut_ref, send_refs, [(0, 1), (2, 3), (4, 5)])


def pair_places():
    return [lax.rem(lax.axis_index(axis), 2) for axis in AXES]


def send_pairs(counts, cut_ref, send_refs, order):
    places = pair_places()
    long = [axis for axis in range(3) if counts[axis] > 2]
    for axis in range(3):
        even, odd = order[axis]
        send_refs[len(long) + axis][...] = cut_ref[jnp.where(places[axis] == 0, even, odd)]
        if axis in long:
            send_refs[long.index(axis)][...] = cut_ref[jnp.where(places[axis] == 0, odd, even)]


def placed(values, ids, block_count):
    rows = lax.broadcasted_iota(jnp.int32, (block_count, BLOCK), 0)
    hit = rows == jnp.broadcast_to(ids >> 7, rows.shape)
    left = [jnp.where(hit, jnp.broadcast_to(v, rows.shape), 0.0) for v in values]
    return jnp.concatenate(left, axis=0).astype(jnp.bfloat16)


def cut_parts(value):
    parts = []
    for _ in range(SPLITS - 1):
        part = value.astype(jnp.bfloat16).astype(jnp.float32)
        parts.append(part)
        value = value - part
    return parts + [value]


def hot_dot(left, right):
    return jnp.dot(left, right, preferred_element_type=jnp.float32)


def came_slots(counts):
    places = pair_places()
    long = [axis for axis in range(3) if counts[axis] > 2]
    slots = []
    for axis in long:
        at = lax.axis_index(AXES[axis])
        edge = jnp.where(places[axis] == 0, at == 0, at == counts[axis] - 1)
        slots.append(jnp.where(edge, -(1 << 10), 2 * axis + places[axis]))
    return slots + [2 * axis + 1 - places[axis] for axis in range(3)]


def moved_axes(counts):
    return [axis for axis in range(3) if counts[axis] > 2] + [0, 1, 2]


def add_slot(read, slot, ids, found):
    blocks, lanes = (ids >> 7) - 2 * slot, ids & (BLOCK - 1)
    found = list(found)
    for h in range(2):
        hit = blocks == h
        for f in range(FIELDS):
            found[f] = jnp.where(hit, pick(read(2 * f + h), lanes), found[f])
    return found


def values_kernel(counts, table_ref, nodes_ref, *refs):
    came_refs, values_ref = refs[:-1], refs[-1]
    owned_slots = table_ref.shape[0]
    slots = [slot for slot, axis in zip(came_slots(counts), moved_axes(counts)) if axis == 0]
    for first in range(0, nodes_ref.shape[0], 8):
        ids = nodes_ref[first : first + 8, :]
        found = [jnp.zeros((8, BLOCK), jnp.float32) for _ in range(FIELDS)]
        for s in range(owned_slots):
            found = add_slot(lambda r: table_ref[s, r : r + 1, :], s, ids, found)
        for ref, slot in zip(came_refs, slots):
            found = add_slot(lambda r: ref[r : r + 1, :], owned_slots + slot, ids, found)
        for f in range(FIELDS):
            values_ref[f, first : first + 8, :] = found[f]


def element_kernel(counts, moves, owned_slots, *refs):
    values_in_ref, nodes_ref, node_hot_ref, grads_ref, volume_ref = refs[:5]
    last = [slot for slot, axis in zip(came_slots(counts), moved_axes(counts)) if axis != 0]
    came_refs, refs = refs[5 : 5 + len(last)], refs[5 + len(last) :]
    own_ref, send_refs = refs[0], refs[1 : 1 + moves]
    values_ref, parts_ref, cut_ref = refs[1 + moves :]
    block_count = 2 * (owned_slots + 6)
    all_rows = nodes_ref.shape[0]
    elem_rows = all_rows // 4
    for first in range(0, all_rows, 8):
        ids = nodes_ref[first : first + 8, :]
        found = [values_in_ref[f, first : first + 8, :] for f in range(FIELDS)]
        for ref, slot in zip(came_refs, last):
            found = add_slot(lambda r: ref[r : r + 1, :], owned_slots + slot, ids, found)
        for f in range(FIELDS):
            values_ref[f, first : first + 8, :] = found[f]
    for first in [*range(0, elem_rows - 7, 8)] + ([elem_rows - 8] if elem_rows % 8 else []):
        at = [slice(r * elem_rows + first, r * elem_rows + first + 8) for r in range(12)]
        values = [[values_ref[f, at[a], :] for f in range(FIELDS)] for a in range(4)]
        grads = [[grads_ref[at[3 * a + j], :] for j in range(3)] for a in range(4)]
        volume = volume_ref[at[0], :]
        velgrad = [[sum(values[a][i] * grads[a][j] for a in range(4)) for j in range(3)] for i in range(3)]
        strain = [[0.5 * (velgrad[i][j] + velgrad[j][i]) if i <= j else None for j in range(3)] for i in range(3)]
        diagonal = sum(strain[i][i] * strain[i][i] for i in range(3))
        corner = sum(strain[i][j] * strain[i][j] for i, j in ((0, 1), (0, 2), (1, 2)))
        second = 0.5 * diagonal + corner
        pressure, temper, damage = [0.25 * (values[0][f] + values[1][f] + values[2][f] + values[3][f]) for f in (3, 4, 5)]
        root = jnp.exp(jnp.log(second + strain_reg) * (-1.0 / 3.0))
        twice = (1.0 - damage) * jnp.exp(-temper) * root
        stress = [[None] * 3 for _ in range(3)]
        for i in range(3):
            for j in range(i, 3):
                stress[i][j] = twice * strain[i][j] - (pressure if i == j else 0.0)
                stress[j][i] = stress[i][j]
        lift = (0.25 * gravity) * volume
        flow = 0.25 * volume * (velgrad[0][0] + velgrad[1][1] + velgrad[2][2])
        for s, part in enumerate(cut_parts(flow)):
            for a in range(4):
                parts_ref[3 * SPLITS + s, at[a], :] = part
        for a in range(4):
            for i in range(3):
                force = volume * sum(stress[i][j] * grads[a][j] for j in range(3))
                if i == 2:
                    force = force + lift
                for s, part in enumerate(cut_parts(force)):
                    parts_ref[i * SPLITS + s, at[a], :] = part

    group = node_hot_ref.shape[1] // BLOCK

    width = 4 * block_count
    total = jnp.zeros((SPLITS * width, BLOCK), jnp.float32)
    for step in range(all_rows // group):
        lefts = []
        for r in range(step * group, (step + 1) * group):
            terms = [parts_ref[c * SPLITS + s, r : r + 1, :] for s in range(SPLITS) for c in range(4)]
            lefts.append(placed(terms, nodes_ref[r : r + 1, :], block_count))
        total = total + hot_dot(jnp.concatenate(lefts, axis=1), node_hot_ref[step])
    total = sum(total[s * width : (s + 1) * width, :] for s in range(SPLITS))
    owned = 2 * owned_slots
    for c in range(4):
        own_ref[c * owned : (c + 1) * owned, :] = total[c * block_count : c * block_count + owned, :]
        for k in range(6):
            first = c * block_count + owned + 2 * k
            cut_ref[k, 2 * c : 2 * c + 2, :] = total[first : first + 2, :]
    send_pairs(counts, cut_ref, send_refs, [(1, 0), (3, 2), (5, 4)])


def placed_few(values, ids, block_count):
    each = 8 // block_count
    rows = lax.broadcasted_iota(jnp.int32, (8, BLOCK), 0)
    hit = (rows & (block_count - 1)) == jnp.broadcast_to(ids >> 7, rows.shape)
    left = []
    for first in range(0, len(values), each):
        tile = jnp.broadcast_to(values[first], rows.shape)
        for i in range(1, each):
            tile = jnp.where(rows >= i * block_count, jnp.broadcast_to(values[first + i], rows.shape), tile)
        left.append(jnp.where(hit, tile, 0.0))
    return jnp.concatenate(left, axis=0).astype(jnp.bfloat16)


def add_returned(total, came_refs, directions, halos_ref, halo_hot_ref):
    owned = total.shape[0] // 4
    lefts, rights = [], []
    for ref, k in zip(came_refs, directions):
        parts = cut_parts(ref[...])
        for h in range(2):
            terms = [parts[s][2 * c + h : 2 * c + h + 1, :] for s in range(SPLITS) for c in range(4)]
            lefts.append(placed_few(terms, halos_ref[pl.ds(2 * k + h, 1), :], owned))
            rights.append(halo_hot_ref[pl.ds(pl.multiple_of((2 * k + h) * BLOCK, BLOCK), BLOCK), :])
    sums = hot_dot(jnp.concatenate(lefts, axis=1), jnp.concatenate(rights, axis=0))
    width = 4 * owned
    return total + sum(sums[s * width : (s + 1) * width, :] for s in range(SPLITS))


def back_directions(counts):
    places = pair_places()
    long = [axis for axis in range(3) if counts[axis] > 2]
    return [2 * axis + 1 - places[axis] for axis in long] + [2 * axis + places[axis] for axis in range(3)]


def early_residual_kernel(counts, own_ref, halos_ref, halo_hot_ref, state_in_ref, *refs):
    refs, state_ref = refs[:-1], refs[-1]
    state_ref[...] = state_in_ref[...]
    directions = [k for k, axis in zip(back_directions(counts), moved_axes(counts)) if axis == 0][::-1]
    refs[-1][...] = add_returned(own_ref[...], refs[:-1], directions, halos_ref, halo_hot_ref)


def residual_kernel(counts, sums_ref, halos_ref, halo_hot_ref, *refs):
    directions = [k for k, axis in zip(back_directions(counts), moved_axes(counts)) if axis != 0]
    total = add_returned(sums_ref[...], refs[:-1], directions, halos_ref, halo_hot_ref)
    owned = total.shape[0] // 4
    for c in range(4):
        for b in range(owned):
            r = c * owned + b
            refs[-1][c : c + 1, b * BLOCK : (b + 1) * BLOCK] = total[r : r + 1, :]


def shaped(*shape):
    return jax.ShapeDtypeStruct(shape, jnp.float32)


def per_device(
    sizes,
    old_state,
    send_blocks,
    node_slots,
    node_weights,
    front_mask,
    halo_lists,
    elem_nodes,
    shape_grads,
    elem_volume,
):
    old_state, send_blocks = old_state[0, 0, 0], send_blocks[0, 0, 0]
    slots = send_blocks.shape[1]
    send_blocks = send_blocks.reshape(-1, 1, slots)
    rows = FIELDS * slots
    arguments = [
        node_slots[0, 0, 0],
        node_weights[0, 0, 0],
        front_mask.reshape(-1, BLOCK),
        halo_lists.reshape(halo_lists.shape[-2], 1, -1),
        elem_nodes[0, 0, 0],
        shape_grads.reshape(-1, BLOCK),
        elem_volume[0, 0],
        send_blocks,
    ]
    old_rows = old_state.reshape(-1, BLOCK)
    count = len(arguments)
    owned = node_slots.shape[-1]
    slot_rows = node_slots.size // BLOCK
    give_rows = 2 * rows + 2 * slot_rows
    give_first, give, old_rows, *held = pl.pallas_call(
        functools.partial(give_kernel, count),
        out_shape=[shaped(2 * rows, BLOCK), shaped(give_rows, BLOCK), shaped(*old_rows.shape)]
        + [jax.ShapeDtypeStruct(a.shape, a.dtype) for a in arguments],
        in_specs=[pl.BlockSpec(memory_space=pltpu.HBM)] * (2 + count),
        out_specs=[VMEM] * (3 + count),
        scratch_shapes=[pltpu.SMEM(send_blocks.shape, jnp.int32), pltpu.SemaphoreType.DMA((2 + count,))],
        compiler_params=params(),
    )(*(pltpu.with_memory_space_constraint(a, pltpu.HBM) for a in (send_blocks, old_rows, *arguments)))
    node_slots, node_weights, mask_rows, halos, elem_nodes, grad_rows, volume, held_blocks = held
    first, second = pl.pallas_call(
        keep_kernel,
        out_shape=(shaped(2 * rows, BLOCK),) * 2,
        in_specs=[SMEM, VMEM],
        out_specs=(VMEM,) * 2,
        compiler_params=params(),
    )(held_blocks, old_rows)
    layers = both_ways([(0, 1)])
    got_first = lax.ppermute(give_first, "layer", layers)
    got = lax.ppermute(give, "layer", layers)
    full = [jnp.concatenate([first, got_first]), jnp.concatenate([second, got[: 2 * rows]])]
    first, second = [
        lax.ppermute(part, ("mapx", "layer"), pairs).reshape(4, rows, BLOCK)
        for part, pairs in zip(full, column_moves(sizes[0]))
    ]
    other_slots, other_weights = got[2 * rows : 2 * rows + slot_rows], got[2 * rows + slot_rows :]

    all_rows = elem_nodes.size // BLOCK
    halo_count = halos.size // BLOCK
    hot_steps = next(n for n in (8, 4, 2, 1) if all_rows % n == 0)
    whole = lambda *shape: jax.ShapeDtypeStruct(shape, jnp.int32)
    found, slots_cut, weights_cut, halos_cut, nodes_cut, volume_cut, halo_hot, node_hot = pl.pallas_call(
        own_kernel,
        out_shape=(
            shaped(2, FIELDS, slot_rows, BLOCK),
            whole(2, slot_rows, BLOCK),
            shaped(slot_rows, BLOCK),
            whole(halo_count, BLOCK),
            whole(all_rows, BLOCK),
            shaped(all_rows // 4, BLOCK),
            jax.ShapeDtypeStruct((halo_count * BLOCK, BLOCK), jnp.bfloat16),
            jax.ShapeDtypeStruct((hot_steps, all_rows // hot_steps * BLOCK, BLOCK), jnp.bfloat16),
        ),
        in_specs=[SMEM] + [VMEM] * 7,
        out_specs=(VMEM,) * 8,
        scratch_shapes=[pltpu.VMEM((2, rows, BLOCK), jnp.float32)],
        compiler_params=params(),
    )(held_blocks, old_rows, other_slots, node_slots, node_weights, halos, elem_nodes, volume)
    found = pl.pallas_call(
        early_kernel,
        out_shape=shaped(2, FIELDS, slot_rows, BLOCK),
        in_specs=[VMEM] * 3,
        out_specs=VMEM,
        compiler_params=params(),
    )(first, slots_cut, found)
    state_rows = FIELDS * owned // BLOCK
    other, mine = [
        pl.pallas_call(
            functools.partial(late_kernel, owned // BLOCK, owner),
            out_shape=shaped(state_rows, BLOCK),
            in_specs=[VMEM] * 4,
            out_specs=VMEM,
            compiler_params=params(),
        )(second, slots_cut, found, weights)
        for owner, weights in ((1, other_weights), (0, weights_cut))
    ]
    other = lax.ppermute(other, "layer", layers)
    moves = 3 + sum(size > 2 for size in sizes)
    chunk = (2 * FIELDS, BLOCK)
    new_state, table, *ghosts = pl.pallas_call(
        functools.partial(state_kernel, sizes),
        out_shape=(shaped(state_rows, BLOCK), shaped(owned // (2 * BLOCK), *chunk)) + (shaped(*chunk),) * moves,
        in_specs=[VMEM] * 4,
        out_specs=(VMEM,) * (2 + moves),
        scratch_shapes=[pltpu.VMEM((6, *chunk), jnp.float32)],
        compiler_params=params(),
    )(mine, other, mask_rows, halos_cut)
    ghosts = swap_all(ghosts, sizes)

    owned_slots = table.shape[0]
    early = [ghost for ghost, axis in zip(ghosts, moved_axes(sizes)) if axis == 0]
    late = [ghost for ghost, axis in zip(ghosts, moved_axes(sizes)) if axis != 0]
    values = pl.pallas_call(
        functools.partial(values_kernel, sizes),
        out_shape=shaped(FIELDS, all_rows, BLOCK),
        in_specs=[VMEM] * (2 + len(early)),
        out_specs=VMEM,
        compiler_params=params(),
    )(table, nodes_cut, *early)
    own, *sums = pl.pallas_call(
        functools.partial(element_kernel, sizes, moves, owned_slots),
        out_shape=(shaped(4 * owned // BLOCK, BLOCK),) + (shaped(8, BLOCK),) * moves,
        in_specs=[VMEM] * (5 + len(late)),
        out_specs=(VMEM,) * (1 + moves),
        scratch_shapes=[
            pltpu.VMEM((FIELDS, all_rows, BLOCK), jnp.float32),
            pltpu.VMEM((4 * SPLITS, all_rows, BLOCK), jnp.float32),
            pltpu.VMEM((6, 8, BLOCK), jnp.float32),
        ],
        compiler_params=params(),
    )(values, nodes_cut, node_hot, grad_rows, volume_cut, *late)
    sums = swap_all(sums, sizes)
    early = [came for came, axis in zip(sums, moved_axes(sizes)) if axis == 0][::-1]
    late = [came for came, axis in zip(sums, moved_axes(sizes)) if axis != 0]
    own, new_state = pl.pallas_call(
        functools.partial(early_residual_kernel, sizes),
        out_shape=(shaped(*own.shape), shaped(*new_state.shape)),
        in_specs=[VMEM] * (4 + len(early)),
        out_specs=(VMEM,) * 2,
        compiler_params=params(),
    )(own, halos_cut, halo_hot, new_state, *early)
    residual = pl.pallas_call(
        functools.partial(residual_kernel, sizes),
        out_shape=shaped(4, owned),
        in_specs=[VMEM] * (3 + len(late)),
        out_specs=VMEM,
        compiler_params=params(),
    )(own, halos_cut, halo_hot, *late)
    return (new_state.reshape(1, 1, 1, FIELDS, owned), residual[None, None, None])


def solution(mesh):
    sizes = tuple(mesh.shape[axis] for axis in AXES)
    row = P("mapx", "mapy", "layer", None)
    table = P("mapx", "mapy", "layer", None, None)
    return jax.shard_map(
        functools.partial(per_device, sizes),
        mesh=mesh,
        in_specs=(table, table, table, table, row, table, table, table, row),
        out_specs=(table, table),
        check_vma=False,
    )
```

```python
import functools

import jax
import jax.numpy as jnp
from jax import lax
from jax.experimental import pallas as pl
from jax.experimental.pallas import tpu as pltpu
from jax.sharding import PartitionSpec as P

BLOCK = 128
REACH = 2
FIELDS = 6
SPLITS = 3

ocean_temp = 0.0
strain_reg = 0.01
gravity = 0.5

AXES = ("mapx", "mapy", "layer")
VMEM = pl.BlockSpec(memory_space=pltpu.VMEM)
SMEM = pl.BlockSpec(memory_space=pltpu.SMEM)


def params():
    return pltpu.CompilerParams(vmem_limit_bytes=32 * 1024 * 1024)


def both_ways(pairs):
    return [way for one, other in pairs for way in ((one, other), (other, one))]


def column_moves(count):
    outside = [(at, at + 1) for at in range(1, count - 1, 2)]
    inside = [(at, at + 1) for at in range(0, count - 1, 2)]
    within = [(at + i, at + i + 2) for at in range(0, count - 3, 4) for i in range(2)]
    across = [(at + i, at + i + 2) for at in range(2, count - 3, 4) for i in range(2)]
    number = lambda pairs, layer: [(one * 2 + layer, other * 2 + layer) for one, other in pairs]
    return [
        both_ways(number(outside, 1) + number(within, 0)),
        both_ways(number(inside, 0) + number(across, 1)),
    ]


def column_offsets(layer):
    at = lax.axis_index("mapx")
    near = jnp.where(lax.rem(at, 2) == 0, 1, -1)
    two = jnp.where(lax.rem(at, 4) < 2, 2, -2)
    return [jnp.where(layer == 0, two, -near), jnp.where(layer == 0, near, -two)]


def pair_swap(value, axis, count, first):
    return lax.ppermute(value, axis, both_ways([(at, at + 1) for at in range(first, count - 1, 2)]))


def swap_all(values, sizes):
    long = [axis for axis in range(3) if sizes[axis] > 2]
    steps = [(axis, 1) for axis in long] + [(axis, 0) for axis in range(3)]
    return [pair_swap(value, AXES[axis], sizes[axis], first) for value, (axis, first) in zip(values, steps)]


def pack_blocks(blocks_ref, old_ref, ref, offset):
    slots = blocks_ref.shape[2]
    stride = old_ref.shape[0] // (FIELDS + 1)
    for to_layer in range(2):
        peer = (offset + REACH) * 2 + to_layer
        start = to_layer * FIELDS * slots
        for c in range(slots):
            rows = pl.ds(blocks_ref[peer, 0, c], FIELDS, stride=stride)
            ref[start + FIELDS * c : start + FIELDS * (c + 1), :] = old_ref[rows, :]


def give_kernel(count, *refs):
    blocks_in_ref, old_in_ref = refs[:2]
    give_first_ref, give_ref, old_ref = refs[2 + count : 5 + count]
    held = refs[5 + count : 5 + 2 * count]
    blocks_ref, sems = refs[5 + 2 * count :]
    first = [pltpu.make_async_copy(blocks_in_ref, blocks_ref, sems.at[0])]
    first += [pltpu.make_async_copy(old_in_ref, old_ref.at[: old_in_ref.shape[0]], sems.at[1])]
    rest = [pltpu.make_async_copy(refs[2 + i], held[i], sems.at[2 + i]) for i in range(count)]
    for copy in first + rest:
        copy.start()
    for copy in first:
        copy.wait()
    offsets = column_offsets(1 - lax.axis_index("layer"))
    pack_blocks(blocks_ref, old_ref, give_first_ref, offsets[0])
    pack_blocks(blocks_ref, old_ref, give_ref, offsets[1])
    for copy in rest:
        copy.wait()
    size = give_first_ref.shape[0]
    slots_ref, weights_ref = held[0], held[1]
    slot_rows = slots_ref.shape[0] * slots_ref.shape[1] // BLOCK
    cut_rows(slots_ref, give_ref.at[size : size + slot_rows])
    cut_rows(weights_ref, give_ref.at[size + slot_rows : size + 2 * slot_rows])


def keep_kernel(blocks_ref, old_ref, first_ref, second_ref):
    offsets = column_offsets(lax.axis_index("layer"))
    pack_blocks(blocks_ref, old_ref, first_ref, offsets[0])
    pack_blocks(blocks_ref, old_ref, second_ref, offsets[1])


def pick(row, lanes):
    return jnp.take_along_axis(jnp.broadcast_to(row, lanes.shape), lanes, axis=1)


def pick_fields(table_ref, block_count, blocks, lanes):
    found = [jnp.zeros((8, BLOCK), jnp.float32) for _ in range(FIELDS)]
    for b in range(block_count):
        hit = blocks == b
        for f in range(FIELDS):
            row = table_ref[b // 2, 2 * f + b % 2 : 2 * f + b % 2 + 1, :]
            found[f] = jnp.where(hit, pick(row, lanes), found[f])
    return found


def add_blocks(ref, chunk, first_block, blocks, lanes, found):
    local = blocks - first_block
    found = list(found)
    for c in range(ref.shape[1] // FIELDS):
        hit = local == c
        for f in range(FIELDS):
            row = ref[chunk, FIELDS * c + f : FIELDS * c + f + 1, :]
            found[f] = jnp.where(hit, pick(row, lanes), found[f])
    return tuple(found)


def add_chunks(ref, numbers, offset, ids, found):
    blocks, lanes = ids >> 7, ids & (BLOCK - 1)
    for chunk, layer in numbers:
        first = ((offset + REACH) * 2 + layer) * (ref.shape[1] // FIELDS)
        found = add_blocks(ref, chunk, first, blocks, lanes, found)
    return found


def load_fields(found_ref, owner, v):
    return tuple(found_ref[owner, f, 8 * v : 8 * v + 8, :] for f in range(FIELDS))


def save_fields(found_ref, owner, v, found):
    for f in range(FIELDS):
        found_ref[owner, f, 8 * v : 8 * v + 8, :] = found[f]


def arrived_chunks(ref, move, ids, found, owner):
    layer = lax.axis_index("layer")
    to_layer = 1 - layer if owner else layer
    numbers = [(to_layer, layer), (2 + to_layer, 1 - layer)]
    return add_chunks(ref, numbers, column_offsets(layer)[move], ids, found)


def cut_rows(from_ref, to_ref):
    count = from_ref.shape[1] // BLOCK
    for r in range(from_ref.shape[0]):
        for i in range(count):
            to_ref[r * count + i : r * count + i + 1, :] = from_ref[
                r : r + 1, i * BLOCK : (i + 1) * BLOCK
            ].astype(to_ref.dtype)


def lane_one_hot(ids):
    rows = lax.broadcasted_iota(jnp.int32, (BLOCK, BLOCK), 0)
    hit = rows == jnp.broadcast_to(ids & (BLOCK - 1), rows.shape)
    return jnp.where(hit, 1.0, 0.0).T.astype(jnp.bfloat16)


def own_kernel(
    blocks_ref,
    old_ref,
    other_slots_ref,
    slots_in_ref,
    weights_in_ref,
    halos_in_ref,
    nodes_in_ref,
    volume_in_ref,
    found_ref,
    slots_ref,
    weights_ref,
    halos_ref,
    nodes_ref,
    volume_ref,
    halo_hot_ref,
    node_hot_ref,
    own_ref,
):
    for layer in range(2):
        chunk_ref = own_ref.at[layer]
        for c in range(blocks_ref.shape[2]):
            rows = pl.ds(blocks_ref[2 * REACH + layer, 0, c], FIELDS, stride=old_ref.shape[0] // (FIELDS + 1))
            chunk_ref[FIELDS * c : FIELDS * (c + 1), :] = old_ref[rows, :]
    for k in range(halos_in_ref.shape[0]):
        cut_rows(halos_in_ref.at[k], halos_ref.at[2 * k : 2 * k + 2])
    cut_rows(slots_in_ref, slots_ref.at[0])
    slots_ref[1] = other_slots_ref[...].astype(jnp.int32)
    cut_rows(weights_in_ref, weights_ref)
    cut_rows(nodes_in_ref, nodes_ref)
    cut_rows(volume_in_ref, volume_ref)
    layer = lax.axis_index("layer")
    for owner in range(2):
        for v in range(slots_ref.shape[1] // 8):
            ids = slots_ref[owner, 8 * v : 8 * v + 8, :]
            found = tuple(jnp.zeros((8, BLOCK), jnp.float32) for _ in range(FIELDS))
            numbers = [(1 - layer if owner else layer, layer)]
            save_fields(found_ref, owner, v, add_chunks(own_ref, numbers, 0, ids, found))
    for r in range(halos_ref.shape[0]):
        halo_hot_ref[r * BLOCK : (r + 1) * BLOCK, :] = lane_one_hot(halos_ref[r : r + 1, :])
    steps, width, _ = node_hot_ref.shape
    group = width // BLOCK

    def hot(step, carry):
        for r in range(group):
            ids = nodes_ref[pl.ds(step * group + r, 1), :]
            node_hot_ref[step, r * BLOCK : (r + 1) * BLOCK, :] = lane_one_hot(ids)
        return carry

    lax.fori_loop(0, steps, hot, 0)


def early_kernel(came_ref, slots_ref, found_in_ref, found_ref):
    for owner in range(2):
        for v in range(slots_ref.shape[1] // 8):
            ids = slots_ref[owner, 8 * v : 8 * v + 8, :]
            found = arrived_chunks(came_ref, 0, ids, load_fields(found_in_ref, owner, v), owner)
            save_fields(found_ref, owner, v, found)


def late_kernel(rows, owner, came_ref, slots_ref, found_ref, weights_ref, out_ref):
    totals = [jnp.zeros((rows, BLOCK), jnp.float32) for _ in range(FIELDS)]
    for v in range(slots_ref.shape[1] // 8):
        ids = slots_ref[owner, 8 * v : 8 * v + 8, :]
        found = arrived_chunks(came_ref, 1, ids, load_fields(found_ref, owner, v), owner)
        for f in range(FIELDS):
            term = found[f] * weights_ref[8 * v : 8 * v + 8, :]
            for k in range(8 // rows):
                totals[f] = totals[f] + term[k * rows : (k + 1) * rows, :]
    for f in range(FIELDS):
        out_ref[f * rows : (f + 1) * rows, :] = totals[f]


def state_kernel(counts, mine_ref, came_ref, mask_ref, halos_ref, state_ref, table_ref, *more_refs):
    send_refs, cut_ref = more_refs[:-1], more_refs[-1]
    front = mask_ref[...] == 1
    rows = mask_ref.shape[0]
    for f in range(FIELDS):
        at = slice(f * rows, (f + 1) * rows)
        total = mine_ref[at, :] + came_ref[at, :]
        if f == 4:
            total = jnp.where(front, ocean_temp, total)
        state_ref[f * rows : (f + 1) * rows, :] = total
        for s in range(rows // 2):
            table_ref[s, 2 * f : 2 * f + 2, :] = total[2 * s : 2 * s + 2, :]
    starts = (0, halos_ref.shape[0] - 8)
    halo = [halos_ref[first : first + 8, :] for first in starts]
    halo_blocks = [i >> 7 for i in halo]
    halo_lanes = [i & (BLOCK - 1) for i in halo]
    for v in range(2):
        cut = pick_fields(table_ref, rows, halo_blocks[v], halo_lanes[v])
        for k in range(6):
            r = 2 * k - starts[v]
            if 0 <= r <= 6:
                for f in range(FIELDS):
                    cut_ref[k, 2 * f : 2 * f + 2, :] = cut[f][r : r + 2, :]
    send_pairs(counts, cut_ref, send_refs, [(0, 1), (2, 3), (4, 5)])


def pair_places():
    return [lax.rem(lax.axis_index(axis), 2) for axis in AXES]


def send_pairs(counts, cut_ref, send_refs, order):
    places = pair_places()
    long = [axis for axis in range(3) if counts[axis] > 2]
    for axis in range(3):
        even, odd = order[axis]
        send_refs[len(long) + axis][...] = cut_ref[jnp.where(places[axis] == 0, even, odd)]
        if axis in long:
            send_refs[long.index(axis)][...] = cut_ref[jnp.where(places[axis] == 0, odd, even)]


def placed(values, ids, block_count):
    rows = lax.broadcasted_iota(jnp.int32, (block_count, BLOCK), 0)
    hit = rows == jnp.broadcast_to(ids >> 7, rows.shape)
    left = [jnp.where(hit, jnp.broadcast_to(v, rows.shape), 0.0) for v in values]
    return jnp.concatenate(left, axis=0).astype(jnp.bfloat16)


def cut_parts(value):
    parts = []
    for _ in range(SPLITS - 1):
        part = value.astype(jnp.bfloat16).astype(jnp.float32)
        parts.append(part)
        value = value - part
    return parts + [value]


def hot_dot(left, right):
    return jnp.dot(left, right, preferred_element_type=jnp.float32)


def came_slots(counts):
    places = pair_places()
    long = [axis for axis in range(3) if counts[axis] > 2]
    slots = []
    for axis in long:
        at = lax.axis_index(AXES[axis])
        edge = jnp.where(places[axis] == 0, at == 0, at == counts[axis] - 1)
        slots.append(jnp.where(edge, -(1 << 10), 2 * axis + places[axis]))
    return slots + [2 * axis + 1 - places[axis] for axis in range(3)]


def moved_axes(counts):
    return [axis for axis in range(3) if counts[axis] > 2] + [0, 1, 2]


def add_slot(read, slot, ids, found):
    blocks, lanes = (ids >> 7) - 2 * slot, ids & (BLOCK - 1)
    found = list(found)
    for h in range(2):
        hit = blocks == h
        for f in range(FIELDS):
            found[f] = jnp.where(hit, pick(read(2 * f + h), lanes), found[f])
    return found


def values_kernel(counts, table_ref, nodes_ref, *refs):
    came_refs, values_ref = refs[:-1], refs[-1]
    owned_slots = table_ref.shape[0]
    slots = [slot for slot, axis in zip(came_slots(counts), moved_axes(counts)) if axis == 0]
    for first in range(0, nodes_ref.shape[0], 8):
        ids = nodes_ref[first : first + 8, :]
        found = [jnp.zeros((8, BLOCK), jnp.float32) for _ in range(FIELDS)]
        for s in range(owned_slots):
            found = add_slot(lambda r: table_ref[s, r : r + 1, :], s, ids, found)
        for ref, slot in zip(came_refs, slots):
            found = add_slot(lambda r: ref[r : r + 1, :], owned_slots + slot, ids, found)
        for f in range(FIELDS):
            values_ref[f, first : first + 8, :] = found[f]


def element_kernel(counts, moves, owned_slots, *refs):
    values_in_ref, nodes_ref, node_hot_ref, grads_ref, volume_ref = refs[:5]
    last = [slot for slot, axis in zip(came_slots(counts), moved_axes(counts)) if axis != 0]
    came_refs, refs = refs[5 : 5 + len(last)], refs[5 + len(last) :]
    own_ref, send_refs = refs[0], refs[1 : 1 + moves]
    values_ref, parts_ref, cut_ref = refs[1 + moves :]
    block_count = 2 * (owned_slots + 6)
    all_rows = nodes_ref.shape[0]
    elem_rows = all_rows // 4
    for first in range(0, all_rows, 8):
        ids = nodes_ref[first : first + 8, :]
        found = [values_in_ref[f, first : first + 8, :] for f in range(FIELDS)]
        for ref, slot in zip(came_refs, last):
            found = add_slot(lambda r: ref[r : r + 1, :], owned_slots + slot, ids, found)
        for f in range(FIELDS):
            values_ref[f, first : first + 8, :] = found[f]
    for first in [*range(0, elem_rows - 7, 8)] + ([elem_rows - 8] if elem_rows % 8 else []):
        at = [slice(r * elem_rows + first, r * elem_rows + first + 8) for r in range(12)]
        values = [[values_ref[f, at[a], :] for f in range(FIELDS)] for a in range(4)]
        grads = [[grads_ref[at[3 * a + j], :] for j in range(3)] for a in range(4)]
        volume = volume_ref[at[0], :]
        velgrad = [[sum(values[a][i] * grads[a][j] for a in range(4)) for j in range(3)] for i in range(3)]
        strain = [[0.5 * (velgrad[i][j] + velgrad[j][i]) if i <= j else None for j in range(3)] for i in range(3)]
        diagonal = sum(strain[i][i] * strain[i][i] for i in range(3))
        corner = sum(strain[i][j] * strain[i][j] for i, j in ((0, 1), (0, 2), (1, 2)))
        second = 0.5 * diagonal + corner
        pressure, temper, damage = [0.25 * (values[0][f] + values[1][f] + values[2][f] + values[3][f]) for f in (3, 4, 5)]
        root = jnp.exp(jnp.log(second + strain_reg) * (-1.0 / 3.0))
        twice = (1.0 - damage) * jnp.exp(-temper) * root
        stress = [[None] * 3 for _ in range(3)]
        for i in range(3):
            for j in range(i, 3):
                stress[i][j] = twice * strain[i][j] - (pressure if i == j else 0.0)
                stress[j][i] = stress[i][j]
        lift = (0.25 * gravity) * volume
        flow = 0.25 * volume * (velgrad[0][0] + velgrad[1][1] + velgrad[2][2])
        for s, part in enumerate(cut_parts(flow)):
            for a in range(4):
                parts_ref[3 * SPLITS + s, at[a], :] = part
        for a in range(4):
            for i in range(3):
                force = volume * sum(stress[i][j] * grads[a][j] for j in range(3))
                if i == 2:
                    force = force + lift
                for s, part in enumerate(cut_parts(force)):
                    parts_ref[i * SPLITS + s, at[a], :] = part

    group = node_hot_ref.shape[1] // BLOCK

    width = 4 * block_count
    total = jnp.zeros((SPLITS * width, BLOCK), jnp.float32)
    for step in range(all_rows // group):
        lefts = []
        for r in range(step * group, (step + 1) * group):
            terms = [parts_ref[c * SPLITS + s, r : r + 1, :] for s in range(SPLITS) for c in range(4)]
            lefts.append(placed(terms, nodes_ref[r : r + 1, :], block_count))
        total = total + hot_dot(jnp.concatenate(lefts, axis=1), node_hot_ref[step])
    total = sum(total[s * width : (s + 1) * width, :] for s in range(SPLITS))
    owned = 2 * owned_slots
    for c in range(4):
        own_ref[c * owned : (c + 1) * owned, :] = total[c * block_count : c * block_count + owned, :]
        for k in range(6):
            first = c * block_count + owned + 2 * k
            cut_ref[k, 2 * c : 2 * c + 2, :] = total[first : first + 2, :]
    send_pairs(counts, cut_ref, send_refs, [(1, 0), (3, 2), (5, 4)])


def placed_few(values, ids, block_count):
    each = 8 // block_count
    rows = lax.broadcasted_iota(jnp.int32, (8, BLOCK), 0)
    hit = (rows & (block_count - 1)) == jnp.broadcast_to(ids >> 7, rows.shape)
    left = []
    for first in range(0, len(values), each):
        tile = jnp.broadcast_to(values[first], rows.shape)
        for i in range(1, each):
            tile = jnp.where(rows >= i * block_count, jnp.broadcast_to(values[first + i], rows.shape), tile)
        left.append(jnp.where(hit, tile, 0.0))
    return jnp.concatenate(left, axis=0).astype(jnp.bfloat16)


def add_returned(total, came_refs, directions, halos_ref, halo_hot_ref):
    owned = total.shape[0] // 4
    lefts, rights = [], []
    for ref, k in zip(came_refs, directions):
        parts = cut_parts(ref[...])
        for h in range(2):
            terms = [parts[s][2 * c + h : 2 * c + h + 1, :] for s in range(SPLITS) for c in range(4)]
            lefts.append(placed_few(terms, halos_ref[pl.ds(2 * k + h, 1), :], owned))
            rights.append(halo_hot_ref[pl.ds(pl.multiple_of((2 * k + h) * BLOCK, BLOCK), BLOCK), :])
    sums = hot_dot(jnp.concatenate(lefts, axis=1), jnp.concatenate(rights, axis=0))
    width = 4 * owned
    return total + sum(sums[s * width : (s + 1) * width, :] for s in range(SPLITS))


def back_directions(counts):
    places = pair_places()
    long = [axis for axis in range(3) if counts[axis] > 2]
    return [2 * axis + 1 - places[axis] for axis in long] + [2 * axis + places[axis] for axis in range(3)]


def early_residual_kernel(counts, own_ref, halos_ref, halo_hot_ref, state_in_ref, *refs):
    refs, state_ref = refs[:-1], refs[-1]
    state_ref[...] = state_in_ref[...]
    directions = [k for k, axis in zip(back_directions(counts), moved_axes(counts)) if axis == 0][::-1]
    refs[-1][...] = add_returned(own_ref[...], refs[:-1], directions, halos_ref, halo_hot_ref)


def residual_kernel(counts, sums_ref, halos_ref, halo_hot_ref, *refs):
    directions = [k for k, axis in zip(back_directions(counts), moved_axes(counts)) if axis != 0]
    total = add_returned(sums_ref[...], refs[:-1], directions, halos_ref, halo_hot_ref)
    owned = total.shape[0] // 4
    for c in range(4):
        for b in range(owned):
            r = c * owned + b
            refs[-1][c : c + 1, b * BLOCK : (b + 1) * BLOCK] = total[r : r + 1, :]


def shaped(*shape):
    return jax.ShapeDtypeStruct(shape, jnp.float32)


def per_device(
    sizes,
    old_state,
    send_blocks,
    node_slots,
    node_weights,
    front_mask,
    halo_lists,
    elem_nodes,
    shape_grads,
    elem_volume,
):
    old_state, send_blocks = old_state[0, 0, 0], send_blocks[0, 0, 0]
    slots = send_blocks.shape[1]
    send_blocks = send_blocks.reshape(-1, 1, slots)
    rows = FIELDS * slots
    arguments = [
        node_slots[0, 0, 0],
        node_weights[0, 0, 0],
        front_mask.reshape(-1, BLOCK),
        halo_lists.reshape(halo_lists.shape[-2], 1, -1),
        elem_nodes[0, 0, 0],
        shape_grads.reshape(-1, BLOCK),
        elem_volume[0, 0],
        send_blocks,
    ]
    old_rows = old_state.reshape(-1, BLOCK)
    count = len(arguments)
    owned = node_slots.shape[-1]
    slot_rows = node_slots.size // BLOCK
    give_rows = 2 * rows + 2 * slot_rows
    give_first, give, old_rows, *held = pl.pallas_call(
        functools.partial(give_kernel, count),
        out_shape=[shaped(2 * rows, BLOCK), shaped(give_rows, BLOCK), shaped(old_rows.shape[0] // FIELDS * (FIELDS + 1), BLOCK)]
        + [jax.ShapeDtypeStruct(a.shape, a.dtype) for a in arguments],
        in_specs=[pl.BlockSpec(memory_space=pltpu.HBM)] * (2 + count),
        out_specs=[VMEM] * (3 + count),
        scratch_shapes=[pltpu.SMEM(send_blocks.shape, jnp.int32), pltpu.SemaphoreType.DMA((2 + count,))],
        compiler_params=params(),
    )(*(pltpu.with_memory_space_constraint(a, pltpu.HBM) for a in (send_blocks, old_rows, *arguments)))
    node_slots, node_weights, mask_rows, halos, elem_nodes, grad_rows, volume, held_blocks = held
    first, second = pl.pallas_call(
        keep_kernel,
        out_shape=(shaped(2 * rows, BLOCK),) * 2,
        in_specs=[SMEM, VMEM],
        out_specs=(VMEM,) * 2,
        compiler_params=params(),
    )(held_blocks, old_rows)
    layers = both_ways([(0, 1)])
    got_first = lax.ppermute(give_first, "layer", layers)
    got = lax.ppermute(give, "layer", layers)
    full = [jnp.concatenate([first, got_first]), jnp.concatenate([second, got[: 2 * rows]])]
    first, second = [
        lax.ppermute(part, ("mapx", "layer"), pairs).reshape(4, rows, BLOCK)
        for part, pairs in zip(full, column_moves(sizes[0]))
    ]
    other_slots, other_weights = got[2 * rows : 2 * rows + slot_rows], got[2 * rows + slot_rows :]

    all_rows = elem_nodes.size // BLOCK
    halo_count = halos.size // BLOCK
    hot_steps = next(n for n in (8, 4, 2, 1) if all_rows % n == 0)
    whole = lambda *shape: jax.ShapeDtypeStruct(shape, jnp.int32)
    found, slots_cut, weights_cut, halos_cut, nodes_cut, volume_cut, halo_hot, node_hot = pl.pallas_call(
        own_kernel,
        out_shape=(
            shaped(2, FIELDS, slot_rows, BLOCK),
            whole(2, slot_rows, BLOCK),
            shaped(slot_rows, BLOCK),
            whole(halo_count, BLOCK),
            whole(all_rows, BLOCK),
            shaped(all_rows // 4, BLOCK),
            jax.ShapeDtypeStruct((halo_count * BLOCK, BLOCK), jnp.bfloat16),
            jax.ShapeDtypeStruct((hot_steps, all_rows // hot_steps * BLOCK, BLOCK), jnp.bfloat16),
        ),
        in_specs=[SMEM] + [VMEM] * 7,
        out_specs=(VMEM,) * 8,
        scratch_shapes=[pltpu.VMEM((2, rows, BLOCK), jnp.float32)],
        compiler_params=params(),
    )(held_blocks, old_rows, other_slots, node_slots, node_weights, halos, elem_nodes, volume)
    found = pl.pallas_call(
        early_kernel,
        out_shape=shaped(2, FIELDS, slot_rows, BLOCK),
        in_specs=[VMEM] * 3,
        out_specs=VMEM,
        compiler_params=params(),
    )(first, slots_cut, found)
    state_rows = FIELDS * owned // BLOCK
    other, mine = [
        pl.pallas_call(
            functools.partial(late_kernel, owned // BLOCK, owner),
            out_shape=shaped(state_rows, BLOCK),
            in_specs=[VMEM] * 4,
            out_specs=VMEM,
            compiler_params=params(),
        )(second, slots_cut, found, weights)
        for owner, weights in ((1, other_weights), (0, weights_cut))
    ]
    other = lax.ppermute(other, "layer", layers)
    moves = 3 + sum(size > 2 for size in sizes)
    chunk = (2 * FIELDS, BLOCK)
    new_state, table, *ghosts = pl.pallas_call(
        functools.partial(state_kernel, sizes),
        out_shape=(shaped(state_rows, BLOCK), shaped(owned // (2 * BLOCK), *chunk)) + (shaped(*chunk),) * moves,
        in_specs=[VMEM] * 4,
        out_specs=(VMEM,) * (2 + moves),
        scratch_shapes=[pltpu.VMEM((6, *chunk), jnp.float32)],
        compiler_params=params(),
    )(mine, other, mask_rows, halos_cut)
    ghosts = swap_all(ghosts, sizes)

    owned_slots = table.shape[0]
    early = [ghost for ghost, axis in zip(ghosts, moved_axes(sizes)) if axis == 0]
    late = [ghost for ghost, axis in zip(ghosts, moved_axes(sizes)) if axis != 0]
    values = pl.pallas_call(
        functools.partial(values_kernel, sizes),
        out_shape=shaped(FIELDS, all_rows, BLOCK),
        in_specs=[VMEM] * (2 + len(early)),
        out_specs=VMEM,
        compiler_params=params(),
    )(table, nodes_cut, *early)
    own, *sums = pl.pallas_call(
        functools.partial(element_kernel, sizes, moves, owned_slots),
        out_shape=(shaped(4 * owned // BLOCK, BLOCK),) + (shaped(8, BLOCK),) * moves,
        in_specs=[VMEM] * (5 + len(late)),
        out_specs=(VMEM,) * (1 + moves),
        scratch_shapes=[
            pltpu.VMEM((FIELDS, all_rows, BLOCK), jnp.float32),
            pltpu.VMEM((4 * SPLITS, all_rows, BLOCK), jnp.float32),
            pltpu.VMEM((6, 8, BLOCK), jnp.float32),
        ],
        compiler_params=params(),
    )(values, nodes_cut, node_hot, grad_rows, volume_cut, *late)
    sums = swap_all(sums, sizes)
    early = [came for came, axis in zip(sums, moved_axes(sizes)) if axis == 0][::-1]
    late = [came for came, axis in zip(sums, moved_axes(sizes)) if axis != 0]
    own, new_state = pl.pallas_call(
        functools.partial(early_residual_kernel, sizes),
        out_shape=(shaped(*own.shape), shaped(*new_state.shape)),
        in_specs=[VMEM] * (4 + len(early)),
        out_specs=(VMEM,) * 2,
        compiler_params=params(),
    )(own, halos_cut, halo_hot, new_state, *early)
    residual = pl.pallas_call(
        functools.partial(residual_kernel, sizes),
        out_shape=shaped(4, owned),
        in_specs=[VMEM] * (3 + len(late)),
        out_specs=VMEM,
        compiler_params=params(),
    )(own, halos_cut, halo_hot, *late)
    return (new_state.reshape(1, 1, 1, FIELDS, owned), residual[None, None, None])


def solution(mesh):
    sizes = tuple(mesh.shape[axis] for axis in AXES)
    row = P("mapx", "mapy", "layer", None)
    table = P("mapx", "mapy", "layer", None, None)
    return jax.shard_map(
        functools.partial(per_device, sizes),
        mesh=mesh,
        in_specs=(table, table, table, table, row, table, table, table, row),
        out_specs=(table, table),
        check_vma=False,
    )
```
